32 devices in a mesh: fsdp: 4 (over y, x), ctx: 2 (over core), tp: 4 (over z).
Axes of the slice: x: 2, y: 2, z: 4, core: 2. Of those that a mesh axis runs over, the one named last changes fastest.
Arguments:
- inputs: bfloat16 [8, 196, 768], P('fsdp', 'ctx'), may hold values from -6 to 6
- norm1_gain: bfloat16 [768], P('fsdp'), may hold values from 0.25 to 1.75
- norm1_bias: bfloat16 [768], P('fsdp'), may hold values from -1.75 to 1.75
- qkv_weight: bfloat16 [768, 3, 768], P('fsdp', None, 'tp'), may hold values from -0.21875 to 0.21875
- qv_bias: bfloat16 [2, 12, 64], P(None, 'tp', 'fsdp'), may hold values from -3 to 3
- proj_weight: bfloat16 [768, 768], P('tp', 'fsdp'), may hold values from -0.875 to 0.875
- proj_bias: bfloat16 [768], P('fsdp'), may hold values from -3 to 3
- norm2_gain: bfloat16 [768], P('fsdp'), may hold values from 0.25 to 1.75
- norm2_bias: bfloat16 [768], P('fsdp'), may hold values from -1.75 to 1.75
- fc1_weight: bfloat16 [768, 3072], P('fsdp', 'tp'), may hold values from -0.21875 to 0.21875
- fc1_bias: bfloat16 [48, 64], P('tp', 'fsdp'), may hold values from -3 to 3
- fc2_weight: bfloat16 [3072, 768], P('tp', 'fsdp'), may hold values from -0.109375 to 0.109375
- fc2_bias: bfloat16 [768], P('fsdp'), may hold values from -3 to 3
- cotangent: bfloat16 [8, 196, 768], P('fsdp', 'ctx'), may hold values from -6 to 6
Outputs:
- output: bfloat16 [8, 196, 768], P('fsdp', 'ctx')
- input_grad: float32 [8, 196, 768], P('fsdp', 'ctx')
- norm1_gain_grad: float32 [768], P('fsdp')
- norm1_bias_grad: float32 [768], P('fsdp')
- qkv_weight_grad: float32 [768, 3, 768], P('fsdp', None, 'tp')
- qv_bias_grad: float32 [2, 12, 64], P(None, 'tp', 'fsdp')
- proj_weight_grad: float32 [768, 768], P('tp', 'fsdp')
- proj_bias_grad: float32 [768], P('fsdp')
- norm2_gain_grad: float32 [768], P('fsdp')
- norm2_bias_grad: float32 [768], P('fsdp')
- fc1_weight_grad: float32 [768, 3072], P('fsdp', 'tp')
- fc1_bias_grad: float32 [48, 64], P('tp', 'fsdp')
- fc2_weight_grad: float32 [3072, 768], P('tp', 'fsdp')
- fc2_bias_grad: float32 [768], P('fsdp')
The draws below stay inside these ranges and needn't reach their ends.
All inputs are finite; a program needn't handle non-finite values.
Results may differ from the reference program's by a relative error of at most 0.02.
Values may be sent and summed in bfloat16 or wider, within the bound.
No kernel may reach another device: no remote copies, remote signals or barrier semaphores. Data moves between devices by JAX's collectives and lax.ppermute only.
A program may use at most 64 MiB of HBM per device.

```python
import math
import jax
import jax.numpy as jnp
from jax import lax

D = 768
H = 12
HD = 64
FF = 3072
PLACES = 196
FRAMES = 8


def block_levels(key, dims, split, smallest, largest):
    def one(dim, shards_of):
        draws = jax.random.uniform(jax.random.fold_in(jax.random.fold_in(key, 6), dim), (shards_of,), jnp.float32, smallest / len(split), largest / len(split))
        return jnp.repeat(jnp.exp(draws), dims[dim] // shards_of).reshape((-1,) + (1,) * (len(dims) - dim - 1))

    gain = one(*split[0])
    for cut in split[1:]:
        gain = gain * one(*cut)
    return gain


def scatter_about(rng, dims, scale, bound, shards=(), kind=jnp.bfloat16):
    drawn = scale * jax.random.normal(rng, dims, jnp.float32)
    if shards:
        drawn = drawn * block_levels(rng, dims, shards, -0.22, 0.18)
    return jnp.clip(drawn, -bound, bound).astype(kind)


def setup_inputs(seed: int = 0) -> dict:
    key_list = jax.random.split(jax.random.key(seed), 15)
    return {
        "inputs": scatter_about(key_list[0], (FRAMES, PLACES, D), 1.0, 6.0, ((0, 4), (1, 2))),
        "norm1_gain": jnp.clip(1.0 + 0.15 * jax.random.normal(key_list[1], (D,), jnp.float32), 0.25, 1.75).astype(jnp.bfloat16),
        "norm1_bias": scatter_about(key_list[2], (D,), 0.3, 1.75, ((0, 4),)),
        "qkv_weight": scatter_about(key_list[3], (D, 3, D), D ** -0.5, 0.21875, ((0, 4), (2, 4))),
        "qv_bias": scatter_about(key_list[4], (2, H, HD), 0.5, 3.0, ((1, 4), (2, 4))),
        "proj_weight": scatter_about(key_list[5], (D, D), (D // 16) ** -0.5, 0.875, ((0, 4), (1, 4))),
        "proj_bias": scatter_about(key_list[6], (D,), 0.5, 3.0, ((0, 4),)),
        "norm2_gain": jnp.clip(1.0 + 0.15 * jax.random.normal(key_list[7], (D,), jnp.float32), 0.25, 1.75).astype(jnp.bfloat16),
        "norm2_bias": scatter_about(key_list[8], (D,), 0.3, 1.75, ((0, 4),)),
        "fc1_weight": scatter_about(key_list[9], (D, FF), D ** -0.5, 0.21875, ((0, 4), (1, 4))),
        "fc1_bias": scatter_about(key_list[10], (FF // HD, HD), 0.5, 3.0, ((0, 4), (1, 4))),
        "fc2_weight": scatter_about(key_list[11], (FF, D), FF ** -0.5, 0.109375, ((0, 4), (1, 4))),
        "fc2_bias": scatter_about(key_list[12], (D,), 0.5, 3.0, ((0, 4),)),
        "cotangent": scatter_about(key_list[13], (FRAMES, PLACES, D), 1.0, 6.0, ((0, 4), (1, 2))),
    }


@jax.custom_vjp
def low(v):
    return lax.optimization_barrier(v.astype(jnp.bfloat16)).astype(jnp.float32)

@jax.custom_vjp
def low_back(v):
    return v

def low_keep(v):
    return (low(v), None)

def low_pass(kept, grad):
    return (grad,)

def back_keep(v):
    return (v, None)

def back_low(kept, grad):
    return (low(grad),)
low.defvjp(low_keep, low_pass)
low_back.defvjp(back_keep, back_low)
HIGHEST = lax.Precision.HIGHEST
EPSILON = 1e-06
QUERY_SCALE = 0.125

def layer_norm(values, norm_gain, norm_bias):
    average = lax.optimization_barrier(jnp.mean(values, axis=-1, keepdims=True))
    centred = values - average
    variance = lax.optimization_barrier(jnp.mean(centred * centred, axis=-1, keepdims=True))
    return centred * lax.rsqrt(variance + EPSILON) * norm_gain + norm_bias

def layer_forward(params, frames):
    norm1_gain, norm1_bias, qkv_weight, qv_bias, proj_weight, proj_bias, norm2_gain, norm2_bias, fc1_weight, fc1_bias, fc2_weight, fc2_bias = params
    frame_count = frames.shape[0]
    place_count = frames.shape[1]
    head_shape = (frame_count, place_count, H, HD)
    normed_one = low(layer_norm(frames, norm1_gain, norm1_bias))
    projected = jnp.einsum('gpd,dce->gpce', normed_one, qkv_weight, precision=HIGHEST)
    bias_flat = qv_bias.reshape(2, -1)
    queries = low(low_back((projected[:, :, 0] + bias_flat[0]) * QUERY_SCALE))
    key_rows = low(low_back(projected[:, :, 1]))
    value_rows = low(low_back(projected[:, :, 2] + bias_flat[1]))
    scores = low_back(jnp.einsum('gqhd,gkhd->ghqk', queries.reshape(head_shape), key_rows.reshape(head_shape), precision=HIGHEST))
    soft_probs = jax.nn.softmax(scores, axis=-1)
    attended = jnp.einsum('ghqk,gkhd->gqhd', low(soft_probs), value_rows.reshape(head_shape), precision=HIGHEST)
    attended = low(low_back(attended.reshape(frame_count, place_count, D)))
    branch = low_back(jnp.einsum('gpe,ed->gpd', attended, proj_weight, precision=HIGHEST))
    middle = frames + branch + proj_bias
    normed_two = low(layer_norm(middle, norm2_gain, norm2_bias))
    pre_act = low_back(jnp.einsum('gpd,df->gpf', normed_two, fc1_weight, precision=HIGHEST) + fc1_bias.reshape(-1))
    hidden = low(jax.nn.gelu(pre_act, approximate=False))
    branch_two = low_back(jnp.einsum('gpf,fd->gpd', hidden, fc2_weight, precision=HIGHEST))
    return middle + branch_two + fc2_bias

def reference(inputs, norm1_gain, norm1_bias, qkv_weight, qv_bias, proj_weight, proj_bias, norm2_gain, norm2_bias, fc1_weight, fc1_bias, fc2_weight, fc2_bias, cotangent):
    params = tuple((weight_item.astype(jnp.float32) for weight_item in (norm1_gain, norm1_bias, qkv_weight, qv_bias, proj_weight, proj_bias, norm2_gain, norm2_bias, fc1_weight, fc1_bias, fc2_weight, fc2_bias)))
    block_frames = math.gcd(FRAMES, 16)
    block_count = FRAMES // block_frames
    in_blocks = inputs.astype(jnp.float32).reshape(block_count, block_frames, PLACES, D)
    cot_blocks = cotangent.astype(jnp.float32).reshape(block_count, block_frames, PLACES, D)

    def one_block(running, block_pair):
        frames, cot_block = block_pair
        result, pull_back = jax.vjp(layer_forward, params, frames)
        grad_params, grad_frames = pull_back(cot_block)
        running = jax.tree.map(jnp.add, running, grad_params)
        return (running, (result, grad_frames))
    start = jax.tree.map(jnp.zeros_like, params)
    totals, (results, grad_inputs) = lax.scan(one_block, start, (in_blocks, cot_blocks))
    output = results.reshape(FRAMES, PLACES, D).astype(jnp.bfloat16)
    input_grad = grad_inputs.reshape(FRAMES, PLACES, D)
    return (output, input_grad, totals[0], totals[1], totals[2], totals[3], totals[4], totals[5], totals[6], totals[7], totals[8], totals[9], totals[10], totals[11])
```

```python
import jax
import jax.numpy as jnp
from jax import lax
from jax.sharding import PartitionSpec as P

HD = 64
EPSILON = 1e-06
QUERY_SCALE = 0.125
F32 = jnp.float32
LOW = jnp.bfloat16


def dot(left, right, dims):
    return lax.dot_general(left, right, (dims, ((), ())), preferred_element_type=F32)


NN = ((1,), (0,))
NT = ((1,), (1,))
TN = ((0,), (0,))


def exact_gelu(values):
    return jax.nn.gelu(values, approximate=False)


def normalise(values):
    average = jnp.mean(values, axis=-1, keepdims=True)
    centred = values - average
    variance = jnp.mean(centred * centred, axis=-1, keepdims=True)
    inverse = lax.rsqrt(variance + EPSILON)
    return centred * inverse, inverse


def norm_backward(grad_normed, normal, inverse, norm_gain):
    scaled = grad_normed * norm_gain
    mean_grad = jnp.mean(scaled, axis=-1, keepdims=True)
    mean_cross = jnp.mean(scaled * normal, axis=-1, keepdims=True)
    return inverse * (scaled - mean_grad - normal * mean_cross)


def xor_pairs(size, step):
    return [(i, i ^ step) for i in range(size)]


def build(nf, nc, nt):
    def local(
        inputs,
        norm1_gain,
        norm1_bias,
        qkv_weight,
        qv_bias,
        proj_weight,
        proj_bias,
        norm2_gain,
        norm2_bias,
        fc1_weight,
        fc1_bias,
        fc2_weight,
        fc2_bias,
        cotangent,
    ):
        frames, half, width = inputs.shape
        shard = width // nf
        heads = qv_bias.shape[1]
        inner = heads * HD
        ff = fc1_weight.shape[1]
        pad = -half % 8
        padded = half + pad
        rows = 2 * padded
        block = -(-(rows // nt) // 8) * 8
        starts = [rows // nt * j // 8 * 8 for j in range(nt)]
        chunk = width // 8
        direct = nf == 4
        c = lax.axis_index("ctx")
        f = lax.axis_index("fsdp")
        t = lax.axis_index("tp")
        b = f if direct else 0
        start_of = jnp.asarray(starts, jnp.int32)

        def other_core(value):
            return lax.ppermute(value, "ctx", [(0, 1), (1, 0)])

        def to_tp(value, k):
            return lax.ppermute(value, "tp", xor_pairs(nt, k))

        def to_fsdp(value, k):
            return lax.ppermute(value, "fsdp", xor_pairs(nf, k))

        def pick(value, index, axis=0):
            return lax.dynamic_index_in_dim(value, index, axis, False)

        def frame(keep, received):
            zero = jnp.zeros((pad, width), keep.dtype)
            return jnp.concatenate([keep, zero, received, zero], 0)

        x_recv = other_core(pick(inputs, 1 - c))
        cot_recv = other_core(pick(cotangent, 1 - c))

        mark = (jnp.arange(nf) == f).astype(LOW)
        vectors = jnp.stack([norm1_gain, norm1_bias, proj_bias, norm2_gain, norm2_bias, fc2_bias])
        vectors = (vectors[:, None, :] * mark[None, :, None]).reshape(6, width)
        up_bias = (fc1_bias[:, None, :] * mark[None, :, None]).reshape(1, ff)
        qv_flat = (qv_bias[:, :, None, :] * mark[None, None, :, None]).reshape(1, 2 * inner)
        qv_flat = jnp.pad(qv_flat, ((0, 0), (0, width - 2 * inner)))
        small = jnp.concatenate([vectors, up_bias, qv_flat], 0)
        small = jnp.concatenate(
            [small[:, : 3 * inner], jnp.pad(small[:, 3 * inner :], ((0, 0), (0, 6 * inner - width)))], 0
        )

        qkv_rows = qkv_weight.reshape(shard, 3 * inner)
        if direct:
            half_qkv = lax.dynamic_slice_in_dim(qkv_rows, c * chunk, chunk, 0)
            sent = jnp.concatenate([half_qkv, small], 0)
            got = [to_fsdp(sent, k) for k in (1, 2, 3)]
            proj_half = lax.dynamic_slice_in_dim(proj_weight.T, c * chunk, chunk, 0)
            proj_parts = [proj_half] + [to_tp(proj_half, k) for k in range(1, nt)]
            shared = [other_core(g) for g in got]
            qkv_all = jnp.zeros((4, 2, chunk, 3 * inner), LOW)
            qkv_all = lax.dynamic_update_slice(qkv_all, qkv_rows.reshape(1, 2, chunk, 3 * inner), (f, 0, 0, 0))
            small_all = small.astype(F32)
            for k in (1, 2, 3):
                qkv_all = lax.dynamic_update_slice(qkv_all, got[k - 1][None, None, :chunk], (f ^ k, c, 0, 0))
                qkv_all = lax.dynamic_update_slice(qkv_all, shared[k - 1][None, None, :chunk], (f ^ k, 1 - c, 0, 0))
                small_all = small_all + got[k - 1][chunk:].astype(F32)
            rest = jnp.concatenate(
                [
                    lax.dynamic_slice_in_dim(fc1_weight, c * chunk, chunk, 0),
                    lax.dynamic_slice_in_dim(fc2_weight.T, c * chunk, chunk, 0),
                ]
                + proj_parts,
                1,
            )
            rest_got = [rest] + [to_fsdp(rest, k) for k in (1, 2, 3)]
            rest_shared = [other_core(g) for g in rest_got]
            rest_all = jnp.zeros((4, 2, chunk, rest.shape[1]), LOW)
            for k in range(4):
                rest_all = lax.dynamic_update_slice(rest_all, rest_got[k][None, None], (f ^ k, c, 0, 0))
                rest_all = lax.dynamic_update_slice(rest_all, rest_shared[k][None, None], (f ^ k, 1 - c, 0, 0))
        else:
            qkv_all = lax.all_gather(qkv_rows, "fsdp", axis=0, tiled=True)
            small_all = jnp.sum(lax.all_gather(small, "fsdp", axis=0).astype(F32), 0)
            proj_t = proj_weight.T
            proj_parts = [proj_t] + [to_tp(proj_t, k) for k in range(1, nt)]
            rest = jnp.concatenate([fc1_weight, fc2_weight.T] + proj_parts, 1)
            rest_all = lax.all_gather(rest, "fsdp", axis=0, tiled=True)
        qkv_all = qkv_all.reshape(width, 3 * inner)
        rest_all = rest_all.reshape(width, -1)
        small_all = jnp.concatenate([small_all[:8], small_all[8:, : width - 3 * inner]], 1)
        gain_one, bias_one, proj_b, gain_two, bias_two, down_b, up_b = [small_all[i : i + 1] for i in range(7)]
        query_b, value_b = small_all[7:8, :inner], small_all[7:8, inner : 2 * inner]
        w_up, w_down_t, w_proj_t = rest_all[:, :ff], rest_all[:, ff : 2 * ff], rest_all[:, 2 * ff :]

        stream = frame(pick(inputs, c), x_recv).astype(F32)
        normal_one, inverse_one = normalise(stream)
        normed_low = (normal_one * gain_one + bias_one).astype(LOW)
        projected = dot(normed_low, qkv_all, NN)
        query = ((projected[:, :inner] + query_b) * QUERY_SCALE).astype(LOW)
        key = projected[:, inner : 2 * inner].astype(LOW)
        value = (projected[:, 2 * inner :] + value_b).astype(LOW)
        valid = (jnp.arange(rows) % padded < half)[None]
        soft = []
        attended = []
        for h in range(heads):
            cut = slice(h * HD, (h + 1) * HD)
            scores = jnp.where(valid, dot(query[:, cut], key[:, cut], NT), -1e30)
            exponent = jnp.exp(scores - jnp.max(scores, -1, keepdims=True))
            soft.append(exponent / jnp.sum(exponent, -1, keepdims=True))
            attended.append(dot(soft[h].astype(LOW), value[:, cut], NN).astype(LOW))
        attended = jnp.concatenate(attended, 1)
        att = [attended] + [to_tp(attended, k) for k in range(1, nt)]

        grad_out_low = frame(pick(cotangent, c), cot_recv)
        grad_out = grad_out_low.astype(F32)
        branch = sum(dot(att[k], w_proj_t[:, k * inner : (k + 1) * inner], NT) for k in range(nt))
        middle = stream + branch + proj_b
        normal_two, inverse_two = normalise(middle)
        normed2_low = (normal_two * gain_two + bias_two).astype(LOW)
        pre_act = dot(normed2_low, w_up, NN) + up_b
        activated, gelu_pull = jax.vjp(exact_gelu, pre_act)
        hidden = activated.astype(LOW)
        grad_pre = gelu_pull(dot(grad_out_low, w_down_t, NN))[0].astype(LOW)
        grad_normed_two = dot(grad_pre, w_up, NT)
        part_middle = grad_out * (1.0 / nt) + norm_backward(grad_normed_two, normal_two, inverse_two, gain_two)
        part_low = part_middle.astype(LOW)
        part_att = dot(part_low, w_proj_t, NN)
        att_got = [to_tp(part_att[:, k * inner : (k + 1) * inner].astype(LOW), k) for k in range(1, nt)]

        out_part = dot(hidden, w_down_t, NT)

        def row_block(value, j):
            return lax.dynamic_slice_in_dim(value, pick(start_of, j), block, 0)

        out_got = [to_tp(row_block(out_part, t ^ k).astype(LOW), k) for k in range(1, nt)]
        out_sum = row_block(out_part, t) + row_block(middle, t) + down_b
        for g in out_got:
            out_sum = out_sum + g.astype(F32)
        out_own = out_sum.astype(LOW)

        def whole_rows(own):
            whole = jnp.zeros((rows, width), own.dtype)
            whole = lax.dynamic_update_slice(whole, own, (pick(start_of, t), 0))
            for k in range(1, nt):
                whole = lax.dynamic_update_slice(whole, to_tp(own, k), (pick(start_of, t ^ k), 0))
            theirs = other_core(whole[padded : padded + half])
            mine = whole[:half]
            return jnp.stack([jnp.where(c == 0, mine, theirs), jnp.where(c == 0, theirs, mine)])

        output = whole_rows(out_own)

        grad_rest = jnp.concatenate(
            [dot(normed2_low, grad_pre, TN), dot(grad_out_low, hidden, TN), dot(part_low, jnp.concatenate(att, 1), TN)], 1
        )

        def scatter(grad):
            if not direct:
                total = lax.psum(grad.astype(LOW), "ctx")
                total = lax.psum_scatter(total, "fsdp", scatter_dimension=0, tiled=True)
                return total.astype(F32)
            parts = grad.reshape(4, 2, chunk, grad.shape[1])
            keep, sent = pick(parts, c, 1), pick(parts, 1 - c, 1)
            total = keep + other_core(sent.astype(LOW)).astype(F32)
            own = pick(total, f)
            for k in (1, 2, 3):
                own = own + to_fsdp(pick(total, f ^ k).astype(LOW), k).astype(F32)
            return own

        def both_halves(own):
            if not direct:
                return own
            theirs = other_core(own.astype(LOW)).astype(F32)
            return jnp.concatenate([jnp.where(c == 0, own, theirs), jnp.where(c == 0, theirs, own)], 0)

        rest_own = scatter(grad_rest)
        proj_own = rest_own[:, 2 * ff : 2 * ff + inner]
        for k in range(1, nt):
            cut = rest_own[:, 2 * ff + k * inner : 2 * ff + (k + 1) * inner]
            proj_own = proj_own + to_tp(cut.astype(LOW), k).astype(F32)
        rest_final = both_halves(jnp.concatenate([rest_own[:, : 2 * ff], proj_own], 1))
        fc1_grad = rest_final[:, :ff]
        fc2_grad = rest_final[:, ff : 2 * ff].T
        proj_grad = rest_final[:, 2 * ff :].T

        grad_att = part_att[:, :inner]
        for g in att_got:
            grad_att = grad_att + g.astype(F32)
        grad_att = grad_att.astype(LOW)
        grads = [[], [], []]
        for h in range(heads):
            cut = slice(h * HD, (h + 1) * HD)
            grad_soft = dot(grad_att[:, cut], value[:, cut], NT)
            delta = jnp.sum(soft[h] * grad_soft, -1, keepdims=True)
            grad_scores = (soft[h] * (grad_soft - delta)).astype(LOW)
            grads[0].append(dot(grad_scores, key[:, cut], NN).astype(LOW) * QUERY_SCALE)
            grads[1].append(dot(grad_scores, query[:, cut], TN).astype(LOW))
            grads[2].append(dot(soft[h].astype(LOW), grad_att[:, cut], TN).astype(LOW))
        grad_qkv = jnp.concatenate(grads[0] + grads[1] + grads[2], 1)
        grad_normed_one = dot(grad_qkv, qkv_all, NT)
        part_input = part_middle + norm_backward(grad_normed_one, normal_one, inverse_one, gain_one)

        def total_rows(value):
            return jnp.sum(value, 0, keepdims=True)

        small_part = jnp.concatenate(
            [
                total_rows(grad_normed_one * normal_one),
                total_rows(grad_normed_one),
                total_rows(part_middle),
                total_rows(grad_normed_two * normal_two),
                total_rows(grad_normed_two),
                total_rows(grad_out) * (1.0 / nt),
                jnp.zeros((2, width), F32),
            ],
            0,
        )

        def input_block(k):
            return jnp.concatenate([row_block(part_input, t ^ k), small_part], 0)

        in_sum = input_block(0)
        for k in range(1, nt):
            in_sum = in_sum + to_tp(input_block(k).astype(LOW), k).astype(F32)
        input_grad = whole_rows(in_sum[:block].astype(LOW)).astype(F32)
        vector_sums = in_sum[block : block + 6].reshape(6, nf, shard)

        up_sum = jnp.sum(grad_pre.astype(F32), 0).reshape(-1, nf, fc1_bias.shape[1])
        both = grad_qkv.astype(F32)
        qv_sum = jnp.stack([jnp.sum(both[:, :inner], 0), jnp.sum(both[:, 2 * inner :], 0)])
        qv_sum = qv_sum.reshape(2 * heads, nf, qv_bias.shape[2])
        small_grads = jnp.concatenate(
            [
                vector_sums.transpose(1, 0, 2).reshape(nf, -1),
                up_sum.transpose(1, 0, 2).reshape(nf, -1),
                qv_sum.transpose(1, 0, 2).reshape(nf, -1),
            ],
            1,
        )
        if direct:
            own = pick(small_grads, f)
            for k in (1, 2, 3):
                own = own + to_fsdp(pick(small_grads, f ^ k).astype(LOW)[None], k)[0].astype(F32)
            own = own + other_core(own.astype(LOW)[None])[0].astype(F32)
        else:
            own = pick(lax.psum(small_grads, ("fsdp", "ctx")), f)
        vector_grads = own[: 6 * shard].reshape(6, shard)
        up_grad = own[6 * shard : 6 * shard + fc1_bias.size].reshape(fc1_bias.shape)
        qv_grad = own[6 * shard + fc1_bias.size :].reshape(qv_bias.shape)

        qkv_grad = both_halves(scatter(dot(normed_low, grad_qkv, TN))).reshape(qkv_weight.shape)
        return (
            output,
            input_grad,
            vector_grads[0],
            vector_grads[1],
            qkv_grad,
            qv_grad,
            proj_grad,
            vector_grads[2],
            vector_grads[3],
            vector_grads[4],
            fc1_grad,
            up_grad,
            fc2_grad,
            vector_grads[5],
        )

    return local


def solution(mesh):
    sizes = mesh.shape
    return jax.shard_map(
        build(sizes["fsdp"], sizes["ctx"], sizes["tp"]),
        mesh=mesh,
        in_specs=(
            P("fsdp", "ctx", None),
            P("fsdp"),
            P("fsdp"),
            P("fsdp", None, "tp"),
            P(None, "tp", "fsdp"),
            P("tp", "fsdp"),
            P("fsdp"),
            P("fsdp"),
            P("fsdp"),
            P("fsdp", "tp"),
            P("tp", "fsdp"),
            P("tp", "fsdp"),
            P("fsdp"),
            P("fsdp", "ctx", None),
        ),
        out_specs=(
            P("fsdp", "ctx", None),
            P("fsdp", "ctx", None),
            P("fsdp"),
            P("fsdp"),
            P("fsdp", None, "tp"),
            P(None, "tp", "fsdp"),
            P("tp", "fsdp"),
            P("fsdp"),
            P("fsdp"),
            P("fsdp"),
            P("fsdp", "tp"),
            P("tp", "fsdp"),
            P("tp", "fsdp"),
            P("fsdp"),
        ),
        check_vma=False,
    )
```

```python
import functools

import jax
import jax.numpy as jnp
from jax import lax
from jax.experimental import pallas as pl
from jax.experimental.pallas import tpu as pltpu
from jax.sharding import PartitionSpec as P

HD = 64
EPSILON = 1e-06
QUERY_SCALE = 0.125
F32 = jnp.float32
LOW = jnp.bfloat16
NN = ((1,), (0,))
NT = ((1,), (1,))
TN = ((0,), (0,))
VMEM = pl.BlockSpec(memory_space=pltpu.VMEM)


def dot(left, right, dims):
    return lax.dot_general(left, right, (dims, ((), ())), preferred_element_type=F32)


def shape(dims, kind):
    return jax.ShapeDtypeStruct(tuple(dims), kind)


def call(kernel, outs, args, scratch=(), name=None, mib=24, out_specs=None):
    return pl.pallas_call(
        kernel,
        out_shape=tuple(outs),
        in_specs=[VMEM] * len(args),
        out_specs=out_specs or tuple([VMEM] * len(outs)),
        scratch_shapes=list(scratch),
        name=name,
        compiler_params=pltpu.CompilerParams(vmem_limit_bytes=mib << 20),
    )(*args)


def gelu_and_slope(v):
    cdf = 0.5 * (1.0 + lax.erf(v * 0.7071067811865476))
    density = jnp.exp(-0.5 * v * v) * 0.3989422804014327
    return v * cdf, cdf + v * density


def mean(v):
    return jnp.mean(v, axis=-1, keepdims=True)


def total_rows(v):
    return jnp.sum(v, axis=0, keepdims=True)


def normalise(v):
    centred = v - mean(v)
    inverse = lax.rsqrt(mean(centred * centred) + EPSILON)
    return centred * inverse, inverse


def norm_backward(grad_normed, normal, inverse, gain):
    scaled = grad_normed * gain
    return inverse * (scaled - mean(scaled) - normal * mean(scaled * normal))


def xor_pairs(size, step):
    return [(i, i ^ step) for i in range(size)]


def lanes(parts):
    return jnp.concatenate(parts, axis=1)


def rows_of(parts):
    return jnp.concatenate(parts, axis=0)


class Sizes:
    def __init__(self, nf, nt, inputs, qv_bias, fc1_weight):
        self.nf, self.nt = nf, nt
        _, self.half, self.width = inputs.shape
        self.shard = self.width // nf
        self.heads = qv_bias.shape[1]
        self.inner = self.heads * HD
        self.ff = fc1_weight.shape[1]
        self.pad = -self.half % 8
        self.padded = self.half + self.pad
        self.rows = 2 * self.padded
        self.block = -(-(self.rows // nt) // 8) * 8
        self.chunk = self.width // 8
        self.direct = nf == 4
        self.cols = 2 * self.ff + nt * self.inner

    def start(self, j):
        return pl.multiple_of(j * (self.rows // self.nt) // 8 * 8, 8)

    def base(self):
        return lax.axis_index("fsdp") if self.direct else 0

    def core(self):
        return lax.axis_index("ctx") if self.direct else 0


EXTRA = 16
UP_AT, QV_AT = 256, 384


def pack_kernel(z, qkv, proj, vec, up_b, qv_b, sent, proj_half):
    c = lax.axis_index("ctx")
    cut = pl.ds(pl.multiple_of(c * z.chunk, 16), z.chunk)
    for i in range(3):
        sent[: z.chunk, i * z.inner : (i + 1) * z.inner] = qkv[i, cut, :]
    tail = jnp.zeros((EXTRA, 3 * z.inner), LOW)
    sent[z.chunk :, :] = tail
    sent[z.chunk : z.chunk + 8, : z.shard] = vec[...]
    sent[z.chunk : z.chunk + up_b.shape[0], UP_AT : UP_AT + up_b.shape[1]] = up_b[...]
    sent[z.chunk : z.chunk + qv_b.shape[0], QV_AT : QV_AT + qv_b.shape[1]] = qv_b[...]
    whole = proj[...].astype(F32).T.astype(LOW)
    proj_half[...] = jnp.where(c == 0, whole[: z.chunk], whole[z.chunk :])


def frame_kernel(z, keep, received, stream, normal, inverse):
    zero = jnp.zeros((z.pad, z.width), F32)
    values = rows_of([keep[...].astype(F32), zero, received[...].astype(F32), zero])
    stream[...] = values.astype(LOW)
    if normal is not None:
        n, i = normalise(values)
        normal[...] = n
        inverse[...] = jnp.broadcast_to(i, inverse.shape)


def cot_kernel(z, keep, received, stream):
    frame_kernel(z, keep, received, stream, None, None)


def attend_kernel(z, *refs):
    refs = list(refs)
    if z.direct:
        qkv, sent = refs[:2]
        got, shared = refs[2:5], refs[5:8]
        refs = refs[8:]
    else:
        qkv, vec_in, up_in, qv_in = refs[:4]
        refs = refs[4:]
    normal, small, w_out, normed_out, act, attended, soft_out = refs[:7]
    c, b = z.core(), z.base()
    if z.direct:
        gather = refs[7]
        own = lanes([qkv[i] for i in range(3)])
        w_out[b, 0] = own[: z.chunk]
        w_out[b, 1] = own[z.chunk :]
        gather[b] = sent[z.chunk :, :].astype(F32)
        for k in (1, 2, 3):
            w_out[b ^ k, c] = got[k - 1][: z.chunk, :]
            w_out[b ^ k, 1 - c] = shared[k - 1][: z.chunk, :]
            gather[b ^ k] = got[k - 1][z.chunk :, :].astype(F32)
        blocks = [gather[i] for i in range(4)]
        wide = blocks[0].shape[1]
        up_w, qv_w = HD // 4, HD // 4
        vec = lanes([g[:8, : z.shard] for g in blocks])
        up = lanes([g[: z.ff // HD, UP_AT : UP_AT + up_w] for g in blocks])
        qv = lanes([g[: 2 * z.heads, QV_AT : QV_AT + qv_w] for g in blocks])
    else:
        w_out[...] = qkv[...]
        vec, up, qv = vec_in[...], up_in[...], qv_in[...]
    up_row = lanes([up[i : i + 1] for i in range(z.ff // HD)])
    query_b = lanes([qv[2 * h : 2 * h + 1] for h in range(z.heads)])
    value_b = lanes([qv[2 * h + 1 : 2 * h + 2] for h in range(z.heads)])
    small[...] = vec
    small[6:7, : z.ff] = up_row
    normed = (normal[...] * vec[0:1] + vec[1:2]).astype(LOW)
    normed_out[...] = normed
    projected = dot(normed, w_out[...].reshape(z.width, 3 * z.inner), NN)
    n = z.inner
    query = ((projected[:, :n] + query_b) * QUERY_SCALE).astype(LOW)
    key = projected[:, n : 2 * n].astype(LOW)
    value = (projected[:, 2 * n :] + value_b).astype(LOW)
    act[0] = query
    act[1] = key
    act[2] = value
    place = lax.broadcasted_iota(jnp.int32, (z.rows, z.rows), 1)
    valid = (place < z.half) | ((place >= z.padded) & (place < z.padded + z.half))
    done = []
    for h in range(z.heads):
        cut = slice(h * HD, (h + 1) * HD)
        scores = jnp.where(valid, dot(query[:, cut], key[:, cut], NT), -1e30)
        exponent = jnp.exp(scores - jnp.max(scores, axis=-1, keepdims=True))
        soft = exponent * (1.0 / jnp.sum(exponent, axis=-1, keepdims=True))
        soft_out[h] = soft
        done.append(dot(soft.astype(LOW), value[:, cut], NN).astype(LOW))
    attended[...] = lanes(done)


def feed_kernel(z, *refs):
    refs = list(refs)
    if z.direct:
        got, shared = refs[:4], refs[4:8]
        refs = refs[8:]
    else:
        whole = refs[0]
        refs = refs[1:]
    att = refs[: z.nt]
    stream, cot, small = refs[z.nt : z.nt + 3]
    (w_out, middle_out, hidden_out, normed_out, pre_out, part_out, low_out, own_att, small_out) = refs[
        z.nt + 3 : z.nt + 12
    ]
    sends = refs[z.nt + 12 :]
    c, b = z.core(), z.base()
    if z.direct:
        for k in range(4):
            w_out[b ^ k, c] = got[k][...]
            w_out[b ^ k, 1 - c] = shared[k][...]
    else:
        w_out[...] = whole[...]
    n = z.inner
    w_up = w_out[:, :, :, : z.ff].reshape(z.width, z.ff)
    w_down_t = w_out[:, :, :, z.ff : 2 * z.ff].reshape(z.width, z.ff)
    w_proj_t = w_out[:, :, :, 2 * z.ff :].reshape(z.width, z.nt * n)
    grad_out_low = cot[...]
    grad_out = grad_out_low.astype(F32)
    branch = dot(lanes([a[...] for a in att]), w_proj_t, NT)
    middle = stream[...].astype(F32) + branch + small[2:3]
    middle_out[...] = middle
    normal, inverse = normalise(middle)
    gain = small[3:4]
    normed = (normal * gain + small[4:5]).astype(LOW)
    normed_out[...] = normed
    hidden, slope = gelu_and_slope(dot(normed, w_up, NN) + small[6:7, : z.ff])
    hidden_out[...] = hidden.astype(LOW)
    grad_pre = (dot(grad_out_low, w_down_t, NN) * slope).astype(LOW)
    pre_out[...] = grad_pre
    grad_normed = dot(grad_pre, w_up, NT)
    part = grad_out * (1.0 / z.nt) + norm_backward(grad_normed, normal, inverse, gain)
    part_out[...] = part
    low = part.astype(LOW)
    low_out[...] = low
    grad_att = dot(low, w_proj_t, NN)
    own_att[...] = grad_att[:, :n]
    for k in range(1, z.nt):
        sends[k - 1][...] = grad_att[:, k * n : (k + 1) * n].astype(LOW)
    small_out[...] = jnp.zeros(small_out.shape, F32)
    small_out[2:3] = total_rows(part)
    small_out[3:4] = total_rows(grad_normed * normal)
    small_out[4:5] = total_rows(grad_normed)
    small_out[5:6] = total_rows(grad_out) * (1.0 / z.nt)
    small_out[6:7, : z.ff] = total_rows(grad_pre.astype(F32))


def down_kernel(z, hidden, w, middle, small, own, *rest):
    sends, scratch = rest[:-1], rest[-1]
    t = lax.axis_index("tp")
    w_down_t = w[:, :, :, z.ff : 2 * z.ff].reshape(z.width, z.ff)
    scratch[...] = dot(hidden[...], w_down_t, NT)
    mine = pl.ds(z.start(t), z.block)
    own[...] = scratch[mine, :] + middle[mine, :] + small[5:6]
    for k in range(1, z.nt):
        sends[k - 1][...] = scratch[pl.ds(z.start(t ^ k), z.block), :].astype(LOW)


def store_halves(z, value, at, keep, sent):
    c, b = z.core(), z.base()
    cols = pl.ds(at, value.shape[1])
    for j in range(4):
        first = value[j * 2 * z.chunk : j * 2 * z.chunk + z.chunk]
        second = value[j * 2 * z.chunk + z.chunk : (j + 1) * 2 * z.chunk]
        if z.direct:
            keep[j ^ b, :, cols] = jnp.where(c == 0, first, second)
            sent[j ^ b, :, cols] = jnp.where(c == 0, second, first).astype(LOW)
        else:
            keep[j, :, cols] = first
            sent[j, :, cols] = second.astype(LOW)


def rest_grad_kernel(z, normed, pre, cot, hidden, low, *refs):
    att, (keep, sent) = refs[:-2], refs[-2:]
    store_halves(z, dot(normed[...], pre[...], TN), 0, keep, sent)
    store_halves(z, dot(cot[...], hidden[...], TN), z.ff, keep, sent)
    store_halves(z, dot(low[...], lanes([a[...] for a in att]), TN), 2 * z.ff, keep, sent)


def sum_cores_kernel(keep, received, own, *sends):
    own[...] = keep[0] + received[0].astype(F32)
    for k in range(1, 4):
        sends[k - 1][...] = (keep[k] + received[k].astype(F32)).astype(LOW)


def sum_fsdp_kernel(z, own, *refs):
    got, (feed, proj_own), sends = refs[:3], refs[3:5], refs[5:]
    total = own[...] + sum(g[...].astype(F32) for g in got)
    feed[...] = total[:, : 2 * z.ff]
    n = z.inner
    proj_own[...] = total[:, 2 * z.ff : 2 * z.ff + n]
    for k in range(1, z.nt):
        sends[k - 1][...] = total[:, 2 * z.ff + k * n : 2 * z.ff + (k + 1) * n].astype(LOW)


def sum_tp_kernel(z, feed, proj_own, *refs):
    got, (sent, own) = refs[:-2], refs[-2:]
    total = proj_own[...] + sum(g[...].astype(F32) for g in got)
    own[:, : 2 * z.ff] = feed[...]
    own[:, 2 * z.ff :] = total
    sent[:, : 2 * z.ff] = feed[...].astype(LOW)
    sent[:, 2 * z.ff :] = total.astype(LOW)


def rest_final_kernel(z, own, theirs, up, down, proj):
    c = lax.axis_index("ctx")
    mine, other = own[...], theirs[...].astype(F32)
    both = rows_of([jnp.where(c == 0, mine, other), jnp.where(c == 0, other, mine)])
    up[...] = both[:, : z.ff]
    down[...] = both[:, z.ff : 2 * z.ff]
    proj[...] = both[:, 2 * z.ff :].T


def back_kernel(z, *refs):
    own_att, got = refs[0], refs[1 : z.nt]
    act, soft, w, normal, inverse, part, small, small_in = refs[z.nt : z.nt + 8]
    grads_out, qv_out, own = refs[z.nt + 8 : z.nt + 11]
    sends, scratch = refs[z.nt + 11 : -1], refs[-1]
    t = lax.axis_index("tp")
    grad_att = (own_att[...] + sum(g[...].astype(F32) for g in got)).astype(LOW)
    parts = [[], [], []]
    query, key, value = act[0], act[1], act[2]
    for h in range(z.heads):
        cut = slice(h * HD, (h + 1) * HD)
        ga = grad_att[:, cut]
        p = soft[h]
        grad_soft = dot(ga, value[:, cut], NT)
        delta = jnp.sum(p * grad_soft, axis=-1, keepdims=True)
        grad_scores = (p * (grad_soft - delta)).astype(LOW)
        parts[0].append((dot(grad_scores, key[:, cut], NN).astype(LOW).astype(F32) * QUERY_SCALE).astype(LOW))
        parts[1].append(dot(grad_scores, query[:, cut], TN).astype(LOW))
        parts[2].append(dot(p.astype(LOW), ga, TN).astype(LOW))
    grads = lanes(parts[0] + parts[1] + parts[2])
    grads_out[...] = grads
    n = z.inner
    qv_out[...] = total_rows(grads.astype(F32))
    grad_normed = dot(grads, w[...].reshape(z.width, 3 * n), NT)
    scratch[...] = part[...] + norm_backward(grad_normed, normal[...], inverse[:, :1], small[0:1])
    row = lax.broadcasted_iota(jnp.int32, (8, z.width), 0)
    vec = small_in[...]
    vec = jnp.where(row == 0, total_rows(grad_normed * normal[...]), vec)
    vec = jnp.where(row == 1, total_rows(grad_normed), vec)
    own[: z.block, :] = scratch[pl.ds(z.start(t), z.block), :]
    own[z.block :, :] = vec
    for k in range(1, z.nt):
        piece = rows_of([scratch[pl.ds(z.start(t ^ k), z.block), :], vec])
        sends[k - 1][...] = piece.astype(LOW)


def qkv_grad_kernel(z, normed, grads, keep, sent):
    store_halves(z, dot(normed[...], grads[...], TN), 0, keep, sent)


def sum_rows_kernel(z, own, *refs):
    got, (block, vec) = refs[:-2], refs[-2:]
    total = own[...] + sum(g[...].astype(F32) for g in got)
    block[...] = total[: z.block].astype(LOW)
    vec[...] = total[z.block :]


def sum_qkv_kernel(z, keep, received, vec, small, qv, own, *rest):
    sends, scratch = rest[:3], rest[3]
    b = z.base()
    vectors = vec[...]
    up = rows_of([small[6:7, i * HD : (i + 1) * HD] for i in range(z.ff // HD)])
    pieces = []
    for h in range(z.heads):
        pieces.append(qv[0:1, h * HD : (h + 1) * HD])
        pieces.append(qv[0:1, 2 * z.inner + h * HD : 2 * z.inner + (h + 1) * HD])
    qv_rows = rows_of(pieces)
    scratch[...] = jnp.zeros(scratch.shape, F32)
    w = HD // 4
    for i in range(4):
        scratch[i, :8, : z.shard] = vectors[:, i * z.shard : (i + 1) * z.shard]
        scratch[i, : z.ff // HD, UP_AT : UP_AT + w] = up[:, i * w : (i + 1) * w]
        scratch[i, : 2 * z.heads, QV_AT : QV_AT + w] = qv_rows[:, i * w : (i + 1) * w]
    own[: z.chunk, :] = keep[0] + received[0].astype(F32)
    own[z.chunk :, :] = scratch[b]
    for k in range(1, 4):
        sends[k - 1][: z.chunk, :] = (keep[k] + received[k].astype(F32)).astype(LOW)
        sends[k - 1][z.chunk :, :] = scratch[b ^ k].astype(LOW)


def sum_last_kernel(own, *refs):
    got, (total, sent) = refs[:3], refs[3:]
    value = own[...] + sum(g[...].astype(F32) for g in got)
    total[...] = value
    sent[...] = value.astype(LOW)


def qkv_final_kernel(z, own, theirs, qkv, vec, up, qv):
    c = lax.axis_index("ctx")
    mine, other = own[: z.chunk, :], theirs[: z.chunk, :].astype(F32)
    both = rows_of([jnp.where(c == 0, mine, other), jnp.where(c == 0, other, mine)])
    for i in range(3):
        qkv[i] = both[:, i * z.inner : (i + 1) * z.inner]
    tail = own[z.chunk :, :] + theirs[z.chunk :, :].astype(F32)
    w = HD // 4
    vec[...] = tail[:8, : z.shard]
    up[...] = tail[: z.ff // HD, UP_AT : UP_AT + w]
    qv[...] = tail[: 2 * z.heads, QV_AT : QV_AT + w]


def rows_kernel(z, own, *refs):
    got, (mine, theirs, scratch) = refs[:-3], refs[-3:]
    t = lax.axis_index("tp")
    for k in range(z.nt):
        piece = own if k == 0 else got[k - 1]
        scratch[pl.ds(z.start(t ^ k), z.block), :] = piece[...].astype(F32)
    mine[...] = scratch[: z.half, :].astype(mine.dtype)
    theirs[...] = scratch[z.padded : z.padded + z.half, :].astype(LOW)


def build(nf, nc, nt):
    def local(
        inputs,
        norm1_gain,
        norm1_bias,
        qkv_weight,
        qv_bias,
        proj_weight,
        proj_bias,
        norm2_gain,
        norm2_bias,
        fc1_weight,
        fc1_bias,
        fc2_weight,
        fc2_bias,
        cotangent,
    ):
        z = Sizes(nf, nt, inputs, qv_bias, fc1_weight)
        part = functools.partial
        rows, width, inner, ff, chunk, block = z.rows, z.width, z.inner, z.ff, z.chunk, z.block
        c = lax.axis_index("ctx")
        f = lax.axis_index("fsdp")

        def other_core(value):
            return lax.ppermute(value, "ctx", [(0, 1), (1, 0)])

        def to_tp(value, k):
            return lax.ppermute(value, "tp", xor_pairs(nt, k))

        def to_fsdp(value, k):
            return lax.ppermute(value, "fsdp", xor_pairs(nf, k))

        def pick(value, index):
            return lax.dynamic_index_in_dim(value, index, 0, False)

        qkv3 = qkv_weight.transpose(1, 0, 2)
        down_t = fc2_weight.T
        row = lax.broadcasted_iota(jnp.int32, (8, z.shard), 0)
        vec = jnp.zeros((8, z.shard), LOW)
        for i, v in enumerate((norm1_gain, norm1_bias, proj_bias, norm2_gain, norm2_bias, fc2_bias)):
            vec = jnp.where(row == i, v[None], vec)
        qv_rows = qv_bias.transpose(1, 0, 2).reshape(2 * z.heads, -1)

        x_recv = other_core(pick(inputs, 1 - c))
        if z.direct:
            sent, proj_half = call(
                part(pack_kernel, z),
                [shape((chunk + EXTRA, 3 * inner), LOW), shape((chunk, inner), LOW)],
                [qkv3, proj_weight, vec, fc1_bias, qv_rows],
                name="pack",
            )
            got = [to_fsdp(sent, k) for k in (1, 2, 3)]
            proj_parts = [proj_half] + [to_tp(proj_half, k) for k in range(1, nt)]
            shared = [other_core(g) for g in got]
            rest = jnp.concatenate(
                [lax.dynamic_slice_in_dim(w, c * chunk, chunk, 0) for w in (fc1_weight, down_t)] + proj_parts, 1
            )
            rest_got = [rest] + [to_fsdp(rest, k) for k in (1, 2, 3)]
            rest_in = rest_got + [other_core(g) for g in rest_got]
            qkv_in = [qkv3, sent] + got + shared
        else:
            whole = lax.all_gather(qkv3, "fsdp", axis=1, tiled=True)
            whole = whole.transpose(1, 0, 2).reshape(4, 2, chunk, 3 * inner)
            vec_all = lax.all_gather(vec.astype(F32), "fsdp", axis=1, tiled=True)
            up_all = lax.all_gather(fc1_bias.astype(F32), "fsdp", axis=1, tiled=True)
            qv_all = lax.all_gather(qv_rows.astype(F32), "fsdp", axis=1, tiled=True)
            qkv_in = [whole, vec_all, up_all, qv_all]
            proj_t = proj_weight.T
            rest = jnp.concatenate([fc1_weight, down_t, proj_t] + [to_tp(proj_t, k) for k in range(1, nt)], 1)
            rest_in = [lax.all_gather(rest, "fsdp", axis=0, tiled=True).reshape(4, 2, chunk, z.cols)]

        stream, normal_one, inverse_one = call(
            part(frame_kernel, z),
            [shape((rows, width), LOW), shape((rows, width), F32), shape((rows, 128), F32)],
            [pick(inputs, c), x_recv],
            name="frame",
        )
        cot_recv = other_core(pick(cotangent, 1 - c))
        (cot,) = call(
            part(cot_kernel, z), [shape((rows, width), LOW)], [pick(cotangent, c), cot_recv], name="cotangent"
        )

        small, w_qkv, normed_one, act, attended, soft = call(
            part(attend_kernel, z),
            [
                shape((8, width), F32),
                shape((4, 2, chunk, 3 * inner), LOW),
                shape((rows, width), LOW),
                shape((3, rows, inner), LOW),
                shape((rows, inner), LOW),
                shape((z.heads, rows, rows), F32),
            ],
            qkv_in + [normal_one],
            [pltpu.VMEM((4, EXTRA, 3 * inner), F32)] if z.direct else [],
            name="attend",
        )
        att = [attended] + [to_tp(attended, k) for k in range(1, nt)]

        (w_rest, middle, hidden, normed_two, grad_pre, part_middle, part_low, own_att, small_two, *att_sends) = call(
            part(feed_kernel, z),
            [
                shape((4, 2, chunk, z.cols), LOW),
                shape((rows, width), F32),
                shape((rows, ff), LOW),
                shape((rows, width), LOW),
                shape((rows, ff), LOW),
                shape((rows, width), F32),
                shape((rows, width), LOW),
                shape((rows, inner), F32),
                shape((8, width), F32),
            ]
            + [shape((rows, inner), LOW)] * (nt - 1),
            rest_in + att + [stream, cot, small],
            name="feed",
        )
        att_got = [to_tp(att_sends[k - 1], k) for k in range(1, nt)]

        out_own, *out_sends = call(
            part(down_kernel, z),
            [shape((block, width), F32)] + [shape((block, width), LOW)] * (nt - 1),
            [hidden, w_rest, middle, small],
            [pltpu.VMEM((rows, width), F32)],
            name="down",
        )
        out_got = [to_tp(out_sends[k - 1], k) for k in range(1, nt)]

        grad_shape = (4, chunk, z.cols)
        keep, sent = call(
            part(rest_grad_kernel, z),
            [shape(grad_shape, F32), shape(grad_shape, LOW)],
            [normed_two, grad_pre, cot, hidden, part_low] + att,
            name="rest_grad",
        )

        grads, qv_sum, in_own, *in_sends = call(
            part(back_kernel, z),
            [shape((rows, 3 * inner), LOW), shape((1, 3 * inner), F32), shape((block + 8, width), F32)]
            + [shape((block + 8, width), LOW)] * (nt - 1),
            [own_att] + att_got + [act, soft, w_qkv, normal_one, inverse_one, part_middle, small, small_two],
            [pltpu.VMEM((rows, width), F32)],
            name="back",
        )
        in_got = [to_tp(in_sends[k - 1], k) for k in range(1, nt)]
        keep_qkv, sent_qkv = call(
            part(qkv_grad_kernel, z),
            [shape((4, chunk, 3 * inner), F32), shape((4, chunk, 3 * inner), LOW)],
            [normed_one, grads],
            name="qkv_grad",
        )
        in_block, vec_sum = call(
            part(sum_rows_kernel, z),
            [shape((block, width), LOW), shape((8, width), F32)],
            [in_own] + in_got,
            name="sum_rows",
        )

        def whole_rows(own, kind):
            mine, theirs = call(
                part(rows_kernel, z),
                [shape((z.half, width), kind), shape((z.half, width), LOW)],
                [own] + [to_tp(own, k) for k in range(1, nt)],
                [pltpu.VMEM((rows, width), F32)],
                name="rows",
            )
            theirs = other_core(theirs).astype(kind)
            return jnp.stack([jnp.where(c == 0, mine, theirs), jnp.where(c == 0, theirs, mine)])

        input_grad = whole_rows(in_block, F32)
        (out_low,) = call(
            lambda own, *refs: refs[-1].__setitem__(
                Ellipsis, (own[...] + sum(g[...].astype(F32) for g in refs[:-1])).astype(LOW)
            ),
            [shape((block, width), LOW)],
            [out_own] + out_got,
            name="out_sum",
        )
        output = whole_rows(out_low, LOW)

        if z.direct:
            own, *sends = call(
                sum_cores_kernel,
                [shape((chunk, z.cols), F32)] + [shape((chunk, z.cols), LOW)] * 3,
                [keep, other_core(sent)],
                name="sum_cores",
            )
            feed_own, proj_own, *sends = call(
                part(sum_fsdp_kernel, z),
                [shape((chunk, 2 * ff), F32), shape((chunk, inner), F32)] + [shape((chunk, inner), LOW)] * (nt - 1),
                [own] + [to_fsdp(sends[k - 1], k) for k in (1, 2, 3)],
                name="sum_fsdp",
            )
            to_other, own = call(
                part(sum_tp_kernel, z),
                [shape((chunk, 2 * ff + inner), LOW), shape((chunk, 2 * ff + inner), F32)],
                [feed_own, proj_own] + [to_tp(sends[k - 1], k) for k in range(1, nt)],
                name="sum_tp",
            )
            fc1_grad, fc2_grad, proj_grad = call(
                part(rest_final_kernel, z),
                [shape((z.shard, ff), F32), shape((z.shard, ff), F32), shape((inner, z.shard), F32)],
                [own, other_core(to_other)],
                name="rest_final",
            )
            own, *sends = call(
                part(sum_qkv_kernel, z),
                [shape((chunk + EXTRA, 3 * inner), F32)] + [shape((chunk + EXTRA, 3 * inner), LOW)] * 3,
                [keep_qkv, other_core(sent_qkv), vec_sum, small_two, qv_sum],
                [pltpu.VMEM((4, EXTRA, 3 * inner), F32)],
                name="sum_qkv",
            )
            own, to_other = call(
                sum_last_kernel,
                [shape((chunk + EXTRA, 3 * inner), F32), shape((chunk + EXTRA, 3 * inner), LOW)],
                [own] + [to_fsdp(sends[k - 1], k) for k in (1, 2, 3)],
                name="sum_last",
            )
            qkv_grad, vec_grad, up_grad, qv_grad = call(
                part(qkv_final_kernel, z),
                [
                    shape((3, z.shard, inner), F32),
                    shape((8, z.shard), F32),
                    shape(fc1_bias.shape, F32),
                    shape(qv_rows.shape, F32),
                ],
                [own, other_core(to_other)],
                name="qkv_final",
            )
        else:

            def scatter(keep, sent):
                whole = jnp.stack([keep.astype(LOW), sent], 1).reshape(width, -1)
                whole = lax.psum(whole, "ctx")
                return lax.psum_scatter(whole, "fsdp", scatter_dimension=0, tiled=True).astype(F32)

            rest_own = scatter(keep, sent)
            fc1_grad, fc2_grad = rest_own[:, :ff], rest_own[:, ff : 2 * ff]
            proj_grad = rest_own[:, 2 * ff : 2 * ff + inner]
            for k in range(1, nt):
                cut = rest_own[:, 2 * ff + k * inner : 2 * ff + (k + 1) * inner]
                proj_grad = proj_grad + to_tp(cut.astype(LOW), k).astype(F32)
            proj_grad = proj_grad.T
            qkv_grad = scatter(keep_qkv, sent_qkv).reshape(z.shard, 3, inner).transpose(1, 0, 2)

            def own_columns(value):
                value = lax.psum(value, ("fsdp", "ctx"))
                return lax.dynamic_slice_in_dim(value, f * (value.shape[1] // nf), value.shape[1] // nf, 1)

            vec_grad = own_columns(vec_sum)
            up_grad = own_columns(small_two[6, :ff].reshape(-1, HD))
            qv_grad = own_columns(
                qv_sum.reshape(3, z.heads, HD)[0::2].transpose(1, 0, 2).reshape(2 * z.heads, HD)
            )
        return (
            output,
            input_grad,
            vec_grad[0],
            vec_grad[1],
            qkv_grad.transpose(1, 0, 2),
            qv_grad.reshape(z.heads, 2, -1).transpose(1, 0, 2),
            proj_grad,
            vec_grad[2],
            vec_grad[3],
            vec_grad[4],
            fc1_grad,
            up_grad,
            fc2_grad.T,
            vec_grad[5],
        )

    return local


def solution(mesh):
    sizes = mesh.shape
    return jax.shard_map(
        build(sizes["fsdp"], sizes["ctx"], sizes["tp"]),
        mesh=mesh,
        in_specs=(
            P("fsdp", "ctx", None),
            P("fsdp"),
            P("fsdp"),
            P("fsdp", None, "tp"),
            P(None, "tp", "fsdp"),
            P("tp", "fsdp"),
            P("fsdp"),
            P("fsdp"),
            P("fsdp"),
            P("fsdp", "tp"),
            P("tp", "fsdp"),
            P("tp", "fsdp"),
            P("fsdp"),
            P("fsdp", "ctx", None),
        ),
        out_specs=(
            P("fsdp", "ctx", None),
            P("fsdp", "ctx", None),
            P("fsdp"),
            P("fsdp"),
            P("fsdp", None, "tp"),
            P(None, "tp", "fsdp"),
            P("tp", "fsdp"),
            P("fsdp"),
            P("fsdp"),
            P("fsdp"),
            P("fsdp", "tp"),
            P("tp", "fsdp"),
            P("tp", "fsdp"),
            P("fsdp"),
        ),
        check_vma=False,
    )
```

```python
import functools

import jax
import jax.numpy as jnp
from jax import lax
from jax.experimental import pallas as pl
from jax.experimental.pallas import tpu as pltpu
from jax.sharding import PartitionSpec as P

HD = 64
EPSILON = 1e-06
QUERY_SCALE = 0.125
F32 = jnp.float32
LOW = jnp.bfloat16
NN = ((1,), (0,))
NT = ((1,), (1,))
TN = ((0,), (0,))
VMEM = pl.BlockSpec(memory_space=pltpu.VMEM)
ANY = pl.BlockSpec(memory_space=pl.ANY)
EXTRA = 16
UP_AT, QV_AT = 256, 384


def dot(left, right, dims):
    return lax.dot_general(left, right, (dims, ((), ())), preferred_element_type=F32)


def shape(dims, kind):
    return jax.ShapeDtypeStruct(tuple(dims), kind)


def call(kernel, outs, args, scratch=(), name=None, mib=20, in_specs=None, alias=None):
    return pl.pallas_call(
        kernel,
        out_shape=tuple(outs),
        in_specs=in_specs or [VMEM] * len(args),
        out_specs=tuple([VMEM] * len(outs)),
        scratch_shapes=list(scratch),
        input_output_aliases=alias or {},
        name=name,
        compiler_params=pltpu.CompilerParams(vmem_limit_bytes=mib << 20),
    )(*args)


def gelu_and_slope(v):
    cdf = 0.5 * (1.0 + lax.erf(v * 0.7071067811865476))
    density = jnp.exp(-0.5 * v * v) * 0.3989422804014327
    return v * cdf, cdf + v * density


def mean(v):
    return jnp.mean(v, axis=-1, keepdims=True)


def total_rows(v):
    return jnp.sum(v, axis=0, keepdims=True)


def normalise(v):
    centred = v - mean(v)
    inverse = lax.rsqrt(mean(centred * centred) + EPSILON)
    return centred * inverse, inverse


def norm_backward(grad_normed, normal, inverse, gain):
    scaled = grad_normed * gain
    return inverse * (scaled - mean(scaled) - normal * mean(scaled * normal))


def lanes(parts):
    return jnp.concatenate(parts, axis=1)


def rows_of(parts):
    return jnp.concatenate(parts, axis=0)


def read(ref):
    return ref[...].astype(F32)


class Sizes:
    def __init__(self, nf, nt, inputs, qv_bias, fc1_weight):
        self.nf, self.nt = nf, nt
        _, self.half, self.width = inputs.shape
        self.shard = self.width // nf
        self.heads = qv_bias.shape[1]
        self.inner = self.heads * HD
        self.ff = fc1_weight.shape[1]
        self.pad = -self.half % 8
        self.padded = self.half + self.pad
        self.rows = 2 * self.padded
        self.block = -(-(self.rows // nt) // 8) * 8
        self.part = self.width // 4
        self.chunk = self.part // 2
        self.direct = nf == 4
        self.cols = 2 * self.ff + nt * self.inner
        self.dense = self.rows * self.inner // 128

    def start(self, j):
        return pl.multiple_of(j * (self.rows // self.nt) // 8 * 8, 8)

    def base(self):
        return lax.axis_index("fsdp") if self.direct else 0

    def half_of(self, c):
        return pl.ds(pl.multiple_of(c * self.chunk, 16), self.chunk)

    def squeeze(self, v):
        return rows_of([v[:, :128], lanes([v[: self.padded, 128:], v[self.padded :, 128:]])])

    def spread(self, v):
        tail = v[self.rows :]
        return lanes([v[: self.rows], rows_of([tail[:, :HD], tail[:, HD:]])])


def pack_kernel(z, *refs):
    sources, (near, far, proj_half, feed, feed_half), copies, sem = refs[:12], refs[12:17], refs[17:29], refs[29]
    moves = [pltpu.make_async_copy(s, d, sem.at[i]) for i, (s, d) in enumerate(zip(sources, copies))]
    for m in moves:
        m.start()
    for m in moves:
        m.wait()
    qkv, proj, up_b, qv_b = copies[:4]
    vectors = copies[4:10]
    c = lax.axis_index("ctx")
    whole = lanes([read(qkv.at[i]) for i in range(3)])
    near[: z.part, :] = whole.astype(LOW)
    far[: z.chunk, :] = jnp.where(c == 0, whole[: z.chunk], whole[z.chunk :]).astype(LOW)
    row = lax.broadcasted_iota(jnp.int32, (EXTRA, z.shard), 0)
    vec = jnp.zeros((EXTRA, z.shard), F32)
    for i, v in enumerate(vectors):
        vec = jnp.where(row == i, read(v).reshape(1, z.shard), vec)
    biases = read(qv_b)
    biases = rows_of([biases[h, i : i + 1] for h in range(z.heads) for i in range(2)])
    for out, at in ((near, z.part), (far, z.chunk)):
        out[at:, :] = jnp.zeros((EXTRA, 3 * z.inner), LOW)
        out[at:, : z.shard] = vec.astype(LOW)
        out[at : at + up_b.shape[0], UP_AT : UP_AT + up_b.shape[1]] = up_b[...]
        out[at : at + 2 * z.heads, QV_AT : QV_AT + biases.shape[1]] = biases.astype(LOW)
    feed[:, : z.ff] = copies[10][...]
    feed[:, z.ff :] = copies[11][...]
    feed_half[...] = feed[z.half_of(c), :]
    turned = read(proj).T
    proj_half[...] = jnp.where(c == 0, turned[: z.chunk], turned[z.chunk :]).astype(LOW)


def pair_kernel(first, second, out):
    out[0] = first[...]
    out[1] = second[...]


def pack_proj_kernel(own, two, pair, out):
    out[...] = lanes([read(own), pair[0].astype(F32), read(two), pair[1].astype(F32)]).astype(LOW)


def pack_near_kernel(z, mine, theirs, out):
    c = lax.axis_index("ctx")
    out[z.half_of(c), :] = mine[...]
    out[z.half_of(1 - c), :] = theirs[...]


def own_frame(z, keep, received):
    c = lax.axis_index("ctx")
    zero = jnp.zeros((z.pad, z.width), F32)
    pieces = []
    for ref in (keep, received):
        pieces.append(jnp.where(c == 0, ref[:, 0, :].astype(F32), ref[:, 1, :].astype(F32)))
        pieces.append(zero)
    return rows_of(pieces)


def frame_kernel(z, keep, received, stream, normal, inverse):
    values = own_frame(z, keep, received)
    stream[...] = values.astype(LOW)
    n, i = normalise(values)
    normal[...] = n
    inverse[...] = jnp.broadcast_to(i, inverse.shape)


def cot_kernel(z, keep, received, stream):
    stream[...] = own_frame(z, keep, received).astype(LOW)


def attend_kernel(z, *refs):
    refs = list(refs)
    if z.direct:
        own, near, near_their, far, far_their = refs[:5]
        refs = refs[5:]
    else:
        whole, vec_in, up_in, qv_in = refs[:4]
        refs = refs[4:]
    normal, small, w_out, normed_out, act, attended, soft_out = refs[:7]
    if z.direct:
        c, b = lax.axis_index("ctx"), lax.axis_index("fsdp")
        gather = refs[7]
        for ref, at in ((own, b), (near, b ^ (1 + c)), (near_their, b ^ (2 - c))):
            w_out[at] = ref[: z.part, :]
            gather[at] = ref[z.part :, :].astype(F32)
        w_out[b ^ 3, z.half_of(c), :] = far[: z.chunk, :]
        w_out[b ^ 3, z.half_of(1 - c), :] = far_their[: z.chunk, :]
        gather[b ^ 3] = far[z.chunk :, :].astype(F32)
        blocks = [gather[i] for i in range(4)]
        w = HD // 4
        vec = lanes([g[:8, : z.shard] for g in blocks])
        up = lanes([g[: z.ff // HD, UP_AT : UP_AT + w] for g in blocks])
        qv = lanes([g[: 2 * z.heads, QV_AT : QV_AT + w] for g in blocks])
    else:
        w_out[...] = whole[...]
        vec, up, qv = vec_in[...], up_in[...], qv_in[...]
    up_row = lanes([up[i : i + 1] for i in range(z.ff // HD)])
    query_b = lanes([qv[2 * h : 2 * h + 1] for h in range(z.heads)])
    value_b = lanes([qv[2 * h + 1 : 2 * h + 2] for h in range(z.heads)])
    small[...] = vec
    small[6:7, : z.ff] = up_row
    normed = (normal[...] * vec[0:1] + vec[1:2]).astype(LOW)
    normed_out[...] = normed
    projected = dot(normed, w_out[...].reshape(z.width, 3 * z.inner), NN)
    n = z.inner
    query = ((projected[:, :n] + query_b) * QUERY_SCALE).astype(LOW)
    key = projected[:, n : 2 * n].astype(LOW)
    value = (projected[:, 2 * n :] + value_b).astype(LOW)
    act[0] = query
    act[1] = key
    act[2] = value
    place = lax.broadcasted_iota(jnp.int32, (z.rows, z.rows), 1)
    valid = (place < z.half) | ((place >= z.padded) & (place < z.padded + z.half))
    done = []
    for h in range(z.heads):
        cut = slice(h * HD, (h + 1) * HD)
        scores = jnp.where(valid, dot(query[:, cut], key[:, cut], NT), -1e30)
        exponent = jnp.exp(scores - jnp.max(scores, axis=-1, keepdims=True))
        soft = exponent * (1.0 / jnp.sum(exponent, axis=-1, keepdims=True))
        soft_out[h] = soft
        done.append(dot(soft.astype(LOW), value[:, cut], NN))
    attended[...] = z.squeeze(lanes(done)).astype(LOW)


def feed_kernel(z, *refs):
    refs = list(refs)
    if z.direct:
        own, one, one_their, two, two_their, near, near_in, near_their, far, far_their = refs[:10]
        refs = refs[10:]
    else:
        whole = refs[0]
        refs = refs[1:]
    att = refs[:3]
    stream, cot, small = refs[3:6]
    (w_out, att_out, middle_out, hidden_out, normed_out, pre_out, part_out, low_out, own_att, small_out) = refs[6:16]
    sends = refs[16:]
    if z.direct:
        c, b = lax.axis_index("ctx"), lax.axis_index("fsdp")
        mine, other = z.half_of(c), z.half_of(1 - c)
        first, last = pl.ds(0, 2 * z.ff), pl.ds(2 * z.ff, z.nt * z.inner)
        w_out[b, :, first] = own[...]
        w_out[b ^ (1 + c), mine, first] = one[...]
        w_out[b ^ (2 - c), other, first] = one_their[...]
        w_out[b ^ (2 - c), mine, first] = two[0]
        w_out[b ^ (1 + c), other, first] = two_their[0]
        w_out[b ^ 3, mine, first] = two[1]
        w_out[b ^ 3, other, first] = two_their[1]
        w_out[b, :, last] = near[...]
        w_out[b ^ (1 + c), :, last] = near_in[...]
        w_out[b ^ (2 - c), :, last] = near_their[...]
        w_out[b ^ 3, mine, last] = far[...]
        w_out[b ^ 3, other, last] = far_their[...]
    else:
        w_out[...] = whole[...]
    n = z.inner
    w_up = w_out[:, :, : z.ff].reshape(z.width, z.ff)
    w_down_t = w_out[:, :, z.ff : 2 * z.ff].reshape(z.width, z.ff)
    w_proj_t = w_out[:, :, 2 * z.ff :].reshape(z.width, z.nt * n)
    grad_out_low = cot[...]
    grad_out = grad_out_low.astype(F32)
    pieces = [read(att[0]), att[2][0].astype(F32), read(att[1]), att[2][1].astype(F32)]
    attended = lanes([z.spread(p) for p in pieces]).astype(LOW)
    att_out[...] = attended
    branch = dot(attended, w_proj_t, NT)
    middle = stream[...].astype(F32) + branch + small[2:3]
    middle_out[...] = middle
    normal, inverse = normalise(middle)
    gain = small[3:4]
    normed = (normal * gain + small[4:5]).astype(LOW)
    normed_out[...] = normed
    hidden, slope = gelu_and_slope(dot(normed, w_up, NN) + small[6:7, : z.ff])
    hidden_out[...] = hidden.astype(LOW)
    grad_pre = (dot(grad_out_low, w_down_t, NN) * slope).astype(LOW)
    pre_out[...] = grad_pre
    grad_normed = dot(grad_pre, w_up, NT)
    part = grad_out * (1.0 / z.nt) + norm_backward(grad_normed, normal, inverse, gain)
    part_out[...] = part
    low = part.astype(LOW)
    low_out[...] = low
    grad_att = dot(low, w_proj_t, NN)
    own_att[...] = grad_att[:, :n]
    for k in range(1, z.nt):
        sends[k - 1][...] = z.squeeze(grad_att[:, k * n : (k + 1) * n]).astype(LOW)
    small_out[...] = jnp.zeros(small_out.shape, F32)
    small_out[2:3] = total_rows(part)
    small_out[3:4] = total_rows(grad_normed * normal)
    small_out[4:5] = total_rows(grad_normed)
    small_out[5:6] = total_rows(grad_out) * (1.0 / z.nt)
    small_out[6:7, : z.ff] = total_rows(grad_pre.astype(F32))


def down_kernel(z, hidden, w, middle, small, own, sent, scratch):
    t = lax.axis_index("tp")
    w_down_t = w[:, :, z.ff : 2 * z.ff].reshape(z.width, z.ff)
    scratch[...] = dot(hidden[...], w_down_t, NT)
    mine = pl.ds(z.start(t), z.block)
    own[0] = scratch[mine, :] + middle[mine, :] + small[5:6]
    own[1] = scratch[pl.ds(z.start(t ^ 2), z.block), :]
    sent[0] = scratch[pl.ds(z.start(t ^ 1), z.block), :].astype(LOW)
    sent[1] = scratch[pl.ds(z.start(t ^ 3), z.block), :].astype(LOW)


def down_pair_kernel(own, received, kept, sent):
    kept[...] = own[0] + received[0].astype(F32)
    sent[...] = (own[1] + received[1].astype(F32)).astype(LOW)


def down_last_kernel(kept, received, out):
    out[...] = (kept[...] + read(received)).astype(LOW)


def store_halves(z, value, at, keep, sent):
    cols = pl.ds(at, value.shape[1])
    c = lax.axis_index("ctx") if z.direct else 0
    b = lax.axis_index("fsdp") if z.direct else 0
    for j in range(4):
        first = value[j * z.part : j * z.part + z.chunk]
        second = value[j * z.part + z.chunk : (j + 1) * z.part]
        if z.direct:
            keep[j ^ b, :, cols] = jnp.where(c == 0, first, second)
            sent[j ^ b, :, cols] = jnp.where(c == 0, second, first).astype(LOW)
        else:
            keep[j, :, cols] = first
            sent[j, :, cols] = second.astype(LOW)


def rest_grad_kernel(z, normed, pre, cot, hidden, low, att, keep, sent):
    store_halves(z, dot(normed[...], pre[...], TN), 0, keep, sent)
    store_halves(z, dot(cot[...], hidden[...], TN), z.ff, keep, sent)
    store_halves(z, dot(low[...], att[...], TN), 2 * z.ff, keep, sent)


def split_sum(z, keep, received, out, kept, cols):
    c = lax.axis_index("ctx")
    rows = pl.ds(0, z.chunk)
    for target, at, kind in ((out, (1 + c, 3), LOW), (kept, (0, 2 - c), F32)):
        for i in range(2):
            total = keep[at[i], :, cols] + received[at[i], :, cols].astype(F32)
            target[i, rows, :] = total.astype(kind)


def rest_one_kernel(z, keep, received, proj, proj_kept, feed, feed_kept):
    split_sum(z, keep, received, proj, proj_kept, pl.ds(2 * z.ff, z.nt * z.inner))
    split_sum(z, keep, received, feed, feed_kept, pl.ds(0, 2 * z.ff))


def second_kernel(kept, received, own, sent):
    own[...] = kept[0] + received[0].astype(F32)
    sent[...] = (kept[1] + received[1].astype(F32)).astype(LOW)


def third_kernel(own, received, total, sent):
    value = own[...] + read(received)
    total[...] = value
    sent[...] = value.astype(LOW)


def by_half(mine, other):
    c = lax.axis_index("ctx")
    return rows_of([jnp.where(c == 0, mine, other), jnp.where(c == 0, other, mine)])


def feed_final_kernel(z, own, theirs, up, down):
    total = by_half(own[...], read(theirs))
    up[...] = total[:, : z.ff]
    down[...] = total[:, z.ff :]


def unfold(z, v):
    return rows_of([v[:, i * z.inner : (i + 1) * z.inner] for i in range(4)])


def fold(v):
    n = v.shape[0] // 4
    return lanes([v[i * n : (i + 1) * n] for i in range(4)])


def proj_final_kernel(z, own, theirs, proj):
    other = theirs[z.padded :, :].astype(F32)
    proj[...] = by_half(unfold(z, own[...]), unfold(z, other)).T


def back_kernel(z, *refs):
    own_att, got = refs[0], refs[1 : z.nt]
    act, soft, w, normal, inverse, part, small, small_in = refs[z.nt : z.nt + 8]
    grads_out, qv_out, own, sent, scratch = refs[z.nt + 8 :]
    t = lax.axis_index("tp")
    grad_att = (own_att[...] + z.spread(sum(read(g) for g in got))).astype(LOW)
    parts = [[], [], []]
    query, key, value = act[0], act[1], act[2]
    for h in range(z.heads):
        cut = slice(h * HD, (h + 1) * HD)
        ga = grad_att[:, cut]
        p = soft[h]
        grad_soft = dot(ga, value[:, cut], NT)
        delta = jnp.sum(p * grad_soft, axis=-1, keepdims=True)
        grad_scores = (p * (grad_soft - delta)).astype(LOW)
        parts[0].append((dot(grad_scores, key[:, cut], NN).astype(LOW).astype(F32) * QUERY_SCALE).astype(LOW))
        parts[1].append(dot(grad_scores, query[:, cut], TN).astype(LOW))
        parts[2].append(dot(p.astype(LOW), ga, TN).astype(LOW))
    grads = lanes(parts[0] + parts[1] + parts[2])
    grads_out[...] = grads
    n = z.inner
    qv_out[...] = total_rows(grads.astype(F32))
    grad_normed = dot(grads, w[...].reshape(z.width, 3 * n), NT)
    scratch[...] = part[...] + norm_backward(grad_normed, normal[...], inverse[:, :1], small[0:1])
    row = lax.broadcasted_iota(jnp.int32, (8, z.width), 0)
    vec = small_in[...]
    vec = jnp.where(row == 0, total_rows(grad_normed * normal[...]), vec)
    vec = jnp.where(row == 1, total_rows(grad_normed), vec)
    for i, k in enumerate((0, 2)):
        own[i] = rows_of([scratch[pl.ds(z.start(t ^ k), z.block), :], vec])
        sent[i] = rows_of([scratch[pl.ds(z.start(t ^ k ^ 1), z.block), :], vec]).astype(LOW)


def qkv_grad_kernel(z, normed, grads, keep, sent):
    store_halves(z, dot(normed[...], grads[...], TN), 0, keep, sent)


def sum_rows_kernel(z, kept, received, small, qv, *refs):
    if z.direct:
        proj, proj_in, out, vec, proj_keep = refs
    else:
        out, vec = refs
    total = kept[...] + read(received)
    out[: z.block, :] = total[: z.block].astype(LOW)
    vec[:8, :] = total[z.block :]
    vec[8:, :] = jnp.zeros((8, z.width), F32)
    vec[8:9, : z.ff] = small[6:7, : z.ff]
    vec[9:10, : 3 * z.inner] = qv[...]
    if z.direct:
        value = proj[...] + read(proj_in)
        parts = [fold(value[:, k * z.inner : (k + 1) * z.inner]) for k in range(4)]
        proj_keep[0] = parts[0]
        proj_keep[1] = parts[1]
        out[z.block :, :] = rows_of(parts[2:]).astype(LOW)


def rows_pair_kernel(z, own, received, *refs):
    if z.direct:
        proj_keep, out, proj_kept = refs
        n = z.chunk // 4
        arrived = received[z.block :, :].astype(F32)
        proj_kept[...] = proj_keep[0] + arrived[:n]
        tail = [(proj_keep[1] + arrived[n:])]
    else:
        (out,) = refs
        tail = []
    blocks = [own[: z.block, :].astype(F32), received[: z.block, :].astype(F32)]
    out[...] = rows_of(blocks + tail).astype(LOW)


def rows_kernel(z, pair, received, *refs):
    if len(refs) > 3:
        proj_kept, mine, theirs, proj_own, scratch = refs
        value = proj_kept[...] + received[2 * z.block :, :].astype(F32)
        proj_own[...] = value
        theirs[z.half : z.padded, :] = jnp.zeros((z.pad, z.width), LOW)
        theirs[z.padded :, :] = value.astype(LOW)
    else:
        mine, theirs, scratch = refs
    t = lax.axis_index("tp")
    for ref, flip in ((pair, 0), (received, 1)):
        for i, k in enumerate((0, 2)):
            piece = ref[i * z.block : (i + 1) * z.block, :].astype(F32)
            scratch[pl.ds(z.start(t ^ k ^ flip), z.block), :] = piece
    mine[...] = scratch[: z.half, :]
    theirs[: z.half, :] = scratch[z.padded : z.padded + z.half, :].astype(LOW)


def qkv_one_kernel(z, keep, received, vec, out, kept, scratch):
    b, c = lax.axis_index("fsdp"), lax.axis_index("ctx")
    vectors = vec[...]
    up = rows_of([vectors[8:9, i * HD : (i + 1) * HD] for i in range(z.ff // HD)])
    pieces = []
    for h in range(z.heads):
        pieces.append(vectors[9:10, h * HD : (h + 1) * HD])
        pieces.append(vectors[9:10, 2 * z.inner + h * HD : 2 * z.inner + (h + 1) * HD])
    qv_rows = rows_of(pieces)
    scratch[...] = jnp.zeros(scratch.shape, F32)
    w = HD // 4
    for i in range(4):
        scratch[i, :8, : z.shard] = vectors[:8, i * z.shard : (i + 1) * z.shard]
        scratch[i, : z.ff // HD, UP_AT : UP_AT + w] = up[:, i * w : (i + 1) * w]
        scratch[i, : 2 * z.heads, QV_AT : QV_AT + w] = qv_rows[:, i * w : (i + 1) * w]
    split_sum(z, keep, received, out, kept, pl.ds(0, 3 * z.inner))
    for i, at in enumerate((1 + c, 3)):
        out[i, z.chunk :, :] = scratch[b ^ at].astype(LOW)
    for i, at in enumerate((0, 2 - c)):
        kept[i, z.chunk :, :] = scratch[b ^ at]


def qkv_final_kernel(z, own, theirs, qkv, up, qv, *vectors):
    both = by_half(own[: z.chunk, :], theirs[: z.chunk, :].astype(F32))
    for i in range(3):
        qkv[i] = both[:, i * z.inner : (i + 1) * z.inner]
    tail = own[z.chunk :, :] + theirs[z.chunk :, :].astype(F32)
    w = HD // 4
    up[...] = tail[: z.ff // HD, UP_AT : UP_AT + w]
    for h in range(z.heads):
        qv[h] = tail[2 * h : 2 * h + 2, QV_AT : QV_AT + w]
    for i, v in enumerate(vectors):
        v[...] = tail[i : i + 1, : z.shard].reshape(z.shard)


def place_kernel(mine, theirs, out, *scratch):
    c = lax.axis_index("ctx")
    target = scratch[0] if scratch else out
    other = theirs[: out.shape[0], :].astype(F32)
    target[:, 0, :] = jnp.where(c == 0, mine[...], other)
    target[:, 1, :] = jnp.where(c == 0, other, mine[...])
    if scratch:
        out[...] = target[...].astype(out.dtype)


def build(nf, nc, nt):
    def local(
        inputs,
        norm1_gain,
        norm1_bias,
        qkv_weight,
        qv_bias,
        proj_weight,
        proj_bias,
        norm2_gain,
        norm2_bias,
        fc1_weight,
        fc1_bias,
        fc2_weight,
        fc2_bias,
        cotangent,
    ):
        z = Sizes(nf, nt, inputs, qv_bias, fc1_weight)
        part = functools.partial
        rows, width, inner, ff, chunk, block = z.rows, z.width, z.inner, z.ff, z.chunk, z.block
        f = lax.axis_index("fsdp")
        tie = lax.optimization_barrier

        def other_core(value):
            return lax.ppermute(value, "ctx", [(0, 1), (1, 0)])

        def to_tp(value, k):
            return lax.ppermute(value, "tp", [(i, i ^ k) for i in range(nt)])

        def to_far(value):
            return lax.ppermute(value, "fsdp", [(i, i ^ 3) for i in range(nf)])

        def neighbours(value, order):
            pairs = [(2 * i + c, 2 * (i ^ order[c]) + c) for i in range(nf) for c in range(2)]
            return lax.ppermute(value, ("fsdp", "ctx"), pairs)

        def to_near(value):
            return neighbours(value, (1, 2))

        def to_cross(value):
            return neighbours(value, (2, 1))

        def pair_of(first, second):
            return call(pair_kernel, [shape((2,) + first.shape, LOW)], [first, second], name="pair")[0]

        qkv3 = qkv_weight.transpose(1, 0, 2)
        down_t = fc2_weight.T
        qv3 = qv_bias.transpose(1, 0, 2)
        x_raw, cot_raw = inputs.transpose(1, 0, 2), cotangent.transpose(1, 0, 2)
        vectors = [norm1_gain, norm1_bias, proj_bias, norm2_gain, norm2_bias, fc2_bias]

        x_recv = other_core(x_raw)
        cot_recv = other_core(cot_raw)
        stream, normal_one, inverse_one = call(
            part(frame_kernel, z),
            [shape((rows, width), LOW), shape((rows, width), F32), shape((rows, 128), F32)],
            [x_raw, x_recv],
            name="frame",
        )
        (cot,) = call(part(cot_kernel, z), [shape((rows, width), LOW)], [cot_raw, cot_recv], name="cotangent")

        if z.direct:
            sources = [qkv3, proj_weight, fc1_bias, qv3] + vectors + [fc1_weight, down_t]
            near, far, proj_half, feed_own, feed_half = call(
                part(pack_kernel, z),
                [
                    shape((z.part + EXTRA, 3 * inner), LOW),
                    shape((chunk + EXTRA, 3 * inner), LOW),
                    shape((chunk, inner), LOW),
                    shape((z.part, 2 * ff), LOW),
                    shape((chunk, 2 * ff), LOW),
                ],
                sources,
                [pltpu.VMEM(s.shape, s.dtype) for s in sources] + [pltpu.SemaphoreType.DMA((len(sources),))],
                name="pack",
                mib=56,
                in_specs=[ANY] * len(sources),
            )
            got = [to_near(near), to_far(far)]
            proj_two = to_tp(proj_half, 2)
            feed_one = to_near(feed_half)
            got, stream, normal_one, inverse_one, cot = tie((got, stream, normal_one, inverse_one, cot))
            shared = [other_core(g) for g in got]
            qkv_in = [near, got[0], shared[0], got[1], shared[1]]
            proj_pair = to_tp(pair_of(proj_half, proj_two), 1)
            feed_two = to_cross(pair_of(feed_half, feed_one))
            (proj_far,) = call(
                pack_proj_kernel, [shape((chunk, nt * inner), LOW)], [proj_half, proj_two, proj_pair], name="pack_proj"
            )
            (proj_near,) = call(
                part(pack_near_kernel, z),
                [shape((z.part, nt * inner), LOW)],
                [proj_far, other_core(proj_far)],
                name="pack_near",
            )
            proj_got = [to_near(proj_near), to_far(proj_far)]
        else:
            whole = lax.all_gather(qkv3, "fsdp", axis=1, tiled=True)
            whole = whole.transpose(1, 0, 2).reshape(4, z.part, 3 * inner)
            vec = jnp.stack(vectors + [vectors[0]] * 2).astype(F32)
            qv_rows = qv3.reshape(2 * z.heads, -1).astype(F32)
            gathered = [lax.all_gather(v, "fsdp", axis=1, tiled=True) for v in (vec, fc1_bias.astype(F32), qv_rows)]
            qkv_in = [whole] + gathered
            proj_t = proj_weight.T
            rest = jnp.concatenate([fc1_weight, down_t, proj_t] + [to_tp(proj_t, k) for k in range(1, nt)], 1)
            rest_in = [lax.all_gather(rest, "fsdp", axis=0, tiled=True).reshape(4, z.part, z.cols)]

        small, w_qkv, normed_one, act, attended, soft = call(
            part(attend_kernel, z),
            [
                shape((8, width), F32),
                shape((4, z.part, 3 * inner), LOW),
                shape((rows, width), LOW),
                shape((3, rows, inner), LOW),
                shape((z.dense, 128), LOW),
                shape((z.heads, rows, rows), F32),
            ],
            qkv_in + [normal_one],
            [pltpu.VMEM((4, EXTRA, 3 * inner), F32)] if z.direct else [],
            name="attend",
        )
        att_two = to_tp(attended, 2)
        att_pair = to_tp(pair_of(attended, att_two), 1)
        if z.direct:
            att_pair, feed_two, proj_got = tie((att_pair, feed_two, proj_got))
            rest_in = [feed_own, feed_one, other_core(feed_one), feed_two, other_core(feed_two)]
            rest_in += [proj_near, proj_got[0], other_core(proj_got[0]), proj_got[1], other_core(proj_got[1])]

        (w_rest, att_all, middle, hidden, normed_two, grad_pre, part_middle, part_low, own_att, small_two, *att_sends) = (
            call(
                part(feed_kernel, z),
                [
                    shape((4, z.part, z.cols), LOW),
                    shape((rows, nt * inner), LOW),
                    shape((rows, width), F32),
                    shape((rows, ff), LOW),
                    shape((rows, width), LOW),
                    shape((rows, ff), LOW),
                    shape((rows, width), F32),
                    shape((rows, width), LOW),
                    shape((rows, inner), F32),
                    shape((8, width), F32),
                ]
                + [shape((z.dense, 128), LOW)] * (nt - 1),
                rest_in + [attended, att_two, att_pair, stream, cot, small],
                name="feed",
            )
        )
        att_got = [to_tp(att_sends[k - 1], k) for k in range(1, nt)]
        keep, sent = call(
            part(rest_grad_kernel, z),
            [shape((4, chunk, z.cols), F32), shape((4, chunk, z.cols), LOW)],
            [normed_two, grad_pre, cot, hidden, part_low, att_all],
            name="rest_grad",
        )
        out_pair, out_sent = call(
            part(down_kernel, z),
            [shape((2, block, width), F32), shape((2, block, width), LOW)],
            [hidden, w_rest, middle, small],
            [pltpu.VMEM((rows, width), F32)],
            name="down",
        )
        out_sent = to_tp(out_sent, 1)
        if z.direct:
            rest_sent = other_core(sent)
            att_got, rest_sent, out_sent = tie((att_got, rest_sent, out_sent))
            proj_sent, proj_kept, feed_sent, feed_kept = call(
                part(rest_one_kernel, z),
                [
                    shape((2, chunk, nt * inner), LOW),
                    shape((2, chunk, nt * inner), F32),
                    shape((2, chunk, 2 * ff), LOW),
                    shape((2, chunk, 2 * ff), F32),
                ],
                [keep, rest_sent],
                name="rest_one",
            )
            proj_in, feed_in = to_near(proj_sent), to_near(feed_sent)
        out_kept, out_sent = call(
            second_kernel,
            [shape((block, width), F32), shape((block, width), LOW)],
            [out_pair, out_sent],
            name="down_pair",
        )
        out_two = to_tp(out_sent, 2)

        grads, qv_sum, in_pair, in_sent = call(
            part(back_kernel, z),
            [
                shape((rows, 3 * inner), LOW),
                shape((1, 3 * inner), F32),
                shape((2, block + 8, width), F32),
                shape((2, block + 8, width), LOW),
            ],
            [own_att] + att_got + [act, soft, w_qkv, normal_one, inverse_one, part_middle, small, small_two],
            [pltpu.VMEM((rows, width), F32)],
            name="back",
        )
        in_one = to_tp(in_sent, 1)
        keep_qkv, sent_qkv = call(
            part(qkv_grad_kernel, z),
            [shape((4, chunk, 3 * inner), F32), shape((4, chunk, 3 * inner), LOW)],
            [normed_one, grads],
            name="qkv_grad",
        )
        in_kept, in_sent = call(
            second_kernel,
            [shape((block + 8, width), F32), shape((block + 8, width), LOW)],
            [in_pair, in_one],
            name="in_pair",
        )
        in_two = to_tp(in_sent, 2)
        if z.direct:
            proj_own, proj_sent = call(
                second_kernel,
                [shape((chunk, nt * inner), F32), shape((chunk, nt * inner), LOW)],
                [proj_kept, proj_in],
                name="proj_second",
            )
            proj_in = to_cross(proj_sent)
            qkv_in = other_core(sent_qkv)

        (out_own,) = call(down_last_kernel, [shape((block, width), LOW)], [out_kept, out_two], name="down_last")
        extra = chunk // 4 if z.direct else 0
        in_block, vec_sum, *proj_keep = call(
            part(sum_rows_kernel, z),
            [shape((block + 2 * extra, width), LOW), shape((16, width), F32)]
            + ([shape((2, extra, width), F32)] if extra else []),
            [in_kept, in_two, small_two, qv_sum] + ([proj_own, proj_in] if extra else []),
            name="sum_rows",
        )
        block_two = to_tp(in_block, 2)
        out_block = to_tp(out_own, 2)
        if z.direct:
            feed_own, feed_sent = call(
                second_kernel,
                [shape((chunk, 2 * ff), F32), shape((chunk, 2 * ff), LOW)],
                [feed_kept, feed_in],
                name="feed_second",
            )
            feed_in = to_cross(feed_sent)
            qkv_sent, qkv_kept = call(
                part(qkv_one_kernel, z),
                [shape((2, chunk + EXTRA, 3 * inner), LOW), shape((2, chunk + EXTRA, 3 * inner), F32)],
                [keep_qkv, qkv_in, vec_sum],
                [pltpu.VMEM((4, EXTRA, 3 * inner), F32)],
                name="qkv_one",
            )
            qkv_in = to_near(qkv_sent)
        in_pair, *proj_kept = call(
            part(rows_pair_kernel, z),
            [shape((2 * block + extra, width), LOW)] + ([shape((extra, width), F32)] if extra else []),
            [in_block, block_two] + proj_keep,
            name="rows_pair",
        )
        block_pair = to_tp(in_pair, 1)
        out_pair = pair_of(out_own, out_block).reshape(2 * block, width)
        out_far = to_tp(out_pair, 1)
        if z.direct:
            feed_own, feed_sent = call(
                third_kernel,
                [shape((chunk, 2 * ff), F32), shape((chunk, 2 * ff), LOW)],
                [feed_own, feed_in],
                name="feed_third",
            )
            feed_in = other_core(feed_sent)
            qkv_own, qkv_sent = call(
                second_kernel,
                [shape((chunk + EXTRA, 3 * inner), F32), shape((chunk + EXTRA, 3 * inner), LOW)],
                [qkv_kept, qkv_in],
                name="qkv_second",
            )
            qkv_in = to_cross(qkv_sent)
        out_mine, out_theirs = call(
            part(rows_kernel, z),
            [shape((z.half, width), F32), shape((z.half, width), LOW)],
            [out_pair, out_far],
            [pltpu.VMEM((rows, width), F32)],
            name="out_rows",
        )
        out_in = other_core(out_theirs)
        in_mine, in_theirs, *proj_own = call(
            part(rows_kernel, z),
            [shape((z.half, width), F32), shape((z.padded + extra if extra else z.half, width), LOW)]
            + ([shape((extra, width), F32)] if extra else []),
            [in_pair, block_pair] + proj_kept,
            [pltpu.VMEM((rows, width), F32)],
            name="in_rows",
        )
        in_in = other_core(in_theirs)
        (output,) = call(
            place_kernel,
            [shape((z.half, 2, width), LOW)],
            [out_mine, out_in],
            [pltpu.VMEM((z.half, 2, width), F32)],
            name="place_out",
        )
        output = output.transpose(1, 0, 2)
        if z.direct:
            fc1_grad, fc2_grad = call(
                part(feed_final_kernel, z), [shape((z.shard, ff), F32)] * 2, [feed_own, feed_in], name="feed_final"
            )
            qkv_own, qkv_sent = call(
                third_kernel,
                [shape((chunk + EXTRA, 3 * inner), F32), shape((chunk + EXTRA, 3 * inner), LOW)],
                [qkv_own, qkv_in],
                name="qkv_third",
            )
            qkv_in = other_core(qkv_sent)
        (input_grad,) = call(place_kernel, [shape((z.half, 2, width), F32)], [in_mine, in_in], name="place_in")
        input_grad = input_grad.transpose(1, 0, 2)
        if z.direct:
            (proj_grad,) = call(
                part(proj_final_kernel, z), [shape((inner, z.shard), F32)], [proj_own[0], in_in], name="proj_final"
            )
            qkv_grad, up_grad, qv_grad, *vec_grads = call(
                part(qkv_final_kernel, z),
                [shape((3, z.shard, inner), F32), shape(fc1_bias.shape, F32), shape(qv3.shape, F32)]
                + [shape((z.shard,), F32)] * 6,
                [qkv_own, qkv_in],
                name="qkv_final",
            )
        else:

            def scatter(keep, sent):
                whole = jnp.stack([keep.astype(LOW), sent], 1).reshape(width, -1)
                whole = lax.psum(whole, "ctx")
                return lax.psum_scatter(whole, "fsdp", scatter_dimension=0, tiled=True).astype(F32)

            rest_own = scatter(keep, sent)
            fc1_grad, fc2_grad = rest_own[:, :ff], rest_own[:, ff : 2 * ff]
            proj_grad = rest_own[:, 2 * ff : 2 * ff + inner]
            for k in range(1, nt):
                cut = rest_own[:, 2 * ff + k * inner : 2 * ff + (k + 1) * inner]
                proj_grad = proj_grad + to_tp(cut.astype(LOW), k).astype(F32)
            proj_grad = proj_grad.T
            qkv_grad = scatter(keep_qkv, sent_qkv).reshape(z.shard, 3, inner).transpose(1, 0, 2)

            def own_columns(value):
                value = lax.psum(value, ("fsdp", "ctx"))
                return lax.dynamic_slice_in_dim(value, f * (value.shape[1] // nf), value.shape[1] // nf, 1)

            vec_grads = own_columns(vec_sum[:6])
            up_grad = own_columns(vec_sum[8, :ff].reshape(-1, HD))
            qv_grad = vec_sum[9, : 3 * inner].reshape(3, z.heads, HD)[0::2].transpose(1, 0, 2)
            qv_grad = own_columns(qv_grad.reshape(2 * z.heads, HD)).reshape(qv3.shape)
        return (
            output,
            input_grad,
            vec_grads[0],
            vec_grads[1],
            qkv_grad.transpose(1, 0, 2),
            qv_grad.transpose(1, 0, 2),
            proj_grad,
            vec_grads[2],
            vec_grads[3],
            vec_grads[4],
            fc1_grad,
            up_grad,
            fc2_grad.T,
            vec_grads[5],
        )

    return local


def solution(mesh):
    sizes = mesh.shape
    return jax.shard_map(
        build(sizes["fsdp"], sizes["ctx"], sizes["tp"]),
        mesh=mesh,
        in_specs=(
            P("fsdp", "ctx", None),
            P("fsdp"),
            P("fsdp"),
            P("fsdp", None, "tp"),
            P(None, "tp", "fsdp"),
            P("tp", "fsdp"),
            P("fsdp"),
            P("fsdp"),
            P("fsdp"),
            P("fsdp", "tp"),
            P("tp", "fsdp"),
            P("tp", "fsdp"),
            P("fsdp"),
            P("fsdp", "ctx", None),
        ),
        out_specs=(
            P("fsdp", "ctx", None),
            P("fsdp", "ctx", None),
            P("fsdp"),
            P("fsdp"),
            P("fsdp", None, "tp"),
            P(None, "tp", "fsdp"),
            P("tp", "fsdp"),
            P("fsdp"),
            P("fsdp"),
            P("fsdp"),
            P("fsdp", "tp"),
            P("tp", "fsdp"),
            P("tp", "fsdp"),
            P("fsdp"),
        ),
        check_vma=False,
    )
```

```python
import functools

import jax
import jax.numpy as jnp
from jax import lax
from jax.experimental import pallas as pl
from jax.experimental.pallas import tpu as pltpu
from jax.sharding import PartitionSpec as P

HD = 64
EPSILON = 1e-06
QUERY_SCALE = 0.125
F32 = jnp.float32
LOW = jnp.bfloat16
NN = ((1,), (0,))
NT = ((1,), (1,))
TN = ((0,), (0,))
VMEM = pl.BlockSpec(memory_space=pltpu.VMEM)
ANY = pl.BlockSpec(memory_space=pl.ANY)
EXTRA = 16
UP_AT, QV_AT = 256, 384


def dot(left, right, dims):
    return lax.dot_general(left, right, (dims, ((), ())), preferred_element_type=F32)


def shape(dims, kind):
    return jax.ShapeDtypeStruct(tuple(dims), kind)


def call(kernel, outs, args, scratch=(), name=None, mib=20, in_specs=None, alias=None):
    return pl.pallas_call(
        kernel,
        out_shape=tuple(outs),
        in_specs=in_specs or [VMEM] * len(args),
        out_specs=tuple([VMEM] * len(outs)),
        scratch_shapes=list(scratch),
        input_output_aliases=alias or {},
        name=name,
        compiler_params=pltpu.CompilerParams(vmem_limit_bytes=mib << 20),
    )(*args)


def gelu_and_slope(v):
    cdf = 0.5 * (1.0 + lax.erf(v * 0.7071067811865476))
    density = jnp.exp(-0.5 * v * v) * 0.3989422804014327
    return v * cdf, cdf + v * density


def mean(v):
    return jnp.mean(v, axis=-1, keepdims=True)


def total_rows(v):
    return jnp.sum(v, axis=0, keepdims=True)


def normalise(v):
    centred = v - mean(v)
    inverse = lax.rsqrt(mean(centred * centred) + EPSILON)
    return centred * inverse, inverse


def norm_backward(grad_normed, normal, inverse, gain):
    scaled = grad_normed * gain
    return inverse * (scaled - mean(scaled) - normal * mean(scaled * normal))


def lanes(parts):
    return jnp.concatenate(parts, axis=1)


def rows_of(parts):
    return jnp.concatenate(parts, axis=0)


def read(ref):
    return ref[...].astype(F32)


class Sizes:
    def __init__(self, nf, nt, inputs, qv_bias, fc1_weight):
        self.nf, self.nt = nf, nt
        _, self.half, self.width = inputs.shape
        self.shard = self.width // nf
        self.heads = qv_bias.shape[1]
        self.inner = self.heads * HD
        self.ff = fc1_weight.shape[1]
        self.pad = -self.half % 8
        self.padded = self.half + self.pad
        self.rows = 2 * self.padded
        self.part = self.width // 4
        self.chunk = self.part // 2
        self.tail = self.part // 4
        self.direct = nf == 4
        self.cols = 2 * self.ff + nt * self.inner
        self.all_cols = 2 * self.ff + -(-3 * self.inner // 128) * 128
        self.dense = self.rows * self.inner // 128

    def half_rows(self, h):
        return pl.ds(pl.multiple_of(h * self.padded, 8), self.padded)

    def half_of(self, c):
        return pl.ds(pl.multiple_of(c * self.chunk, 16), self.chunk)

    def squeeze(self, v):
        return rows_of([v[:, :128], lanes([v[: self.padded, 128:], v[self.padded :, 128:]])])

    def spread(self, v):
        tail = v[self.rows :]
        return lanes([v[: self.rows], rows_of([tail[:, :HD], tail[:, HD:]])])


def fetch(sources, copies, sem):
    moves = [pltpu.make_async_copy(s, d, sem.at[i]) for i, (s, d) in enumerate(zip(sources, copies))]
    for m in moves:
        m.start()
    for m in moves:
        m.wait()


def stage_kernel(z, up, down_t, out, one, two, sem):
    fetch((up, down_t), (one, two), sem)
    out[:, : z.ff] = one[...]
    out[:, z.ff :] = two[...]


def pack_kernel(z, *refs):
    sources, (near, far, proj_t, proj_half) = refs[:10], refs[10:14]
    copies, sem = refs[14:24], refs[24]
    fetch(sources, copies, sem)
    qkv, proj, up_b, qv_b = copies[:4]
    vectors = copies[4:]
    c = lax.axis_index("ctx")
    whole = lanes([read(qkv.at[i]) for i in range(3)])
    near[: z.part, :] = whole.astype(LOW)
    far[: z.chunk, :] = jnp.where(c == 0, whole[: z.chunk], whole[z.chunk :]).astype(LOW)
    row = lax.broadcasted_iota(jnp.int32, (EXTRA, z.shard), 0)
    vec = jnp.zeros((EXTRA, z.shard), F32)
    for i, v in enumerate(vectors):
        vec = jnp.where(row == i, read(v).reshape(1, z.shard), vec)
    biases = read(qv_b)
    biases = rows_of([biases[h, i : i + 1] for h in range(z.heads) for i in range(2)])
    for out, at in ((near, z.part), (far, z.chunk)):
        out[at:, :] = jnp.zeros((EXTRA, 3 * z.inner), LOW)
        out[at:, : z.shard] = vec.astype(LOW)
        out[at : at + up_b.shape[0], UP_AT : UP_AT + up_b.shape[1]] = up_b[...]
        out[at : at + 2 * z.heads, QV_AT : QV_AT + biases.shape[1]] = biases.astype(LOW)
    turned = read(proj).T
    proj_t[...] = turned.astype(LOW)
    proj_half[...] = jnp.where(c == 0, turned[: z.chunk], turned[z.chunk :]).astype(LOW)


def pair_kernel(first, second, out):
    out[0] = first[...]
    out[1] = second[...]


def pack_rest_kernel(z, feed, proj_t, near_in, near_their, far_in, far_their, near, far, scratch):
    c, t = lax.axis_index("ctx"), lax.axis_index("tp")
    scratch[t] = read(proj_t)
    scratch[t ^ (1 + c)] = read(near_in)
    scratch[t ^ (2 - c)] = read(near_their)
    scratch[t ^ 3, z.half_of(c), :] = read(far_in)
    scratch[t ^ 3, z.half_of(1 - c), :] = read(far_their)
    near[...] = lanes([scratch[i] for i in range(4)]).astype(LOW)
    far[:, : 2 * z.ff] = feed[z.half_of(c), :]
    far[:, 2 * z.ff :] = near[z.half_of(c), :]


def own_frame(z, keep, received):
    c = lax.axis_index("ctx")
    zero = jnp.zeros((z.pad, z.width), F32)
    pieces = []
    for ref in (keep, received):
        pieces.append(jnp.where(c == 0, ref[:, 0, :].astype(F32), ref[:, 1, :].astype(F32)))
        pieces.append(zero)
    return rows_of(pieces)


def frame_kernel(z, keep, received, stream, normal, inverse):
    values = own_frame(z, keep, received)
    stream[...] = values.astype(LOW)
    n, i = normalise(values)
    normal[...] = n
    inverse[...] = jnp.broadcast_to(i, inverse.shape)


def cot_kernel(z, keep, received, stream):
    stream[...] = own_frame(z, keep, received).astype(LOW)


def attend_kernel(z, *refs):
    refs = list(refs)
    if z.direct:
        own, near, near_their, far, far_their = refs[:5]
        refs = refs[5:]
    else:
        whole, vec_in, up_in, qv_in = refs[:4]
        refs = refs[4:]
    normal, small, w_out, normed_out, act, attended, soft_out = refs[:7]
    if z.direct:
        c, b = lax.axis_index("ctx"), lax.axis_index("fsdp")
        gather = refs[7]
        for ref, at in ((own, b), (near, b ^ (1 + c)), (near_their, b ^ (2 - c))):
            w_out[at] = ref[: z.part, :]
            gather[at] = ref[z.part :, :].astype(F32)
        w_out[b ^ 3, z.half_of(c), :] = far[: z.chunk, :]
        w_out[b ^ 3, z.half_of(1 - c), :] = far_their[: z.chunk, :]
        gather[b ^ 3] = far[z.chunk :, :].astype(F32)
        blocks = [gather[i] for i in range(4)]
        w = HD // 4
        vec = lanes([g[:8, : z.shard] for g in blocks])
        up = lanes([g[: z.ff // HD, UP_AT : UP_AT + w] for g in blocks])
        qv = lanes([g[: 2 * z.heads, QV_AT : QV_AT + w] for g in blocks])
    else:
        w_out[...] = whole[...]
        vec, up, qv = vec_in[...], up_in[...], qv_in[...]
    up_row = lanes([up[i : i + 1] for i in range(z.ff // HD)])
    query_b = lanes([qv[2 * h : 2 * h + 1] for h in range(z.heads)])
    value_b = lanes([qv[2 * h + 1 : 2 * h + 2] for h in range(z.heads)])
    small[...] = vec
    small[6:7, : z.ff] = up_row
    normed = (normal[...] * vec[0:1] + vec[1:2]).astype(LOW)
    normed_out[...] = normed
    projected = dot(normed, w_out[...].reshape(z.width, 3 * z.inner), NN)
    n = z.inner
    query = ((projected[:, :n] + query_b) * QUERY_SCALE).astype(LOW)
    key = projected[:, n : 2 * n].astype(LOW)
    value = (projected[:, 2 * n :] + value_b).astype(LOW)
    act[0] = query
    act[1] = key
    act[2] = value
    place = lax.broadcasted_iota(jnp.int32, (z.rows, z.rows), 1)
    valid = (place < z.half) | ((place >= z.padded) & (place < z.padded + z.half))
    done = []
    for h in range(z.heads):
        cut = slice(h * HD, (h + 1) * HD)
        scores = jnp.where(valid, dot(query[:, cut], key[:, cut], NT), -1e30)
        exponent = jnp.exp(scores - jnp.max(scores, axis=-1, keepdims=True))
        soft = exponent * (1.0 / jnp.sum(exponent, axis=-1, keepdims=True))
        soft_out[h] = soft
        done.append(dot(soft.astype(LOW), value[:, cut], NN))
    attended[...] = z.squeeze(lanes(done)).astype(LOW)


def feed_kernel(z, *refs):
    refs = list(refs)
    if z.direct:
        feed, feed_in, feed_their, near, near_in, near_their, far, far_their = refs[:8]
        refs = refs[8:]
    else:
        whole = refs[0]
        refs = refs[1:]
    att = refs[: z.nt]
    stream, cot, small = refs[z.nt : z.nt + 3]
    (w_out, att_out, middle_out, hidden_out, normed_out, pre_out, part_out, low_out, own_att, small_out) = refs[
        z.nt + 3 : z.nt + 13
    ]
    sends, heads = refs[z.nt + 13 : -1], refs[-1]
    t = lax.axis_index("tp")
    if z.direct:
        c, b = lax.axis_index("ctx"), lax.axis_index("fsdp")
        mine, other = z.half_of(c), z.half_of(1 - c)
        first, last = pl.ds(0, 2 * z.ff), pl.ds(2 * z.ff, z.nt * z.inner)
        for at, rest, proj in ((b, feed, near), (b ^ (1 + c), feed_in, near_in), (b ^ (2 - c), feed_their, near_their)):
            w_out[at, :, first] = rest[...]
            w_out[at, :, last] = proj[...]
        w_out[b ^ 3, mine, :] = far[...]
        w_out[b ^ 3, other, :] = far_their[...]
    else:
        w_out[...] = whole[...]
    n = z.inner
    w_up = w_out[:, :, : z.ff].reshape(z.width, z.ff)
    w_down_t = w_out[:, :, z.ff : 2 * z.ff].reshape(z.width, z.ff)
    w_proj_t = w_out[:, :, 2 * z.ff :].reshape(z.width, z.nt * n)
    grad_out_low = cot[...]
    grad_out = grad_out_low.astype(F32)
    for k in range(z.nt):
        heads[t ^ k] = z.spread(read(att[k]))
    attended = lanes([heads[i] for i in range(z.nt)]).astype(LOW)
    att_out[...] = attended
    branch = dot(attended, w_proj_t, NT)
    middle = stream[...].astype(F32) + branch + small[2:3]
    middle_out[...] = middle
    normal, inverse = normalise(middle)
    gain = small[3:4]
    normed = (normal * gain + small[4:5]).astype(LOW)
    normed_out[...] = normed
    hidden, slope = gelu_and_slope(dot(normed, w_up, NN) + small[6:7, : z.ff])
    hidden_out[...] = hidden.astype(LOW)
    grad_pre = (dot(grad_out_low, w_down_t, NN) * slope).astype(LOW)
    pre_out[...] = grad_pre
    grad_normed = dot(grad_pre, w_up, NT)
    part = grad_out * (1.0 / z.nt) + norm_backward(grad_normed, normal, inverse, gain)
    part_out[...] = part
    low = part.astype(LOW)
    low_out[...] = low
    grad_att = dot(low, w_proj_t, NN)
    for i in range(z.nt):
        heads[i] = grad_att[:, i * n : (i + 1) * n]
    own_att[...] = heads[t]
    for k in range(1, z.nt):
        sends[k - 1][...] = z.squeeze(heads[t ^ k]).astype(LOW)
    small_out[...] = jnp.zeros(small_out.shape, F32)
    small_out[2:3] = total_rows(part)
    small_out[3:4] = total_rows(grad_normed * normal)
    small_out[4:5] = total_rows(grad_normed)
    small_out[5:6] = total_rows(grad_out) * (1.0 / z.nt)
    small_out[6:7, : z.ff] = total_rows(grad_pre.astype(F32))


def down_kernel(z, hidden, w, kept, sent, scratch):
    h = lax.axis_index("tp") & 1
    w_down_t = w[:, :, z.ff : 2 * z.ff].reshape(z.width, z.ff)
    scratch[...] = dot(hidden[...], w_down_t, NT)
    kept[...] = scratch[z.half_rows(h), :]
    sent[...] = scratch[z.half_rows(1 - h), :].astype(LOW)


def add_low_kernel(kept, received, out):
    rows = kept.shape[0]
    out[:rows, :] = (kept[...] + read(received)).astype(LOW)
    if out.shape[0] > rows:
        out[rows:, :] = jnp.zeros((out.shape[0] - rows, out.shape[1]), LOW)


def store_halves(z, value, at, keep, sent, sent_at=None):
    cols = pl.ds(at, value.shape[1])
    sent_cols = pl.ds(at if sent_at is None else sent_at, value.shape[1])
    c = lax.axis_index("ctx") if z.direct else 0
    b = lax.axis_index("fsdp") if z.direct else 0
    for j in range(4):
        first = value[j * z.part : j * z.part + z.chunk]
        second = value[j * z.part + z.chunk : (j + 1) * z.part]
        if z.direct:
            keep[j ^ b, :, cols] = jnp.where(c == 0, first, second)
            rows = pl.ds(pl.multiple_of((j ^ b) * z.chunk, 16), z.chunk)
            sent[rows, sent_cols] = jnp.where(c == 0, second, first).astype(LOW)
        else:
            keep[j, :, cols] = first
            sent[pl.ds(j * z.chunk, z.chunk), sent_cols] = second.astype(LOW)


def feed_grad_kernel(z, normed, pre, cot, hidden, keep, sent):
    store_halves(z, dot(normed[...], pre[...], TN), 0, keep, sent)
    store_halves(z, dot(cot[...], hidden[...], TN), z.ff, keep, sent)


def qkv_grad_kernel(z, feed_sent, normed, grads, keep, sent):
    sent[:, : 2 * z.ff] = feed_sent[...]
    sent[:, 2 * z.ff + 3 * z.inner :] = jnp.zeros((sent.shape[0], z.all_cols - 2 * z.ff - 3 * z.inner), LOW)
    store_halves(z, dot(normed[...], grads[...], TN), 0, keep, sent, 2 * z.ff)


def proj_grad_kernel(z, low, att, keep, sent=None):
    value = dot(low[...], att[...], TN)
    b = lax.axis_index("fsdp") if z.direct else 0
    for j in range(4):
        keep[j ^ b] = value[j * z.part : (j + 1) * z.part]
    if z.direct:
        c = lax.axis_index("ctx")
        sent[: z.part, :] = keep[2 - c].astype(LOW)
        sent[z.part :, :] = keep[3, z.half_of(1 - c), :].astype(LOW)


def split_kernel(z, keep, keep_qkv, received, out, kept):
    c = lax.axis_index("ctx")
    for target, at, kind in ((out, (1 + c, 3), LOW), (kept, (0, 2 - c), F32)):
        for i in range(2):
            rows = pl.ds(pl.multiple_of(at[i] * z.chunk, 16), z.chunk)
            total = keep[at[i]] + received[rows, : 2 * z.ff].astype(F32)
            target[i, :, : 2 * z.ff] = total.astype(kind)
            last = pl.ds(2 * z.ff, 3 * z.inner)
            total = keep_qkv[at[i]] + received[rows, last].astype(F32)
            target[i, :, last] = total.astype(kind)
            target[i, :, 2 * z.ff + 3 * z.inner :] = jnp.zeros((z.chunk, z.all_cols - 2 * z.ff - 3 * z.inner), kind)


def proj_one_kernel(z, keep, received, near, far):
    c = lax.axis_index("ctx")
    near[...] = (keep[1 + c] + received[: z.part, :].astype(F32)).astype(LOW)
    far[...] = (keep[3, z.half_of(c), :] + received[z.part :, :].astype(F32)).astype(LOW)


def by_half(mine, other):
    c = lax.axis_index("ctx")
    return rows_of([jnp.where(c == 0, mine, other), jnp.where(c == 0, other, mine)])


def feed_final_kernel(z, own, theirs, up, down):
    total = by_half(own[...], read(theirs))
    up[...] = total[:, : z.ff]
    down[...] = total[:, z.ff :]


def unfold(z, v):
    return rows_of([v[:, i * z.inner : (i + 1) * z.inner] for i in range(4)])


def fold(v):
    n = v.shape[0] // 4
    return lanes([v[i * n : (i + 1) * n] for i in range(4)])


def back_kernel(z, *refs):
    own_att, got = refs[0], refs[1 : z.nt]
    act, soft, w, normal, inverse, part, small, small_in = refs[z.nt : z.nt + 8]
    grads_out, qv_out, kept, sent, scratch = refs[z.nt + 8 :]
    t = lax.axis_index("tp")
    grad_att = (own_att[...] + z.spread(sum(read(g) for g in got))).astype(LOW)
    parts = [[], [], []]
    query, key, value = act[0], act[1], act[2]
    for h in range(z.heads):
        cut = slice(h * HD, (h + 1) * HD)
        ga = grad_att[:, cut]
        p = soft[h]
        grad_soft = dot(ga, value[:, cut], NT)
        delta = jnp.sum(p * grad_soft, axis=-1, keepdims=True)
        grad_scores = (p * (grad_soft - delta)).astype(LOW)
        parts[0].append((dot(grad_scores, key[:, cut], NN).astype(LOW).astype(F32) * QUERY_SCALE).astype(LOW))
        parts[1].append(dot(grad_scores, query[:, cut], TN).astype(LOW))
        parts[2].append(dot(p.astype(LOW), ga, TN).astype(LOW))
    grads = lanes(parts[0] + parts[1] + parts[2])
    grads_out[...] = grads
    n = z.inner
    qv_out[...] = total_rows(grads.astype(F32))
    grad_normed = dot(grads, w[...].reshape(z.width, 3 * n), NT)
    scratch[...] = part[...] + norm_backward(grad_normed, normal[...], inverse[:, :1], small[0:1])
    row = lax.broadcasted_iota(jnp.int32, (8, z.width), 0)
    vec = small_in[...]
    vec = jnp.where(row == 0, total_rows(grad_normed * normal[...]), vec)
    vec = jnp.where(row == 1, total_rows(grad_normed), vec)
    h = t & 1
    kept[: z.padded, :] = scratch[z.half_rows(h), :]
    kept[z.padded :, :] = vec
    sent[: z.padded, :] = scratch[z.half_rows(1 - h), :].astype(LOW)
    sent[z.padded :, :] = vec.astype(LOW)


def out_total_kernel(z, own, received, middle, small, out):
    rows = z.half_rows(lax.axis_index("tp") & 1)
    total = (read(own) + read(received))[: z.padded]
    out[...] = (middle[rows, :] + total + small[5:6]).astype(LOW)


def proj_two_kernel(z, keep, near, far, out, kept, scratch):
    c, t = lax.axis_index("ctx"), lax.axis_index("tp")
    other = read(far)
    zero = jnp.zeros(other.shape, F32)
    proj = keep[0] + read(near) + rows_of([jnp.where(c == 0, other, zero), jnp.where(c == 0, zero, other)])
    for i in range(z.nt):
        scratch[i] = fold(proj[:, i * z.inner : (i + 1) * z.inner])
    kept[0] = scratch[t]
    kept[1] = scratch[t ^ 2]
    out[...] = rows_of([scratch[t ^ 1], scratch[t ^ 3]]).astype(LOW)


def sum_rows_kernel(z, own, received, small, qv, out, vec):
    total = read(own) + read(received)
    out[...] = total[: z.padded].astype(LOW)
    vec[:8, :] = total[z.padded :]
    vec[8:, :] = jnp.zeros((8, z.width), F32)
    vec[8:9, : z.ff] = small[6:7, : z.ff]
    vec[9:10, : 3 * z.inner] = qv[...]


def proj_pair_kernel(z, kept, received, own, sent):
    arrived = read(received)
    own[...] = kept[0] + arrived[: z.tail]
    sent[...] = (kept[1] + arrived[z.tail :]).astype(LOW)


def cross_kernel(kept, received, own, out):
    own[...] = kept[0] + received[0].astype(F32)
    out[...] = (kept[1] + received[1].astype(F32)).astype(LOW)


def small_kernel(z, vec, their, near, far, own, scratch):
    c, b = lax.axis_index("ctx"), lax.axis_index("fsdp")
    vectors = vec[...] + their[...]
    up = rows_of([vectors[8:9, i * HD : (i + 1) * HD] for i in range(z.ff // HD)])
    pieces = []
    for h in range(z.heads):
        pieces.append(vectors[9:10, h * HD : (h + 1) * HD])
        pieces.append(vectors[9:10, 2 * z.inner + h * HD : 2 * z.inner + (h + 1) * HD])
    qv_rows = rows_of(pieces)
    scratch[...] = jnp.zeros(scratch.shape, F32)
    w = HD // 4
    for i in range(4):
        scratch[i, :8, : z.shard] = vectors[:8, i * z.shard : (i + 1) * z.shard]
        scratch[i, : z.ff // HD, UP_AT : UP_AT + w] = up[:, i * w : (i + 1) * w]
        scratch[i, : 2 * z.heads, QV_AT : QV_AT + w] = qv_rows[:, i * w : (i + 1) * w]
    once = jnp.where(c == 0, 1.0, 0.0)
    near[...] = scratch[b ^ (1 + c)].astype(LOW)
    far[...] = (scratch[b ^ 3] * once).astype(LOW)
    own[...] = scratch[b] * once


def halves_of(z, own, received):
    h = lax.axis_index("tp") & 1
    return jnp.where(h == 0, own, received), jnp.where(h == 0, received, own)


def swap_kernel(z, out_own, out_in, in_own, in_in, *refs):
    out_mine, out_theirs = halves_of(z, read(out_own), read(out_in))
    in_mine, in_theirs = halves_of(z, read(in_own), read(in_in))
    theirs = [out_theirs, in_theirs]
    if z.direct:
        proj_own, proj_in, mine, sent, proj = refs
        total = proj_own[...] + read(proj_in)
        proj[...] = total
        theirs.append(total)
    else:
        mine, sent = refs
    mine[0] = out_mine
    mine[1] = in_mine
    sent[...] = rows_of(theirs).astype(LOW)


def last_kernel(z, own, cross, small, near, far, feed_total, feed_sent, qkv_total, qkv_sent):
    value = own[...] + read(cross)
    feed_total[...] = value[:, : 2 * z.ff]
    feed_sent[...] = value[:, : 2 * z.ff].astype(LOW)
    tail = small[...] + read(near) + read(far)
    for out, kind in ((qkv_total, F32), (qkv_sent, LOW)):
        out[: z.chunk, :] = value[:, 2 * z.ff : 2 * z.ff + 3 * z.inner].astype(kind)
        out[z.chunk :, :] = tail.astype(kind)


def qkv_final_kernel(z, own, theirs, qkv, up, qv, *vectors):
    both = by_half(own[: z.chunk, :], theirs[: z.chunk, :].astype(F32))
    for i in range(3):
        qkv[i] = both[:, i * z.inner : (i + 1) * z.inner]
    tail = own[z.chunk :, :] + theirs[z.chunk :, :].astype(F32)
    w = HD // 4
    up[...] = tail[: z.ff // HD, UP_AT : UP_AT + w]
    for h in range(z.heads):
        qv[h] = tail[2 * h : 2 * h + 2, QV_AT : QV_AT + w]
    for i, v in enumerate(vectors):
        v[...] = tail[i : i + 1, : z.shard].reshape(z.shard)


def place_kernel(z, mine, theirs, out, *scratch):
    c = lax.axis_index("ctx")
    target = scratch[0] if scratch else out
    mine, theirs = mine[: z.half], theirs[: z.half]
    target[:, 0, :] = jnp.where(c == 0, mine, theirs)
    target[:, 1, :] = jnp.where(c == 0, theirs, mine)
    if scratch:
        out[...] = target[...].astype(out.dtype)


def final_kernel(z, mine, theirs, *refs):
    if z.direct:
        proj_own, feed_own, feed_in, qkv_own, qkv_in, output, input_grad, proj, up, down, *rest = refs
        total = proj_own[...] + theirs[2 * z.padded :, :].astype(F32)
        proj[...] = unfold(z, total).T
        feed_final_kernel(z, feed_own, feed_in, up, down)
        qkv_final_kernel(z, qkv_own, qkv_in, *rest[:-1])
        scratch = rest[-1]
    else:
        output, input_grad, scratch = refs
    place_kernel(z, mine[1], theirs[z.padded : 2 * z.padded, :].astype(F32), input_grad)
    place_kernel(z, mine[0], theirs[: z.padded, :].astype(F32), output, scratch)


def build(nf, nc, nt):
    def local(
        inputs,
        norm1_gain,
        norm1_bias,
        qkv_weight,
        qv_bias,
        proj_weight,
        proj_bias,
        norm2_gain,
        norm2_bias,
        fc1_weight,
        fc1_bias,
        fc2_weight,
        fc2_bias,
        cotangent,
    ):
        z = Sizes(nf, nt, inputs, qv_bias, fc1_weight)
        part = functools.partial
        rows, width, inner, ff, chunk = z.rows, z.width, z.inner, z.ff, z.chunk
        f = lax.axis_index("fsdp")
        tie = lax.optimization_barrier

        def other_core(value):
            return lax.ppermute(value, "ctx", [(0, 1), (1, 0)])

        def to_tp(value, k):
            return lax.ppermute(value, "tp", [(i, i ^ k) for i in range(nt)])

        def to_far(value):
            return lax.ppermute(value, "fsdp", [(i, i ^ 3) for i in range(nf)])

        def neighbours(value, order):
            pairs = [(2 * i + c, 2 * (i ^ order[c]) + c) for i in range(nf) for c in range(2)]
            return lax.ppermute(value, ("fsdp", "ctx"), pairs)

        def to_near(value):
            return neighbours(value, (1, 2))

        def to_cross(value):
            return neighbours(value, (2, 1))

        def proj_near(value):
            pairs = [(c * nt + i, c * nt + (i ^ (1 + c))) for i in range(nt) for c in range(2)]
            return lax.ppermute(value, ("ctx", "tp"), pairs)

        def pair_of(first, second):
            return call(pair_kernel, [shape((2,) + first.shape, LOW)], [first, second], name="pair")[0]

        qkv3 = qkv_weight.transpose(1, 0, 2)
        down_t = fc2_weight.T
        qv3 = qv_bias.transpose(1, 0, 2)
        x_raw, cot_raw = inputs.transpose(1, 0, 2), cotangent.transpose(1, 0, 2)
        vectors = [norm1_gain, norm1_bias, proj_bias, norm2_gain, norm2_bias, fc2_bias]

        x_recv = other_core(x_raw)
        cot_recv = other_core(cot_raw)
        def frames(x_recv, cot_recv):
            stream, normal_one, inverse_one = call(
                part(frame_kernel, z),
                [shape((rows, width), LOW), shape((rows, width), F32), shape((rows, 128), F32)],
                [x_raw, x_recv],
                name="frame",
            )
            (cot,) = call(part(cot_kernel, z), [shape((rows, width), LOW)], [cot_raw, cot_recv], name="cotangent")
            return stream, normal_one, inverse_one, cot

        if z.direct:
            sources = [qkv3, proj_weight, fc1_bias, qv3] + vectors
            near, far, proj_t, proj_half = call(
                part(pack_kernel, z),
                [
                    shape((z.part + EXTRA, 3 * inner), LOW),
                    shape((chunk + EXTRA, 3 * inner), LOW),
                    shape((z.part, inner), LOW),
                    shape((chunk, inner), LOW),
                ],
                sources,
                [pltpu.VMEM(s.shape, s.dtype) for s in sources] + [pltpu.SemaphoreType.DMA((len(sources),))],
                name="pack",
                mib=56,
                in_specs=[ANY] * len(sources),
            )
            near, far, proj_t, proj_half, x_recv, cot_recv = tie((near, far, proj_t, proj_half, x_recv, cot_recv))
            got = [to_near(near), to_far(far)]
            proj_got = [proj_near(proj_t), to_tp(proj_half, 3)]
            (feed_own,) = call(
                part(stage_kernel, z),
                [shape((z.part, 2 * ff), LOW)],
                [fc1_weight, down_t],
                [pltpu.VMEM((z.part, ff), LOW)] * 2 + [pltpu.SemaphoreType.DMA((2,))],
                name="stage",
                mib=56,
                in_specs=[ANY] * 2,
            )
            stream, normal_one, inverse_one, cot = frames(x_recv, cot_recv)
            got, proj_got, feed_own, stream, normal_one, inverse_one, cot = tie(
                (got, proj_got, feed_own, stream, normal_one, inverse_one, cot)
            )
            feed_in = to_near(feed_own)
            shared = [other_core(g) for g in got]
            qkv_in = [near, got[0], shared[0], got[1], shared[1]]
            rest_near, rest_far = call(
                part(pack_rest_kernel, z),
                [shape((z.part, nt * inner), LOW), shape((chunk, z.cols), LOW)],
                [feed_own, proj_t, proj_got[0], other_core(proj_got[0]), proj_got[1], other_core(proj_got[1])],
                [pltpu.VMEM((nt, z.part, inner), F32)],
                name="pack_rest",
            )
            near_in, far_in = to_near(rest_near), to_far(rest_far)
        else:
            stream, normal_one, inverse_one, cot = frames(x_recv, cot_recv)
            whole = lax.all_gather(qkv3, "fsdp", axis=1, tiled=True)
            whole = whole.transpose(1, 0, 2).reshape(4, z.part, 3 * inner)
            vec = jnp.stack(vectors + [vectors[0]] * 2).astype(F32)
            qv_rows = qv3.reshape(2 * z.heads, -1).astype(F32)
            gathered = [lax.all_gather(v, "fsdp", axis=1, tiled=True) for v in (vec, fc1_bias.astype(F32), qv_rows)]
            qkv_in = [whole] + gathered
            proj_t = proj_weight.T
            rest = jnp.concatenate([fc1_weight, down_t, lax.all_gather(proj_t, "tp", axis=1, tiled=True)], 1)
            rest_in = [lax.all_gather(rest, "fsdp", axis=0, tiled=True).reshape(4, z.part, z.cols)]

        small, w_qkv, normed_one, act, attended, soft = call(
            part(attend_kernel, z),
            [
                shape((8, width), F32),
                shape((4, z.part, 3 * inner), LOW),
                shape((rows, width), LOW),
                shape((3, rows, inner), LOW),
                shape((z.dense, 128), LOW),
                shape((z.heads, rows, rows), F32),
            ],
            qkv_in + [normal_one],
            [pltpu.VMEM((4, EXTRA, 3 * inner), F32)] if z.direct else [],
            name="attend",
        )
        att = [to_tp(attended, k) for k in range(1, nt)]
        if z.direct:
            att, near_in, far_in = tie((att, near_in, far_in))
            rest_in = [feed_own, feed_in, other_core(feed_in), rest_near, near_in, other_core(near_in)]
            rest_in += [far_in, other_core(far_in)]

        (w_rest, att_all, middle, hidden, normed_two, grad_pre, part_middle, part_low, own_att, small_two, *att_sends) = (
            call(
                part(feed_kernel, z),
                [
                    shape((4, z.part, z.cols), LOW),
                    shape((rows, nt * inner), LOW),
                    shape((rows, width), F32),
                    shape((rows, ff), LOW),
                    shape((rows, width), LOW),
                    shape((rows, ff), LOW),
                    shape((rows, width), F32),
                    shape((rows, width), LOW),
                    shape((rows, inner), F32),
                    shape((8, width), F32),
                ]
                + [shape((z.dense, 128), LOW)] * (nt - 1),
                rest_in + [attended] + att + [stream, cot, small],
                [pltpu.VMEM((nt, rows, inner), F32)],
                name="feed",
            )
        )
        att_got = [to_tp(att_sends[k - 1], k) for k in range(1, nt)]
        all_cols = z.all_cols
        keep, sent = call(
            part(feed_grad_kernel, z),
            [shape((4, chunk, 2 * ff), F32), shape((4 * chunk, 2 * ff), LOW)],
            [normed_two, grad_pre, cot, hidden],
            name="feed_grad",
        )
        keep_proj, *sent_proj = call(
            part(proj_grad_kernel, z),
            [shape((4, z.part, nt * inner), F32)]
            + ([shape((z.part + chunk, nt * inner), LOW)] if z.direct else []),
            [part_low, att_all],
            name="proj_grad",
        )
        out_kept, out_sent = call(
            part(down_kernel, z),
            [shape((z.padded, width), F32), shape((z.padded, width), LOW)],
            [hidden, w_rest],
            [pltpu.VMEM((rows, width), F32)],
            name="down",
        )
        out_one = to_tp(out_sent, 1)
        if z.direct:
            proj_in = other_core(sent_proj[0])
            att_got, out_one, keep, sent, proj_in = tie((att_got, out_one, keep, sent, proj_in))
            near, far = call(
                part(proj_one_kernel, z),
                [shape((z.part, nt * inner), LOW), shape((chunk, nt * inner), LOW)],
                [keep_proj, proj_in],
                name="proj_one",
            )
            proj_in = [to_near(near), to_far(far)]
        (out_low,) = call(add_low_kernel, [shape((z.padded + 16, width), LOW)], [out_kept, out_one], name="out_pair")
        out_two = to_tp(out_low, 2)

        grads, qv_sum, in_kept, in_sent = call(
            part(back_kernel, z),
            [
                shape((rows, 3 * inner), LOW),
                shape((1, 3 * inner), F32),
                shape((z.padded + 8, width), F32),
                shape((z.padded + 8, width), LOW),
            ],
            [own_att] + att_got + [act, soft, w_qkv, normal_one, inverse_one, part_middle, small, small_two],
            [pltpu.VMEM((rows, width), F32)],
            name="back",
        )
        in_one = to_tp(in_sent, 1)
        keep_qkv, sent = call(
            part(qkv_grad_kernel, z),
            [shape((4, chunk, 3 * inner), F32), shape((4 * chunk, all_cols), LOW)],
            [sent, normed_one, grads],
            name="qkv_grad",
        )
        if z.direct:
            sent = other_core(sent)
            in_one, out_two, proj_in, sent = tie((in_one, out_two, proj_in, sent))
            grad_sent, grad_kept = call(
                part(split_kernel, z),
                [shape((2, chunk, all_cols), LOW), shape((2, chunk, all_cols), F32)],
                [keep, keep_qkv, sent],
                name="split",
            )
            grad_in = to_near(grad_sent)
        (in_low,) = call(add_low_kernel, [shape((z.padded + 8, width), LOW)], [in_kept, in_one], name="in_pair")
        in_two = to_tp(in_low, 2)
        (out_low,) = call(
            part(out_total_kernel, z),
            [shape((z.padded, width), LOW)],
            [out_low, out_two, middle, small],
            name="out_total",
        )
        out_in = to_tp(out_low, 1)
        if z.direct:
            proj_sent, proj_kept = call(
                part(proj_two_kernel, z),
                [shape((2 * z.tail, width), LOW), shape((2, z.tail, width), F32)],
                [keep_proj] + proj_in,
                [pltpu.VMEM((nt, z.tail, width), F32)],
                name="proj_two",
            )
            proj_in = to_tp(proj_sent, 1)
        if z.direct:
            in_two, out_in, grad_in, proj_in = tie((in_two, out_in, grad_in, proj_in))
        in_low, vec = call(
            part(sum_rows_kernel, z),
            [shape((z.padded, width), LOW), shape((16, width), F32)],
            [in_low, in_two, small_two, qv_sum],
            name="sum_rows",
        )
        in_in = to_tp(in_low, 1)
        proj_all = []
        if z.direct:
            grad_own, cross = call(
                cross_kernel,
                [shape((chunk, all_cols), F32), shape((chunk, all_cols), LOW)],
                [grad_kept, grad_in],
                name="cross",
            )
            cross = to_cross(cross)
            proj_own, proj_sent = call(
                part(proj_pair_kernel, z),
                [shape((z.tail, width), F32), shape((z.tail, width), LOW)],
                [proj_kept, proj_in],
                name="proj_pair",
            )
            proj_two = to_tp(proj_sent, 2)
            near, far, small_own = call(
                part(small_kernel, z),
                [shape((EXTRA, 3 * inner), LOW)] * 2 + [shape((EXTRA, 3 * inner), F32)],
                [vec, other_core(vec)],
                [pltpu.VMEM((4, EXTRA, 3 * inner), F32)],
                name="small",
            )
            near, far = to_near(near), to_far(far)
            in_in, proj_two, cross, near, far = tie((in_in, proj_two, cross, near, far))
            proj_all = [proj_own, proj_two]
            feed_own, feed_sent, qkv_own, qkv_sent = call(
                part(last_kernel, z),
                [
                    shape((chunk, 2 * ff), F32),
                    shape((chunk, 2 * ff), LOW),
                    shape((chunk + EXTRA, 3 * inner), F32),
                    shape((chunk + EXTRA, 3 * inner), LOW),
                ],
                [grad_own, cross, small_own, near, far],
                name="last",
            )
            feed_in, qkv_in = other_core(feed_sent), other_core(qkv_sent)
        mine, theirs, *proj_own = call(
            part(swap_kernel, z),
            [shape((2, z.padded, width), F32), shape((rows + (z.tail if proj_all else 0), width), LOW)]
            + ([shape((z.tail, width), F32)] if proj_all else []),
            [out_low, out_in, in_low, in_in] + proj_all,
            name="swap",
        )
        theirs = other_core(theirs)
        results = [shape((z.half, 2, width), LOW), shape((z.half, 2, width), F32)]
        scratch = [pltpu.VMEM((z.half, 2, width), F32)]
        if z.direct:
            output, input_grad, proj_grad, fc1_grad, fc2_grad, qkv_grad, up_grad, qv_grad, *vec_grads = call(
                part(final_kernel, z),
                results
                + [
                    shape((inner, z.shard), F32),
                    shape((z.shard, ff), F32),
                    shape((z.shard, ff), F32),
                    shape((3, z.shard, inner), F32),
                    shape(fc1_bias.shape, F32),
                    shape(qv3.shape, F32),
                ]
                + [shape((z.shard,), F32)] * 6,
                [mine, theirs, proj_own[0], feed_own, feed_in, qkv_own, qkv_in],
                scratch,
                name="final",
            )
        else:
            output, input_grad = call(part(final_kernel, z), results, [mine, theirs], scratch, name="final")

            def joined(keep, sent):
                return jnp.stack([keep.astype(LOW), sent.reshape(keep.shape)], 1).reshape(width, -1)

            def scatter(whole):
                whole = lax.psum(whole, "ctx")
                return lax.psum_scatter(whole, "fsdp", scatter_dimension=0, tiled=True).astype(F32)

            extra = all_cols - 2 * ff - 3 * inner
            total = scatter(joined(jnp.concatenate([keep, jnp.pad(keep_qkv, ((0, 0), (0, 0), (0, extra)))], 2), sent))
            fc1_grad, fc2_grad = total[:, :ff], total[:, ff : 2 * ff]
            qkv_grad = total[:, 2 * ff : 2 * ff + 3 * inner].reshape(z.shard, 3, inner).transpose(1, 0, 2)
            proj_grad = scatter(keep_proj.reshape(width, -1).astype(LOW)).astype(LOW)
            proj_grad = lax.psum_scatter(proj_grad, "tp", scatter_dimension=1, tiled=True).astype(F32).T

            def own_columns(value):
                value = lax.psum(value, ("fsdp", "ctx"))
                return lax.dynamic_slice_in_dim(value, f * (value.shape[1] // nf), value.shape[1] // nf, 1)

            vec_grads = own_columns(vec[:6])
            up_grad = own_columns(vec[8, :ff].reshape(-1, HD))
            qv_grad = vec[9, : 3 * inner].reshape(3, z.heads, HD)[0::2].transpose(1, 0, 2)
            qv_grad = own_columns(qv_grad.reshape(2 * z.heads, HD)).reshape(qv3.shape)
        return (
            output.transpose(1, 0, 2),
            input_grad.transpose(1, 0, 2),
            vec_grads[0],
            vec_grads[1],
            qkv_grad.transpose(1, 0, 2),
            qv_grad.transpose(1, 0, 2),
            proj_grad,
            vec_grads[2],
            vec_grads[3],
            vec_grads[4],
            fc1_grad,
            up_grad,
            fc2_grad.T,
            vec_grads[5],
        )

    return local


def solution(mesh):
    sizes = mesh.shape
    return jax.shard_map(
        build(sizes["fsdp"], sizes["ctx"], sizes["tp"]),
        mesh=mesh,
        in_specs=(
            P("fsdp", "ctx", None),
            P("fsdp"),
            P("fsdp"),
            P("fsdp", None, "tp"),
            P(None, "tp", "fsdp"),
            P("tp", "fsdp"),
            P("fsdp"),
            P("fsdp"),
            P("fsdp"),
            P("fsdp", "tp"),
            P("tp", "fsdp"),
            P("tp", "fsdp"),
            P("fsdp"),
            P("fsdp", "ctx", None),
        ),
        out_specs=(
            P("fsdp", "ctx", None),
            P("fsdp", "ctx", None),
            P("fsdp"),
            P("fsdp"),
            P("fsdp", None, "tp"),
            P(None, "tp", "fsdp"),
            P("tp", "fsdp"),
            P("fsdp"),
            P("fsdp"),
            P("fsdp"),
            P("fsdp", "tp"),
            P("tp", "fsdp"),
            P("tp", "fsdp"),
            P("fsdp"),
        ),
        check_vma=False,
    )
```

```python
import functools

import jax
import jax.numpy as jnp
from jax import lax
from jax.experimental import pallas as pl
from jax.experimental.pallas import tpu as pltpu
from jax.sharding import PartitionSpec as P

HD = 64
EPSILON = 1e-06
QUERY_SCALE = 0.125
F32 = jnp.float32
LOW = jnp.bfloat16
NN = ((1,), (0,))
NT = ((1,), (1,))
TN = ((0,), (0,))
VMEM = pl.BlockSpec(memory_space=pltpu.VMEM)
ANY = pl.BlockSpec(memory_space=pl.ANY)
EXTRA = 16
VEC_ROWS = 144
UP_AT, QV_AT = 256, 384


def dot(left, right, dims):
    return lax.dot_general(left, right, (dims, ((), ())), preferred_element_type=F32)


def shape(dims, kind):
    return jax.ShapeDtypeStruct(tuple(dims), kind)


def call(kernel, outs, args, scratch=(), name=None, mib=20, in_specs=None, alias=None):
    return pl.pallas_call(
        kernel,
        out_shape=tuple(outs),
        in_specs=in_specs or [VMEM] * len(args),
        out_specs=tuple([VMEM] * len(outs)),
        scratch_shapes=list(scratch),
        input_output_aliases=alias or {},
        name=name,
        compiler_params=pltpu.CompilerParams(vmem_limit_bytes=mib << 20),
    )(*args)


def gelu_and_slope(v):
    cdf = 0.5 * (1.0 + lax.erf(v * 0.7071067811865476))
    density = jnp.exp(-0.5 * v * v) * 0.3989422804014327
    return v * cdf, cdf + v * density


def mean(v):
    return jnp.mean(v, axis=-1, keepdims=True)


def total_rows(v):
    return jnp.sum(v, axis=0, keepdims=True)


def normalise(v):
    centred = v - mean(v)
    inverse = lax.rsqrt(mean(centred * centred) + EPSILON)
    return centred * inverse, inverse


def norm_backward(grad_normed, normal, inverse, gain):
    scaled = grad_normed * gain
    return inverse * (scaled - mean(scaled) - normal * mean(scaled * normal))


def row_half(t):
    return (t ^ (t >> 1)) & 1


def lanes(parts):
    return jnp.concatenate(parts, axis=1)


def rows_of(parts):
    return jnp.concatenate(parts, axis=0)


def read(ref):
    return ref[...].astype(F32)


class Sizes:
    def __init__(self, nf, nt, inputs, qv_bias, fc1_weight):
        self.nf, self.nt = nf, nt
        _, self.half, self.width = inputs.shape
        self.shard = self.width // nf
        self.heads = qv_bias.shape[1]
        self.inner = self.heads * HD
        self.ff = fc1_weight.shape[1]
        self.pad = -self.half % 8
        self.padded = self.half + self.pad
        self.rows = 2 * self.padded
        self.part = self.width // 4
        self.chunk = self.part // 2
        self.tail = self.part // 4
        self.direct = nf == 4
        self.cols = 2 * self.ff + nt * self.inner
        self.early = 1152 if self.ff == 768 else self.ff
        self.all_cols = 2 * self.ff + -(-3 * self.inner // 128) * 128
        self.dense = self.rows * self.inner // 128

    def half_rows(self, h):
        return pl.ds(pl.multiple_of(h * self.padded, 8), self.padded)

    def half_of(self, c):
        return pl.ds(pl.multiple_of(c * self.chunk, 16), self.chunk)

    def squeeze(self, v):
        return rows_of([v[:, :128], lanes([v[: self.padded, 128:], v[self.padded :, 128:]])])

    def spread(self, v):
        tail = v[self.rows :]
        return lanes([v[: self.rows], rows_of([tail[:, :HD], tail[:, HD:]])])


def fetch(sources, copies, sem):
    moves = [pltpu.make_async_copy(s, d, sem.at[i]) for i, (s, d) in enumerate(zip(sources, copies))]
    for m in moves:
        m.start()
    for m in moves:
        m.wait()


def stage_kernel(z, up, down_t, out, rest, one, two, sem):
    fetch((up, down_t), (one, two), sem)
    first = z.early - z.ff
    out[:, : z.ff] = one[...]
    out[:, z.ff :] = two[:, :first]
    rest[...] = two[:, first:]


def pack_kernel(z, *refs):
    sources, (near, far, proj_t, proj_half) = refs[:10], refs[10:14]
    copies, sem = refs[14:24], refs[24]
    fetch(sources, copies, sem)
    qkv, proj, up_b, qv_b = copies[:4]
    vectors = copies[4:]
    c = lax.axis_index("ctx")
    whole = lanes([read(qkv.at[i]) for i in range(3)])
    near[: z.part, :] = whole.astype(LOW)
    far[: z.chunk, :] = jnp.where(c == 0, whole[: z.chunk], whole[z.chunk :]).astype(LOW)
    row = lax.broadcasted_iota(jnp.int32, (EXTRA, z.shard), 0)
    vec = jnp.zeros((EXTRA, z.shard), F32)
    for i, v in enumerate(vectors):
        vec = jnp.where(row == i, read(v).reshape(1, z.shard), vec)
    biases = read(qv_b)
    biases = rows_of([biases[h, i : i + 1] for h in range(z.heads) for i in range(2)])
    for out, at in ((near, z.part), (far, z.chunk)):
        out[at:, :] = jnp.zeros((EXTRA, 3 * z.inner), LOW)
        out[at:, : z.shard] = vec.astype(LOW)
        out[at : at + up_b.shape[0], UP_AT : UP_AT + up_b.shape[1]] = up_b[...]
        out[at : at + 2 * z.heads, QV_AT : QV_AT + biases.shape[1]] = biases.astype(LOW)
    turned = read(proj).T
    proj_t[...] = turned.astype(LOW)
    proj_half[...] = jnp.where(c == 0, turned[: z.chunk], turned[z.chunk :]).astype(LOW)


def pair_kernel(first, second, out):
    out[0] = first[...]
    out[1] = second[...]


def pack_rest_kernel(z, feed, rest, proj_t, near_in, near_their, far_in, far_their, near, far, scratch):
    c, t = lax.axis_index("ctx"), lax.axis_index("tp")
    scratch[t] = read(proj_t)
    scratch[t ^ (1 + 2 * c)] = read(near_in)
    scratch[t ^ (3 - 2 * c)] = read(near_their)
    scratch[t ^ 2, z.half_of(c), :] = read(far_in)
    scratch[t ^ 2, z.half_of(1 - c), :] = read(far_their)
    near[:, : 2 * z.ff - z.early] = rest[...]
    near[:, 2 * z.ff - z.early :] = lanes([scratch[i] for i in range(4)]).astype(LOW)
    far[:, : z.early] = feed[z.half_of(c), :]
    far[:, z.early :] = near[z.half_of(c), :]


def own_frame(z, keep, received):
    c = lax.axis_index("ctx")
    zero = jnp.zeros((z.pad, z.width), F32)
    pieces = []
    for ref in (keep, received):
        pieces.append(jnp.where(c == 0, ref[:, 0, :].astype(F32), ref[:, 1, :].astype(F32)))
        pieces.append(zero)
    return rows_of(pieces)


def frame_kernel(z, keep, received, stream, normal, inverse):
    values = own_frame(z, keep, received)
    stream[...] = values.astype(LOW)
    n, i = normalise(values)
    normal[...] = n
    inverse[...] = jnp.broadcast_to(i, inverse.shape)


def cot_kernel(z, keep, received, stream):
    stream[...] = own_frame(z, keep, received).astype(LOW)


def attend_kernel(z, *refs):
    refs = list(refs)
    if z.direct:
        own, near, near_their, far, far_their = refs[:5]
        refs = refs[5:]
    else:
        whole, vec_in, up_in, qv_in = refs[:4]
        refs = refs[4:]
    normal, small, w_out, normed_out, act, attended, soft_out = refs[:7]
    if z.direct:
        c, b = lax.axis_index("ctx"), lax.axis_index("fsdp")
        gather = refs[7]
        for ref, at in ((own, b), (near, b ^ (1 + c)), (near_their, b ^ (2 - c))):
            w_out[at] = ref[: z.part, :]
            gather[at] = ref[z.part :, :].astype(F32)
        w_out[b ^ 3, z.half_of(c), :] = far[: z.chunk, :]
        w_out[b ^ 3, z.half_of(1 - c), :] = far_their[: z.chunk, :]
        gather[b ^ 3] = far[z.chunk :, :].astype(F32)
        blocks = [gather[i] for i in range(4)]
        w = HD // 4
        vec = lanes([g[:8, : z.shard] for g in blocks])
        up = lanes([g[: z.ff // HD, UP_AT : UP_AT + w] for g in blocks])
        qv = lanes([g[: 2 * z.heads, QV_AT : QV_AT + w] for g in blocks])
    else:
        w_out[...] = whole[...]
        vec, up, qv = vec_in[...], up_in[...], qv_in[...]
    up_row = lanes([up[i : i + 1] for i in range(z.ff // HD)])
    query_b = lanes([qv[2 * h : 2 * h + 1] for h in range(z.heads)])
    value_b = lanes([qv[2 * h + 1 : 2 * h + 2] for h in range(z.heads)])
    small[...] = vec
    small[6:7, : z.ff] = up_row
    normed = (normal[...] * vec[0:1] + vec[1:2]).astype(LOW)
    normed_out[...] = normed
    projected = dot(normed, w_out[...].reshape(z.width, 3 * z.inner), NN)
    n = z.inner
    query = ((projected[:, :n] + query_b) * QUERY_SCALE).astype(LOW)
    key = projected[:, n : 2 * n].astype(LOW)
    value = (projected[:, 2 * n :] + value_b).astype(LOW)
    act[0] = query
    act[1] = key
    act[2] = value
    place = lax.broadcasted_iota(jnp.int32, (z.rows, z.rows), 1)
    valid = (place < z.half) | ((place >= z.padded) & (place < z.padded + z.half))
    done = []
    for h in range(z.heads):
        cut = slice(h * HD, (h + 1) * HD)
        scores = jnp.where(valid, dot(query[:, cut], key[:, cut], NT), -1e30)
        exponent = jnp.exp(scores - jnp.max(scores, axis=-1, keepdims=True))
        soft = exponent * (1.0 / jnp.sum(exponent, axis=-1, keepdims=True))
        soft_out[h] = soft
        done.append(dot(soft.astype(LOW), value[:, cut], NN))
    attended[...] = z.squeeze(lanes(done)).astype(LOW)


def feed_kernel(z, *refs):
    refs = list(refs)
    if z.direct:
        feed, feed_in, feed_their, near, near_in, near_their, far, far_their = refs[:8]
        refs = refs[8:]
    else:
        whole = refs[0]
        refs = refs[1:]
    att = refs[: z.nt]
    stream, cot, small = refs[z.nt : z.nt + 3]
    (w_out, att_out, middle_out, hidden_out, normed_out, pre_out, part_out, low_out, own_att, small_out) = refs[
        z.nt + 3 : z.nt + 13
    ]
    sends, heads = refs[z.nt + 13 : -1], refs[-1]
    t = lax.axis_index("tp")
    if z.direct:
        c, b = lax.axis_index("ctx"), lax.axis_index("fsdp")
        mine, other = z.half_of(c), z.half_of(1 - c)
        first, last = pl.ds(0, z.early), pl.ds(z.early, z.cols - z.early)
        for at, one, two in ((b, feed, near), (b ^ (1 + c), feed_in, near_in), (b ^ (2 - c), feed_their, near_their)):
            w_out[at, :, first] = one[...]
            w_out[at, :, last] = two[...]
        w_out[b ^ 3, mine, :] = far[...]
        w_out[b ^ 3, other, :] = far_their[...]
    else:
        w_out[...] = whole[...]
    n = z.inner
    w_up = w_out[:, :, : z.ff].reshape(z.width, z.ff)
    w_down_t = w_out[:, :, z.ff : 2 * z.ff].reshape(z.width, z.ff)
    w_proj_t = w_out[:, :, 2 * z.ff :].reshape(z.width, z.nt * n)
    grad_out_low = cot[...]
    grad_out = grad_out_low.astype(F32)
    for k in range(z.nt):
        heads[t ^ k] = z.spread(read(att[k]))
    attended = lanes([heads[i] for i in range(z.nt)]).astype(LOW)
    att_out[...] = attended
    branch = dot(attended, w_proj_t, NT)
    middle = stream[...].astype(F32) + branch + small[2:3]
    middle_out[...] = middle
    normal, inverse = normalise(middle)
    gain = small[3:4]
    normed = (normal * gain + small[4:5]).astype(LOW)
    normed_out[...] = normed
    hidden, slope = gelu_and_slope(dot(normed, w_up, NN) + small[6:7, : z.ff])
    hidden_out[...] = hidden.astype(LOW)
    grad_pre = (dot(grad_out_low, w_down_t, NN) * slope).astype(LOW)
    pre_out[...] = grad_pre
    grad_normed = dot(grad_pre, w_up, NT)
    part = grad_out * (1.0 / z.nt) + norm_backward(grad_normed, normal, inverse, gain)
    part_out[...] = part
    low = part.astype(LOW)
    low_out[...] = low
    grad_att = dot(low, w_proj_t, NN)
    for i in range(z.nt):
        heads[i] = grad_att[:, i * n : (i + 1) * n]
    own_att[...] = heads[t]
    for k in range(1, z.nt):
        sends[k - 1][...] = z.squeeze(heads[t ^ k]).astype(LOW)
    small_out[...] = jnp.zeros(small_out.shape, F32)
    small_out[2:3] = total_rows(part)
    small_out[3:4] = total_rows(grad_normed * normal)
    small_out[4:5] = total_rows(grad_normed)
    small_out[5:6] = total_rows(grad_out) * (1.0 / z.nt)
    small_out[6:7, : z.ff] = total_rows(grad_pre.astype(F32))


def down_kernel(z, hidden, w, kept, sent, scratch):
    h = row_half(lax.axis_index("tp"))
    w_down_t = w[:, :, z.ff : 2 * z.ff].reshape(z.width, z.ff)
    scratch[...] = dot(hidden[...], w_down_t, NT)
    kept[...] = scratch[z.half_rows(h), :]
    sent[...] = scratch[z.half_rows(1 - h), :].astype(LOW)


def add_low_kernel(kept, received, out):
    rows = kept.shape[0]
    out[:rows, :] = (kept[...] + read(received)).astype(LOW)
    if out.shape[0] > rows:
        out[rows:, :] = jnp.zeros((out.shape[0] - rows, out.shape[1]), LOW)


def store_halves(z, value, at, keep, sent, sent_at=None):
    cols = pl.ds(at, value.shape[1])
    sent_cols = pl.ds(at if sent_at is None else sent_at, value.shape[1])
    c = lax.axis_index("ctx") if z.direct else 0
    b = lax.axis_index("fsdp") if z.direct else 0
    for j in range(4):
        first = value[j * z.part : j * z.part + z.chunk]
        second = value[j * z.part + z.chunk : (j + 1) * z.part]
        if z.direct:
            keep[j ^ b, :, cols] = jnp.where(c == 0, first, second)
            rows = pl.ds(pl.multiple_of((j ^ b) * z.chunk, 16), z.chunk)
            sent[rows, sent_cols] = jnp.where(c == 0, second, first).astype(LOW)
        else:
            keep[j, :, cols] = first
            sent[pl.ds(j * z.chunk, z.chunk), sent_cols] = second.astype(LOW)


def feed_grad_kernel(z, normed, pre, cot, hidden, keep, sent):
    store_halves(z, dot(normed[...], pre[...], TN), 0, keep, sent)
    store_halves(z, dot(cot[...], hidden[...], TN), z.ff, keep, sent)


def qkv_grad_kernel(z, feed_sent, normed, grads, keep, sent):
    sent[:, : 2 * z.ff] = feed_sent[...]
    sent[:, 2 * z.ff + 3 * z.inner :] = jnp.zeros((sent.shape[0], z.all_cols - 2 * z.ff - 3 * z.inner), LOW)
    store_halves(z, dot(normed[...], grads[...], TN), 0, keep, sent, 2 * z.ff)


def proj_grad_kernel(z, low, att, keep, sent=None):
    value = dot(low[...], att[...], TN)
    b = lax.axis_index("fsdp") if z.direct else 0
    for j in range(4):
        keep[j ^ b] = value[j * z.part : (j + 1) * z.part]
    if z.direct:
        c = lax.axis_index("ctx")
        sent[: z.part, :] = keep[2 - c].astype(LOW)
        sent[z.part :, :] = keep[3, z.half_of(1 - c), :].astype(LOW)


def split_kernel(z, keep, keep_qkv, received, out, kept):
    c = lax.axis_index("ctx")
    for target, at, kind in ((out, (1 + c, 3), LOW), (kept, (0, 2 - c), F32)):
        for i in range(2):
            rows = pl.ds(pl.multiple_of(at[i] * z.chunk, 16), z.chunk)
            total = keep[at[i]] + received[rows, : 2 * z.ff].astype(F32)
            target[i, :, : 2 * z.ff] = total.astype(kind)
            last = pl.ds(2 * z.ff, 3 * z.inner)
            total = keep_qkv[at[i]] + received[rows, last].astype(F32)
            target[i, :, last] = total.astype(kind)
            target[i, :, 2 * z.ff + 3 * z.inner :] = jnp.zeros((z.chunk, z.all_cols - 2 * z.ff - 3 * z.inner), kind)


def proj_one_kernel(z, keep, received, near, far):
    c = lax.axis_index("ctx")
    near[...] = (keep[1 + c] + received[: z.part, :].astype(F32)).astype(LOW)
    far[...] = (keep[3, z.half_of(c), :] + received[z.part :, :].astype(F32)).astype(LOW)


def by_half(mine, other):
    c = lax.axis_index("ctx")
    return rows_of([jnp.where(c == 0, mine, other), jnp.where(c == 0, other, mine)])


def feed_final_kernel(z, own, theirs, up, down):
    total = by_half(own[...], read(theirs))
    up[...] = total[:, : z.ff]
    down[...] = total[:, z.ff :]


def unfold(z, v):
    return rows_of([v[:, i * z.inner : (i + 1) * z.inner] for i in range(4)])


def fold(v):
    n = v.shape[0] // 4
    return lanes([v[i * n : (i + 1) * n] for i in range(4)])


def back_kernel(z, *refs):
    own_att, got = refs[0], refs[1 : z.nt]
    act, soft, w, normal, inverse, part, small, small_in = refs[z.nt : z.nt + 8]
    grads_out, qv_out, kept, sent, scratch = refs[z.nt + 8 :]
    t = lax.axis_index("tp")
    grad_att = (own_att[...] + z.spread(sum(read(g) for g in got))).astype(LOW)
    parts = [[], [], []]
    query, key, value = act[0], act[1], act[2]
    for h in range(z.heads):
        cut = slice(h * HD, (h + 1) * HD)
        ga = grad_att[:, cut]
        p = soft[h]
        grad_soft = dot(ga, value[:, cut], NT)
        delta = jnp.sum(p * grad_soft, axis=-1, keepdims=True)
        grad_scores = (p * (grad_soft - delta)).astype(LOW)
        parts[0].append((dot(grad_scores, key[:, cut], NN).astype(LOW).astype(F32) * QUERY_SCALE).astype(LOW))
        parts[1].append(dot(grad_scores, query[:, cut], TN).astype(LOW))
        parts[2].append(dot(p.astype(LOW), ga, TN).astype(LOW))
    grads = lanes(parts[0] + parts[1] + parts[2])
    grads_out[...] = grads
    n = z.inner
    qv_out[...] = total_rows(grads.astype(F32))
    grad_normed = dot(grads, w[...].reshape(z.width, 3 * n), NT)
    scratch[...] = part[...] + norm_backward(grad_normed, normal[...], inverse[:, :1], small[0:1])
    row = lax.broadcasted_iota(jnp.int32, (8, z.width), 0)
    vec = small_in[...]
    vec = jnp.where(row == 0, total_rows(grad_normed * normal[...]), vec)
    vec = jnp.where(row == 1, total_rows(grad_normed), vec)
    h = row_half(t)
    kept[: z.padded, :] = scratch[z.half_rows(h), :]
    kept[z.padded :, :] = vec
    sent[: z.padded, :] = scratch[z.half_rows(1 - h), :].astype(LOW)
    sent[z.padded :, :] = vec.astype(LOW)


def out_total_kernel(z, own, received, middle, small, *refs):
    if z.direct:
        keep, near, far, kept, out, scratch = refs
        proj_two_kernel(z, keep, near, far, out, kept, scratch)
    else:
        (out,) = refs
    rows = z.half_rows(row_half(lax.axis_index("tp")))
    total = (read(own) + read(received))[: z.padded]
    out[: z.padded, :] = (middle[rows, :] + total + small[5:6]).astype(LOW)


def proj_two_kernel(z, keep, near, far, out, kept, scratch):
    c, t = lax.axis_index("ctx"), lax.axis_index("tp")
    other = read(far)
    zero = jnp.zeros(other.shape, F32)
    proj = keep[0] + read(near) + rows_of([jnp.where(c == 0, other, zero), jnp.where(c == 0, zero, other)])
    for i in range(z.nt):
        scratch[i] = fold(proj[:, i * z.inner : (i + 1) * z.inner])
    kept[0] = scratch[t]
    kept[1] = scratch[t ^ 3]
    out[z.padded :, :] = rows_of([scratch[t ^ 1], scratch[t ^ 2]]).astype(LOW)


def sum_rows_kernel(z, own, received, small, qv, out, vec):
    total = read(own) + read(received)
    out[...] = total[: z.padded].astype(LOW)
    vec[:8, :] = total[z.padded :]
    vec[8:, :] = jnp.zeros((vec.shape[0] - 8, z.width), F32)
    vec[8:9, : z.ff] = small[6:7, : z.ff]
    vec[9:10, : 3 * z.inner] = qv[...]


def proj_pair_kernel(z, kept, received, own, sent):
    arrived = received[z.padded :, :].astype(F32)
    own[...] = kept[0] + arrived[: z.tail]
    sent[...] = (kept[1] + arrived[z.tail :]).astype(LOW)


def cross_kernel(kept, received, own, out):
    own[...] = kept[0] + received[0].astype(F32)
    out[...] = (kept[1] + received[1].astype(F32)).astype(LOW)


def small_kernel(z, vec, their, near, far, own, scratch):
    c, b = lax.axis_index("ctx"), lax.axis_index("fsdp")
    vectors = vec[:16, :] + their[:16, :]
    up = rows_of([vectors[8:9, i * HD : (i + 1) * HD] for i in range(z.ff // HD)])
    pieces = []
    for h in range(z.heads):
        pieces.append(vectors[9:10, h * HD : (h + 1) * HD])
        pieces.append(vectors[9:10, 2 * z.inner + h * HD : 2 * z.inner + (h + 1) * HD])
    qv_rows = rows_of(pieces)
    scratch[...] = jnp.zeros(scratch.shape, F32)
    w = HD // 4
    for i in range(4):
        scratch[i, :8, : z.shard] = vectors[:8, i * z.shard : (i + 1) * z.shard]
        scratch[i, : z.ff // HD, UP_AT : UP_AT + w] = up[:, i * w : (i + 1) * w]
        scratch[i, : 2 * z.heads, QV_AT : QV_AT + w] = qv_rows[:, i * w : (i + 1) * w]
    once = jnp.where(c == 0, 1.0, 0.0)
    near[...] = scratch[b ^ (1 + c)].astype(LOW)
    far[...] = (scratch[b ^ 3] * once).astype(LOW)
    own[...] = scratch[b] * once


def halves_of(z, own, received):
    h = row_half(lax.axis_index("tp"))
    return jnp.where(h == 0, own, received), jnp.where(h == 0, received, own)


def swap_kernel(z, out_own, out_in, in_own, in_in, *refs):
    out_mine, out_theirs = halves_of(z, out_own[: z.padded, :].astype(F32), out_in[: z.padded, :].astype(F32))
    in_mine, in_theirs = halves_of(z, read(in_own), read(in_in))
    theirs = [out_theirs, in_theirs]
    if z.direct:
        proj_own, proj_in, mine, sent, proj = refs
        total = proj_own[...] + read(proj_in)
        proj[...] = total
        theirs.append(total)
    else:
        mine, sent = refs
    mine[0] = out_mine
    mine[1] = in_mine
    sent[...] = rows_of(theirs).astype(LOW)


def last_kernel(z, own, cross, small, near, far, feed_total, feed_sent, qkv_total, qkv_sent):
    value = own[...] + read(cross)
    feed_total[...] = value[:, : 2 * z.ff]
    feed_sent[...] = value[:, : 2 * z.ff].astype(LOW)
    tail = small[...] + read(near) + read(far)
    for out, kind in ((qkv_total, F32), (qkv_sent, LOW)):
        out[: z.chunk, :] = value[:, 2 * z.ff : 2 * z.ff + 3 * z.inner].astype(kind)
        out[z.chunk :, :] = tail.astype(kind)


def qkv_final_kernel(z, own, theirs, qkv, up, qv, *vectors):
    both = by_half(own[: z.chunk, :], theirs[: z.chunk, :].astype(F32))
    for i in range(3):
        qkv[i] = both[:, i * z.inner : (i + 1) * z.inner]
    tail = own[z.chunk :, :] + theirs[z.chunk :, :].astype(F32)
    w = HD // 4
    up[...] = tail[: z.ff // HD, UP_AT : UP_AT + w]
    for h in range(z.heads):
        qv[h] = tail[2 * h : 2 * h + 2, QV_AT : QV_AT + w]
    for i, v in enumerate(vectors):
        v[...] = tail[i : i + 1, : z.shard].reshape(z.shard)


def place_kernel(z, mine, theirs, out, *scratch):
    c = lax.axis_index("ctx")
    target = scratch[0] if scratch else out
    mine, theirs = mine[: z.half], theirs[: z.half]
    target[:, 0, :] = jnp.where(c == 0, mine, theirs)
    target[:, 1, :] = jnp.where(c == 0, theirs, mine)
    if scratch:
        out[...] = target[...].astype(out.dtype)


def final_kernel(z, mine, theirs, *refs):
    if z.direct:
        proj_own, feed_own, feed_in, qkv_own, qkv_in, output, input_grad, proj, up, down, *rest = refs
        total = proj_own[...] + theirs[2 * z.padded :, :].astype(F32)
        proj[...] = unfold(z, total).T
        feed_final_kernel(z, feed_own, feed_in, up, down)
        qkv_final_kernel(z, qkv_own, qkv_in, *rest[:-1])
        scratch = rest[-1]
    else:
        output, input_grad, scratch = refs
    place_kernel(z, mine[1], theirs[z.padded : 2 * z.padded, :].astype(F32), input_grad)
    place_kernel(z, mine[0], theirs[: z.padded, :].astype(F32), output, scratch)


def build(nf, nc, nt):
    def local(
        inputs,
        norm1_gain,
        norm1_bias,
        qkv_weight,
        qv_bias,
        proj_weight,
        proj_bias,
        norm2_gain,
        norm2_bias,
        fc1_weight,
        fc1_bias,
        fc2_weight,
        fc2_bias,
        cotangent,
    ):
        z = Sizes(nf, nt, inputs, qv_bias, fc1_weight)
        part = functools.partial
        rows, width, inner, ff, chunk = z.rows, z.width, z.inner, z.ff, z.chunk
        f = lax.axis_index("fsdp")
        tie = lax.optimization_barrier

        def other_core(value):
            return lax.ppermute(value, "ctx", [(0, 1), (1, 0)])

        def to_tp(value, k):
            return lax.ppermute(value, "tp", [(i, i ^ k) for i in range(nt)])

        def to_far(value):
            return lax.ppermute(value, "fsdp", [(i, i ^ 3) for i in range(nf)])

        def neighbours(value, order):
            pairs = [(2 * i + c, 2 * (i ^ order[c]) + c) for i in range(nf) for c in range(2)]
            return lax.ppermute(value, ("fsdp", "ctx"), pairs)

        def to_near(value):
            return neighbours(value, (1, 2))

        def to_cross(value):
            return neighbours(value, (2, 1))

        def proj_near(value):
            pairs = [(c * nt + i, c * nt + (i ^ (1 + 2 * c))) for i in range(nt) for c in range(2)]
            return lax.ppermute(value, ("ctx", "tp"), pairs)

        def pair_of(first, second):
            return call(pair_kernel, [shape((2,) + first.shape, LOW)], [first, second], name="pair")[0]

        qkv3 = qkv_weight.transpose(1, 0, 2)
        down_t = fc2_weight.T
        qv3 = qv_bias.transpose(1, 0, 2)
        x_raw, cot_raw = inputs.transpose(1, 0, 2), cotangent.transpose(1, 0, 2)
        vectors = [norm1_gain, norm1_bias, proj_bias, norm2_gain, norm2_bias, fc2_bias]

        x_recv = other_core(x_raw)
        cot_recv = other_core(cot_raw)
        def frames(x_recv, cot_recv):
            stream, normal_one, inverse_one = call(
                part(frame_kernel, z),
                [shape((rows, width), LOW), shape((rows, width), F32), shape((rows, 128), F32)],
                [x_raw, x_recv],
                name="frame",
            )
            (cot,) = call(part(cot_kernel, z), [shape((rows, width), LOW)], [cot_raw, cot_recv], name="cotangent")
            return stream, normal_one, inverse_one, cot

        if z.direct:
            sources = [qkv3, proj_weight, fc1_bias, qv3] + vectors
            near, far, proj_t, proj_half = call(
                part(pack_kernel, z),
                [
                    shape((z.part + EXTRA, 3 * inner), LOW),
                    shape((chunk + EXTRA, 3 * inner), LOW),
                    shape((z.part, inner), LOW),
                    shape((chunk, inner), LOW),
                ],
                sources,
                [pltpu.VMEM(s.shape, s.dtype) for s in sources] + [pltpu.SemaphoreType.DMA((len(sources),))],
                name="pack",
                mib=56,
                in_specs=[ANY] * len(sources),
            )
            near, far, proj_t, proj_half, x_recv, cot_recv = tie((near, far, proj_t, proj_half, x_recv, cot_recv))
            got = [to_near(near), to_far(far)]
            proj_got = [proj_near(proj_t), to_tp(proj_half, 2)]
            feed_own, feed_rest = call(
                part(stage_kernel, z),
                [shape((z.part, z.early), LOW), shape((z.part, 2 * ff - z.early), LOW)],
                [fc1_weight, down_t],
                [pltpu.VMEM((z.part, ff), LOW)] * 2 + [pltpu.SemaphoreType.DMA((2,))],
                name="stage",
                mib=20,
                in_specs=[ANY] * 2,
            )
            stream, normal_one, inverse_one, cot = frames(x_recv, cot_recv)
            feed_in = to_near(feed_own)
            got, proj_got, feed_rest, stream, normal_one, inverse_one, cot = tie(
                (got, proj_got, feed_rest, stream, normal_one, inverse_one, cot)
            )
            shared = [other_core(g) for g in got]
            qkv_in = [near, got[0], shared[0], got[1], shared[1]]
            rest_near, rest_far = call(
                part(pack_rest_kernel, z),
                [shape((z.part, z.cols - z.early), LOW), shape((chunk, z.cols), LOW)],
                [feed_own, feed_rest, proj_t, proj_got[0], other_core(proj_got[0]), proj_got[1], other_core(proj_got[1])],
                [pltpu.VMEM((nt, z.part, inner), F32)],
                name="pack_rest",
            )
            near_in, far_in = to_near(rest_near), to_far(rest_far)
        else:
            stream, normal_one, inverse_one, cot = frames(x_recv, cot_recv)
            whole = lax.all_gather(qkv3, "fsdp", axis=1, tiled=True)
            whole = whole.transpose(1, 0, 2).reshape(4, z.part, 3 * inner)
            vec = jnp.stack(vectors + [vectors[0]] * 2).astype(F32)
            qv_rows = qv3.reshape(2 * z.heads, -1).astype(F32)
            gathered = [lax.all_gather(v, "fsdp", axis=1, tiled=True) for v in (vec, fc1_bias.astype(F32), qv_rows)]
            qkv_in = [whole] + gathered
            proj_t = proj_weight.T
            rest = jnp.concatenate([fc1_weight, down_t, lax.all_gather(proj_t, "tp", axis=1, tiled=True)], 1)
            rest_in = [lax.all_gather(rest, "fsdp", axis=0, tiled=True).reshape(4, z.part, z.cols)]

        small, w_qkv, normed_one, act, attended, soft = call(
            part(attend_kernel, z),
            [
                shape((8, width), F32),
                shape((4, z.part, 3 * inner), LOW),
                shape((rows, width), LOW),
                shape((3, rows, inner), LOW),
                shape((z.dense, 128), LOW),
                shape((z.heads, rows, rows), F32),
            ],
            qkv_in + [normal_one],
            [pltpu.VMEM((4, EXTRA, 3 * inner), F32)] if z.direct else [],
            name="attend",
        )
        att = [to_tp(attended, k) for k in range(1, nt)]
        if z.direct:
            att, feed_in, near_in, far_in = tie((att, feed_in, near_in, far_in))
            rest_in = [feed_own, feed_in, other_core(feed_in)] + [rest_near, near_in, other_core(near_in)]
            rest_in += [far_in, other_core(far_in)]

        (w_rest, att_all, middle, hidden, normed_two, grad_pre, part_middle, part_low, own_att, small_two, *att_sends) = (
            call(
                part(feed_kernel, z),
                [
                    shape((4, z.part, z.cols), LOW),
                    shape((rows, nt * inner), LOW),
                    shape((rows, width), F32),
                    shape((rows, ff), LOW),
                    shape((rows, width), LOW),
                    shape((rows, ff), LOW),
                    shape((rows, width), F32),
                    shape((rows, width), LOW),
                    shape((rows, inner), F32),
                    shape((8, width), F32),
                ]
                + [shape((z.dense, 128), LOW)] * (nt - 1),
                rest_in + [attended] + att + [stream, cot, small],
                [pltpu.VMEM((nt, rows, inner), F32)],
                name="feed",
            )
        )
        att_got = [to_tp(att_sends[k - 1], k) for k in range(1, nt)]
        all_cols = z.all_cols
        keep, sent = call(
            part(feed_grad_kernel, z),
            [shape((4, chunk, 2 * ff), F32), shape((4 * chunk, 2 * ff), LOW)],
            [normed_two, grad_pre, cot, hidden],
            name="feed_grad",
        )
        keep_proj, *sent_proj = call(
            part(proj_grad_kernel, z),
            [shape((4, z.part, nt * inner), F32)]
            + ([shape((z.part + chunk, nt * inner), LOW)] if z.direct else []),
            [part_low, att_all],
            name="proj_grad",
        )
        out_kept, out_sent = call(
            part(down_kernel, z),
            [shape((z.padded, width), F32), shape((z.padded, width), LOW)],
            [hidden, w_rest],
            [pltpu.VMEM((rows, width), F32)],
            name="down",
        )
        out_one = to_tp(out_sent, 1)
        if z.direct:
            proj_in = other_core(sent_proj[0])
            att_got, out_one, keep, sent, proj_in = tie((att_got, out_one, keep, sent, proj_in))
            near, far = call(
                part(proj_one_kernel, z),
                [shape((z.part, nt * inner), LOW), shape((chunk, nt * inner), LOW)],
                [keep_proj, proj_in],
                name="proj_one",
            )
            proj_in = [to_near(near), to_far(far)]
        (out_low,) = call(add_low_kernel, [shape((z.padded, width), LOW)], [out_kept, out_one], name="out_pair")
        out_two = to_tp(out_low, 3)

        grads, qv_sum, in_kept, in_sent = call(
            part(back_kernel, z),
            [
                shape((rows, 3 * inner), LOW),
                shape((1, 3 * inner), F32),
                shape((z.padded + 8, width), F32),
                shape((z.padded + 8, width), LOW),
            ],
            [own_att] + att_got + [act, soft, w_qkv, normal_one, inverse_one, part_middle, small, small_two],
            [pltpu.VMEM((rows, width), F32)],
            name="back",
        )
        in_one = to_tp(in_sent, 1)
        keep_qkv, sent = call(
            part(qkv_grad_kernel, z),
            [shape((4, chunk, 3 * inner), F32), shape((4 * chunk, all_cols), LOW)],
            [sent, normed_one, grads],
            name="qkv_grad",
        )
        if z.direct:
            sent = other_core(sent)
            in_one, out_two, proj_in, sent = tie((in_one, out_two, proj_in, sent))
            grad_sent, grad_kept = call(
                part(split_kernel, z),
                [shape((2, chunk, all_cols), LOW), shape((2, chunk, all_cols), F32)],
                [keep, keep_qkv, sent],
                name="split",
            )
            grad_in = to_near(grad_sent)
        (in_low,) = call(add_low_kernel, [shape((z.padded + 8, width), LOW)], [in_kept, in_one], name="in_pair")
        in_two = to_tp(in_low, 3)
        *proj_kept, out_low = call(
            part(out_total_kernel, z),
            ([shape((2, z.tail, width), F32)] if z.direct else [])
            + [shape((z.padded + (2 * z.tail if z.direct else 0), width), LOW)],
            [out_low, out_two, middle, small] + ([keep_proj] + proj_in if z.direct else []),
            [pltpu.VMEM((nt, z.tail, width), F32)] if z.direct else [],
            name="out_total",
        )
        out_in = to_tp(out_low, 1)
        if z.direct:
            in_two, out_in, grad_in = tie((in_two, out_in, grad_in))
        in_low, vec = call(
            part(sum_rows_kernel, z),
            [shape((z.padded, width), LOW), shape((VEC_ROWS, width), F32)],
            [in_low, in_two, small_two, qv_sum],
            name="sum_rows",
        )
        in_in = to_tp(in_low, 1)
        proj_all = []
        if z.direct:
            grad_own, cross = call(
                cross_kernel,
                [shape((chunk, all_cols), F32), shape((chunk, all_cols), LOW)],
                [grad_kept, grad_in],
                name="cross",
            )
            cross = to_cross(cross)
            proj_own, proj_sent = call(
                part(proj_pair_kernel, z),
                [shape((z.tail, width), F32), shape((z.tail, width), LOW)],
                [proj_kept[0], out_in],
                name="proj_pair",
            )
            proj_two = to_tp(proj_sent, 3)
            near, far, small_own = call(
                part(small_kernel, z),
                [shape((EXTRA, 3 * inner), LOW)] * 2 + [shape((EXTRA, 3 * inner), F32)],
                [vec, other_core(vec)],
                [pltpu.VMEM((4, EXTRA, 3 * inner), F32)],
                name="small",
            )
            near, far = to_near(near), to_far(far)
            in_in, proj_two, cross, near, far = tie((in_in, proj_two, cross, near, far))
            proj_all = [proj_own, proj_two]
            feed_own, feed_sent, qkv_own, qkv_sent = call(
                part(last_kernel, z),
                [
                    shape((chunk, 2 * ff), F32),
                    shape((chunk, 2 * ff), LOW),
                    shape((chunk + EXTRA, 3 * inner), F32),
                    shape((chunk + EXTRA, 3 * inner), LOW),
                ],
                [grad_own, cross, small_own, near, far],
                name="last",
            )
            feed_in, qkv_in = other_core(feed_sent), other_core(qkv_sent)
        mine, theirs, *proj_own = call(
            part(swap_kernel, z),
            [shape((2, z.padded, width), F32), shape((rows + (z.tail if proj_all else 0), width), LOW)]
            + ([shape((z.tail, width), F32)] if proj_all else []),
            [out_low, out_in, in_low, in_in] + proj_all,
            name="swap",
        )
        theirs = other_core(theirs)
        results = [shape((z.half, 2, width), LOW), shape((z.half, 2, width), F32)]
        scratch = [pltpu.VMEM((z.half, 2, width), F32)]
        if z.direct:
            output, input_grad, proj_grad, fc1_grad, fc2_grad, qkv_grad, up_grad, qv_grad, *vec_grads = call(
                part(final_kernel, z),
                results
                + [
                    shape((inner, z.shard), F32),
                    shape((z.shard, ff), F32),
                    shape((z.shard, ff), F32),
                    shape((3, z.shard, inner), F32),
                    shape(fc1_bias.shape, F32),
                    shape(qv3.shape, F32),
                ]
                + [shape((z.shard,), F32)] * 6,
                [mine, theirs, proj_own[0], feed_own, feed_in, qkv_own, qkv_in],
                scratch,
                name="final",
            )
        else:
            output, input_grad = call(part(final_kernel, z), results, [mine, theirs], scratch, name="final")

            def joined(keep, sent):
                return jnp.stack([keep.astype(LOW), sent.reshape(keep.shape)], 1).reshape(width, -1)

            def scatter(whole):
                whole = lax.psum(whole, "ctx")
                return lax.psum_scatter(whole, "fsdp", scatter_dimension=0, tiled=True).astype(F32)

            extra = all_cols - 2 * ff - 3 * inner
            total = scatter(joined(jnp.concatenate([keep, jnp.pad(keep_qkv, ((0, 0), (0, 0), (0, extra)))], 2), sent))
            fc1_grad, fc2_grad = total[:, :ff], total[:, ff : 2 * ff]
            qkv_grad = total[:, 2 * ff : 2 * ff + 3 * inner].reshape(z.shard, 3, inner).transpose(1, 0, 2)
            proj_grad = scatter(keep_proj.reshape(width, -1).astype(LOW)).astype(LOW)
            proj_grad = lax.psum_scatter(proj_grad, "tp", scatter_dimension=1, tiled=True).astype(F32).T

            def own_columns(value):
                value = lax.psum(value, ("fsdp", "ctx"))
                return lax.dynamic_slice_in_dim(value, f * (value.shape[1] // nf), value.shape[1] // nf, 1)

            vec_grads = own_columns(vec[:6])
            up_grad = own_columns(vec[8, :ff].reshape(-1, HD))
            qv_grad = vec[9, : 3 * inner].reshape(3, z.heads, HD)[0::2].transpose(1, 0, 2)
            qv_grad = own_columns(qv_grad.reshape(2 * z.heads, HD)).reshape(qv3.shape)
        return (
            output.transpose(1, 0, 2),
            input_grad.transpose(1, 0, 2),
            vec_grads[0],
            vec_grads[1],
            qkv_grad.transpose(1, 0, 2),
            qv_grad.transpose(1, 0, 2),
            proj_grad,
            vec_grads[2],
            vec_grads[3],
            vec_grads[4],
            fc1_grad,
            up_grad,
            fc2_grad.T,
            vec_grads[5],
        )

    return local


def solution(mesh):
    sizes = mesh.shape
    return jax.shard_map(
        build(sizes["fsdp"], sizes["ctx"], sizes["tp"]),
        mesh=mesh,
        in_specs=(
            P("fsdp", "ctx", None),
            P("fsdp"),
            P("fsdp"),
            P("fsdp", None, "tp"),
            P(None, "tp", "fsdp"),
            P("tp", "fsdp"),
            P("fsdp"),
            P("fsdp"),
            P("fsdp"),
            P("fsdp", "tp"),
            P("tp", "fsdp"),
            P("tp", "fsdp"),
            P("fsdp"),
            P("fsdp", "ctx", None),
        ),
        out_specs=(
            P("fsdp", "ctx", None),
            P("fsdp", "ctx", None),
            P("fsdp"),
            P("fsdp"),
            P("fsdp", None, "tp"),
            P(None, "tp", "fsdp"),
            P("tp", "fsdp"),
            P("fsdp"),
            P("fsdp"),
            P("fsdp"),
            P("fsdp", "tp"),
            P("tp", "fsdp"),
            P("tp", "fsdp"),
            P("fsdp"),
        ),
        check_vma=False,
    )
```

```python
import functools

import jax
import jax.numpy as jnp
from jax import lax
from jax.experimental import pallas as pl
from jax.experimental.pallas import tpu as pltpu
from jax.sharding import PartitionSpec as P

HD = 64
EPSILON = 1e-06
QUERY_SCALE = 0.125
F32 = jnp.float32
LOW = jnp.bfloat16
NN = ((1,), (0,))
NT = ((1,), (1,))
TN = ((0,), (0,))
VMEM = pl.BlockSpec(memory_space=pltpu.VMEM)
ANY = pl.BlockSpec(memory_space=pl.ANY)
EXTRA = 16
VEC_ROWS = 144
UP_AT, QV_AT = 256, 384


def dot(left, right, dims):
    return lax.dot_general(left, right, (dims, ((), ())), preferred_element_type=F32)


def shape(dims, kind):
    return jax.ShapeDtypeStruct(tuple(dims), kind)


def call(kernel, outs, args, scratch=(), name=None, mib=20, in_specs=None, alias=None):
    return pl.pallas_call(
        kernel,
        out_shape=tuple(outs),
        in_specs=in_specs or [VMEM] * len(args),
        out_specs=tuple([VMEM] * len(outs)),
        scratch_shapes=list(scratch),
        input_output_aliases=alias or {},
        name=name,
        compiler_params=pltpu.CompilerParams(vmem_limit_bytes=mib << 20),
    )(*args)


def gelu_and_slope(v):
    cdf = 0.5 * (1.0 + lax.erf(v * 0.7071067811865476))
    density = jnp.exp(-0.5 * v * v) * 0.3989422804014327
    return v * cdf, cdf + v * density


def mean(v):
    return jnp.mean(v, axis=-1, keepdims=True)


def total_rows(v):
    return jnp.sum(v, axis=0, keepdims=True)


def normalise(v):
    centred = v - mean(v)
    inverse = lax.rsqrt(mean(centred * centred) + EPSILON)
    return centred * inverse, inverse


def norm_backward(grad_normed, normal, inverse, gain):
    scaled = grad_normed * gain
    return inverse * (scaled - mean(scaled) - normal * mean(scaled * normal))


def row_half(t):
    return (t ^ (t >> 1)) & 1


def lanes(parts):
    return jnp.concatenate(parts, axis=1)


def rows_of(parts):
    return jnp.concatenate(parts, axis=0)


def read(ref):
    return ref[...].astype(F32)


class Sizes:
    def __init__(self, nf, nt, inputs, qv_bias, fc1_weight):
        self.nf, self.nt = nf, nt
        _, self.half, self.width = inputs.shape
        self.shard = self.width // nf
        self.heads = qv_bias.shape[1]
        self.inner = self.heads * HD
        self.ff = fc1_weight.shape[1]
        self.pad = -self.half % 8
        self.padded = self.half + self.pad
        self.rows = 2 * self.padded
        self.part = self.width // 4
        self.chunk = self.part // 2
        self.tail = self.part // 4
        self.direct = nf == 4
        self.cols = 2 * self.ff + nt * self.inner
        self.early = 1280 if self.ff == 768 else self.ff
        self.all_cols = 2 * self.ff + -(-3 * self.inner // 128) * 128
        self.dense = self.rows * self.inner // 128

    def half_rows(self, h):
        return pl.ds(pl.multiple_of(h * self.padded, 8), self.padded)

    def half_of(self, c):
        return pl.ds(pl.multiple_of(c * self.chunk, 16), self.chunk)

    def squeeze(self, v):
        return rows_of([v[:, :128], lanes([v[: self.padded, 128:], v[self.padded :, 128:]])])

    def spread(self, v):
        tail = v[self.rows :]
        return lanes([v[: self.rows], rows_of([tail[:, :HD], tail[:, HD:]])])


def fetch(sources, copies, sem):
    moves = [pltpu.make_async_copy(s, d, sem.at[i]) for i, (s, d) in enumerate(zip(sources, copies))]
    for m in moves:
        m.start()
    for m in moves:
        m.wait()


def stage_kernel(z, up, down_t, out, rest, one, two, sem):
    fetch((up, down_t), (one, two), sem)
    first = z.early - z.ff
    out[:, : z.ff] = one[...]
    out[:, z.ff :] = two[:, :first]
    rest[...] = two[:, first:]


def pack_kernel(z, *refs):
    sources, (near, far, proj_t, proj_half) = refs[:10], refs[10:14]
    copies, sem = refs[14:24], refs[24]
    fetch(sources, copies, sem)
    qkv, proj, up_b, qv_b = copies[:4]
    vectors = copies[4:]
    c = lax.axis_index("ctx")
    whole = lanes([read(qkv.at[i]) for i in range(3)])
    near[: z.part, :] = whole.astype(LOW)
    far[: z.chunk, :] = jnp.where(c == 0, whole[: z.chunk], whole[z.chunk :]).astype(LOW)
    row = lax.broadcasted_iota(jnp.int32, (EXTRA, z.shard), 0)
    vec = jnp.zeros((EXTRA, z.shard), F32)
    for i, v in enumerate(vectors):
        vec = jnp.where(row == i, read(v).reshape(1, z.shard), vec)
    biases = read(qv_b)
    biases = rows_of([biases[h, i : i + 1] for h in range(z.heads) for i in range(2)])
    for out, at in ((near, z.part), (far, z.chunk)):
        out[at:, :] = jnp.zeros((EXTRA, 3 * z.inner), LOW)
        out[at:, : z.shard] = vec.astype(LOW)
        out[at : at + up_b.shape[0], UP_AT : UP_AT + up_b.shape[1]] = up_b[...]
        out[at : at + 2 * z.heads, QV_AT : QV_AT + biases.shape[1]] = biases.astype(LOW)
    turned = read(proj).T
    proj_t[...] = rows_of([turned, jnp.zeros((proj_t.shape[0] - z.part, z.inner), F32)]).astype(LOW)
    proj_half[...] = jnp.where(c == 0, turned[: z.chunk], turned[z.chunk :]).astype(LOW)


def cut_kernel(z, value, out):
    out[...] = value[z.half_of(lax.axis_index("ctx")), :]


def pair_kernel(first, second, out):
    rows = first.shape[0]
    out[0, :rows, :] = first[...]
    out[1, :rows, :] = second[...]
    out[:, rows:, :] = jnp.zeros((2, out.shape[1] - rows, out.shape[2]), LOW)


def pack_rest_kernel(z, rest, proj_t, near_in, near_their, far_in, far_their, near, scratch):
    c, t = lax.axis_index("ctx"), lax.axis_index("tp")
    scratch[t] = proj_t[: z.part, :].astype(F32)
    scratch[t ^ (1 + 2 * c)] = near_in[: z.part, :].astype(F32)
    scratch[t ^ (3 - 2 * c)] = near_their[: z.part, :].astype(F32)
    scratch[t ^ 2, z.half_of(c), :] = far_in[: z.chunk, :].astype(F32)
    scratch[t ^ 2, z.half_of(1 - c), :] = far_their[: z.chunk, :].astype(F32)
    near[:, : 2 * z.ff - z.early] = rest[...]
    near[:, 2 * z.ff - z.early :] = lanes([scratch[i] for i in range(4)]).astype(LOW)


def own_frame(z, keep, received):
    c = lax.axis_index("ctx")
    zero = jnp.zeros((z.pad, z.width), F32)
    pieces = []
    for ref in (keep, received):
        pieces.append(jnp.where(c == 0, ref[:, 0, :].astype(F32), ref[:, 1, :].astype(F32)))
        pieces.append(zero)
    return rows_of(pieces)


def frame_kernel(z, keep, received, stream, normal, inverse):
    values = own_frame(z, keep, received)
    stream[...] = values.astype(LOW)
    n, i = normalise(values)
    normal[...] = n
    inverse[...] = jnp.broadcast_to(i, inverse.shape)


def cot_kernel(z, keep, received, stream):
    stream[...] = own_frame(z, keep, received).astype(LOW)


def attend_kernel(z, *refs):
    refs = list(refs)
    if z.direct:
        own, near, near_their, far, far_their = refs[:5]
        refs = refs[5:]
    else:
        whole, vec_in, up_in, qv_in = refs[:4]
        refs = refs[4:]
    normal, small, w_out, normed_out, act, attended, soft_out = refs[:7]
    if z.direct:
        c, b = lax.axis_index("ctx"), lax.axis_index("fsdp")
        gather = refs[7]
        for ref, at in ((own, b), (near, b ^ (1 + c)), (near_their, b ^ (2 - c))):
            w_out[at] = ref[: z.part, :]
            gather[at] = ref[z.part :, :].astype(F32)
        w_out[b ^ 3, z.half_of(c), :] = far[: z.chunk, :]
        w_out[b ^ 3, z.half_of(1 - c), :] = far_their[: z.chunk, :]
        gather[b ^ 3] = far[z.chunk :, :].astype(F32)
        blocks = [gather[i] for i in range(4)]
        w = HD // 4
        vec = lanes([g[:8, : z.shard] for g in blocks])
        up = lanes([g[: z.ff // HD, UP_AT : UP_AT + w] for g in blocks])
        qv = lanes([g[: 2 * z.heads, QV_AT : QV_AT + w] for g in blocks])
    else:
        w_out[...] = whole[...]
        vec, up, qv = vec_in[...], up_in[...], qv_in[...]
    up_row = lanes([up[i : i + 1] for i in range(z.ff // HD)])
    query_b = lanes([qv[2 * h : 2 * h + 1] for h in range(z.heads)])
    value_b = lanes([qv[2 * h + 1 : 2 * h + 2] for h in range(z.heads)])
    small[...] = vec
    small[6:7, : z.ff] = up_row
    normed = (normal[...] * vec[0:1] + vec[1:2]).astype(LOW)
    normed_out[...] = normed
    projected = dot(normed, w_out[...].reshape(z.width, 3 * z.inner), NN)
    n = z.inner
    query = ((projected[:, :n] + query_b) * QUERY_SCALE).astype(LOW)
    key = projected[:, n : 2 * n].astype(LOW)
    value = (projected[:, 2 * n :] + value_b).astype(LOW)
    act[0] = query
    act[1] = key
    act[2] = value
    place = lax.broadcasted_iota(jnp.int32, (z.rows, z.rows), 1)
    valid = (place < z.half) | ((place >= z.padded) & (place < z.padded + z.half))
    done = []
    for h in range(z.heads):
        cut = slice(h * HD, (h + 1) * HD)
        scores = jnp.where(valid, dot(query[:, cut], key[:, cut], NT), -1e30)
        exponent = jnp.exp(scores - jnp.max(scores, axis=-1, keepdims=True))
        soft = exponent * (1.0 / jnp.sum(exponent, axis=-1, keepdims=True))
        soft_out[h] = soft
        done.append(dot(soft.astype(LOW), value[:, cut], NN))
    attended[...] = z.squeeze(lanes(done)).astype(LOW)


def feed_kernel(z, *refs):
    refs = list(refs)
    if z.direct:
        feed, feed_in, feed_their, near, near_in, near_their, far, far_their, last_far, last_far_their = refs[:10]
        refs = refs[10:]
    else:
        whole = refs[0]
        refs = refs[1:]
    att = refs[:3]
    stream, cot, small = refs[3:6]
    (w_out, att_out, middle_out, hidden_out, normed_out, pre_out, part_out, low_out, own_att, small_out) = refs[6:16]
    sends, heads = refs[16:-1], refs[-1]
    t = lax.axis_index("tp")
    if z.direct:
        c, b = lax.axis_index("ctx"), lax.axis_index("fsdp")
        mine, other = z.half_of(c), z.half_of(1 - c)
        first, last = pl.ds(0, z.early), pl.ds(z.early, z.cols - z.early)
        for at, one, two in ((b, feed, near), (b ^ (1 + c), feed_in, near_in), (b ^ (2 - c), feed_their, near_their)):
            w_out[at, :, first] = one[...]
            w_out[at, :, last] = two[...]
        w_out[b ^ 3, mine, first] = far[...]
        w_out[b ^ 3, other, first] = far_their[...]
        w_out[b ^ 3, mine, last] = last_far[...]
        w_out[b ^ 3, other, last] = last_far_their[...]
    else:
        w_out[...] = whole[...]
    n = z.inner
    w_up = w_out[:, :, : z.ff].reshape(z.width, z.ff)
    w_down_t = w_out[:, :, z.ff : 2 * z.ff].reshape(z.width, z.ff)
    w_proj_t = w_out[:, :, 2 * z.ff :].reshape(z.width, z.nt * n)
    grad_out_low = cot[...]
    grad_out = grad_out_low.astype(F32)
    heads[t] = z.spread(read(att[0]))
    heads[t ^ 2] = z.spread(read(att[1]))
    heads[t ^ 1] = z.spread(att[2][0, : z.dense, :].astype(F32))
    heads[t ^ 3] = z.spread(att[2][1, : z.dense, :].astype(F32))
    attended = lanes([heads[i] for i in range(z.nt)]).astype(LOW)
    att_out[...] = attended
    branch = dot(attended, w_proj_t, NT)
    middle = stream[...].astype(F32) + branch + small[2:3]
    middle_out[...] = middle
    normal, inverse = normalise(middle)
    gain = small[3:4]
    normed = (normal * gain + small[4:5]).astype(LOW)
    normed_out[...] = normed
    hidden, slope = gelu_and_slope(dot(normed, w_up, NN) + small[6:7, : z.ff])
    hidden_out[...] = hidden.astype(LOW)
    grad_pre = (dot(grad_out_low, w_down_t, NN) * slope).astype(LOW)
    pre_out[...] = grad_pre
    grad_normed = dot(grad_pre, w_up, NT)
    part = grad_out * (1.0 / z.nt) + norm_backward(grad_normed, normal, inverse, gain)
    part_out[...] = part
    low = part.astype(LOW)
    low_out[...] = low
    grad_att = dot(low, w_proj_t, NN)
    for i in range(z.nt):
        heads[i] = grad_att[:, i * n : (i + 1) * n]
    own_att[...] = heads[t]
    for k in range(1, z.nt):
        sends[k - 1][...] = z.squeeze(heads[t ^ k]).astype(LOW)
    small_out[...] = jnp.zeros(small_out.shape, F32)
    small_out[2:3] = total_rows(part)
    small_out[3:4] = total_rows(grad_normed * normal)
    small_out[4:5] = total_rows(grad_normed)
    small_out[5:6] = total_rows(grad_out) * (1.0 / z.nt)
    small_out[6:7, : z.ff] = total_rows(grad_pre.astype(F32))


def down_kernel(z, hidden, w, kept, sent, scratch):
    h = row_half(lax.axis_index("tp"))
    w_down_t = w[:, :, z.ff : 2 * z.ff].reshape(z.width, z.ff)
    scratch[...] = dot(hidden[...], w_down_t, NT)
    kept[...] = scratch[z.half_rows(h), :]
    sent[...] = scratch[z.half_rows(1 - h), :].astype(LOW)


def add_low_kernel(kept, received, out):
    rows = kept.shape[0]
    out[:rows, :] = (kept[...] + read(received)).astype(LOW)
    if out.shape[0] > rows:
        out[rows:, :] = jnp.zeros((out.shape[0] - rows, out.shape[1]), LOW)


def store_halves(z, value, at, keep, sent, sent_at=None):
    cols = pl.ds(at, value.shape[1])
    sent_cols = pl.ds(at if sent_at is None else sent_at, value.shape[1])
    c = lax.axis_index("ctx") if z.direct else 0
    b = lax.axis_index("fsdp") if z.direct else 0
    for j in range(4):
        first = value[j * z.part : j * z.part + z.chunk]
        second = value[j * z.part + z.chunk : (j + 1) * z.part]
        if z.direct:
            keep[j ^ b, :, cols] = jnp.where(c == 0, first, second)
            rows = pl.ds(pl.multiple_of((j ^ b) * z.chunk, 16), z.chunk)
            sent[rows, sent_cols] = jnp.where(c == 0, second, first).astype(LOW)
        else:
            keep[j, :, cols] = first
            sent[pl.ds(j * z.chunk, z.chunk), sent_cols] = second.astype(LOW)


def feed_grad_kernel(z, normed, pre, cot, hidden, keep, sent):
    store_halves(z, dot(normed[...], pre[...], TN), 0, keep, sent)
    store_halves(z, dot(cot[...], hidden[...], TN), z.ff, keep, sent)


def qkv_grad_kernel(z, feed_sent, normed, grads, keep, sent):
    sent[:, : 2 * z.ff] = feed_sent[...]
    sent[:, 2 * z.ff + 3 * z.inner :] = jnp.zeros((sent.shape[0], z.all_cols - 2 * z.ff - 3 * z.inner), LOW)
    store_halves(z, dot(normed[...], grads[...], TN), 0, keep, sent, 2 * z.ff)


def proj_grad_kernel(z, low, att, keep, sent=None):
    value = dot(low[...], att[...], TN)
    b = lax.axis_index("fsdp") if z.direct else 0
    for j in range(4):
        keep[j ^ b] = value[j * z.part : (j + 1) * z.part]
    if z.direct:
        c = lax.axis_index("ctx")
        sent[: z.part, :] = keep[2 - c].astype(LOW)
        sent[z.part :, :] = keep[3, z.half_of(1 - c), :].astype(LOW)


def split_kernel(z, keep, keep_qkv, received, out, kept):
    c = lax.axis_index("ctx")
    for target, at, kind in ((out, (1 + c, 3), LOW), (kept, (0, 2 - c), F32)):
        for i in range(2):
            rows = pl.ds(pl.multiple_of(at[i] * z.chunk, 16), z.chunk)
            total = keep[at[i]] + received[rows, : 2 * z.ff].astype(F32)
            target[i, :, : 2 * z.ff] = total.astype(kind)
            last = pl.ds(2 * z.ff, 3 * z.inner)
            total = keep_qkv[at[i]] + received[rows, last].astype(F32)
            target[i, :, last] = total.astype(kind)
            target[i, :, 2 * z.ff + 3 * z.inner :] = jnp.zeros((z.chunk, z.all_cols - 2 * z.ff - 3 * z.inner), kind)


def proj_one_kernel(z, keep, received, near, far):
    c = lax.axis_index("ctx")
    near[...] = (keep[1 + c] + received[: z.part, :].astype(F32)).astype(LOW)
    far[...] = (keep[3, z.half_of(c), :] + received[z.part :, :].astype(F32)).astype(LOW)


def by_half(mine, other):
    c = lax.axis_index("ctx")
    return rows_of([jnp.where(c == 0, mine, other), jnp.where(c == 0, other, mine)])


def feed_final_kernel(z, own, theirs, up, down):
    total = by_half(own[...], read(theirs))
    up[...] = total[:, : z.ff]
    down[...] = total[:, z.ff :]


def unfold(z, v):
    return rows_of([v[:, i * z.inner : (i + 1) * z.inner] for i in range(4)])


def fold(v):
    n = v.shape[0] // 4
    return lanes([v[i * n : (i + 1) * n] for i in range(4)])


def back_kernel(z, *refs):
    own_att, got = refs[0], refs[1 : z.nt]
    act, soft, w, normal, inverse, part, small, small_in = refs[z.nt : z.nt + 8]
    grads_out, qv_out, kept, sent, scratch = refs[z.nt + 8 :]
    t = lax.axis_index("tp")
    grad_att = (own_att[...] + z.spread(sum(read(g) for g in got))).astype(LOW)
    parts = [[], [], []]
    query, key, value = act[0], act[1], act[2]
    for h in range(z.heads):
        cut = slice(h * HD, (h + 1) * HD)
        ga = grad_att[:, cut]
        p = soft[h]
        grad_soft = dot(ga, value[:, cut], NT)
        delta = jnp.sum(p * grad_soft, axis=-1, keepdims=True)
        grad_scores = (p * (grad_soft - delta)).astype(LOW)
        parts[0].append((dot(grad_scores, key[:, cut], NN).astype(LOW).astype(F32) * QUERY_SCALE).astype(LOW))
        parts[1].append(dot(grad_scores, query[:, cut], TN).astype(LOW))
        parts[2].append(dot(p.astype(LOW), ga, TN).astype(LOW))
    grads = lanes(parts[0] + parts[1] + parts[2])
    grads_out[...] = grads
    n = z.inner
    qv_out[...] = total_rows(grads.astype(F32))
    grad_normed = dot(grads, w[...].reshape(z.width, 3 * n), NT)
    scratch[...] = part[...] + norm_backward(grad_normed, normal[...], inverse[:, :1], small[0:1])
    row = lax.broadcasted_iota(jnp.int32, (8, z.width), 0)
    vec = small_in[...]
    vec = jnp.where(row == 0, total_rows(grad_normed * normal[...]), vec)
    vec = jnp.where(row == 1, total_rows(grad_normed), vec)
    h = row_half(t)
    kept[: z.padded, :] = scratch[z.half_rows(h), :]
    kept[z.padded :, :] = vec
    sent[: z.padded, :] = scratch[z.half_rows(1 - h), :].astype(LOW)
    sent[z.padded :, :] = vec.astype(LOW)


def out_total_kernel(z, own, received, middle, small, *refs):
    if z.direct:
        keep, near, far, kept, out, scratch = refs
        proj_two_kernel(z, keep, near, far, out, kept, scratch)
    else:
        (out,) = refs
    rows = z.half_rows(row_half(lax.axis_index("tp")))
    total = (read(own) + read(received))[: z.padded]
    out[: z.padded, :] = (middle[rows, :] + total + small[5:6]).astype(LOW)


def proj_two_kernel(z, keep, near, far, out, kept, scratch):
    c, t = lax.axis_index("ctx"), lax.axis_index("tp")
    other = read(far)
    zero = jnp.zeros(other.shape, F32)
    proj = keep[0] + read(near) + rows_of([jnp.where(c == 0, other, zero), jnp.where(c == 0, zero, other)])
    for i in range(z.nt):
        scratch[i] = fold(proj[:, i * z.inner : (i + 1) * z.inner])
    kept[0] = scratch[t]
    kept[1] = scratch[t ^ 3]
    out[z.padded :, :] = rows_of([scratch[t ^ 1], scratch[t ^ 2]]).astype(LOW)


def sum_rows_kernel(z, own, received, small, qv, out, vec):
    total = read(own) + read(received)
    out[...] = total[: z.padded].astype(LOW)
    vec[:8, :] = total[z.padded :]
    vec[8:, :] = jnp.zeros((vec.shape[0] - 8, z.width), F32)
    vec[8:9, : z.ff] = small[6:7, : z.ff]
    vec[9:10, : 3 * z.inner] = qv[...]


def proj_pair_kernel(z, kept, received, own, sent):
    arrived = received[z.padded :, :].astype(F32)
    own[...] = kept[0] + arrived[: z.tail]
    sent[...] = (kept[1] + arrived[z.tail :]).astype(LOW)


def cross_kernel(kept, received, own, out):
    own[...] = kept[0] + received[0].astype(F32)
    out[...] = (kept[1] + received[1].astype(F32)).astype(LOW)


def small_kernel(z, vec, their, near, far, own, scratch):
    c, b = lax.axis_index("ctx"), lax.axis_index("fsdp")
    vectors = vec[:16, :] + their[:16, :]
    up = rows_of([vectors[8:9, i * HD : (i + 1) * HD] for i in range(z.ff // HD)])
    pieces = []
    for h in range(z.heads):
        pieces.append(vectors[9:10, h * HD : (h + 1) * HD])
        pieces.append(vectors[9:10, 2 * z.inner + h * HD : 2 * z.inner + (h + 1) * HD])
    qv_rows = rows_of(pieces)
    scratch[...] = jnp.zeros(scratch.shape, F32)
    w = HD // 4
    for i in range(4):
        scratch[i, :8, : z.shard] = vectors[:8, i * z.shard : (i + 1) * z.shard]
        scratch[i, : z.ff // HD, UP_AT : UP_AT + w] = up[:, i * w : (i + 1) * w]
        scratch[i, : 2 * z.heads, QV_AT : QV_AT + w] = qv_rows[:, i * w : (i + 1) * w]
    once = jnp.where(c == 0, 1.0, 0.0)
    near[...] = scratch[b ^ (1 + c)].astype(LOW)
    far[...] = (scratch[b ^ 3] * once).astype(LOW)
    own[...] = scratch[b] * once


def halves_of(z, own, received):
    h = row_half(lax.axis_index("tp"))
    return jnp.where(h == 0, own, received), jnp.where(h == 0, received, own)


def swap_kernel(z, out_own, out_in, in_own, in_in, *refs):
    out_mine, out_theirs = halves_of(z, out_own[: z.padded, :].astype(F32), out_in[: z.padded, :].astype(F32))
    in_mine, in_theirs = halves_of(z, read(in_own), read(in_in))
    theirs = [out_theirs, in_theirs]
    if z.direct:
        proj_own, proj_in, mine, sent, proj = refs
        total = proj_own[...] + read(proj_in)
        proj[...] = total
        theirs.append(total)
    else:
        mine, sent = refs
    mine[0] = out_mine
    mine[1] = in_mine
    sent[...] = rows_of(theirs).astype(LOW)


def last_kernel(z, own, cross, small, near, far, feed_total, feed_sent, qkv_total, qkv_sent):
    value = own[...] + read(cross)
    feed_total[...] = value[:, : 2 * z.ff]
    feed_sent[...] = value[:, : 2 * z.ff].astype(LOW)
    tail = small[...] + read(near) + read(far)
    for out, kind in ((qkv_total, F32), (qkv_sent, LOW)):
        out[: z.chunk, :] = value[:, 2 * z.ff : 2 * z.ff + 3 * z.inner].astype(kind)
        out[z.chunk :, :] = tail.astype(kind)


def qkv_final_kernel(z, own, theirs, qkv, up, qv, *vectors):
    both = by_half(own[: z.chunk, :], theirs[: z.chunk, :].astype(F32))
    for i in range(3):
        qkv[i] = both[:, i * z.inner : (i + 1) * z.inner]
    tail = own[z.chunk :, :] + theirs[z.chunk :, :].astype(F32)
    w = HD // 4
    up[...] = tail[: z.ff // HD, UP_AT : UP_AT + w]
    for h in range(z.heads):
        qv[h] = tail[2 * h : 2 * h + 2, QV_AT : QV_AT + w]
    for i, v in enumerate(vectors):
        v[...] = tail[i : i + 1, : z.shard].reshape(z.shard)


def place_kernel(z, mine, theirs, out, *scratch):
    c = lax.axis_index("ctx")
    target = scratch[0] if scratch else out
    mine, theirs = mine[: z.half], theirs[: z.half]
    target[:, 0, :] = jnp.where(c == 0, mine, theirs)
    target[:, 1, :] = jnp.where(c == 0, theirs, mine)
    if scratch:
        out[...] = target[...].astype(out.dtype)


def final_kernel(z, mine, theirs, *refs):
    if z.direct:
        proj_own, feed_own, feed_in, qkv_own, qkv_in, output, input_grad, proj, up, down, *rest = refs
        total = proj_own[...] + theirs[2 * z.padded :, :].astype(F32)
        proj[...] = unfold(z, total).T
        feed_final_kernel(z, feed_own, feed_in, up, down)
        qkv_final_kernel(z, qkv_own, qkv_in, *rest[:-1])
        scratch = rest[-1]
    else:
        output, input_grad, scratch = refs
    place_kernel(z, mine[1], theirs[z.padded : 2 * z.padded, :].astype(F32), input_grad)
    place_kernel(z, mine[0], theirs[: z.padded, :].astype(F32), output, scratch)


def build(nf, nc, nt):
    def local(
        inputs,
        norm1_gain,
        norm1_bias,
        qkv_weight,
        qv_bias,
        proj_weight,
        proj_bias,
        norm2_gain,
        norm2_bias,
        fc1_weight,
        fc1_bias,
        fc2_weight,
        fc2_bias,
        cotangent,
    ):
        z = Sizes(nf, nt, inputs, qv_bias, fc1_weight)
        part = functools.partial
        rows, width, inner, ff, chunk = z.rows, z.width, z.inner, z.ff, z.chunk
        f = lax.axis_index("fsdp")
        tie = lax.optimization_barrier

        def other_core(value):
            return lax.ppermute(value, "ctx", [(0, 1), (1, 0)])

        def to_tp(value, k):
            return lax.ppermute(value, "tp", [(i, i ^ k) for i in range(nt)])

        def to_far(value):
            return lax.ppermute(value, "fsdp", [(i, i ^ 3) for i in range(nf)])

        def neighbours(value, order):
            pairs = [(2 * i + c, 2 * (i ^ order[c]) + c) for i in range(nf) for c in range(2)]
            return lax.ppermute(value, ("fsdp", "ctx"), pairs)

        def to_near(value):
            return neighbours(value, (1, 2))

        def to_cross(value):
            return neighbours(value, (2, 1))

        def proj_near(value):
            pairs = [(c * nt + i, c * nt + (i ^ (1 + 2 * c))) for i in range(nt) for c in range(2)]
            return lax.ppermute(value, ("ctx", "tp"), pairs)

        def pair_of(first, second):
            return call(pair_kernel, [shape((2,) + first.shape, LOW)], [first, second], name="pair")[0]

        qkv3 = qkv_weight.transpose(1, 0, 2)
        down_t = fc2_weight.T
        qv3 = qv_bias.transpose(1, 0, 2)
        x_raw, cot_raw = inputs.transpose(1, 0, 2), cotangent.transpose(1, 0, 2)
        vectors = [norm1_gain, norm1_bias, proj_bias, norm2_gain, norm2_bias, fc2_bias]

        x_recv = other_core(x_raw)
        cot_recv = other_core(cot_raw)
        def frames(x_recv, cot_recv):
            stream, normal_one, inverse_one = call(
                part(frame_kernel, z),
                [shape((rows, width), LOW), shape((rows, width), F32), shape((rows, 128), F32)],
                [x_raw, x_recv],
                name="frame",
            )
            (cot,) = call(part(cot_kernel, z), [shape((rows, width), LOW)], [cot_raw, cot_recv], name="cotangent")
            return stream, normal_one, inverse_one, cot

        if z.direct:
            sources = [qkv3, proj_weight, fc1_bias, qv3] + vectors
            near, far, proj_t, proj_half = call(
                part(pack_kernel, z),
                [
                    shape((z.part + EXTRA, 3 * inner), LOW),
                    shape((chunk + EXTRA, 3 * inner), LOW),
                    shape((z.part + 104, inner), LOW),
                    shape((chunk, inner), LOW),
                ],
                sources,
                [pltpu.VMEM(s.shape, s.dtype) for s in sources] + [pltpu.SemaphoreType.DMA((len(sources),))],
                name="pack",
                mib=56,
                in_specs=[ANY] * len(sources),
            )
            near, far, proj_t, proj_half, x_recv, cot_recv = tie((near, far, proj_t, proj_half, x_recv, cot_recv))
            got = [to_near(near), to_far(far)]
            proj_got = [proj_near(proj_t), to_tp(proj_half, 2)]
            feed_own, feed_rest = call(
                part(stage_kernel, z),
                [shape((z.part, z.early), LOW), shape((z.part, 2 * ff - z.early), LOW)],
                [fc1_weight, down_t],
                [pltpu.VMEM((z.part, ff), LOW)] * 2 + [pltpu.SemaphoreType.DMA((2,))],
                name="stage",
                mib=20,
                in_specs=[ANY] * 2,
            )
            stream, normal_one, inverse_one, cot = frames(x_recv, cot_recv)
            feed_in = to_near(feed_own)
            got, proj_got, feed_rest, stream, normal_one, inverse_one, cot = tie(
                (got, proj_got, feed_rest, stream, normal_one, inverse_one, cot)
            )
            shared = [other_core(g) for g in got]
            qkv_in = [near, got[0], shared[0], got[1], shared[1]]
            (rest_near,) = call(
                part(pack_rest_kernel, z),
                [shape((z.part, z.cols - z.early), LOW)],
                [feed_rest, proj_t, proj_got[0], other_core(proj_got[0]), proj_got[1], other_core(proj_got[1])],
                [pltpu.VMEM((nt, z.part, inner), F32)],
                name="pack_rest",
            )
            near_in = to_near(rest_near)
            far_in = []
            for value in (feed_in, near_in):
                (half,) = call(part(cut_kernel, z), [shape((chunk, value.shape[1]), LOW)], [value], name="cut")
                far_in.append(to_cross(half))
        else:
            stream, normal_one, inverse_one, cot = frames(x_recv, cot_recv)
            whole = lax.all_gather(qkv3, "fsdp", axis=1, tiled=True)
            whole = whole.transpose(1, 0, 2).reshape(4, z.part, 3 * inner)
            vec = jnp.stack(vectors + [vectors[0]] * 2).astype(F32)
            qv_rows = qv3.reshape(2 * z.heads, -1).astype(F32)
            gathered = [lax.all_gather(v, "fsdp", axis=1, tiled=True) for v in (vec, fc1_bias.astype(F32), qv_rows)]
            qkv_in = [whole] + gathered
            proj_t = proj_weight.T
            rest = jnp.concatenate([fc1_weight, down_t, lax.all_gather(proj_t, "tp", axis=1, tiled=True)], 1)
            rest_in = [lax.all_gather(rest, "fsdp", axis=0, tiled=True).reshape(4, z.part, z.cols)]

        small, w_qkv, normed_one, act, attended, soft = call(
            part(attend_kernel, z),
            [
                shape((8, width), F32),
                shape((4, z.part, 3 * inner), LOW),
                shape((rows, width), LOW),
                shape((3, rows, inner), LOW),
                shape((z.dense, 128), LOW),
                shape((z.heads, rows, rows), F32),
            ],
            qkv_in + [normal_one],
            [pltpu.VMEM((4, EXTRA, 3 * inner), F32)] if z.direct else [],
            name="attend",
        )
        att_one = to_tp(attended, 2)
        (att_two,) = call(pair_kernel, [shape((2, z.dense + 16, 128), LOW)], [attended, att_one], name="pair")
        att_two = to_tp(att_two, 1)
        if z.direct:
            att_two, far_in = tie((att_two, far_in))
            rest_in = [feed_own, feed_in, other_core(feed_in), rest_near, near_in, other_core(near_in)]
            rest_in += [far_in[0], other_core(far_in[0]), far_in[1], other_core(far_in[1])]

        (w_rest, att_all, middle, hidden, normed_two, grad_pre, part_middle, part_low, own_att, small_two, *att_sends) = (
            call(
                part(feed_kernel, z),
                [
                    shape((4, z.part, z.cols), LOW),
                    shape((rows, nt * inner), LOW),
                    shape((rows, width), F32),
                    shape((rows, ff), LOW),
                    shape((rows, width), LOW),
                    shape((rows, ff), LOW),
                    shape((rows, width), F32),
                    shape((rows, width), LOW),
                    shape((rows, inner), F32),
                    shape((8, width), F32),
                ]
                + [shape((z.dense, 128), LOW)] * (nt - 1),
                rest_in + [attended, att_one, att_two, stream, cot, small],
                [pltpu.VMEM((nt, rows, inner), F32)],
                name="feed",
            )
        )
        att_got = [to_tp(att_sends[k - 1], k) for k in range(1, nt)]
        all_cols = z.all_cols
        keep, sent = call(
            part(feed_grad_kernel, z),
            [shape((4, chunk, 2 * ff), F32), shape((4 * chunk, 2 * ff), LOW)],
            [normed_two, grad_pre, cot, hidden],
            name="feed_grad",
        )
        keep_proj, *sent_proj = call(
            part(proj_grad_kernel, z),
            [shape((4, z.part, nt * inner), F32)]
            + ([shape((z.part + chunk, nt * inner), LOW)] if z.direct else []),
            [part_low, att_all],
            name="proj_grad",
        )
        out_kept, out_sent = call(
            part(down_kernel, z),
            [shape((z.padded, width), F32), shape((z.padded, width), LOW)],
            [hidden, w_rest],
            [pltpu.VMEM((rows, width), F32)],
            name="down",
        )
        out_one = to_tp(out_sent, 1)
        if z.direct:
            proj_in = other_core(sent_proj[0])
            att_got, out_one, keep, sent, proj_in = tie((att_got, out_one, keep, sent, proj_in))
            near, far = call(
                part(proj_one_kernel, z),
                [shape((z.part, nt * inner), LOW), shape((chunk, nt * inner), LOW)],
                [keep_proj, proj_in],
                name="proj_one",
            )
            proj_in = [to_near(near), to_far(far)]
        (out_low,) = call(add_low_kernel, [shape((z.padded, width), LOW)], [out_kept, out_one], name="out_pair")
        out_two = to_tp(out_low, 3)

        grads, qv_sum, in_kept, in_sent = call(
            part(back_kernel, z),
            [
                shape((rows, 3 * inner), LOW),
                shape((1, 3 * inner), F32),
                shape((z.padded + 8, width), F32),
                shape((z.padded + 8, width), LOW),
            ],
            [own_att] + att_got + [act, soft, w_qkv, normal_one, inverse_one, part_middle, small, small_two],
            [pltpu.VMEM((rows, width), F32)],
            name="back",
        )
        in_one = to_tp(in_sent, 1)
        keep_qkv, sent = call(
            part(qkv_grad_kernel, z),
            [shape((4, chunk, 3 * inner), F32), shape((4 * chunk, all_cols), LOW)],
            [sent, normed_one, grads],
            name="qkv_grad",
        )
        if z.direct:
            sent = other_core(sent)
            in_one, out_two, proj_in, sent = tie((in_one, out_two, proj_in, sent))
            grad_sent, grad_kept = call(
                part(split_kernel, z),
                [shape((2, chunk, all_cols), LOW), shape((2, chunk, all_cols), F32)],
                [keep, keep_qkv, sent],
                name="split",
            )
            grad_in = to_near(grad_sent)
        (in_low,) = call(add_low_kernel, [shape((z.padded + 8, width), LOW)], [in_kept, in_one], name="in_pair")
        in_two = to_tp(in_low, 3)
        *proj_kept, out_low = call(
            part(out_total_kernel, z),
            ([shape((2, z.tail, width), F32)] if z.direct else [])
            + [shape((z.padded + (2 * z.tail if z.direct else 0), width), LOW)],
            [out_low, out_two, middle, small] + ([keep_proj] + proj_in if z.direct else []),
            [pltpu.VMEM((nt, z.tail, width), F32)] if z.direct else [],
            name="out_total",
        )
        out_in = to_tp(out_low, 1)
        if z.direct:
            in_two, out_in, grad_in = tie((in_two, out_in, grad_in))
        in_low, vec = call(
            part(sum_rows_kernel, z),
            [shape((z.padded, width), LOW), shape((VEC_ROWS, width), F32)],
            [in_low, in_two, small_two, qv_sum],
            name="sum_rows",
        )
        in_in = to_tp(in_low, 1)
        proj_all = []
        if z.direct:
            grad_own, cross = call(
                cross_kernel,
                [shape((chunk, all_cols), F32), shape((chunk, all_cols), LOW)],
                [grad_kept, grad_in],
                name="cross",
            )
            cross = to_cross(cross)
            proj_own, proj_sent = call(
                part(proj_pair_kernel, z),
                [shape((z.tail, width), F32), shape((z.tail, width), LOW)],
                [proj_kept[0], out_in],
                name="proj_pair",
            )
            proj_two = to_tp(proj_sent, 3)
            near, far, small_own = call(
                part(small_kernel, z),
                [shape((EXTRA, 3 * inner), LOW)] * 2 + [shape((EXTRA, 3 * inner), F32)],
                [vec, other_core(vec)],
                [pltpu.VMEM((4, EXTRA, 3 * inner), F32)],
                name="small",
            )
            near, far = to_near(near), to_far(far)
            in_in, proj_two, cross, near, far = tie((in_in, proj_two, cross, near, far))
            proj_all = [proj_own, proj_two]
            feed_own, feed_sent, qkv_own, qkv_sent = call(
                part(last_kernel, z),
                [
                    shape((chunk, 2 * ff), F32),
                    shape((chunk, 2 * ff), LOW),
                    shape((chunk + EXTRA, 3 * inner), F32),
                    shape((chunk + EXTRA, 3 * inner), LOW),
                ],
                [grad_own, cross, small_own, near, far],
                name="last",
            )
            feed_in, qkv_in = other_core(feed_sent), other_core(qkv_sent)
        mine, theirs, *proj_own = call(
            part(swap_kernel, z),
            [shape((2, z.padded, width), F32), shape((rows + (z.tail if proj_all else 0), width), LOW)]
            + ([shape((z.tail, width), F32)] if proj_all else []),
            [out_low, out_in, in_low, in_in] + proj_all,
            name="swap",
        )
        theirs = other_core(theirs)
        results = [shape((z.half, 2, width), LOW), shape((z.half, 2, width), F32)]
        scratch = [pltpu.VMEM((z.half, 2, width), F32)]
        if z.direct:
            output, input_grad, proj_grad, fc1_grad, fc2_grad, qkv_grad, up_grad, qv_grad, *vec_grads = call(
                part(final_kernel, z),
                results
                + [
                    shape((inner, z.shard), F32),
                    shape((z.shard, ff), F32),
                    shape((z.shard, ff), F32),
                    shape((3, z.shard, inner), F32),
                    shape(fc1_bias.shape, F32),
                    shape(qv3.shape, F32),
                ]
                + [shape((z.shard,), F32)] * 6,
                [mine, theirs, proj_own[0], feed_own, feed_in, qkv_own, qkv_in],
                scratch,
                name="final",
            )
        else:
            output, input_grad = call(part(final_kernel, z), results, [mine, theirs], scratch, name="final")

            def joined(keep, sent):
                return jnp.stack([keep.astype(LOW), sent.reshape(keep.shape)], 1).reshape(width, -1)

            def scatter(whole):
                whole = lax.psum(whole, "ctx")
                return lax.psum_scatter(whole, "fsdp", scatter_dimension=0, tiled=True).astype(F32)

            extra = all_cols - 2 * ff - 3 * inner
            total = scatter(joined(jnp.concatenate([keep, jnp.pad(keep_qkv, ((0, 0), (0, 0), (0, extra)))], 2), sent))
            fc1_grad, fc2_grad = total[:, :ff], total[:, ff : 2 * ff]
            qkv_grad = total[:, 2 * ff : 2 * ff + 3 * inner].reshape(z.shard, 3, inner).transpose(1, 0, 2)
            proj_grad = scatter(keep_proj.reshape(width, -1).astype(LOW)).astype(LOW)
            proj_grad = lax.psum_scatter(proj_grad, "tp", scatter_dimension=1, tiled=True).astype(F32).T

            def own_columns(value):
                value = lax.psum(value, ("fsdp", "ctx"))
                return lax.dynamic_slice_in_dim(value, f * (value.shape[1] // nf), value.shape[1] // nf, 1)

            vec_grads = own_columns(vec[:6])
            up_grad = own_columns(vec[8, :ff].reshape(-1, HD))
            qv_grad = vec[9, : 3 * inner].reshape(3, z.heads, HD)[0::2].transpose(1, 0, 2)
            qv_grad = own_columns(qv_grad.reshape(2 * z.heads, HD)).reshape(qv3.shape)
        return (
            output.transpose(1, 0, 2),
            input_grad.transpose(1, 0, 2),
            vec_grads[0],
            vec_grads[1],
            qkv_grad.transpose(1, 0, 2),
            qv_grad.transpose(1, 0, 2),
            proj_grad,
            vec_grads[2],
            vec_grads[3],
            vec_grads[4],
            fc1_grad,
            up_grad,
            fc2_grad.T,
            vec_grads[5],
        )

    return local


def solution(mesh):
    sizes = mesh.shape
    return jax.shard_map(
        build(sizes["fsdp"], sizes["ctx"], sizes["tp"]),
        mesh=mesh,
        in_specs=(
            P("fsdp", "ctx", None),
            P("fsdp"),
            P("fsdp"),
            P("fsdp", None, "tp"),
            P(None, "tp", "fsdp"),
            P("tp", "fsdp"),
            P("fsdp"),
            P("fsdp"),
            P("fsdp"),
            P("fsdp", "tp"),
            P("tp", "fsdp"),
            P("tp", "fsdp"),
            P("fsdp"),
            P("fsdp", "ctx", None),
        ),
        out_specs=(
            P("fsdp", "ctx", None),
            P("fsdp", "ctx", None),
            P("fsdp"),
            P("fsdp"),
            P("fsdp", None, "tp"),
            P(None, "tp", "fsdp"),
            P("tp", "fsdp"),
            P("fsdp"),
            P("fsdp"),
            P("fsdp"),
            P("fsdp", "tp"),
            P("tp", "fsdp"),
            P("tp", "fsdp"),
            P("fsdp"),
        ),
        check_vma=False,
    )
```

```python
import functools

import jax
import jax.numpy as jnp
from jax import lax
from jax.experimental import pallas as pl
from jax.experimental.pallas import tpu as pltpu
from jax.sharding import PartitionSpec as P

HD = 64
EPSILON = 1e-06
QUERY_SCALE = 0.125
F32 = jnp.float32
LOW = jnp.bfloat16
NN = ((1,), (0,))
NT = ((1,), (1,))
TN = ((0,), (0,))
VMEM = pl.BlockSpec(memory_space=pltpu.VMEM)
ANY = pl.BlockSpec(memory_space=pl.ANY)
EXTRA = 16
VEC_ROWS = 144
UP_AT, QV_AT = 256, 384


def dot(left, right, dims):
    return lax.dot_general(left, right, (dims, ((), ())), preferred_element_type=F32)


def shape(dims, kind):
    return jax.ShapeDtypeStruct(tuple(dims), kind)


def call(kernel, outs, args, scratch=(), name=None, mib=20, in_specs=None, alias=None):
    return pl.pallas_call(
        kernel,
        out_shape=tuple(outs),
        in_specs=in_specs or [VMEM] * len(args),
        out_specs=tuple([VMEM] * len(outs)),
        scratch_shapes=list(scratch),
        input_output_aliases=alias or {},
        name=name,
        compiler_params=pltpu.CompilerParams(vmem_limit_bytes=mib << 20),
    )(*args)


def gelu_and_slope(v):
    cdf = 0.5 * (1.0 + lax.erf(v * 0.7071067811865476))
    density = jnp.exp(-0.5 * v * v) * 0.3989422804014327
    return v * cdf, cdf + v * density


def mean(v):
    return jnp.mean(v, axis=-1, keepdims=True)


def total_rows(v):
    return jnp.sum(v, axis=0, keepdims=True)


def normalise(v):
    centred = v - mean(v)
    inverse = lax.rsqrt(mean(centred * centred) + EPSILON)
    return centred * inverse, inverse


def norm_backward(grad_normed, normal, inverse, gain):
    scaled = grad_normed * gain
    return inverse * (scaled - mean(scaled) - normal * mean(scaled * normal))


def row_half(t):
    return t & 1


def lanes(parts):
    return jnp.concatenate(parts, axis=1)


def rows_of(parts):
    return jnp.concatenate(parts, axis=0)


def read(ref):
    return ref[...].astype(F32)


class Sizes:
    def __init__(self, nf, nt, inputs, qv_bias, fc1_weight):
        self.nf, self.nt = nf, nt
        _, self.half, self.width = inputs.shape
        self.shard = self.width // nf
        self.heads = qv_bias.shape[1]
        self.inner = self.heads * HD
        self.ff = fc1_weight.shape[1]
        self.pad = -self.half % 8
        self.padded = self.half + self.pad
        self.rows = 2 * self.padded
        self.part = self.width // 4
        self.chunk = self.part // 2
        self.tail = self.chunk // 4
        self.direct = nf == 4
        self.cols = 2 * self.ff + nt * self.inner
        self.early = 1280 if self.ff == 768 else self.ff
        self.first = 3 * self.ff // 2
        self.all_cols = 2 * self.ff + -(-3 * self.inner // 128) * 128
        self.dense = self.rows * self.inner // 128

    def half_rows(self, h):
        return pl.ds(pl.multiple_of(h * self.padded, 8), self.padded)

    def half_of(self, c):
        return pl.ds(pl.multiple_of(c * self.chunk, 16), self.chunk)

    def squeeze(self, v):
        return rows_of([v[:, :128], lanes([v[: self.padded, 128:], v[self.padded :, 128:]])])

    def spread(self, v):
        tail = v[self.rows :]
        return lanes([v[: self.rows], rows_of([tail[:, :HD], tail[:, HD:]])])


def fetch(sources, copies, sem):
    moves = [pltpu.make_async_copy(s, d, sem.at[i]) for i, (s, d) in enumerate(zip(sources, copies))]
    for m in moves:
        m.start()
    for m in moves:
        m.wait()


def stage_kernel(z, up, down_t, out, rest, one, two, sem):
    fetch((up, down_t), (one, two), sem)
    first = z.early - z.ff
    out[:, : z.ff] = one[...]
    out[:, z.ff :] = two[:, :first]
    rest[...] = two[:, first:]


def pack_kernel(z, *refs):
    sources, (near, far, proj_t, proj_half) = refs[:10], refs[10:14]
    copies, sem = refs[14:24], refs[24]
    fetch(sources, copies, sem)
    qkv, proj, up_b, qv_b = copies[:4]
    vectors = copies[4:]
    c = lax.axis_index("ctx")
    whole = lanes([read(qkv.at[i]) for i in range(3)])
    near[: z.part, :] = whole.astype(LOW)
    far[: z.chunk, :] = jnp.where(c == 0, whole[: z.chunk], whole[z.chunk :]).astype(LOW)
    row = lax.broadcasted_iota(jnp.int32, (EXTRA, z.shard), 0)
    vec = jnp.zeros((EXTRA, z.shard), F32)
    for i, v in enumerate(vectors):
        vec = jnp.where(row == i, read(v).reshape(1, z.shard), vec)
    biases = read(qv_b)
    biases = rows_of([biases[h, i : i + 1] for h in range(z.heads) for i in range(2)])
    for out, at in ((near, z.part), (far, z.chunk)):
        out[at:, :] = jnp.zeros((EXTRA, 3 * z.inner), LOW)
        out[at:, : z.shard] = vec.astype(LOW)
        out[at : at + up_b.shape[0], UP_AT : UP_AT + up_b.shape[1]] = up_b[...]
        out[at : at + 2 * z.heads, QV_AT : QV_AT + biases.shape[1]] = biases.astype(LOW)
    turned = read(proj).T
    proj_t[...] = rows_of([turned, jnp.zeros((proj_t.shape[0] - z.part, z.inner), F32)]).astype(LOW)
    proj_half[...] = jnp.where(c == 0, turned[: z.chunk], turned[z.chunk :]).astype(LOW)


def cut_kernel(z, value, out):
    out[...] = value[z.half_of(lax.axis_index("ctx")), :]


def pair_kernel(first, second, out):
    rows = first.shape[0]
    out[0, :rows, :] = first[...]
    out[1, :rows, :] = second[...]
    out[:, rows:, :] = jnp.zeros((2, out.shape[1] - rows, out.shape[2]), LOW)


def pack_rest_kernel(z, rest, proj_t, near_in, near_their, far_in, far_their, near, scratch):
    c, t = lax.axis_index("ctx"), lax.axis_index("tp")
    scratch[t] = proj_t[: z.part, :].astype(F32)
    scratch[t ^ (1 + 2 * c)] = near_in[: z.part, :].astype(F32)
    scratch[t ^ (3 - 2 * c)] = near_their[: z.part, :].astype(F32)
    scratch[t ^ 2, z.half_of(c), :] = far_in[: z.chunk, :].astype(F32)
    scratch[t ^ 2, z.half_of(1 - c), :] = far_their[: z.chunk, :].astype(F32)
    near[:, : 2 * z.ff - z.early] = rest[...]
    near[:, 2 * z.ff - z.early :] = lanes([scratch[i] for i in range(4)]).astype(LOW)


def own_frame(z, keep, received):
    c = lax.axis_index("ctx")
    zero = jnp.zeros((z.pad, z.width), F32)
    pieces = []
    for ref in (keep, received):
        pieces.append(jnp.where(c == 0, ref[:, 0, :].astype(F32), ref[:, 1, :].astype(F32)))
        pieces.append(zero)
    return rows_of(pieces)


def frame_kernel(z, keep, received, stream, normal, inverse):
    values = own_frame(z, keep, received)
    stream[...] = values.astype(LOW)
    n, i = normalise(values)
    normal[...] = n
    inverse[...] = jnp.broadcast_to(i, inverse.shape)


def cot_kernel(z, keep, received, stream):
    stream[...] = own_frame(z, keep, received).astype(LOW)


def attend_kernel(z, *refs):
    refs = list(refs)
    if z.direct:
        own, near, near_their, far, far_their = refs[:5]
        refs = refs[5:]
    else:
        whole, vec_in, up_in, qv_in = refs[:4]
        refs = refs[4:]
    normal, small, w_out, normed_out, act, attended, soft_out = refs[:7]
    if z.direct:
        c, b = lax.axis_index("ctx"), lax.axis_index("fsdp")
        gather = refs[7]
        for ref, at in ((own, b), (near, b ^ (1 + c)), (near_their, b ^ (2 - c))):
            w_out[at] = ref[: z.part, :]
            gather[at] = ref[z.part :, :].astype(F32)
        w_out[b ^ 3, z.half_of(c), :] = far[: z.chunk, :]
        w_out[b ^ 3, z.half_of(1 - c), :] = far_their[: z.chunk, :]
        gather[b ^ 3] = far[z.chunk :, :].astype(F32)
        blocks = [gather[i] for i in range(4)]
        w = HD // 4
        vec = lanes([g[:8, : z.shard] for g in blocks])
        up = lanes([g[: z.ff // HD, UP_AT : UP_AT + w] for g in blocks])
        qv = lanes([g[: 2 * z.heads, QV_AT : QV_AT + w] for g in blocks])
    else:
        w_out[...] = whole[...]
        vec, up, qv = vec_in[...], up_in[...], qv_in[...]
    up_row = lanes([up[i : i + 1] for i in range(z.ff // HD)])
    query_b = lanes([qv[2 * h : 2 * h + 1] for h in range(z.heads)])
    value_b = lanes([qv[2 * h + 1 : 2 * h + 2] for h in range(z.heads)])
    small[...] = vec
    small[6:7, : z.ff] = up_row
    normed = (normal[...] * vec[0:1] + vec[1:2]).astype(LOW)
    normed_out[...] = normed
    projected = dot(normed, w_out[...].reshape(z.width, 3 * z.inner), NN)
    n = z.inner
    query = ((projected[:, :n] + query_b) * QUERY_SCALE).astype(LOW)
    key = projected[:, n : 2 * n].astype(LOW)
    value = (projected[:, 2 * n :] + value_b).astype(LOW)
    act[0] = query
    act[1] = key
    act[2] = value
    place = lax.broadcasted_iota(jnp.int32, (z.rows, z.rows), 1)
    valid = (place < z.half) | ((place >= z.padded) & (place < z.padded + z.half))
    done = []
    for h in range(z.heads):
        cut = slice(h * HD, (h + 1) * HD)
        scores = jnp.where(valid, dot(query[:, cut], key[:, cut], NT), -1e30)
        exponent = jnp.exp(scores - jnp.max(scores, axis=-1, keepdims=True))
        soft = exponent * (1.0 / jnp.sum(exponent, axis=-1, keepdims=True))
        soft_out[h] = soft
        done.append(dot(soft.astype(LOW), value[:, cut], NN))
    attended[...] = z.squeeze(lanes(done)).astype(LOW)


def feed_kernel(z, *refs):
    refs = list(refs)
    if z.direct:
        feed, feed_in, feed_their, near, near_in, near_their, far, far_their, last_far, last_far_their = refs[:10]
        refs = refs[10:]
    else:
        whole = refs[0]
        refs = refs[1:]
    att = refs[:3]
    stream, cot, small = refs[3:6]
    (w_out, att_out, middle_out, hidden_out, normed_out, pre_out, part_out, low_out, own_att, small_out) = refs[6:16]
    sends, heads = refs[16:-1], refs[-1]
    t = lax.axis_index("tp")
    if z.direct:
        c, b = lax.axis_index("ctx"), lax.axis_index("fsdp")
        mine, other = z.half_of(c), z.half_of(1 - c)
        first, last = pl.ds(0, z.early), pl.ds(z.early, z.cols - z.early)
        for at, one, two in ((b, feed, near), (b ^ (1 + c), feed_in, near_in), (b ^ (2 - c), feed_their, near_their)):
            w_out[at, :, first] = one[...]
            w_out[at, :, last] = two[...]
        w_out[b ^ 3, mine, first] = far[...]
        w_out[b ^ 3, other, first] = far_their[...]
        w_out[b ^ 3, mine, last] = last_far[...]
        w_out[b ^ 3, other, last] = last_far_their[...]
    else:
        w_out[...] = whole[...]
    n = z.inner
    w_up = w_out[:, :, : z.ff].reshape(z.width, z.ff)
    w_down_t = w_out[:, :, z.ff : 2 * z.ff].reshape(z.width, z.ff)
    w_proj_t = w_out[:, :, 2 * z.ff :].reshape(z.width, z.nt * n)
    grad_out_low = cot[...]
    grad_out = grad_out_low.astype(F32)
    heads[t] = z.spread(read(att[0]))
    heads[t ^ 2] = z.spread(read(att[1]))
    heads[t ^ 1] = z.spread(att[2][0, : z.dense, :].astype(F32))
    heads[t ^ 3] = z.spread(att[2][1, : z.dense, :].astype(F32))
    attended = lanes([heads[i] for i in range(z.nt)]).astype(LOW)
    att_out[...] = attended
    branch = dot(attended, w_proj_t, NT)
    middle = stream[...].astype(F32) + branch + small[2:3]
    middle_out[...] = middle
    normal, inverse = normalise(middle)
    gain = small[3:4]
    normed = (normal * gain + small[4:5]).astype(LOW)
    normed_out[...] = normed
    hidden, slope = gelu_and_slope(dot(normed, w_up, NN) + small[6:7, : z.ff])
    hidden_out[...] = hidden.astype(LOW)
    grad_pre = (dot(grad_out_low, w_down_t, NN) * slope).astype(LOW)
    pre_out[...] = grad_pre
    grad_normed = dot(grad_pre, w_up, NT)
    part = grad_out * (1.0 / z.nt) + norm_backward(grad_normed, normal, inverse, gain)
    part_out[...] = part
    low = part.astype(LOW)
    low_out[...] = low
    grad_att = dot(low, w_proj_t, NN)
    for i in range(z.nt):
        heads[i] = grad_att[:, i * n : (i + 1) * n]
    own_att[...] = heads[t]
    for k in range(1, z.nt):
        sends[k - 1][...] = z.squeeze(heads[t ^ k]).astype(LOW)
    small_out[...] = jnp.zeros(small_out.shape, F32)
    small_out[2:3] = total_rows(part)
    small_out[3:4] = total_rows(grad_normed * normal)
    small_out[4:5] = total_rows(grad_normed)
    small_out[5:6] = total_rows(grad_out) * (1.0 / z.nt)
    small_out[6:7, : z.ff] = total_rows(grad_pre.astype(F32))


def down_kernel(z, hidden, w, kept, sent, scratch):
    h = row_half(lax.axis_index("tp"))
    w_down_t = w[:, :, z.ff : 2 * z.ff].reshape(z.width, z.ff)
    scratch[...] = dot(hidden[...], w_down_t, NT)
    kept[...] = scratch[z.half_rows(h), :]
    sent[...] = scratch[z.half_rows(1 - h), :].astype(LOW)


def add_low_kernel(kept, received, out):
    rows = kept.shape[0]
    out[:rows, :] = (kept[...] + read(received)).astype(LOW)
    if out.shape[0] > rows:
        out[rows:, :] = jnp.zeros((out.shape[0] - rows, out.shape[1]), LOW)


def store_halves(z, value, at, keep, sent, sent_at=None):
    cols = pl.ds(at, value.shape[1])
    sent_cols = pl.ds(at if sent_at is None else sent_at, value.shape[1])
    c = lax.axis_index("ctx") if z.direct else 0
    b = lax.axis_index("fsdp") if z.direct else 0
    for j in range(4):
        first = value[j * z.part : j * z.part + z.chunk]
        second = value[j * z.part + z.chunk : (j + 1) * z.part]
        if z.direct:
            keep[j ^ b, :, cols] = jnp.where(c == 0, first, second)
            rows = pl.ds(pl.multiple_of((j ^ b) * z.chunk, 16), z.chunk)
            sent[rows, sent_cols] = jnp.where(c == 0, second, first).astype(LOW)
        else:
            keep[j, :, cols] = first
            sent[pl.ds(j * z.chunk, z.chunk), sent_cols] = second.astype(LOW)


def feed_grad_kernel(z, normed, pre, cot, hidden, keep, sent):
    store_halves(z, dot(normed[...], pre[...], TN), 0, keep, sent)
    store_halves(z, dot(cot[...], hidden[...], TN), z.ff, keep, sent)


def qkv_grad_kernel(z, feed_sent, normed, grads, keep, sent):
    sent[:, : 2 * z.ff] = feed_sent[...]
    sent[:, 2 * z.ff + 3 * z.inner :] = jnp.zeros((sent.shape[0], z.all_cols - 2 * z.ff - 3 * z.inner), LOW)
    store_halves(z, dot(normed[...], grads[...], TN), 0, keep, sent, 2 * z.ff)


def proj_grad_kernel(z, low, att, keep, sent):
    store_halves(z, dot(low[...], att[...], TN), 0, keep, sent)


def split_kernel(z, keep, received, out, kept):
    c = lax.axis_index("ctx")
    cols = pl.ds(0, z.first)
    for target, at, kind in ((out, (1 + c, 3), LOW), (kept, (0, 2 - c), F32)):
        for i in range(2):
            rows = pl.ds(pl.multiple_of(at[i] * z.chunk, 16), z.chunk)
            target[i] = (keep[at[i], :, cols] + received[rows, cols].astype(F32)).astype(kind)


def split_rest_kernel(z, keep, keep_qkv, received, out, kept):
    c = lax.axis_index("ctx")
    for target, at, kind in ((out, (1 + c, 3), LOW), (kept, (0, 2 - c), F32)):
        for i in range(2):
            rows = pl.ds(pl.multiple_of(at[i] * z.chunk, 16), z.chunk)
            n, m = 2 * z.ff - z.first, 3 * z.inner
            total = keep[at[i], :, z.first :] + received[rows, z.first : 2 * z.ff].astype(F32)
            target[i, :, :n] = total.astype(kind)
            total = keep_qkv[at[i]] + received[rows, 2 * z.ff : 2 * z.ff + m].astype(F32)
            target[i, :, n : n + m] = total.astype(kind)
            target[i, :, n + m :] = jnp.zeros((z.chunk, target.shape[2] - n - m), kind)


def proj_one_kernel(z, keep, received, own, *sends):
    for k in range(4):
        total = keep[k] + received[k * z.chunk : (k + 1) * z.chunk, :].astype(F32)
        if k == 0:
            own[...] = total
        else:
            sends[k - 1][...] = total.astype(LOW)


def by_half(mine, other):
    c = lax.axis_index("ctx")
    return rows_of([jnp.where(c == 0, mine, other), jnp.where(c == 0, other, mine)])


def feed_final_kernel(z, own, theirs, up, down):
    total = by_half(own[...], read(theirs))
    up[...] = total[:, : z.ff]
    down[...] = total[:, z.ff :]


def unfold(z, v):
    return rows_of([v[:, i * z.inner : (i + 1) * z.inner] for i in range(4)])


def fold(v):
    n = v.shape[0] // 4
    return lanes([v[i * n : (i + 1) * n] for i in range(4)])


def back_kernel(z, *refs):
    own_att, got = refs[0], refs[1 : z.nt]
    act, soft, w, normal, inverse, part, small, small_in = refs[z.nt : z.nt + 8]
    grads_out, qv_out, kept, sent, scratch = refs[z.nt + 8 :]
    t = lax.axis_index("tp")
    grad_att = (own_att[...] + z.spread(sum(read(g) for g in got))).astype(LOW)
    parts = [[], [], []]
    query, key, value = act[0], act[1], act[2]
    for h in range(z.heads):
        cut = slice(h * HD, (h + 1) * HD)
        ga = grad_att[:, cut]
        p = soft[h]
        grad_soft = dot(ga, value[:, cut], NT)
        delta = jnp.sum(p * grad_soft, axis=-1, keepdims=True)
        grad_scores = (p * (grad_soft - delta)).astype(LOW)
        parts[0].append((dot(grad_scores, key[:, cut], NN).astype(LOW).astype(F32) * QUERY_SCALE).astype(LOW))
        parts[1].append(dot(grad_scores, query[:, cut], TN).astype(LOW))
        parts[2].append(dot(p.astype(LOW), ga, TN).astype(LOW))
    grads = lanes(parts[0] + parts[1] + parts[2])
    grads_out[...] = grads
    n = z.inner
    qv_out[...] = total_rows(grads.astype(F32))
    grad_normed = dot(grads, w[...].reshape(z.width, 3 * n), NT)
    scratch[...] = part[...] + norm_backward(grad_normed, normal[...], inverse[:, :1], small[0:1])
    row = lax.broadcasted_iota(jnp.int32, (8, z.width), 0)
    vec = small_in[...]
    vec = jnp.where(row == 0, total_rows(grad_normed * normal[...]), vec)
    vec = jnp.where(row == 1, total_rows(grad_normed), vec)
    h = row_half(t)
    kept[: z.padded, :] = scratch[z.half_rows(h), :]
    kept[z.padded :, :] = vec
    sent[: z.padded, :] = scratch[z.half_rows(1 - h), :].astype(LOW)
    sent[z.padded :, :] = vec.astype(LOW)


def out_total_kernel(z, own, received, middle, small, *refs):
    if z.direct:
        keep, *parts, kept, out, scratch = refs
        proj_two_kernel(z, keep, parts, out, kept, scratch)
    else:
        (out,) = refs
    rows = z.half_rows(row_half(lax.axis_index("tp")))
    total = (read(own) + read(received))[: z.padded]
    out[: z.padded, :] = (middle[rows, :] + total + small[5:6]).astype(LOW)


def proj_two_kernel(z, own, parts, out, kept, scratch):
    t = lax.axis_index("tp")
    proj = own[...] + sum(read(p) for p in parts)
    for i in range(z.nt):
        scratch[i] = fold(proj[:, i * z.inner : (i + 1) * z.inner])
    kept[0] = scratch[t]
    kept[1] = scratch[t ^ 2]
    out[z.padded :, :] = rows_of([scratch[t ^ 1], scratch[t ^ 3]]).astype(LOW)


def sum_rows_kernel(z, own, received, small, qv, out, vec):
    total = read(own) + read(received)
    out[...] = total[: z.padded].astype(LOW)
    vec[:8, :] = total[z.padded :]
    vec[8:, :] = jnp.zeros((vec.shape[0] - 8, z.width), F32)
    vec[8:9, : z.ff] = small[6:7, : z.ff]
    vec[9:10, : 3 * z.inner] = qv[...]


def proj_pair_kernel(z, kept, received, own, sent):
    arrived = received[z.padded :, :].astype(F32)
    own[...] = kept[0] + arrived[: z.tail]
    sent[...] = (kept[1] + arrived[z.tail :]).astype(LOW)


def cross_kernel(z, kept, rest_kept, received, rest_received, own, out):
    own[:, : z.first] = kept[0] + received[0].astype(F32)
    own[:, z.first :] = rest_kept[0] + rest_received[0].astype(F32)
    out[:, : z.first] = (kept[1] + received[1].astype(F32)).astype(LOW)
    out[:, z.first :] = (rest_kept[1] + rest_received[1].astype(F32)).astype(LOW)


def small_kernel(z, vec, their, near, far, own, scratch):
    c, b = lax.axis_index("ctx"), lax.axis_index("fsdp")
    vectors = vec[:16, :] + their[:16, :]
    up = rows_of([vectors[8:9, i * HD : (i + 1) * HD] for i in range(z.ff // HD)])
    pieces = []
    for h in range(z.heads):
        pieces.append(vectors[9:10, h * HD : (h + 1) * HD])
        pieces.append(vectors[9:10, 2 * z.inner + h * HD : 2 * z.inner + (h + 1) * HD])
    qv_rows = rows_of(pieces)
    scratch[...] = jnp.zeros(scratch.shape, F32)
    w = HD // 4
    for i in range(4):
        scratch[i, :8, : z.shard] = vectors[:8, i * z.shard : (i + 1) * z.shard]
        scratch[i, : z.ff // HD, UP_AT : UP_AT + w] = up[:, i * w : (i + 1) * w]
        scratch[i, : 2 * z.heads, QV_AT : QV_AT + w] = qv_rows[:, i * w : (i + 1) * w]
    once = jnp.where(c == 0, 1.0, 0.0)
    near[...] = scratch[b ^ (1 + c)].astype(LOW)
    far[...] = (scratch[b ^ 3] * once).astype(LOW)
    own[...] = scratch[b] * once


def halves_of(z, own, received):
    h = row_half(lax.axis_index("tp"))
    return jnp.where(h == 0, own, received), jnp.where(h == 0, received, own)


def swap_kernel(z, out_own, out_in, in_own, in_in, *refs):
    out_mine, out_theirs = halves_of(z, out_own[: z.padded, :].astype(F32), out_in[: z.padded, :].astype(F32))
    in_mine, in_theirs = halves_of(z, read(in_own), read(in_in))
    theirs = [out_theirs, in_theirs]
    if z.direct:
        proj_own, proj_in, mine, sent, proj = refs
        total = proj_own[...] + read(proj_in)
        proj[...] = total
        theirs.append(total)
    else:
        mine, sent = refs
    mine[0] = out_mine
    mine[1] = in_mine
    sent[...] = rows_of(theirs).astype(LOW)


def last_kernel(z, own, cross, small, near, far, feed_total, feed_sent, qkv_total, qkv_sent):
    value = own[...] + read(cross)
    feed_total[...] = value[:, : 2 * z.ff]
    feed_sent[...] = value[:, : 2 * z.ff].astype(LOW)
    tail = small[...] + read(near) + read(far)
    for out, kind in ((qkv_total, F32), (qkv_sent, LOW)):
        out[: z.chunk, :] = value[:, 2 * z.ff : 2 * z.ff + 3 * z.inner].astype(kind)
        out[z.chunk :, :] = tail.astype(kind)


def qkv_final_kernel(z, own, theirs, qkv, up, qv, *vectors):
    both = by_half(own[: z.chunk, :], theirs[: z.chunk, :].astype(F32))
    for i in range(3):
        qkv[i] = both[:, i * z.inner : (i + 1) * z.inner]
    tail = own[z.chunk :, :] + theirs[z.chunk :, :].astype(F32)
    w = HD // 4
    up[...] = tail[: z.ff // HD, UP_AT : UP_AT + w]
    for h in range(z.heads):
        qv[h] = tail[2 * h : 2 * h + 2, QV_AT : QV_AT + w]
    for i, v in enumerate(vectors):
        v[...] = tail[i : i + 1, : z.shard].reshape(z.shard)


def place_kernel(z, mine, theirs, out, *scratch):
    c = lax.axis_index("ctx")
    target = scratch[0] if scratch else out
    mine, theirs = mine[: z.half], theirs[: z.half]
    target[:, 0, :] = jnp.where(c == 0, mine, theirs)
    target[:, 1, :] = jnp.where(c == 0, theirs, mine)
    if scratch:
        out[...] = target[...].astype(out.dtype)


def final_kernel(z, mine, theirs, *refs):
    if z.direct:
        proj_own, feed_own, feed_in, qkv_own, qkv_in, output, input_grad, proj, up, down, *rest = refs
        other = theirs[2 * z.padded :, :].astype(F32)
        proj[...] = by_half(unfold(z, proj_own[...]), unfold(z, other)).T
        feed_final_kernel(z, feed_own, feed_in, up, down)
        qkv_final_kernel(z, qkv_own, qkv_in, *rest[:-1])
        scratch = rest[-1]
    else:
        output, input_grad, scratch = refs
    place_kernel(z, mine[1], theirs[z.padded : 2 * z.padded, :].astype(F32), input_grad)
    place_kernel(z, mine[0], theirs[: z.padded, :].astype(F32), output, scratch)


def build(nf, nc, nt):
    def local(
        inputs,
        norm1_gain,
        norm1_bias,
        qkv_weight,
        qv_bias,
        proj_weight,
        proj_bias,
        norm2_gain,
        norm2_bias,
        fc1_weight,
        fc1_bias,
        fc2_weight,
        fc2_bias,
        cotangent,
    ):
        z = Sizes(nf, nt, inputs, qv_bias, fc1_weight)
        part = functools.partial
        rows, width, inner, ff, chunk = z.rows, z.width, z.inner, z.ff, z.chunk
        f = lax.axis_index("fsdp")
        tie = lax.optimization_barrier

        def other_core(value):
            return lax.ppermute(value, "ctx", [(0, 1), (1, 0)])

        def to_tp(value, k):
            return lax.ppermute(value, "tp", [(i, i ^ k) for i in range(nt)])

        def to_far(value):
            return lax.ppermute(value, "fsdp", [(i, i ^ 3) for i in range(nf)])

        def neighbours(value, order):
            pairs = [(2 * i + c, 2 * (i ^ order[c]) + c) for i in range(nf) for c in range(2)]
            return lax.ppermute(value, ("fsdp", "ctx"), pairs)

        def to_near(value):
            return neighbours(value, (1, 2))

        def to_cross(value):
            return neighbours(value, (2, 1))

        def proj_near(value):
            pairs = [(c * nt + i, c * nt + (i ^ (1 + 2 * c))) for i in range(nt) for c in range(2)]
            return lax.ppermute(value, ("ctx", "tp"), pairs)

        def pair_of(first, second):
            return call(pair_kernel, [shape((2,) + first.shape, LOW)], [first, second], name="pair")[0]

        qkv3 = qkv_weight.transpose(1, 0, 2)
        down_t = fc2_weight.T
        qv3 = qv_bias.transpose(1, 0, 2)
        x_raw, cot_raw = inputs.transpose(1, 0, 2), cotangent.transpose(1, 0, 2)
        vectors = [norm1_gain, norm1_bias, proj_bias, norm2_gain, norm2_bias, fc2_bias]

        x_recv = other_core(x_raw)
        cot_recv = other_core(cot_raw)
        def frames(x_recv, cot_recv):
            stream, normal_one, inverse_one = call(
                part(frame_kernel, z),
                [shape((rows, width), LOW), shape((rows, width), F32), shape((rows, 128), F32)],
                [x_raw, x_recv],
                name="frame",
            )
            (cot,) = call(part(cot_kernel, z), [shape((rows, width), LOW)], [cot_raw, cot_recv], name="cotangent")
            return stream, normal_one, inverse_one, cot

        if z.direct:
            sources = [qkv3, proj_weight, fc1_bias, qv3] + vectors
            near, far, proj_t, proj_half = call(
                part(pack_kernel, z),
                [
                    shape((z.part + EXTRA, 3 * inner), LOW),
                    shape((chunk + EXTRA, 3 * inner), LOW),
                    shape((z.part + 104, inner), LOW),
                    shape((chunk, inner), LOW),
                ],
                sources,
                [pltpu.VMEM(s.shape, s.dtype) for s in sources] + [pltpu.SemaphoreType.DMA((len(sources),))],
                name="pack",
                mib=56,
                in_specs=[ANY] * len(sources),
            )
            near, far, proj_t, proj_half, x_recv, cot_recv = tie((near, far, proj_t, proj_half, x_recv, cot_recv))
            got = [to_near(near), to_far(far)]
            proj_got = [proj_near(proj_t), to_tp(proj_half, 2)]
            feed_own, feed_rest = call(
                part(stage_kernel, z),
                [shape((z.part, z.early), LOW), shape((z.part, 2 * ff - z.early), LOW)],
                [fc1_weight, down_t],
                [pltpu.VMEM((z.part, ff), LOW)] * 2 + [pltpu.SemaphoreType.DMA((2,))],
                name="stage",
                mib=20,
                in_specs=[ANY] * 2,
            )
            stream, normal_one, inverse_one, cot = frames(x_recv, cot_recv)
            feed_in = to_near(feed_own)
            got, proj_got, feed_rest, stream, normal_one, inverse_one, cot = tie(
                (got, proj_got, feed_rest, stream, normal_one, inverse_one, cot)
            )
            shared = [other_core(g) for g in got]
            qkv_in = [near, got[0], shared[0], got[1], shared[1]]
            (rest_near,) = call(
                part(pack_rest_kernel, z),
                [shape((z.part, z.cols - z.early), LOW)],
                [feed_rest, proj_t, proj_got[0], other_core(proj_got[0]), proj_got[1], other_core(proj_got[1])],
                [pltpu.VMEM((nt, z.part, inner), F32)],
                name="pack_rest",
            )
            near_in = to_near(rest_near)
            far_in = []
            for value in (feed_in, near_in):
                (half,) = call(part(cut_kernel, z), [shape((chunk, value.shape[1]), LOW)], [value], name="cut")
                far_in.append(to_cross(half))
        else:
            stream, normal_one, inverse_one, cot = frames(x_recv, cot_recv)
            whole = lax.all_gather(qkv3, "fsdp", axis=1, tiled=True)
            whole = whole.transpose(1, 0, 2).reshape(4, z.part, 3 * inner)
            vec = jnp.stack(vectors + [vectors[0]] * 2).astype(F32)
            qv_rows = qv3.reshape(2 * z.heads, -1).astype(F32)
            gathered = [lax.all_gather(v, "fsdp", axis=1, tiled=True) for v in (vec, fc1_bias.astype(F32), qv_rows)]
            qkv_in = [whole] + gathered
            proj_t = proj_weight.T
            rest = jnp.concatenate([fc1_weight, down_t, lax.all_gather(proj_t, "tp", axis=1, tiled=True)], 1)
            rest_in = [lax.all_gather(rest, "fsdp", axis=0, tiled=True).reshape(4, z.part, z.cols)]

        small, w_qkv, normed_one, act, attended, soft = call(
            part(attend_kernel, z),
            [
                shape((8, width), F32),
                shape((4, z.part, 3 * inner), LOW),
                shape((rows, width), LOW),
                shape((3, rows, inner), LOW),
                shape((z.dense, 128), LOW),
                shape((z.heads, rows, rows), F32),
            ],
            qkv_in + [normal_one],
            [pltpu.VMEM((4, EXTRA, 3 * inner), F32)] if z.direct else [],
            name="attend",
        )
        att_one = to_tp(attended, 2)
        (att_two,) = call(pair_kernel, [shape((2, z.dense + 16, 128), LOW)], [attended, att_one], name="pair")
        att_two = to_tp(att_two, 1)
        if z.direct:
            att_two, far_in = tie((att_two, far_in))
            rest_in = [feed_own, feed_in, other_core(feed_in), rest_near, near_in, other_core(near_in)]
            rest_in += [far_in[0], other_core(far_in[0]), far_in[1], other_core(far_in[1])]

        (w_rest, att_all, middle, hidden, normed_two, grad_pre, part_middle, part_low, own_att, small_two, *att_sends) = (
            call(
                part(feed_kernel, z),
                [
                    shape((4, z.part, z.cols), LOW),
                    shape((rows, nt * inner), LOW),
                    shape((rows, width), F32),
                    shape((rows, ff), LOW),
                    shape((rows, width), LOW),
                    shape((rows, ff), LOW),
                    shape((rows, width), F32),
                    shape((rows, width), LOW),
                    shape((rows, inner), F32),
                    shape((8, width), F32),
                ]
                + [shape((z.dense, 128), LOW)] * (nt - 1),
                rest_in + [attended, att_one, att_two, stream, cot, small],
                [pltpu.VMEM((nt, rows, inner), F32)],
                name="feed",
            )
        )
        att_got = [to_tp(att_sends[k - 1], k) for k in range(1, nt)]
        all_cols = z.all_cols
        keep, sent = call(
            part(feed_grad_kernel, z),
            [shape((4, chunk, 2 * ff), F32), shape((4 * chunk, 2 * ff), LOW)],
            [normed_two, grad_pre, cot, hidden],
            name="feed_grad",
        )
        keep_proj, sent_proj = call(
            part(proj_grad_kernel, z),
            [shape((4, chunk, nt * inner), F32), shape((4 * chunk, nt * inner), LOW)],
            [part_low, att_all],
            name="proj_grad",
        )
        out_kept, out_sent = call(
            part(down_kernel, z),
            [shape((z.padded, width), F32), shape((z.padded, width), LOW)],
            [hidden, w_rest],
            [pltpu.VMEM((rows, width), F32)],
            name="down",
        )
        out_one = to_tp(out_sent, 1)
        if z.direct:
            proj_in = other_core(sent_proj)
            att_got, out_one, keep, sent, proj_in = tie((att_got, out_one, keep, sent, proj_in))
            proj_own, *sends = call(
                part(proj_one_kernel, z),
                [shape((chunk, nt * inner), F32)] + [shape((chunk, nt * inner), LOW)] * 3,
                [keep_proj, proj_in],
                name="proj_one",
            )
            proj_in = [lax.ppermute(sends[k - 1], "fsdp", [(i, i ^ k) for i in range(nf)]) for k in (3, 1)]
        (out_low,) = call(add_low_kernel, [shape((z.padded, width), LOW)], [out_kept, out_one], name="out_pair")
        out_two = to_tp(out_low, 2)

        grads, qv_sum, in_kept, in_sent = call(
            part(back_kernel, z),
            [
                shape((rows, 3 * inner), LOW),
                shape((1, 3 * inner), F32),
                shape((z.padded + 8, width), F32),
                shape((z.padded + 8, width), LOW),
            ],
            [own_att] + att_got + [act, soft, w_qkv, normal_one, inverse_one, part_middle, small, small_two],
            [pltpu.VMEM((rows, width), F32)],
            name="back",
        )
        in_one = to_tp(in_sent, 1)
        keep_qkv, sent = call(
            part(qkv_grad_kernel, z),
            [shape((4, chunk, 3 * inner), F32), shape((4 * chunk, all_cols), LOW)],
            [sent, normed_one, grads],
            name="qkv_grad",
        )
        if z.direct:
            sent = other_core(sent)
            sent, last_send = tie((sent, sends[1]))
            proj_in.append(lax.ppermute(last_send, "fsdp", [(i, i ^ 2) for i in range(nf)]))
            grad_sent, grad_kept = call(
                part(split_kernel, z),
                [shape((2, chunk, z.first), LOW), shape((2, chunk, z.first), F32)],
                [keep, sent],
                name="split",
            )
            grad_in = to_near(grad_sent)
            in_one, out_two, proj_in, sent = tie((in_one, out_two, proj_in, sent))
            rest_sent, rest_kept = call(
                part(split_rest_kernel, z),
                [shape((2, chunk, all_cols - z.first), LOW), shape((2, chunk, all_cols - z.first), F32)],
                [keep, keep_qkv, sent],
                name="split_rest",
            )
            rest_in = to_near(rest_sent)
        (in_low,) = call(add_low_kernel, [shape((z.padded + 8, width), LOW)], [in_kept, in_one], name="in_pair")
        in_two = to_tp(in_low, 2)
        *proj_kept, out_low = call(
            part(out_total_kernel, z),
            ([shape((2, z.tail, width), F32)] if z.direct else [])
            + [shape((z.padded + (2 * z.tail if z.direct else 0), width), LOW)],
            [out_low, out_two, middle, small] + ([proj_own] + proj_in if z.direct else []),
            [pltpu.VMEM((nt, z.tail, width), F32)] if z.direct else [],
            name="out_total",
        )
        out_in = to_tp(out_low, 1)
        if z.direct:
            in_two, out_in, grad_in, rest_in = tie((in_two, out_in, grad_in, rest_in))
        in_low, vec = call(
            part(sum_rows_kernel, z),
            [shape((z.padded, width), LOW), shape((VEC_ROWS, width), F32)],
            [in_low, in_two, small_two, qv_sum],
            name="sum_rows",
        )
        in_in = to_tp(in_low, 1)
        proj_all = []
        if z.direct:
            grad_own, cross = call(
                part(cross_kernel, z),
                [shape((chunk, all_cols), F32), shape((chunk, all_cols), LOW)],
                [grad_kept, rest_kept, grad_in, rest_in],
                name="cross",
            )
            cross = to_cross(cross)
            proj_own, proj_sent = call(
                part(proj_pair_kernel, z),
                [shape((z.tail, width), F32), shape((z.tail, width), LOW)],
                [proj_kept[0], out_in],
                name="proj_pair",
            )
            proj_two = to_tp(proj_sent, 2)
            near, far, small_own = call(
                part(small_kernel, z),
                [shape((EXTRA, 3 * inner), LOW)] * 2 + [shape((EXTRA, 3 * inner), F32)],
                [vec, other_core(vec)],
                [pltpu.VMEM((4, EXTRA, 3 * inner), F32)],
                name="small",
            )
            near, far = to_near(near), to_far(far)
            in_in, proj_two, cross, near, far = tie((in_in, proj_two, cross, near, far))
            proj_all = [proj_own, proj_two]
            feed_own, feed_sent, qkv_own, qkv_sent = call(
                part(last_kernel, z),
                [
                    shape((chunk, 2 * ff), F32),
                    shape((chunk, 2 * ff), LOW),
                    shape((chunk + EXTRA, 3 * inner), F32),
                    shape((chunk + EXTRA, 3 * inner), LOW),
                ],
                [grad_own, cross, small_own, near, far],
                name="last",
            )
            feed_in, qkv_in = other_core(feed_sent), other_core(qkv_sent)
        mine, theirs, *proj_own = call(
            part(swap_kernel, z),
            [shape((2, z.padded, width), F32), shape((rows + (z.tail if proj_all else 0), width), LOW)]
            + ([shape((z.tail, width), F32)] if proj_all else []),
            [out_low, out_in, in_low, in_in] + proj_all,
            name="swap",
        )
        theirs = other_core(theirs)
        results = [shape((z.half, 2, width), LOW), shape((z.half, 2, width), F32)]
        scratch = [pltpu.VMEM((z.half, 2, width), F32)]
        if z.direct:
            output, input_grad, proj_grad, fc1_grad, fc2_grad, qkv_grad, up_grad, qv_grad, *vec_grads = call(
                part(final_kernel, z),
                results
                + [
                    shape((inner, z.shard), F32),
                    shape((z.shard, ff), F32),
                    shape((z.shard, ff), F32),
                    shape((3, z.shard, inner), F32),
                    shape(fc1_bias.shape, F32),
                    shape(qv3.shape, F32),
                ]
                + [shape((z.shard,), F32)] * 6,
                [mine, theirs, proj_own[0], feed_own, feed_in, qkv_own, qkv_in],
                scratch,
                name="final",
            )
        else:
            output, input_grad = call(part(final_kernel, z), results, [mine, theirs], scratch, name="final")

            def joined(keep, sent):
                return jnp.stack([keep.astype(LOW), sent.reshape(keep.shape)], 1).reshape(width, -1)

            def scatter(whole):
                whole = lax.psum(whole, "ctx")
                return lax.psum_scatter(whole, "fsdp", scatter_dimension=0, tiled=True).astype(F32)

            extra = all_cols - 2 * ff - 3 * inner
            total = scatter(joined(jnp.concatenate([keep, jnp.pad(keep_qkv, ((0, 0), (0, 0), (0, extra)))], 2), sent))
            fc1_grad, fc2_grad = total[:, :ff], total[:, ff : 2 * ff]
            qkv_grad = total[:, 2 * ff : 2 * ff + 3 * inner].reshape(z.shard, 3, inner).transpose(1, 0, 2)
            proj_grad = scatter(joined(keep_proj, sent_proj)).astype(LOW)
            proj_grad = lax.psum_scatter(proj_grad, "tp", scatter_dimension=1, tiled=True).astype(F32).T

            def own_columns(value):
                value = lax.psum(value, ("fsdp", "ctx"))
                return lax.dynamic_slice_in_dim(value, f * (value.shape[1] // nf), value.shape[1] // nf, 1)

            vec_grads = own_columns(vec[:6])
            up_grad = own_columns(vec[8, :ff].reshape(-1, HD))
            qv_grad = vec[9, : 3 * inner].reshape(3, z.heads, HD)[0::2].transpose(1, 0, 2)
            qv_grad = own_columns(qv_grad.reshape(2 * z.heads, HD)).reshape(qv3.shape)
        return (
            output.transpose(1, 0, 2),
            input_grad.transpose(1, 0, 2),
            vec_grads[0],
            vec_grads[1],
            qkv_grad.transpose(1, 0, 2),
            qv_grad.transpose(1, 0, 2),
            proj_grad,
            vec_grads[2],
            vec_grads[3],
            vec_grads[4],
            fc1_grad,
            up_grad,
            fc2_grad.T,
            vec_grads[5],
        )

    return local


def solution(mesh):
    sizes = mesh.shape
    return jax.shard_map(
        build(sizes["fsdp"], sizes["ctx"], sizes["tp"]),
        mesh=mesh,
        in_specs=(
            P("fsdp", "ctx", None),
            P("fsdp"),
            P("fsdp"),
            P("fsdp", None, "tp"),
            P(None, "tp", "fsdp"),
            P("tp", "fsdp"),
            P("fsdp"),
            P("fsdp"),
            P("fsdp"),
            P("fsdp", "tp"),
            P("tp", "fsdp"),
            P("tp", "fsdp"),
            P("fsdp"),
            P("fsdp", "ctx", None),
        ),
        out_specs=(
            P("fsdp", "ctx", None),
            P("fsdp", "ctx", None),
            P("fsdp"),
            P("fsdp"),
            P("fsdp", None, "tp"),
            P(None, "tp", "fsdp"),
            P("tp", "fsdp"),
            P("fsdp"),
            P("fsdp"),
            P("fsdp"),
            P("fsdp", "tp"),
            P("tp", "fsdp"),
            P("tp", "fsdp"),
            P("fsdp"),
        ),
        check_vma=False,
    )
```

```python
import functools

import jax
import jax.numpy as jnp
from jax import lax
from jax.experimental import pallas as pl
from jax.experimental.pallas import tpu as pltpu
from jax.sharding import PartitionSpec as P

HD = 64
EPSILON = 1e-06
QUERY_SCALE = 0.125
F32 = jnp.float32
LOW = jnp.bfloat16
NN = ((1,), (0,))
NT = ((1,), (1,))
TN = ((0,), (0,))
VMEM = pl.BlockSpec(memory_space=pltpu.VMEM)
ANY = pl.BlockSpec(memory_space=pl.ANY)
EXTRA = 16
VEC_ROWS = 16
UP_AT, QV_AT = 256, 384


def dot(left, right, dims):
    return lax.dot_general(left, right, (dims, ((), ())), preferred_element_type=F32)


def shape(dims, kind):
    return jax.ShapeDtypeStruct(tuple(dims), kind)


def call(kernel, outs, args, scratch=(), name=None, mib=20, in_specs=None, alias=None):
    return pl.pallas_call(
        kernel,
        out_shape=tuple(outs),
        in_specs=in_specs or [VMEM] * len(args),
        out_specs=tuple([VMEM] * len(outs)),
        scratch_shapes=list(scratch),
        input_output_aliases=alias or {},
        name=name,
        compiler_params=pltpu.CompilerParams(vmem_limit_bytes=mib << 20),
    )(*args)


def gelu_and_slope(v):
    cdf = 0.5 * (1.0 + lax.erf(v * 0.7071067811865476))
    density = jnp.exp(-0.5 * v * v) * 0.3989422804014327
    return v * cdf, cdf + v * density


def mean(v):
    return jnp.mean(v, axis=-1, keepdims=True)


def total_rows(v):
    return jnp.sum(v, axis=0, keepdims=True)


def normalise(v):
    centred = v - mean(v)
    inverse = lax.rsqrt(mean(centred * centred) + EPSILON)
    return centred * inverse, inverse


def norm_backward(grad_normed, normal, inverse, gain):
    scaled = grad_normed * gain
    return inverse * (scaled - mean(scaled) - normal * mean(scaled * normal))


def row_half(t):
    return t & 1


def lanes(parts):
    return jnp.concatenate(parts, axis=1)


def rows_of(parts):
    return jnp.concatenate(parts, axis=0)


def read(ref):
    return ref[...].astype(F32)


class Sizes:
    def __init__(self, nf, nt, inputs, qv_bias, fc1_weight):
        self.nf, self.nt = nf, nt
        _, self.half, self.width = inputs.shape
        self.shard = self.width // nf
        self.heads = qv_bias.shape[1]
        self.inner = self.heads * HD
        self.ff = fc1_weight.shape[1]
        self.pad = -self.half % 8
        self.padded = self.half + self.pad
        self.rows = 2 * self.padded
        self.part = self.width // 4
        self.chunk = self.part // 2
        self.tail = self.chunk // 4
        self.direct = nf == 4
        self.cols = 2 * self.ff + nt * self.inner
        self.early = 1280 if self.ff == 768 else self.ff
        self.wide = 2 * self.ff
        self.dense = self.rows * self.inner // 128

    def live_rows(self, h):
        return pl.ds(pl.multiple_of(h * self.padded, 8), self.half)

    def half_rows(self, h):
        return pl.ds(pl.multiple_of(h * self.padded, 8), self.padded)

    def half_of(self, c):
        return pl.ds(pl.multiple_of(c * self.chunk, 16), self.chunk)

    def squeeze(self, v):
        return rows_of([v[:, :128], lanes([v[: self.padded, 128:], v[self.padded :, 128:]])])

    def spread(self, v):
        tail = v[self.rows :]
        return lanes([v[: self.rows], rows_of([tail[:, :HD], tail[:, HD:]])])


def fetch(sources, copies, sem):
    moves = [pltpu.make_async_copy(s, d, sem.at[i]) for i, (s, d) in enumerate(zip(sources, copies))]
    for m in moves:
        m.start()
    for m in moves:
        m.wait()


def stage_kernel(z, up, down_t, out, rest, one, two, sem):
    fetch((up, down_t), (one, two), sem)
    first = z.early - z.ff
    out[:, : z.ff] = one[...]
    out[:, z.ff :] = two[:, :first]
    rest[...] = two[:, first:]


def pack_kernel(z, *refs):
    sources, (near, far, proj_t, proj_half) = refs[:10], refs[10:14]
    copies, sem = refs[14:24], refs[24]
    fetch(sources, copies, sem)
    qkv, proj, up_b, qv_b = copies[:4]
    vectors = copies[4:]
    c = lax.axis_index("ctx")
    whole = lanes([read(qkv.at[i]) for i in range(3)])
    near[: z.part, :] = whole.astype(LOW)
    far[: z.chunk, :] = jnp.where(c == 0, whole[: z.chunk], whole[z.chunk :]).astype(LOW)
    row = lax.broadcasted_iota(jnp.int32, (EXTRA, z.shard), 0)
    vec = jnp.zeros((EXTRA, z.shard), F32)
    for i, v in enumerate(vectors):
        vec = jnp.where(row == i, read(v).reshape(1, z.shard), vec)
    biases = read(qv_b)
    biases = rows_of([biases[h, i : i + 1] for h in range(z.heads) for i in range(2)])
    for out, at in ((near, z.part), (far, z.chunk)):
        out[at:, :] = jnp.zeros((EXTRA, 3 * z.inner), LOW)
        out[at:, : z.shard] = vec.astype(LOW)
        out[at : at + up_b.shape[0], UP_AT : UP_AT + up_b.shape[1]] = up_b[...]
        out[at : at + 2 * z.heads, QV_AT : QV_AT + biases.shape[1]] = biases.astype(LOW)
    turned = read(proj).T
    proj_t[...] = rows_of([turned, jnp.zeros((proj_t.shape[0] - z.part, z.inner), F32)]).astype(LOW)
    proj_half[...] = jnp.where(c == 0, turned[: z.chunk], turned[z.chunk :]).astype(LOW)


def cut_kernel(z, value, out):
    out[...] = value[z.half_of(lax.axis_index("ctx")), :]


def pair_kernel(first, second, out):
    rows = first.shape[0]
    out[0, :rows, :] = first[...]
    out[1, :rows, :] = second[...]
    out[:, rows:, :] = jnp.zeros((2, out.shape[1] - rows, out.shape[2]), LOW)


def pack_rest_kernel(z, rest, proj_t, near_in, near_their, far_in, far_their, near, scratch):
    c, t = lax.axis_index("ctx"), lax.axis_index("tp")
    scratch[t] = proj_t[: z.part, :].astype(F32)
    scratch[t ^ (1 + 2 * c)] = near_in[: z.part, :].astype(F32)
    scratch[t ^ (3 - 2 * c)] = near_their[: z.part, :].astype(F32)
    scratch[t ^ 2, z.half_of(c), :] = far_in[: z.chunk, :].astype(F32)
    scratch[t ^ 2, z.half_of(1 - c), :] = far_their[: z.chunk, :].astype(F32)
    near[:, : 2 * z.ff - z.early] = rest[...]
    near[:, 2 * z.ff - z.early :] = lanes([scratch[i] for i in range(4)]).astype(LOW)


def frame_of(z, keep, received, frame):
    zero = jnp.zeros((z.pad, z.width), F32)
    pieces = []
    for ref in (keep, received):
        pieces.append(jnp.where(frame == 0, ref[:, 0, :].astype(F32), ref[:, 1, :].astype(F32)))
        pieces.append(zero)
    return rows_of(pieces)


def frame_kernel(z, keep, received, stream, normal, inverse, normal_their):
    c = lax.axis_index("ctx")
    values = frame_of(z, keep, received, c)
    stream[...] = values.astype(LOW)
    n, i = normalise(values)
    normal[...] = n
    inverse[...] = jnp.broadcast_to(i, inverse.shape)
    normal_their[...] = normalise(frame_of(z, received, keep, 1 - c))[0]


def cot_kernel(z, keep, received, out):
    c = lax.axis_index("ctx")
    out[0] = frame_of(z, keep, received, c).astype(LOW)
    out[1] = frame_of(z, received, keep, 1 - c).astype(LOW)


def attend_kernel(z, *refs):
    refs = list(refs)
    if z.direct:
        own, near, near_their, far, far_their = refs[:5]
        refs = refs[5:]
    else:
        whole, vec_in, up_in, qv_in = refs[:4]
        refs = refs[4:]
    normal, small, w_out, normed_out, act, attended, soft_out = refs[:7]
    if z.direct:
        c, b = lax.axis_index("ctx"), lax.axis_index("fsdp")
        gather = refs[7]
        for ref, at in ((own, b), (near, b ^ (1 + c)), (near_their, b ^ (2 - c))):
            w_out[at] = ref[: z.part, :]
            gather[at] = ref[z.part :, :].astype(F32)
        w_out[b ^ 3, z.half_of(c), :] = far[: z.chunk, :]
        w_out[b ^ 3, z.half_of(1 - c), :] = far_their[: z.chunk, :]
        gather[b ^ 3] = far[z.chunk :, :].astype(F32)
        blocks = [gather[i] for i in range(4)]
        w = HD // 4
        vec = lanes([g[:8, : z.shard] for g in blocks])
        up = lanes([g[: z.ff // HD, UP_AT : UP_AT + w] for g in blocks])
        qv = lanes([g[: 2 * z.heads, QV_AT : QV_AT + w] for g in blocks])
    else:
        w_out[...] = whole[...]
        vec, up, qv = vec_in[...], up_in[...], qv_in[...]
    up_row = lanes([up[i : i + 1] for i in range(z.ff // HD)])
    query_b = lanes([qv[2 * h : 2 * h + 1] for h in range(z.heads)])
    value_b = lanes([qv[2 * h + 1 : 2 * h + 2] for h in range(z.heads)])
    small[...] = vec
    small[6:7, : z.ff] = up_row
    normed = (normal[...] * vec[0:1] + vec[1:2]).astype(LOW)
    normed_out[...] = normed
    projected = dot(normed, w_out[...].reshape(z.width, 3 * z.inner), NN)
    n = z.inner
    query = ((projected[:, :n] + query_b) * QUERY_SCALE).astype(LOW)
    key = projected[:, n : 2 * n].astype(LOW)
    value = (projected[:, 2 * n :] + value_b).astype(LOW)
    act[0] = query
    act[1] = key
    act[2] = value
    place = lax.broadcasted_iota(jnp.int32, (z.rows, z.rows), 1)
    valid = (place < z.half) | ((place >= z.padded) & (place < z.padded + z.half))
    done = []
    for h in range(z.heads):
        cut = slice(h * HD, (h + 1) * HD)
        scores = jnp.where(valid, dot(query[:, cut], key[:, cut], NT), -1e30)
        exponent = jnp.exp(scores - jnp.max(scores, axis=-1, keepdims=True))
        soft = exponent * (1.0 / jnp.sum(exponent, axis=-1, keepdims=True))
        soft_out[h] = soft
        done.append(dot(soft.astype(LOW), value[:, cut], NN))
    attended[...] = z.squeeze(lanes(done)).astype(LOW)


def feed_kernel(z, *refs):
    refs = list(refs)
    if z.direct:
        feed, feed_in, feed_their, near, near_in, near_their, far, far_their, last_far, last_far_their = refs[:10]
        refs = refs[10:]
    else:
        whole = refs[0]
        refs = refs[1:]
    att = refs[:3]
    stream, cot, small = refs[3:6]
    w_out, middle_out, acts, part_out, own_att, small_out = refs[6:12]
    sends, heads = refs[12:-1], refs[-1]
    t = lax.axis_index("tp")
    if z.direct:
        c, b = lax.axis_index("ctx"), lax.axis_index("fsdp")
        mine, other = z.half_of(c), z.half_of(1 - c)
        first, last = pl.ds(0, z.early), pl.ds(z.early, z.cols - z.early)
        for at, one, two in ((b, feed, near), (b ^ (1 + c), feed_in, near_in), (b ^ (2 - c), feed_their, near_their)):
            w_out[at, :, first] = one[...]
            w_out[at, :, last] = two[...]
        w_out[b ^ 3, mine, first] = far[...]
        w_out[b ^ 3, other, first] = far_their[...]
        w_out[b ^ 3, mine, last] = last_far[...]
        w_out[b ^ 3, other, last] = last_far_their[...]
    else:
        w_out[...] = whole[...]
    n = z.inner
    w_up = w_out[:, :, : z.ff].reshape(z.width, z.ff)
    w_down_t = w_out[:, :, z.ff : 2 * z.ff].reshape(z.width, z.ff)
    w_proj_t = w_out[:, :, 2 * z.ff :].reshape(z.width, z.nt * n)
    grad_out_low = cot[0]
    grad_out = grad_out_low.astype(F32)
    heads[t] = z.spread(read(att[0]))
    heads[t ^ 2] = z.spread(read(att[1]))
    heads[t ^ 1] = z.spread(att[2][0, : z.dense, :].astype(F32))
    heads[t ^ 3] = z.spread(att[2][1, : z.dense, :].astype(F32))
    attended = lanes([heads[i] for i in range(z.nt)]).astype(LOW)
    acts[4] = attended
    branch = dot(attended, w_proj_t, NT)
    middle = stream[...].astype(F32) + branch + small[2:3]
    middle_out[...] = middle
    normal, inverse = normalise(middle)
    gain = small[3:4]
    normed = (normal * gain + small[4:5]).astype(LOW)
    acts[0] = normed
    hidden, slope = gelu_and_slope(dot(normed, w_up, NN) + small[6:7, : z.ff])
    acts[1] = hidden.astype(LOW)
    grad_pre = (dot(grad_out_low, w_down_t, NN) * slope).astype(LOW)
    acts[2] = grad_pre
    grad_normed = dot(grad_pre, w_up, NT)
    part = grad_out * (1.0 / z.nt) + norm_backward(grad_normed, normal, inverse, gain)
    part_out[...] = part
    low = part.astype(LOW)
    acts[3] = low
    grad_att = dot(low, w_proj_t, NN)
    for i in range(z.nt):
        heads[i] = grad_att[:, i * n : (i + 1) * n]
    own_att[...] = heads[t]
    for k in range(1, z.nt):
        sends[k - 1][...] = z.squeeze(heads[t ^ k]).astype(LOW)
    small_out[...] = jnp.zeros(small_out.shape, F32)
    small_out[2:3] = total_rows(part)
    small_out[3:4] = total_rows(grad_normed * normal)
    small_out[4:5] = total_rows(grad_normed)
    small_out[5:6] = total_rows(grad_out) * (1.0 / z.nt)
    small_out[6:7, : z.ff] = total_rows(grad_pre.astype(F32))


def down_kernel(z, acts, w, kept, sent, scratch):
    h = row_half(lax.axis_index("tp"))
    w_down_t = w[:, :, z.ff : 2 * z.ff].reshape(z.width, z.ff)
    scratch[...] = dot(acts[1], w_down_t, NT)
    kept[...] = scratch[z.live_rows(h), :]
    sent[...] = scratch[z.live_rows(1 - h), :].astype(LOW)


def add_low_kernel(kept, received, out):
    rows = kept.shape[0]
    out[:rows, :] = (kept[...] + read(received)).astype(LOW)
    if out.shape[0] > rows:
        out[rows:, :] = jnp.zeros((out.shape[0] - rows, out.shape[1]), LOW)


def store_own(z, value, at, keep):
    cols = pl.ds(at, value.shape[1])
    c, b = (lax.axis_index("ctx"), lax.axis_index("fsdp")) if z.direct else (0, 0)
    for j in range(4):
        whole = value[j * z.part : (j + 1) * z.part]
        if z.direct:
            keep[j ^ b, :, cols] = jnp.where(c == 0, whole[: z.chunk], whole[z.chunk :])
        else:
            keep[j, :, cols] = whole


def both_frames(left, right, left_their, right_their):
    return dot(left, right, TN) + dot(left_their, right_their, TN)


def feed_grad_kernel(z, acts, theirs, cot, keep):
    store_own(z, both_frames(acts[0], acts[2], theirs[0], theirs[2]), 0, keep)
    store_own(z, both_frames(cot[0], acts[1], cot[1], theirs[1]), z.ff, keep)


def proj_grad_kernel(z, acts, theirs, own, *refs):
    value = both_frames(acts[3], acts[4], theirs[3], theirs[4])
    if not z.direct:
        store_own(z, value, 0, own)
        return
    sends, keep = refs[:3], refs[3]
    store_own(z, value, 0, keep)
    own[...] = keep[0]
    for k in range(1, 4):
        sends[k - 1][...] = keep[k].astype(LOW)


def qkv_grad_kernel(z, normed, grads, normal_their, grads_their, small, keep):
    normed_their = (normal_their[...] * small[0:1] + small[1:2]).astype(LOW)
    store_own(z, both_frames(normed[...], grads[...], normed_their, grads_their[...]), 0, keep)


def split_kernel(keep, out, kept):
    c = lax.axis_index("ctx")
    n = keep.shape[2]
    for target, at, kind in ((out, (1 + c, 3), LOW), (kept, (0, 2 - c), F32)):
        for i in range(2):
            target[i, :, :n] = keep[at[i]].astype(kind)
            if target.shape[2] > n:
                target[i, :, n:] = jnp.zeros((target.shape[1], target.shape[2] - n), kind)


def by_half(mine, other):
    c = lax.axis_index("ctx")
    return rows_of([jnp.where(c == 0, mine, other), jnp.where(c == 0, other, mine)])


def feed_final_kernel(z, own, theirs, up, down):
    total = by_half(own[...], read(theirs))
    up[...] = total[:, : z.ff]
    down[...] = total[:, z.ff :]


def unfold(z, v):
    return rows_of([v[:, i * z.inner : (i + 1) * z.inner] for i in range(4)])


def fold(v):
    n = v.shape[0] // 4
    return lanes([v[i * n : (i + 1) * n] for i in range(4)])


def back_kernel(z, *refs):
    own_att, got = refs[0], refs[1 : z.nt]
    act, soft, w, normal, inverse, part, small, small_in = refs[z.nt : z.nt + 8]
    grads_out, qv_out, kept, sent, scratch = refs[z.nt + 8 :]
    t = lax.axis_index("tp")
    grad_att = (own_att[...] + z.spread(sum(read(g) for g in got))).astype(LOW)
    parts = [[], [], []]
    query, key, value = act[0], act[1], act[2]
    for h in range(z.heads):
        cut = slice(h * HD, (h + 1) * HD)
        ga = grad_att[:, cut]
        p = soft[h]
        grad_soft = dot(ga, value[:, cut], NT)
        delta = jnp.sum(p * grad_soft, axis=-1, keepdims=True)
        grad_scores = (p * (grad_soft - delta)).astype(LOW)
        parts[0].append((dot(grad_scores, key[:, cut], NN).astype(LOW).astype(F32) * QUERY_SCALE).astype(LOW))
        parts[1].append(dot(grad_scores, query[:, cut], TN).astype(LOW))
        parts[2].append(dot(p.astype(LOW), ga, TN).astype(LOW))
    grads = lanes(parts[0] + parts[1] + parts[2])
    grads_out[...] = grads
    n = z.inner
    qv_out[...] = total_rows(grads.astype(F32))
    grad_normed = dot(grads, w[...].reshape(z.width, 3 * n), NT)
    scratch[...] = part[...] + norm_backward(grad_normed, normal[...], inverse[:, :1], small[0:1])
    row = lax.broadcasted_iota(jnp.int32, (8, z.width), 0)
    vec = small_in[...]
    vec = jnp.where(row == 0, total_rows(grad_normed * normal[...]), vec)
    vec = jnp.where(row == 1, total_rows(grad_normed), vec)
    h = row_half(t)
    for at in (z.half, z.padded + z.half):
        scratch[at : at + 6, :] = vec[:6]
    kept[...] = scratch[z.half_rows(h), :]
    sent[...] = scratch[z.half_rows(1 - h), :].astype(LOW)


def out_total_kernel(z, own, received, middle, small, out):
    rows = z.live_rows(row_half(lax.axis_index("tp")))
    out[...] = (middle[rows, :] + read(own) + read(received) + small[5:6]).astype(LOW)


def in_pair_kernel(z, kept, received, own, *refs):
    parts, (out, proj_kept, scratch) = refs[:3], refs[3:]
    out[: z.padded, :] = (kept[...] + read(received)).astype(LOW)
    t = lax.axis_index("tp")
    proj = own[...] + sum(read(p) for p in parts)
    for i in range(z.nt):
        scratch[i] = fold(proj[:, i * z.inner : (i + 1) * z.inner])
    proj_kept[0] = scratch[t]
    proj_kept[1] = scratch[t ^ 1]
    out[z.padded :, :] = rows_of([scratch[t ^ 2], scratch[t ^ 3]]).astype(LOW)


def sum_rows_kernel(z, own, received, small, qv, *refs):
    if z.direct:
        proj_kept, out, vec, proj_own = refs
        arrived = received[z.padded :, :].astype(F32)
        proj_own[...] = proj_kept[0] + arrived[: z.tail]
        out[z.padded :, :] = (proj_kept[1] + arrived[z.tail :]).astype(LOW)
    else:
        out, vec = refs
    total = own[: z.padded, :].astype(F32) + received[: z.padded, :].astype(F32)
    out[: z.padded, :] = total.astype(LOW)
    vec[...] = jnp.zeros(vec.shape, F32)
    vec[:6, :] = total[z.half : z.half + 6]
    vec[8:9, : z.ff] = small[6:7, : z.ff]
    vec[9:10, : 3 * z.inner] = qv[...]


def cross_kernel(kept, received, own, out):
    n = kept.shape[2]
    own[...] = kept[0] + received[0, :, :n].astype(F32)
    out[...] = (kept[1] + received[1, :, :n].astype(F32)).astype(LOW)


def cross_qkv_kernel(z, kept, received, small, own, out):
    own[...] = kept[0] + received[0].astype(F32)
    out[: z.chunk, :] = (kept[1] + received[1].astype(F32)).astype(LOW)
    out[z.chunk :, :] = small[...].astype(LOW)


def small_kernel(z, vec, near, cross, far, own, scratch):
    c, b = lax.axis_index("ctx"), lax.axis_index("fsdp")
    vectors = vec[...]
    up = rows_of([vectors[8:9, i * HD : (i + 1) * HD] for i in range(z.ff // HD)])
    pieces = []
    for h in range(z.heads):
        pieces.append(vectors[9:10, h * HD : (h + 1) * HD])
        pieces.append(vectors[9:10, 2 * z.inner + h * HD : 2 * z.inner + (h + 1) * HD])
    qv_rows = rows_of(pieces)
    scratch[...] = jnp.zeros(scratch.shape, F32)
    w = HD // 4
    for i in range(4):
        scratch[i, :8, : z.shard] = vectors[:8, i * z.shard : (i + 1) * z.shard]
        scratch[i, : z.ff // HD, UP_AT : UP_AT + w] = up[:, i * w : (i + 1) * w]
        scratch[i, : 2 * z.heads, QV_AT : QV_AT + w] = qv_rows[:, i * w : (i + 1) * w]
    near[...] = scratch[b ^ (1 + c)].astype(LOW)
    cross[...] = scratch[b ^ (2 - c)]
    far[...] = scratch[b ^ 3].astype(LOW)
    own[...] = scratch[b]


def halves_of(z, own, received):
    h = row_half(lax.axis_index("tp"))
    return jnp.where(h == 0, own, received), jnp.where(h == 0, received, own)


def swap_kernel(z, out_own, out_in, in_own, in_in, *refs):
    n = z.padded
    pad = jnp.zeros((z.pad, z.width), F32)
    out_mine, out_theirs = halves_of(z, read(out_own), read(out_in))
    in_mine, in_theirs = halves_of(z, in_own[:n, :].astype(F32), in_in[:n, :].astype(F32))
    theirs = [out_theirs, pad, in_theirs]
    if z.direct:
        proj_own, mine, sent, proj = refs
        total = proj_own[...] + in_in[n:, :].astype(F32)
        proj[...] = total
        theirs.append(total)
    else:
        mine, sent = refs
    mine[0] = rows_of([out_mine, pad])
    mine[1] = in_mine
    sent[...] = rows_of(theirs).astype(LOW)


def last_kernel(z, feed, feed_in, qkv, qkv_in, small, near, far, feed_total, feed_sent, qkv_total, qkv_sent):
    value = feed[...] + read(feed_in)
    feed_total[...] = value
    feed_sent[...] = value.astype(LOW)
    value = qkv[...] + qkv_in[: z.chunk, :].astype(F32)
    tail = small[...] + read(near) + read(far) + qkv_in[z.chunk :, :].astype(F32)
    for out, kind in ((qkv_total, F32), (qkv_sent, LOW)):
        out[: z.chunk, :] = value.astype(kind)
        out[z.chunk :, :] = tail.astype(kind)


def qkv_final_kernel(z, own, theirs, qkv, up, qv, *vectors):
    both = by_half(own[: z.chunk, :], theirs[: z.chunk, :].astype(F32))
    for i in range(3):
        qkv[i] = both[:, i * z.inner : (i + 1) * z.inner]
    tail = own[z.chunk :, :] + theirs[z.chunk :, :].astype(F32)
    w = HD // 4
    up[...] = tail[: z.ff // HD, UP_AT : UP_AT + w]
    for h in range(z.heads):
        qv[h] = tail[2 * h : 2 * h + 2, QV_AT : QV_AT + w]
    for i, v in enumerate(vectors):
        v[...] = tail[i : i + 1, : z.shard].reshape(z.shard)


def place_kernel(z, mine, theirs, out, *scratch):
    c = lax.axis_index("ctx")
    target = scratch[0] if scratch else out
    mine, theirs = mine[: z.half], theirs[: z.half]
    target[:, 0, :] = jnp.where(c == 0, mine, theirs)
    target[:, 1, :] = jnp.where(c == 0, theirs, mine)
    if scratch:
        out[...] = target[...].astype(out.dtype)


def final_kernel(z, mine, theirs, *refs):
    if z.direct:
        proj_own, feed_own, feed_in, qkv_own, qkv_in, output, input_grad, proj, up, down, *rest = refs
        other = theirs[2 * z.padded :, :].astype(F32)
        proj[...] = by_half(unfold(z, proj_own[...]), unfold(z, other)).T
        feed_final_kernel(z, feed_own, feed_in, up, down)
        qkv_final_kernel(z, qkv_own, qkv_in, *rest[:-1])
        scratch = rest[-1]
    else:
        output, input_grad, scratch = refs
    place_kernel(z, mine[1], theirs[z.padded : 2 * z.padded, :].astype(F32), input_grad)
    place_kernel(z, mine[0], theirs[: z.padded, :].astype(F32), output, scratch)


def build(nf, nc, nt):
    def local(
        inputs,
        norm1_gain,
        norm1_bias,
        qkv_weight,
        qv_bias,
        proj_weight,
        proj_bias,
        norm2_gain,
        norm2_bias,
        fc1_weight,
        fc1_bias,
        fc2_weight,
        fc2_bias,
        cotangent,
    ):
        z = Sizes(nf, nt, inputs, qv_bias, fc1_weight)
        part = functools.partial
        rows, width, inner, ff, chunk = z.rows, z.width, z.inner, z.ff, z.chunk
        f = lax.axis_index("fsdp")
        tie = lax.optimization_barrier

        def other_core(value):
            return lax.ppermute(value, "ctx", [(0, 1), (1, 0)])

        def to_tp(value, k):
            return lax.ppermute(value, "tp", [(i, i ^ k) for i in range(nt)])

        def to_far(value):
            return lax.ppermute(value, "fsdp", [(i, i ^ 3) for i in range(nf)])

        def neighbours(value, order):
            pairs = [(2 * i + c, 2 * (i ^ order[c]) + c) for i in range(nf) for c in range(2)]
            return lax.ppermute(value, ("fsdp", "ctx"), pairs)

        def to_near(value):
            return neighbours(value, (1, 2))

        def to_cross(value):
            return neighbours(value, (2, 1))

        def proj_near(value):
            pairs = [(c * nt + i, c * nt + (i ^ (1 + 2 * c))) for i in range(nt) for c in range(2)]
            return lax.ppermute(value, ("ctx", "tp"), pairs)

        def pair_of(first, second):
            return call(pair_kernel, [shape((2,) + first.shape, LOW)], [first, second], name="pair")[0]

        qkv3 = qkv_weight.transpose(1, 0, 2)
        down_t = fc2_weight.T
        qv3 = qv_bias.transpose(1, 0, 2)
        x_raw, cot_raw = inputs.transpose(1, 0, 2), cotangent.transpose(1, 0, 2)
        vectors = [norm1_gain, norm1_bias, proj_bias, norm2_gain, norm2_bias, fc2_bias]

        x_recv = other_core(x_raw)
        cot_recv = other_core(cot_raw)
        def frames(x_recv, cot_recv):
            stream, normal_one, inverse_one, normal_their = call(
                part(frame_kernel, z),
                [shape((rows, width), LOW), shape((rows, width), F32), shape((rows, 128), F32), shape((rows, width), F32)],
                [x_raw, x_recv],
                name="frame",
            )
            (cot,) = call(part(cot_kernel, z), [shape((2, rows, width), LOW)], [cot_raw, cot_recv], name="cotangent")
            return stream, normal_one, inverse_one, normal_their, cot

        if z.direct:
            sources = [qkv3, proj_weight, fc1_bias, qv3] + vectors
            near, far, proj_t, proj_half = call(
                part(pack_kernel, z),
                [
                    shape((z.part + EXTRA, 3 * inner), LOW),
                    shape((chunk + EXTRA, 3 * inner), LOW),
                    shape((z.part + 104, inner), LOW),
                    shape((chunk, inner), LOW),
                ],
                sources,
                [pltpu.VMEM(s.shape, s.dtype) for s in sources] + [pltpu.SemaphoreType.DMA((len(sources),))],
                name="pack",
                mib=56,
                in_specs=[ANY] * len(sources),
            )
            near, far, proj_t, proj_half, x_recv, cot_recv = tie((near, far, proj_t, proj_half, x_recv, cot_recv))
            got = [to_near(near), to_far(far)]
            proj_got = [proj_near(proj_t), to_tp(proj_half, 2)]
            feed_own, feed_rest = call(
                part(stage_kernel, z),
                [shape((z.part, z.early), LOW), shape((z.part, 2 * ff - z.early), LOW)],
                [fc1_weight, down_t],
                [pltpu.VMEM((z.part, ff), LOW)] * 2 + [pltpu.SemaphoreType.DMA((2,))],
                name="stage",
                mib=20,
                in_specs=[ANY] * 2,
            )
            stream, normal_one, inverse_one, normal_their, cot = frames(x_recv, cot_recv)
            feed_in = to_near(feed_own)
            got, proj_got, feed_rest, stream, normal_one, inverse_one, normal_their, cot = tie(
                (got, proj_got, feed_rest, stream, normal_one, inverse_one, normal_their, cot)
            )
            shared = [other_core(g) for g in got]
            qkv_in = [near, got[0], shared[0], got[1], shared[1]]
            (rest_near,) = call(
                part(pack_rest_kernel, z),
                [shape((z.part, z.cols - z.early), LOW)],
                [feed_rest, proj_t, proj_got[0], other_core(proj_got[0]), proj_got[1], other_core(proj_got[1])],
                [pltpu.VMEM((nt, z.part, inner), F32)],
                name="pack_rest",
            )
            near_in = to_near(rest_near)
            far_in = []
            for value in (feed_in, near_in):
                (half,) = call(part(cut_kernel, z), [shape((chunk, value.shape[1]), LOW)], [value], name="cut")
                far_in.append(to_cross(half))
        else:
            stream, normal_one, inverse_one, normal_their, cot = frames(x_recv, cot_recv)
            whole = lax.all_gather(qkv3, "fsdp", axis=1, tiled=True)
            whole = whole.transpose(1, 0, 2).reshape(4, z.part, 3 * inner)
            vec = jnp.stack(vectors + [vectors[0]] * 2).astype(F32)
            qv_rows = qv3.reshape(2 * z.heads, -1).astype(F32)
            gathered = [lax.all_gather(v, "fsdp", axis=1, tiled=True) for v in (vec, fc1_bias.astype(F32), qv_rows)]
            qkv_in = [whole] + gathered
            proj_t = proj_weight.T
            rest = jnp.concatenate([fc1_weight, down_t, lax.all_gather(proj_t, "tp", axis=1, tiled=True)], 1)
            rest_in = [lax.all_gather(rest, "fsdp", axis=0, tiled=True).reshape(4, z.part, z.cols)]

        small, w_qkv, normed_one, act, attended, soft = call(
            part(attend_kernel, z),
            [
                shape((8, width), F32),
                shape((4, z.part, 3 * inner), LOW),
                shape((rows, width), LOW),
                shape((3, rows, inner), LOW),
                shape((z.dense, 128), LOW),
                shape((z.heads, rows, rows), F32),
            ],
            qkv_in + [normal_one],
            [pltpu.VMEM((4, EXTRA, 3 * inner), F32)] if z.direct else [],
            name="attend",
        )
        att_one = to_tp(attended, 2)
        (att_two,) = call(pair_kernel, [shape((2, z.dense + 16, 128), LOW)], [attended, att_one], name="pair")
        att_two = to_tp(att_two, 1)
        if z.direct:
            att_two, far_in = tie((att_two, far_in))
            rest_in = [feed_own, feed_in, other_core(feed_in), rest_near, near_in, other_core(near_in)]
            rest_in += [far_in[0], other_core(far_in[0]), far_in[1], other_core(far_in[1])]

        (w_rest, middle, acts, part_middle, own_att, small_two, *att_sends) = (
            call(
                part(feed_kernel, z),
                [
                    shape((4, z.part, z.cols), LOW),
                    shape((rows, width), F32),
                    shape((5, rows, width), LOW),
                    shape((rows, width), F32),
                    shape((rows, inner), F32),
                    shape((8, width), F32),
                ]
                + [shape((z.dense, 128), LOW)] * (nt - 1),
                rest_in + [attended, att_one, att_two, stream, cot, small],
                [pltpu.VMEM((nt, rows, inner), F32)],
                name="feed",
            )
        )
        att_got = [to_tp(att_sends[k - 1], k) for k in (2, 3, 1)]
        acts_their = other_core(acts)
        kept_rows = chunk if z.direct else z.part
        (keep,) = call(
            part(feed_grad_kernel, z),
            [shape((4, kept_rows, 2 * ff), F32)],
            [acts, acts_their, cot],
            name="feed_grad",
        )
        proj_own, *sends = call(
            part(proj_grad_kernel, z),
            [shape((chunk, nt * inner), F32)] + [shape((chunk, nt * inner), LOW)] * 3
            if z.direct
            else [shape((4, z.part, nt * inner), F32)],
            [acts, acts_their],
            [pltpu.VMEM((4, chunk, nt * inner), F32)] if z.direct else [],
            name="proj_grad",
        )
        proj_full = proj_own
        out_kept, out_sent = call(
            part(down_kernel, z),
            [shape((z.half, width), F32), shape((z.half, width), LOW)],
            [acts, w_rest],
            [pltpu.VMEM((rows, width), F32)],
            name="down",
        )
        out_one = to_tp(out_sent, 1)
        if z.direct:
            grad_sent, grad_kept = call(
                split_kernel,
                [shape((2, chunk, z.wide), LOW), shape((2, chunk, 2 * ff), F32)],
                [keep],
                name="split",
            )
            grad_in = to_near(grad_sent)
            att_got, out_one, grad_kept, proj_own, sends = tie((att_got, out_one, grad_kept, proj_own, sends))
            proj_in = [lax.ppermute(sends[k - 1], "fsdp", [(i, i ^ k) for i in range(nf)]) for k in (3, 1)]
        (out_low,) = call(add_low_kernel, [shape((z.half, width), LOW)], [out_kept, out_one], name="out_pair")
        out_two = to_tp(out_low, 2)

        grads, qv_sum, in_kept, in_sent = call(
            part(back_kernel, z),
            [
                shape((rows, 3 * inner), LOW),
                shape((1, 3 * inner), F32),
                shape((z.padded, width), F32),
                shape((z.padded, width), LOW),
            ],
            [own_att] + att_got + [act, soft, w_qkv, normal_one, inverse_one, part_middle, small, small_two],
            [pltpu.VMEM((rows, width), F32)],
            name="back",
        )
        in_one = to_tp(in_sent, 1)
        grads_their = other_core(grads)
        if z.direct:
            grads_their, last_send = tie((grads_their, sends[1]))
            proj_in.append(lax.ppermute(last_send, "fsdp", [(i, i ^ 2) for i in range(nf)]))
        (keep_qkv,) = call(
            part(qkv_grad_kernel, z),
            [shape((4, kept_rows, 3 * inner), F32)],
            [normed_one, grads, normal_their, grads_their, small],
            name="qkv_grad",
        )
        extra = z.tail if z.direct else 0
        if z.direct:
            in_one, out_two, proj_in, keep_qkv = tie((in_one, out_two, proj_in, keep_qkv))
            in_low, proj_kept = call(
                part(in_pair_kernel, z),
                [shape((z.padded + 2 * extra, width), LOW), shape((2, extra, width), F32)],
                [in_kept, in_one, proj_own] + proj_in,
                [pltpu.VMEM((nt, extra, width), F32)],
                name="in_pair",
            )
            qkv_sent, qkv_kept = call(
                split_kernel,
                [shape((2, chunk, 3 * inner), LOW), shape((2, chunk, 3 * inner), F32)],
                [keep_qkv],
                name="split_qkv",
            )
            qkv_in = to_near(qkv_sent)
        else:
            (in_low,) = call(add_low_kernel, [shape((z.padded, width), LOW)], [in_kept, in_one], name="in_pair")
        in_two = to_tp(in_low, 2)
        (out_low,) = call(
            part(out_total_kernel, z), [shape((z.half, width), LOW)], [out_low, out_two, middle, small], name="out_total"
        )
        out_in = to_tp(out_low, 1)
        if z.direct:
            grad_own, cross = call(
                cross_kernel,
                [shape((chunk, 2 * ff), F32), shape((chunk, 2 * ff), LOW)],
                [grad_kept, grad_in],
                name="cross",
            )
            cross = to_cross(cross)
            in_two, out_in, qkv_in = tie((in_two, out_in, qkv_in))
        in_low, vec, *proj_own = call(
            part(sum_rows_kernel, z),
            [shape((z.padded + extra, width), LOW), shape((VEC_ROWS, width), F32)]
            + ([shape((extra, width), F32)] if extra else []),
            [in_low, in_two, small_two, qv_sum] + ([proj_kept] if extra else []),
            name="sum_rows",
        )
        in_in = to_tp(in_low, 1)
        proj_all = []
        if z.direct:
            near, side, far, small_own = call(
                part(small_kernel, z),
                [shape((EXTRA, 3 * inner), LOW), shape((EXTRA, 3 * inner), F32)] * 2,
                [vec],
                [pltpu.VMEM((4, EXTRA, 3 * inner), F32)],
                name="small",
            )
            qkv_own, qkv_sent = call(
                part(cross_qkv_kernel, z),
                [shape((chunk, 3 * inner), F32), shape((chunk + EXTRA, 3 * inner), LOW)],
                [qkv_kept, qkv_in, side],
                name="cross_qkv",
            )
            qkv_in = to_cross(qkv_sent)
            near, far = to_near(near), to_far(far)
            in_in, cross, qkv_in, near, far = tie((in_in, cross, qkv_in, near, far))
            proj_all = proj_own
            feed_own, feed_sent, qkv_own, qkv_sent = call(
                part(last_kernel, z),
                [
                    shape((chunk, 2 * ff), F32),
                    shape((chunk, 2 * ff), LOW),
                    shape((chunk + EXTRA, 3 * inner), F32),
                    shape((chunk + EXTRA, 3 * inner), LOW),
                ],
                [grad_own, cross, qkv_own, qkv_in, small_own, near, far],
                name="last",
            )
            feed_in, qkv_in = other_core(feed_sent), other_core(qkv_sent)
        mine, theirs, *proj_own = call(
            part(swap_kernel, z),
            [shape((2, z.padded, width), F32), shape((rows + (z.tail if proj_all else 0), width), LOW)]
            + ([shape((z.tail, width), F32)] if proj_all else []),
            [out_low, out_in, in_low, in_in] + proj_all,
            name="swap",
        )
        theirs = other_core(theirs)
        results = [shape((z.half, 2, width), LOW), shape((z.half, 2, width), F32)]
        scratch = [pltpu.VMEM((z.half, 2, width), F32)]
        if z.direct:
            output, input_grad, proj_grad, fc1_grad, fc2_grad, qkv_grad, up_grad, qv_grad, *vec_grads = call(
                part(final_kernel, z),
                results
                + [
                    shape((inner, z.shard), F32),
                    shape((z.shard, ff), F32),
                    shape((z.shard, ff), F32),
                    shape((3, z.shard, inner), F32),
                    shape(fc1_bias.shape, F32),
                    shape(qv3.shape, F32),
                ]
                + [shape((z.shard,), F32)] * 6,
                [mine, theirs, proj_own[0], feed_own, feed_in, qkv_own, qkv_in],
                scratch,
                name="final",
            )
        else:
            output, input_grad = call(part(final_kernel, z), results, [mine, theirs], scratch, name="final")

            def scatter(value):
                value = value.reshape(width, -1).astype(LOW)
                return lax.psum_scatter(value, "fsdp", scatter_dimension=0, tiled=True).astype(F32)

            total = scatter(keep)
            fc1_grad, fc2_grad = total[:, :ff], total[:, ff:]
            qkv_grad = scatter(keep_qkv).reshape(z.shard, 3, inner).transpose(1, 0, 2)
            proj_grad = scatter(proj_full).astype(LOW)
            proj_grad = lax.psum_scatter(proj_grad, "tp", scatter_dimension=1, tiled=True).astype(F32).T

            def own_columns(value):
                value = lax.psum(value, ("fsdp", "ctx"))
                return lax.dynamic_slice_in_dim(value, f * (value.shape[1] // nf), value.shape[1] // nf, 1)

            vec_grads = own_columns(vec[:6])
            up_grad = own_columns(vec[8, :ff].reshape(-1, HD))
            qv_grad = vec[9, : 3 * inner].reshape(3, z.heads, HD)[0::2].transpose(1, 0, 2)
            qv_grad = own_columns(qv_grad.reshape(2 * z.heads, HD)).reshape(qv3.shape)
        return (
            output.transpose(1, 0, 2),
            input_grad.transpose(1, 0, 2),
            vec_grads[0],
            vec_grads[1],
            qkv_grad.transpose(1, 0, 2),
            qv_grad.transpose(1, 0, 2),
            proj_grad,
            vec_grads[2],
            vec_grads[3],
            vec_grads[4],
            fc1_grad,
            up_grad,
            fc2_grad.T,
            vec_grads[5],
        )

    return local


def solution(mesh):
    sizes = mesh.shape
    return jax.shard_map(
        build(sizes["fsdp"], sizes["ctx"], sizes["tp"]),
        mesh=mesh,
        in_specs=(
            P("fsdp", "ctx", None),
            P("fsdp"),
            P("fsdp"),
            P("fsdp", None, "tp"),
            P(None, "tp", "fsdp"),
            P("tp", "fsdp"),
            P("fsdp"),
            P("fsdp"),
            P("fsdp"),
            P("fsdp", "tp"),
            P("tp", "fsdp"),
            P("tp", "fsdp"),
            P("fsdp"),
            P("fsdp", "ctx", None),
        ),
        out_specs=(
            P("fsdp", "ctx", None),
            P("fsdp", "ctx", None),
            P("fsdp"),
            P("fsdp"),
            P("fsdp", None, "tp"),
            P(None, "tp", "fsdp"),
            P("tp", "fsdp"),
            P("fsdp"),
            P("fsdp"),
            P("fsdp"),
            P("fsdp", "tp"),
            P("tp", "fsdp"),
            P("tp", "fsdp"),
            P("fsdp"),
        ),
        check_vma=False,
    )
```

```python
import functools

import jax
import jax.numpy as jnp
from jax import lax
from jax.experimental import pallas as pl
from jax.experimental.pallas import tpu as pltpu
from jax.sharding import PartitionSpec as P

HD = 64
EPSILON = 1e-06
QUERY_SCALE = 0.125
F32 = jnp.float32
LOW = jnp.bfloat16
NN = ((1,), (0,))
NT = ((1,), (1,))
TN = ((0,), (0,))
VMEM = pl.BlockSpec(memory_space=pltpu.VMEM)
ANY = pl.BlockSpec(memory_space=pl.ANY)
EXTRA = 16
VEC_ROWS = 16
UP_AT, QV_AT = 256, 384


def dot(left, right, dims):
    return lax.dot_general(left, right, (dims, ((), ())), preferred_element_type=F32)


def shape(dims, kind):
    return jax.ShapeDtypeStruct(tuple(dims), kind)


def call(kernel, outs, args, scratch=(), name=None, mib=20, in_specs=None, alias=None):
    return pl.pallas_call(
        kernel,
        out_shape=tuple(outs),
        in_specs=in_specs or [VMEM] * len(args),
        out_specs=tuple([VMEM] * len(outs)),
        scratch_shapes=list(scratch),
        input_output_aliases=alias or {},
        name=name,
        compiler_params=pltpu.CompilerParams(vmem_limit_bytes=mib << 20),
    )(*args)


def gelu_and_slope(v):
    cdf = 0.5 * (1.0 + lax.erf(v * 0.7071067811865476))
    density = jnp.exp(-0.5 * v * v) * 0.3989422804014327
    return v * cdf, cdf + v * density


def mean(v):
    return jnp.mean(v, axis=-1, keepdims=True)


def total_rows(v):
    return jnp.sum(v, axis=0, keepdims=True)


def normalise(v):
    centred = v - mean(v)
    inverse = lax.rsqrt(mean(centred * centred) + EPSILON)
    return centred * inverse, inverse


def norm_backward(grad_normed, normal, inverse, gain):
    scaled = grad_normed * gain
    return inverse * (scaled - mean(scaled) - normal * mean(scaled * normal))


def row_half(t):
    return t & 1


def lanes(parts):
    return jnp.concatenate(parts, axis=1)


def rows_of(parts):
    return jnp.concatenate(parts, axis=0)


def read(ref):
    return ref[...].astype(F32)


class Sizes:
    def __init__(self, nf, nt, inputs, qv_bias, fc1_weight):
        self.nf, self.nt = nf, nt
        _, self.half, self.width = inputs.shape
        self.shard = self.width // nf
        self.heads = qv_bias.shape[1]
        self.inner = self.heads * HD
        self.ff = fc1_weight.shape[1]
        self.pad = -self.half % 8
        self.padded = self.half + self.pad
        self.rows = 2 * self.padded
        self.part = self.width // 4
        self.chunk = self.part // 2
        self.tail = self.chunk // 4
        self.direct = nf == 4
        self.cols = 2 * self.ff + nt * self.inner
        self.early = 1280 if self.ff == 768 else self.ff
        self.wide = 2 * self.ff
        self.dense = self.rows * self.inner // 128

    def live_rows(self, h):
        return pl.ds(pl.multiple_of(h * self.padded, 8), self.half)

    def half_rows(self, h):
        return pl.ds(pl.multiple_of(h * self.padded, 8), self.padded)

    def half_of(self, c):
        return pl.ds(pl.multiple_of(c * self.chunk, 16), self.chunk)

    def squeeze(self, v):
        return rows_of([v[:, :128], lanes([v[: self.padded, 128:], v[self.padded :, 128:]])])

    def spread(self, v):
        tail = v[self.rows :]
        return lanes([v[: self.rows], rows_of([tail[:, :HD], tail[:, HD:]])])


def fetch(sources, copies, sem):
    moves = [pltpu.make_async_copy(s, d, sem.at[i]) for i, (s, d) in enumerate(zip(sources, copies))]
    for m in moves:
        m.start()
    for m in moves:
        m.wait()


def stage_kernel(z, up, down_t, out, rest, one, two, sem):
    fetch((up, down_t), (one, two), sem)
    first = z.early - z.ff
    out[:, : z.ff] = one[...]
    out[:, z.ff :] = two[:, :first]
    rest[...] = two[:, first:]


def pack_kernel(z, *refs):
    sources, (near, far, proj_t, proj_half) = refs[:10], refs[10:14]
    copies, sem = refs[14:24], refs[24]
    fetch(sources, copies, sem)
    qkv, proj, up_b, qv_b = copies[:4]
    vectors = copies[4:]
    c = lax.axis_index("ctx")
    whole = lanes([read(qkv.at[i]) for i in range(3)])
    near[: z.part, :] = whole.astype(LOW)
    far[: z.chunk, :] = jnp.where(c == 0, whole[: z.chunk], whole[z.chunk :]).astype(LOW)
    row = lax.broadcasted_iota(jnp.int32, (EXTRA, z.shard), 0)
    vec = jnp.zeros((EXTRA, z.shard), F32)
    for i, v in enumerate(vectors):
        vec = jnp.where(row == i, read(v).reshape(1, z.shard), vec)
    biases = read(qv_b)
    biases = rows_of([biases[h, i : i + 1] for h in range(z.heads) for i in range(2)])
    for out, at in ((near, z.part), (far, z.chunk)):
        out[at:, :] = jnp.zeros((EXTRA, 3 * z.inner), LOW)
        out[at:, : z.shard] = vec.astype(LOW)
        out[at : at + up_b.shape[0], UP_AT : UP_AT + up_b.shape[1]] = up_b[...]
        out[at : at + 2 * z.heads, QV_AT : QV_AT + biases.shape[1]] = biases.astype(LOW)
    turned = read(proj).T
    proj_t[...] = rows_of([turned, jnp.zeros((proj_t.shape[0] - z.part, z.inner), F32)]).astype(LOW)
    proj_half[...] = jnp.where(c == 0, turned[: z.chunk], turned[z.chunk :]).astype(LOW)


def cut_kernel(z, value, out):
    out[...] = value[z.half_of(lax.axis_index("ctx")), :]


def pair_kernel(first, second, out):
    rows = first.shape[0]
    out[0, :rows, :] = first[...]
    out[1, :rows, :] = second[...]
    out[:, rows:, :] = jnp.zeros((2, out.shape[1] - rows, out.shape[2]), LOW)


def pack_rest_kernel(z, rest, proj_t, near_in, near_their, far_in, far_their, near, scratch):
    c, t = lax.axis_index("ctx"), lax.axis_index("tp")
    scratch[t] = proj_t[: z.part, :].astype(F32)
    scratch[t ^ (1 + 2 * c)] = near_in[: z.part, :].astype(F32)
    scratch[t ^ (3 - 2 * c)] = near_their[: z.part, :].astype(F32)
    scratch[t ^ 2, z.half_of(c), :] = far_in[: z.chunk, :].astype(F32)
    scratch[t ^ 2, z.half_of(1 - c), :] = far_their[: z.chunk, :].astype(F32)
    near[:, : 2 * z.ff - z.early] = rest[...]
    near[:, 2 * z.ff - z.early :] = lanes([scratch[i] for i in range(4)]).astype(LOW)


def frame_of(z, keep, received, frame):
    zero = jnp.zeros((z.pad, z.width), F32)
    pieces = []
    for ref in (keep, received):
        pieces.append(jnp.where(frame == 0, ref[:, 0, :].astype(F32), ref[:, 1, :].astype(F32)))
        pieces.append(zero)
    return rows_of(pieces)


def frame_kernel(z, keep, received, stream, normal, inverse, normal_their):
    c = lax.axis_index("ctx")
    values = frame_of(z, keep, received, c)
    stream[...] = values.astype(LOW)
    n, i = normalise(values)
    normal[...] = n
    inverse[...] = jnp.broadcast_to(i, inverse.shape)
    normal_their[...] = normalise(frame_of(z, received, keep, 1 - c))[0]


def cot_kernel(z, keep, received, out):
    c = lax.axis_index("ctx")
    out[0] = frame_of(z, keep, received, c).astype(LOW)
    out[1] = frame_of(z, received, keep, 1 - c).astype(LOW)


def attend_kernel(z, *refs):
    refs = list(refs)
    if z.direct:
        own, near, near_their, far, far_their = refs[:5]
        refs = refs[5:]
    else:
        whole, vec_in, up_in, qv_in = refs[:4]
        refs = refs[4:]
    normal, small, w_out, normed_out, act, attended, soft_out = refs[:7]
    if z.direct:
        c, b = lax.axis_index("ctx"), lax.axis_index("fsdp")
        gather = refs[7]
        for ref, at in ((own, b), (near, b ^ (1 + c)), (near_their, b ^ (2 - c))):
            w_out[at] = ref[: z.part, :]
            gather[at] = ref[z.part :, :].astype(F32)
        w_out[b ^ 3, z.half_of(c), :] = far[: z.chunk, :]
        w_out[b ^ 3, z.half_of(1 - c), :] = far_their[: z.chunk, :]
        gather[b ^ 3] = far[z.chunk :, :].astype(F32)
        blocks = [gather[i] for i in range(4)]
        w = HD // 4
        vec = lanes([g[:8, : z.shard] for g in blocks])
        up = lanes([g[: z.ff // HD, UP_AT : UP_AT + w] for g in blocks])
        qv = lanes([g[: 2 * z.heads, QV_AT : QV_AT + w] for g in blocks])
    else:
        w_out[...] = whole[...]
        vec, up, qv = vec_in[...], up_in[...], qv_in[...]
    up_row = lanes([up[i : i + 1] for i in range(z.ff // HD)])
    query_b = lanes([qv[2 * h : 2 * h + 1] for h in range(z.heads)])
    value_b = lanes([qv[2 * h + 1 : 2 * h + 2] for h in range(z.heads)])
    small[...] = vec
    small[6:7, : z.ff] = up_row
    normed = (normal[...] * vec[0:1] + vec[1:2]).astype(LOW)
    normed_out[...] = normed
    projected = dot(normed, w_out[...].reshape(z.width, 3 * z.inner), NN)
    n = z.inner
    query = ((projected[:, :n] + query_b) * QUERY_SCALE).astype(LOW)
    key = projected[:, n : 2 * n].astype(LOW)
    value = (projected[:, 2 * n :] + value_b).astype(LOW)
    act[0] = query
    act[1] = key
    act[2] = value
    place = lax.broadcasted_iota(jnp.int32, (z.rows, z.rows), 1)
    valid = (place < z.half) | ((place >= z.padded) & (place < z.padded + z.half))
    done = []
    for h in range(z.heads):
        cut = slice(h * HD, (h + 1) * HD)
        scores = jnp.where(valid, dot(query[:, cut], key[:, cut], NT), -1e30)
        exponent = jnp.exp(scores - jnp.max(scores, axis=-1, keepdims=True))
        soft = exponent * (1.0 / jnp.sum(exponent, axis=-1, keepdims=True))
        soft_out[h] = soft
        done.append(dot(soft.astype(LOW), value[:, cut], NN))
    attended[...] = z.squeeze(lanes(done)).astype(LOW)


def feed_kernel(z, *refs):
    refs = list(refs)
    if z.direct:
        feed, feed_in, feed_their, near, near_in, near_their, far, far_their, last_far, last_far_their = refs[:10]
        refs = refs[10:]
    else:
        whole = refs[0]
        refs = refs[1:]
    att = refs[:3]
    stream, cot, small = refs[3:6]
    w_out, middle_out, acts, part_out, own_att, small_out = refs[6:12]
    sends, heads = refs[12:-1], refs[-1]
    t = lax.axis_index("tp")
    if z.direct:
        c, b = lax.axis_index("ctx"), lax.axis_index("fsdp")
        mine, other = z.half_of(c), z.half_of(1 - c)
        first, last = pl.ds(0, z.early), pl.ds(z.early, z.cols - z.early)
        for at, one, two in ((b, feed, near), (b ^ (1 + c), feed_in, near_in), (b ^ (2 - c), feed_their, near_their)):
            w_out[at, :, first] = one[...]
            w_out[at, :, last] = two[...]
        w_out[b ^ 3, mine, first] = far[...]
        w_out[b ^ 3, other, first] = far_their[...]
        w_out[b ^ 3, mine, last] = last_far[...]
        w_out[b ^ 3, other, last] = last_far_their[...]
    else:
        w_out[...] = whole[...]
    n = z.inner
    w_up = w_out[:, :, : z.ff].reshape(z.width, z.ff)
    w_down_t = w_out[:, :, z.ff : 2 * z.ff].reshape(z.width, z.ff)
    w_proj_t = w_out[:, :, 2 * z.ff :].reshape(z.width, z.nt * n)
    grad_out_low = cot[0]
    grad_out = grad_out_low.astype(F32)
    heads[t] = z.spread(read(att[0]))
    heads[t ^ 3] = z.spread(read(att[1]))
    heads[t ^ 1] = z.spread(att[2][0, : z.dense, :].astype(F32))
    heads[t ^ 2] = z.spread(att[2][1, : z.dense, :].astype(F32))
    attended = lanes([heads[i] for i in range(z.nt)]).astype(LOW)
    acts[4] = attended
    branch = dot(attended, w_proj_t, NT)
    middle = stream[...].astype(F32) + branch + small[2:3]
    middle_out[...] = middle
    normal, inverse = normalise(middle)
    gain = small[3:4]
    normed = (normal * gain + small[4:5]).astype(LOW)
    acts[0] = normed
    hidden, slope = gelu_and_slope(dot(normed, w_up, NN) + small[6:7, : z.ff])
    acts[1] = hidden.astype(LOW)
    grad_pre = (dot(grad_out_low, w_down_t, NN) * slope).astype(LOW)
    acts[2] = grad_pre
    grad_normed = dot(grad_pre, w_up, NT)
    part = grad_out * (1.0 / z.nt) + norm_backward(grad_normed, normal, inverse, gain)
    part_out[...] = part
    low = part.astype(LOW)
    acts[3] = low
    grad_att = dot(low, w_proj_t, NN)
    for i in range(z.nt):
        heads[i] = grad_att[:, i * n : (i + 1) * n]
    own_att[...] = heads[t]
    for k in range(1, z.nt):
        sends[k - 1][...] = z.squeeze(heads[t ^ k]).astype(LOW)
    small_out[...] = jnp.zeros(small_out.shape, F32)
    small_out[2:3] = total_rows(part)
    small_out[3:4] = total_rows(grad_normed * normal)
    small_out[4:5] = total_rows(grad_normed)
    small_out[5:6] = total_rows(grad_out) * (1.0 / z.nt)
    small_out[6:7, : z.ff] = total_rows(grad_pre.astype(F32))


def down_kernel(z, acts, w, kept, sent, scratch):
    h = row_half(lax.axis_index("tp"))
    w_down_t = w[:, :, z.ff : 2 * z.ff].reshape(z.width, z.ff)
    scratch[...] = dot(acts[1], w_down_t, NT)
    kept[...] = scratch[z.live_rows(h), :]
    sent[...] = scratch[z.live_rows(1 - h), :].astype(LOW)


def add_low_kernel(kept, received, out):
    rows = kept.shape[0]
    out[:rows, :] = (kept[...] + read(received)).astype(LOW)
    if out.shape[0] > rows:
        out[rows:, :] = jnp.zeros((out.shape[0] - rows, out.shape[1]), LOW)


def store_own(z, value, at, keep):
    cols = pl.ds(at, value.shape[1])
    c, b = (lax.axis_index("ctx"), lax.axis_index("fsdp")) if z.direct else (0, 0)
    for j in range(4):
        whole = value[j * z.part : (j + 1) * z.part]
        if z.direct:
            keep[j ^ b, :, cols] = jnp.where(c == 0, whole[: z.chunk], whole[z.chunk :])
        else:
            keep[j, :, cols] = whole


def both_frames(left, right, left_their, right_their):
    return dot(left, right, TN) + dot(left_their, right_their, TN)


def feed_grad_kernel(z, acts, theirs, cot, keep):
    store_own(z, both_frames(acts[0], acts[2], theirs[0], theirs[2]), 0, keep)
    store_own(z, both_frames(cot[0], acts[1], cot[1], theirs[1]), z.ff, keep)


def proj_grad_kernel(z, acts, theirs, own, *refs):
    value = both_frames(acts[3], acts[4], theirs[3], theirs[4])
    if not z.direct:
        store_own(z, value, 0, own)
        return
    sends, keep = refs[:3], refs[3]
    store_own(z, value, 0, keep)
    own[...] = keep[0]
    for k in range(1, 4):
        sends[k - 1][...] = keep[k].astype(LOW)


def qkv_grad_kernel(z, normed, grads, normal_their, grads_their, small, keep):
    normed_their = (normal_their[...] * small[0:1] + small[1:2]).astype(LOW)
    store_own(z, both_frames(normed[...], grads[...], normed_their, grads_their[...]), 0, keep)


def split_kernel(keep, out, kept):
    c = lax.axis_index("ctx")
    n = keep.shape[2]
    for target, at, kind in ((out, (1 + c, 3), LOW), (kept, (0, 2 - c), F32)):
        for i in range(2):
            target[i, :, :n] = keep[at[i]].astype(kind)
            if target.shape[2] > n:
                target[i, :, n:] = jnp.zeros((target.shape[1], target.shape[2] - n), kind)


def by_half(mine, other):
    c = lax.axis_index("ctx")
    return rows_of([jnp.where(c == 0, mine, other), jnp.where(c == 0, other, mine)])


def feed_final_kernel(z, own, theirs, up, down):
    total = by_half(own[...], read(theirs))
    up[...] = total[:, : z.ff]
    down[...] = total[:, z.ff :]


def unfold(z, v):
    return rows_of([v[:, i * z.inner : (i + 1) * z.inner] for i in range(4)])


def fold(v):
    n = v.shape[0] // 4
    return lanes([v[i * n : (i + 1) * n] for i in range(4)])


def back_kernel(z, *refs):
    own_att, got = refs[0], refs[1 : z.nt]
    act, soft, w, normal, inverse, part, small, small_in = refs[z.nt : z.nt + 8]
    grads_out, qv_out, kept, sent, scratch = refs[z.nt + 8 :]
    t = lax.axis_index("tp")
    grad_att = (own_att[...] + z.spread(sum(read(g) for g in got))).astype(LOW)
    parts = [[], [], []]
    query, key, value = act[0], act[1], act[2]
    for h in range(z.heads):
        cut = slice(h * HD, (h + 1) * HD)
        ga = grad_att[:, cut]
        p = soft[h]
        grad_soft = dot(ga, value[:, cut], NT)
        delta = jnp.sum(p * grad_soft, axis=-1, keepdims=True)
        grad_scores = (p * (grad_soft - delta)).astype(LOW)
        parts[0].append((dot(grad_scores, key[:, cut], NN).astype(LOW).astype(F32) * QUERY_SCALE).astype(LOW))
        parts[1].append(dot(grad_scores, query[:, cut], TN).astype(LOW))
        parts[2].append(dot(p.astype(LOW), ga, TN).astype(LOW))
    grads = lanes(parts[0] + parts[1] + parts[2])
    grads_out[...] = grads
    n = z.inner
    qv_out[...] = total_rows(grads.astype(F32))
    grad_normed = dot(grads, w[...].reshape(z.width, 3 * n), NT)
    scratch[...] = part[...] + norm_backward(grad_normed, normal[...], inverse[:, :1], small[0:1])
    row = lax.broadcasted_iota(jnp.int32, (8, z.width), 0)
    vec = small_in[...]
    vec = jnp.where(row == 0, total_rows(grad_normed * normal[...]), vec)
    vec = jnp.where(row == 1, total_rows(grad_normed), vec)
    h = row_half(t)
    for at in (z.half, z.padded + z.half):
        scratch[at : at + 6, :] = vec[:6]
    kept[...] = scratch[z.half_rows(h), :]
    sent[...] = scratch[z.half_rows(1 - h), :].astype(LOW)


def out_total_kernel(z, own, received, middle, small, out):
    rows = z.live_rows(row_half(lax.axis_index("tp")))
    out[...] = (middle[rows, :] + read(own) + read(received) + small[5:6]).astype(LOW)


def in_pair_kernel(z, kept, received, own, *refs):
    parts, (out, proj_kept, scratch) = refs[:3], refs[3:]
    out[: z.padded, :] = (kept[...] + read(received)).astype(LOW)
    t = lax.axis_index("tp")
    proj = own[...] + sum(read(p) for p in parts)
    for i in range(z.nt):
        scratch[i] = fold(proj[:, i * z.inner : (i + 1) * z.inner])
    proj_kept[0] = scratch[t]
    proj_kept[1] = scratch[t ^ 1]
    out[z.padded :, :] = rows_of([scratch[t ^ 2], scratch[t ^ 3]]).astype(LOW)


def sum_rows_kernel(z, own, received, small, qv, *refs):
    if z.direct:
        proj_kept, out, vec, proj_own = refs
        arrived = received[z.padded :, :].astype(F32)
        proj_own[...] = proj_kept[0] + arrived[: z.tail]
        out[z.padded :, :] = (proj_kept[1] + arrived[z.tail :]).astype(LOW)
    else:
        out, vec = refs
    total = own[: z.padded, :].astype(F32) + received[: z.padded, :].astype(F32)
    out[: z.padded, :] = total.astype(LOW)
    vec[...] = jnp.zeros(vec.shape, F32)
    vec[:6, :] = total[z.half : z.half + 6]
    vec[8:9, : z.ff] = small[6:7, : z.ff]
    vec[9:10, : 3 * z.inner] = qv[...]


def cross_kernel(kept, received, own, out):
    n = kept.shape[2]
    own[...] = kept[0] + received[0, :, :n].astype(F32)
    out[...] = (kept[1] + received[1, :, :n].astype(F32)).astype(LOW)


def cross_qkv_kernel(z, kept, received, small, own, out):
    own[...] = kept[0] + received[0].astype(F32)
    out[: z.chunk, :] = (kept[1] + received[1].astype(F32)).astype(LOW)
    out[z.chunk :, :] = small[...].astype(LOW)


def small_kernel(z, vec, near, cross, far, own, scratch):
    c, b = lax.axis_index("ctx"), lax.axis_index("fsdp")
    vectors = vec[...]
    up = rows_of([vectors[8:9, i * HD : (i + 1) * HD] for i in range(z.ff // HD)])
    pieces = []
    for h in range(z.heads):
        pieces.append(vectors[9:10, h * HD : (h + 1) * HD])
        pieces.append(vectors[9:10, 2 * z.inner + h * HD : 2 * z.inner + (h + 1) * HD])
    qv_rows = rows_of(pieces)
    scratch[...] = jnp.zeros(scratch.shape, F32)
    w = HD // 4
    for i in range(4):
        scratch[i, :8, : z.shard] = vectors[:8, i * z.shard : (i + 1) * z.shard]
        scratch[i, : z.ff // HD, UP_AT : UP_AT + w] = up[:, i * w : (i + 1) * w]
        scratch[i, : 2 * z.heads, QV_AT : QV_AT + w] = qv_rows[:, i * w : (i + 1) * w]
    near[...] = scratch[b ^ (1 + c)].astype(LOW)
    cross[...] = scratch[b ^ (2 - c)]
    far[...] = scratch[b ^ 3].astype(LOW)
    own[...] = scratch[b]


def halves_of(z, own, received):
    h = row_half(lax.axis_index("tp"))
    return jnp.where(h == 0, own, received), jnp.where(h == 0, received, own)


def swap_kernel(z, out_own, out_in, in_own, in_in, *refs):
    n = z.padded
    pad = jnp.zeros((z.pad, z.width), F32)
    out_mine, out_theirs = halves_of(z, read(out_own), read(out_in))
    in_mine, in_theirs = halves_of(z, in_own[:n, :].astype(F32), in_in[:n, :].astype(F32))
    theirs = [out_theirs, pad, in_theirs]
    if z.direct:
        proj_own, mine, sent, proj = refs
        total = proj_own[...] + in_in[n:, :].astype(F32)
        proj[...] = total
        theirs.append(total)
    else:
        mine, sent = refs
    mine[0] = rows_of([out_mine, pad])
    mine[1] = in_mine
    sent[...] = rows_of(theirs).astype(LOW)


def last_kernel(z, feed, feed_in, qkv, qkv_in, small, near, far, feed_total, feed_sent, qkv_total, qkv_sent):
    value = feed[...] + read(feed_in)
    feed_total[...] = value
    feed_sent[...] = value.astype(LOW)
    value = qkv[...] + qkv_in[: z.chunk, :].astype(F32)
    tail = small[...] + read(near) + read(far) + qkv_in[z.chunk :, :].astype(F32)
    for out, kind in ((qkv_total, F32), (qkv_sent, LOW)):
        out[: z.chunk, :] = value.astype(kind)
        out[z.chunk :, :] = tail.astype(kind)


def qkv_final_kernel(z, own, theirs, qkv, up, qv, *vectors):
    both = by_half(own[: z.chunk, :], theirs[: z.chunk, :].astype(F32))
    for i in range(3):
        qkv[i] = both[:, i * z.inner : (i + 1) * z.inner]
    tail = own[z.chunk :, :] + theirs[z.chunk :, :].astype(F32)
    w = HD // 4
    up[...] = tail[: z.ff // HD, UP_AT : UP_AT + w]
    for h in range(z.heads):
        qv[h] = tail[2 * h : 2 * h + 2, QV_AT : QV_AT + w]
    for i, v in enumerate(vectors):
        v[...] = tail[i : i + 1, : z.shard].reshape(z.shard)


def place_kernel(z, mine, theirs, out, *scratch):
    c = lax.axis_index("ctx")
    target = scratch[0] if scratch else out
    mine, theirs = mine[: z.half], theirs[: z.half]
    target[:, 0, :] = jnp.where(c == 0, mine, theirs)
    target[:, 1, :] = jnp.where(c == 0, theirs, mine)
    if scratch:
        out[...] = target[...].astype(out.dtype)


def final_kernel(z, mine, theirs, *refs):
    if z.direct:
        proj_own, feed_own, feed_in, qkv_own, qkv_in, output, input_grad, proj, up, down, *rest = refs
        other = theirs[2 * z.padded :, :].astype(F32)
        proj[...] = by_half(unfold(z, proj_own[...]), unfold(z, other)).T
        feed_final_kernel(z, feed_own, feed_in, up, down)
        qkv_final_kernel(z, qkv_own, qkv_in, *rest[:-1])
        scratch = rest[-1]
    else:
        output, input_grad, scratch = refs
    place_kernel(z, mine[1], theirs[z.padded : 2 * z.padded, :].astype(F32), input_grad)
    place_kernel(z, mine[0], theirs[: z.padded, :].astype(F32), output, scratch)


def build(nf, nc, nt):
    def local(
        inputs,
        norm1_gain,
        norm1_bias,
        qkv_weight,
        qv_bias,
        proj_weight,
        proj_bias,
        norm2_gain,
        norm2_bias,
        fc1_weight,
        fc1_bias,
        fc2_weight,
        fc2_bias,
        cotangent,
    ):
        z = Sizes(nf, nt, inputs, qv_bias, fc1_weight)
        part = functools.partial
        rows, width, inner, ff, chunk = z.rows, z.width, z.inner, z.ff, z.chunk
        f = lax.axis_index("fsdp")
        tie = lax.optimization_barrier

        def other_core(value):
            return lax.ppermute(value, "ctx", [(0, 1), (1, 0)])

        def to_tp(value, k):
            return lax.ppermute(value, "tp", [(i, i ^ k) for i in range(nt)])

        def to_far(value):
            return lax.ppermute(value, "fsdp", [(i, i ^ 3) for i in range(nf)])

        def neighbours(value, order):
            pairs = [(2 * i + c, 2 * (i ^ order[c]) + c) for i in range(nf) for c in range(2)]
            return lax.ppermute(value, ("fsdp", "ctx"), pairs)

        def to_near(value):
            return neighbours(value, (1, 2))

        def to_cross(value):
            return neighbours(value, (2, 1))

        def proj_near(value):
            pairs = [(c * nt + i, c * nt + (i ^ (1 + 2 * c))) for i in range(nt) for c in range(2)]
            return lax.ppermute(value, ("ctx", "tp"), pairs)

        def pair_of(first, second):
            return call(pair_kernel, [shape((2,) + first.shape, LOW)], [first, second], name="pair")[0]

        qkv3 = qkv_weight.transpose(1, 0, 2)
        down_t = fc2_weight.T
        qv3 = qv_bias.transpose(1, 0, 2)
        x_raw, cot_raw = inputs.transpose(1, 0, 2), cotangent.transpose(1, 0, 2)
        vectors = [norm1_gain, norm1_bias, proj_bias, norm2_gain, norm2_bias, fc2_bias]

        x_recv = other_core(x_raw)
        cot_recv = other_core(cot_raw)
        def frames(x_recv, cot_recv):
            stream, normal_one, inverse_one, normal_their = call(
                part(frame_kernel, z),
                [shape((rows, width), LOW), shape((rows, width), F32), shape((rows, 128), F32), shape((rows, width), F32)],
                [x_raw, x_recv],
                name="frame",
            )
            (cot,) = call(part(cot_kernel, z), [shape((2, rows, width), LOW)], [cot_raw, cot_recv], name="cotangent")
            return stream, normal_one, inverse_one, normal_their, cot

        if z.direct:
            sources = [qkv3, proj_weight, fc1_bias, qv3] + vectors
            near, far, proj_t, proj_half = call(
                part(pack_kernel, z),
                [
                    shape((z.part + EXTRA, 3 * inner), LOW),
                    shape((chunk + EXTRA, 3 * inner), LOW),
                    shape((z.part + 104, inner), LOW),
                    shape((chunk, inner), LOW),
                ],
                sources,
                [pltpu.VMEM(s.shape, s.dtype) for s in sources] + [pltpu.SemaphoreType.DMA((len(sources),))],
                name="pack",
                mib=56,
                in_specs=[ANY] * len(sources),
            )
            near, far, proj_t, proj_half, x_recv, cot_recv = tie((near, far, proj_t, proj_half, x_recv, cot_recv))
            got = [to_near(near), to_far(far)]
            proj_got = [proj_near(proj_t), to_tp(proj_half, 2)]
            feed_own, feed_rest = call(
                part(stage_kernel, z),
                [shape((z.part, z.early), LOW), shape((z.part, 2 * ff - z.early), LOW)],
                [fc1_weight, down_t],
                [pltpu.VMEM((z.part, ff), LOW)] * 2 + [pltpu.SemaphoreType.DMA((2,))],
                name="stage",
                mib=20,
                in_specs=[ANY] * 2,
            )
            stream, normal_one, inverse_one, normal_their, cot = frames(x_recv, cot_recv)
            feed_in = to_near(feed_own)
            got, proj_got, feed_rest, stream, normal_one, inverse_one, normal_their, cot = tie(
                (got, proj_got, feed_rest, stream, normal_one, inverse_one, normal_their, cot)
            )
            shared = [other_core(g) for g in got]
            qkv_in = [near, got[0], shared[0], got[1], shared[1]]
            (rest_near,) = call(
                part(pack_rest_kernel, z),
                [shape((z.part, z.cols - z.early), LOW)],
                [feed_rest, proj_t, proj_got[0], other_core(proj_got[0]), proj_got[1], other_core(proj_got[1])],
                [pltpu.VMEM((nt, z.part, inner), F32)],
                name="pack_rest",
            )
            near_in = to_near(rest_near)
            far_in = []
            for value in (feed_in, near_in):
                (half,) = call(part(cut_kernel, z), [shape((chunk, value.shape[1]), LOW)], [value], name="cut")
                far_in.append(to_cross(half))
        else:
            stream, normal_one, inverse_one, normal_their, cot = frames(x_recv, cot_recv)
            whole = lax.all_gather(qkv3, "fsdp", axis=1, tiled=True)
            whole = whole.transpose(1, 0, 2).reshape(4, z.part, 3 * inner)
            vec = jnp.stack(vectors + [vectors[0]] * 2).astype(F32)
            qv_rows = qv3.reshape(2 * z.heads, -1).astype(F32)
            gathered = [lax.all_gather(v, "fsdp", axis=1, tiled=True) for v in (vec, fc1_bias.astype(F32), qv_rows)]
            qkv_in = [whole] + gathered
            proj_t = proj_weight.T
            rest = jnp.concatenate([fc1_weight, down_t, lax.all_gather(proj_t, "tp", axis=1, tiled=True)], 1)
            rest_in = [lax.all_gather(rest, "fsdp", axis=0, tiled=True).reshape(4, z.part, z.cols)]

        small, w_qkv, normed_one, act, attended, soft = call(
            part(attend_kernel, z),
            [
                shape((8, width), F32),
                shape((4, z.part, 3 * inner), LOW),
                shape((rows, width), LOW),
                shape((3, rows, inner), LOW),
                shape((z.dense, 128), LOW),
                shape((z.heads, rows, rows), F32),
            ],
            qkv_in + [normal_one],
            [pltpu.VMEM((4, EXTRA, 3 * inner), F32)] if z.direct else [],
            name="attend",
        )
        att_one = to_tp(attended, 3)
        (att_two,) = call(pair_kernel, [shape((2, z.dense + 16, 128), LOW)], [attended, att_one], name="pair")
        att_two = to_tp(att_two, 1)
        if z.direct:
            att_two, far_in = tie((att_two, far_in))
            rest_in = [feed_own, feed_in, other_core(feed_in), rest_near, near_in, other_core(near_in)]
            rest_in += [far_in[0], other_core(far_in[0]), far_in[1], other_core(far_in[1])]

        (w_rest, middle, acts, part_middle, own_att, small_two, *att_sends) = (
            call(
                part(feed_kernel, z),
                [
                    shape((4, z.part, z.cols), LOW),
                    shape((rows, width), F32),
                    shape((5, rows, width), LOW),
                    shape((rows, width), F32),
                    shape((rows, inner), F32),
                    shape((8, width), F32),
                ]
                + [shape((z.dense, 128), LOW)] * (nt - 1),
                rest_in + [attended, att_one, att_two, stream, cot, small],
                [pltpu.VMEM((nt, rows, inner), F32)],
                name="feed",
            )
        )
        att_got = [to_tp(att_sends[k - 1], k) for k in (3, 2, 1)]
        acts_their = other_core(acts)
        kept_rows = chunk if z.direct else z.part
        (keep,) = call(
            part(feed_grad_kernel, z),
            [shape((4, kept_rows, 2 * ff), F32)],
            [acts, acts_their, cot],
            name="feed_grad",
        )
        proj_own, *sends = call(
            part(proj_grad_kernel, z),
            [shape((chunk, nt * inner), F32)] + [shape((chunk, nt * inner), LOW)] * 3
            if z.direct
            else [shape((4, z.part, nt * inner), F32)],
            [acts, acts_their],
            [pltpu.VMEM((4, chunk, nt * inner), F32)] if z.direct else [],
            name="proj_grad",
        )
        proj_full = proj_own
        out_kept, out_sent = call(
            part(down_kernel, z),
            [shape((z.half, width), F32), shape((z.half, width), LOW)],
            [acts, w_rest],
            [pltpu.VMEM((rows, width), F32)],
            name="down",
        )
        out_one = to_tp(out_sent, 1)
        if z.direct:
            grad_sent, grad_kept = call(
                split_kernel,
                [shape((2, chunk, z.wide), LOW), shape((2, chunk, 2 * ff), F32)],
                [keep],
                name="split",
            )
            grad_in = to_near(grad_sent)
            att_got, out_one, grad_kept, proj_own, sends = tie((att_got, out_one, grad_kept, proj_own, sends))
            proj_in = [lax.ppermute(sends[k - 1], "fsdp", [(i, i ^ k) for i in range(nf)]) for k in (3, 1)]
        (out_low,) = call(add_low_kernel, [shape((z.half, width), LOW)], [out_kept, out_one], name="out_pair")
        out_two = to_tp(out_low, 2)

        grads, qv_sum, in_kept, in_sent = call(
            part(back_kernel, z),
            [
                shape((rows, 3 * inner), LOW),
                shape((1, 3 * inner), F32),
                shape((z.padded, width), F32),
                shape((z.padded, width), LOW),
            ],
            [own_att] + att_got + [act, soft, w_qkv, normal_one, inverse_one, part_middle, small, small_two],
            [pltpu.VMEM((rows, width), F32)],
            name="back",
        )
        in_one = to_tp(in_sent, 1)
        grads_their = other_core(grads)
        if z.direct:
            grads_their, last_send = tie((grads_their, sends[1]))
            proj_in.append(lax.ppermute(last_send, "fsdp", [(i, i ^ 2) for i in range(nf)]))
        (keep_qkv,) = call(
            part(qkv_grad_kernel, z),
            [shape((4, kept_rows, 3 * inner), F32)],
            [normed_one, grads, normal_their, grads_their, small],
            name="qkv_grad",
        )
        extra = z.tail if z.direct else 0
        if z.direct:
            in_one, out_two, proj_in, keep_qkv = tie((in_one, out_two, proj_in, keep_qkv))
            in_low, proj_kept = call(
                part(in_pair_kernel, z),
                [shape((z.padded + 2 * extra, width), LOW), shape((2, extra, width), F32)],
                [in_kept, in_one, proj_own] + proj_in,
                [pltpu.VMEM((nt, extra, width), F32)],
                name="in_pair",
            )
            qkv_sent, qkv_kept = call(
                split_kernel,
                [shape((2, chunk, 3 * inner), LOW), shape((2, chunk, 3 * inner), F32)],
                [keep_qkv],
                name="split_qkv",
            )
            qkv_in = to_near(qkv_sent)
        else:
            (in_low,) = call(add_low_kernel, [shape((z.padded, width), LOW)], [in_kept, in_one], name="in_pair")
        in_two = to_tp(in_low, 2)
        (out_low,) = call(
            part(out_total_kernel, z), [shape((z.half, width), LOW)], [out_low, out_two, middle, small], name="out_total"
        )
        out_in = to_tp(out_low, 1)
        if z.direct:
            grad_own, cross = call(
                cross_kernel,
                [shape((chunk, 2 * ff), F32), shape((chunk, 2 * ff), LOW)],
                [grad_kept, grad_in],
                name="cross",
            )
            cross = to_cross(cross)
            in_two, out_in, qkv_in = tie((in_two, out_in, qkv_in))
        in_low, vec, *proj_own = call(
            part(sum_rows_kernel, z),
            [shape((z.padded + extra, width), LOW), shape((VEC_ROWS, width), F32)]
            + ([shape((extra, width), F32)] if extra else []),
            [in_low, in_two, small_two, qv_sum] + ([proj_kept] if extra else []),
            name="sum_rows",
        )
        in_in = to_tp(in_low, 1)
        proj_all = []
        if z.direct:
            near, side, far, small_own = call(
                part(small_kernel, z),
                [shape((EXTRA, 3 * inner), LOW), shape((EXTRA, 3 * inner), F32)] * 2,
                [vec],
                [pltpu.VMEM((4, EXTRA, 3 * inner), F32)],
                name="small",
            )
            qkv_own, qkv_sent = call(
                part(cross_qkv_kernel, z),
                [shape((chunk, 3 * inner), F32), shape((chunk + EXTRA, 3 * inner), LOW)],
                [qkv_kept, qkv_in, side],
                name="cross_qkv",
            )
            qkv_in = to_cross(qkv_sent)
            far = to_far(far)
            near = to_near(near)
            in_in, cross, qkv_in, near, far = tie((in_in, cross, qkv_in, near, far))
            proj_all = proj_own
            feed_own, feed_sent, qkv_own, qkv_sent = call(
                part(last_kernel, z),
                [
                    shape((chunk, 2 * ff), F32),
                    shape((chunk, 2 * ff), LOW),
                    shape((chunk + EXTRA, 3 * inner), F32),
                    shape((chunk + EXTRA, 3 * inner), LOW),
                ],
                [grad_own, cross, qkv_own, qkv_in, small_own, near, far],
                name="last",
            )
            feed_in, qkv_in = other_core(feed_sent), other_core(qkv_sent)
        mine, theirs, *proj_own = call(
            part(swap_kernel, z),
            [shape((2, z.padded, width), F32), shape((rows + (z.tail if proj_all else 0), width), LOW)]
            + ([shape((z.tail, width), F32)] if proj_all else []),
            [out_low, out_in, in_low, in_in] + proj_all,
            name="swap",
        )
        theirs = other_core(theirs)
        results = [shape((z.half, 2, width), LOW), shape((z.half, 2, width), F32)]
        scratch = [pltpu.VMEM((z.half, 2, width), F32)]
        if z.direct:
            output, input_grad, proj_grad, fc1_grad, fc2_grad, qkv_grad, up_grad, qv_grad, *vec_grads = call(
                part(final_kernel, z),
                results
                + [
                    shape((inner, z.shard), F32),
                    shape((z.shard, ff), F32),
                    shape((z.shard, ff), F32),
                    shape((3, z.shard, inner), F32),
                    shape(fc1_bias.shape, F32),
                    shape(qv3.shape, F32),
                ]
                + [shape((z.shard,), F32)] * 6,
                [mine, theirs, proj_own[0], feed_own, feed_in, qkv_own, qkv_in],
                scratch,
                name="final",
            )
        else:
            output, input_grad = call(part(final_kernel, z), results, [mine, theirs], scratch, name="final")

            def scatter(value):
                value = value.reshape(width, -1).astype(LOW)
                return lax.psum_scatter(value, "fsdp", scatter_dimension=0, tiled=True).astype(F32)

            total = scatter(keep)
            fc1_grad, fc2_grad = total[:, :ff], total[:, ff:]
            qkv_grad = scatter(keep_qkv).reshape(z.shard, 3, inner).transpose(1, 0, 2)
            proj_grad = scatter(proj_full).astype(LOW)
            proj_grad = lax.psum_scatter(proj_grad, "tp", scatter_dimension=1, tiled=True).astype(F32).T

            def own_columns(value):
                value = lax.psum(value, ("fsdp", "ctx"))
                return lax.dynamic_slice_in_dim(value, f * (value.shape[1] // nf), value.shape[1] // nf, 1)

            vec_grads = own_columns(vec[:6])
            up_grad = own_columns(vec[8, :ff].reshape(-1, HD))
            qv_grad = vec[9, : 3 * inner].reshape(3, z.heads, HD)[0::2].transpose(1, 0, 2)
            qv_grad = own_columns(qv_grad.reshape(2 * z.heads, HD)).reshape(qv3.shape)
        return (
            output.transpose(1, 0, 2),
            input_grad.transpose(1, 0, 2),
            vec_grads[0],
            vec_grads[1],
            qkv_grad.transpose(1, 0, 2),
            qv_grad.transpose(1, 0, 2),
            proj_grad,
            vec_grads[2],
            vec_grads[3],
            vec_grads[4],
            fc1_grad,
            up_grad,
            fc2_grad.T,
            vec_grads[5],
        )

    return local


def solution(mesh):
    sizes = mesh.shape
    return jax.shard_map(
        build(sizes["fsdp"], sizes["ctx"], sizes["tp"]),
        mesh=mesh,
        in_specs=(
            P("fsdp", "ctx", None),
            P("fsdp"),
            P("fsdp"),
            P("fsdp", None, "tp"),
            P(None, "tp", "fsdp"),
            P("tp", "fsdp"),
            P("fsdp"),
            P("fsdp"),
            P("fsdp"),
            P("fsdp", "tp"),
            P("tp", "fsdp"),
            P("tp", "fsdp"),
            P("fsdp"),
            P("fsdp", "ctx", None),
        ),
        out_specs=(
            P("fsdp", "ctx", None),
            P("fsdp", "ctx", None),
            P("fsdp"),
            P("fsdp"),
            P("fsdp", None, "tp"),
            P(None, "tp", "fsdp"),
            P("tp", "fsdp"),
            P("fsdp"),
            P("fsdp"),
            P("fsdp"),
            P("fsdp", "tp"),
            P("tp", "fsdp"),
            P("tp", "fsdp"),
            P("fsdp"),
        ),
        check_vma=False,
    )
```

```python
import functools

import jax
import jax.numpy as jnp
from jax import lax
from jax.experimental import pallas as pl
from jax.experimental.pallas import tpu as pltpu
from jax.sharding import PartitionSpec as P

HD = 64
EPSILON = 1e-06
QUERY_SCALE = 0.125
F32 = jnp.float32
LOW = jnp.bfloat16
NN = ((1,), (0,))
NT = ((1,), (1,))
TN = ((0,), (0,))
VMEM = pl.BlockSpec(memory_space=pltpu.VMEM)
ANY = pl.BlockSpec(memory_space=pl.ANY)
EXTRA = 16
VEC_ROWS = 16
UP_AT, QV_AT = 256, 384


def dot(left, right, dims):
    return lax.dot_general(left, right, (dims, ((), ())), preferred_element_type=F32)


def shape(dims, kind):
    return jax.ShapeDtypeStruct(tuple(dims), kind)


def call(kernel, outs, args, scratch=(), name=None, mib=20, in_specs=None, alias=None):
    return pl.pallas_call(
        kernel,
        out_shape=tuple(outs),
        in_specs=in_specs or [VMEM] * len(args),
        out_specs=tuple([VMEM] * len(outs)),
        scratch_shapes=list(scratch),
        input_output_aliases=alias or {},
        name=name,
        compiler_params=pltpu.CompilerParams(vmem_limit_bytes=mib << 20),
    )(*args)


def gelu_and_slope(v):
    cdf = 0.5 * (1.0 + lax.erf(v * 0.7071067811865476))
    density = jnp.exp(-0.5 * v * v) * 0.3989422804014327
    return v * cdf, cdf + v * density


def mean(v):
    return jnp.mean(v, axis=-1, keepdims=True)


def total_rows(v):
    return jnp.sum(v, axis=0, keepdims=True)


def normalise(v):
    centred = v - mean(v)
    inverse = lax.rsqrt(mean(centred * centred) + EPSILON)
    return centred * inverse, inverse


def norm_backward(grad_normed, normal, inverse, gain):
    scaled = grad_normed * gain
    return inverse * (scaled - mean(scaled) - normal * mean(scaled * normal))


def row_half(t):
    return t & 1


def lanes(parts):
    return jnp.concatenate(parts, axis=1)


def rows_of(parts):
    return jnp.concatenate(parts, axis=0)


def read(ref):
    return ref[...].astype(F32)


class Sizes:
    def __init__(self, nf, nt, inputs, qv_bias, fc1_weight):
        self.nf, self.nt = nf, nt
        _, self.half, self.width = inputs.shape
        self.shard = self.width // nf
        self.heads = qv_bias.shape[1]
        self.inner = self.heads * HD
        self.ff = fc1_weight.shape[1]
        self.pad = -self.half % 8
        self.padded = self.half + self.pad
        self.rows = 2 * self.padded
        self.part = self.width // 4
        self.chunk = self.part // 2
        self.tail = self.chunk // 4
        self.direct = nf == 4
        self.cols = 2 * self.ff + nt * self.inner
        self.early = 1280 if self.ff == 768 else self.ff
        self.wide = 2 * self.ff
        self.dense = self.rows * self.inner // 128

    def live_rows(self, h):
        return pl.ds(pl.multiple_of(h * self.padded, 8), self.half)

    def half_rows(self, h):
        return pl.ds(pl.multiple_of(h * self.padded, 8), self.padded)

    def half_of(self, c):
        return pl.ds(pl.multiple_of(c * self.chunk, 16), self.chunk)

    def squeeze(self, v):
        return rows_of([v[:, :128], lanes([v[: self.padded, 128:], v[self.padded :, 128:]])])

    def spread(self, v):
        tail = v[self.rows :]
        return lanes([v[: self.rows], rows_of([tail[:, :HD], tail[:, HD:]])])


def fetch(sources, copies, sem):
    moves = [pltpu.make_async_copy(s, d, sem.at[i]) for i, (s, d) in enumerate(zip(sources, copies))]
    for m in moves:
        m.start()
    for m in moves:
        m.wait()


def stage_kernel(z, up, down_t, out, rest, one, two, sem):
    fetch((up, down_t), (one, two), sem)
    first = z.early - z.ff
    out[:, : z.ff] = one[...]
    out[:, z.ff :] = two[:, :first]
    rest[...] = two[:, first:]


def pack_kernel(z, *refs):
    sources, (near, far, proj_t, proj_half) = refs[:10], refs[10:14]
    copies, sem = refs[14:24], refs[24]
    fetch(sources, copies, sem)
    qkv, proj, up_b, qv_b = copies[:4]
    vectors = copies[4:]
    c = lax.axis_index("ctx")
    whole = lanes([read(qkv.at[i]) for i in range(3)])
    near[: z.part, :] = whole.astype(LOW)
    far[: z.chunk, :] = jnp.where(c == 0, whole[: z.chunk], whole[z.chunk :]).astype(LOW)
    row = lax.broadcasted_iota(jnp.int32, (EXTRA, z.shard), 0)
    vec = jnp.zeros((EXTRA, z.shard), F32)
    for i, v in enumerate(vectors):
        vec = jnp.where(row == i, read(v).reshape(1, z.shard), vec)
    biases = read(qv_b)
    biases = rows_of([biases[h, i : i + 1] for h in range(z.heads) for i in range(2)])
    for out, at in ((near, z.part), (far, z.chunk)):
        out[at:, :] = jnp.zeros((EXTRA, 3 * z.inner), LOW)
        out[at:, : z.shard] = vec.astype(LOW)
        out[at : at + up_b.shape[0], UP_AT : UP_AT + up_b.shape[1]] = up_b[...]
        out[at : at + 2 * z.heads, QV_AT : QV_AT + biases.shape[1]] = biases.astype(LOW)
    turned = read(proj).T
    proj_t[...] = rows_of([turned, jnp.zeros((proj_t.shape[0] - z.part, z.inner), F32)]).astype(LOW)
    proj_half[...] = jnp.where(c == 0, turned[: z.chunk], turned[z.chunk :]).astype(LOW)


def cut_kernel(z, value, out):
    out[...] = value[z.half_of(lax.axis_index("ctx")), :]


def pair_kernel(first, second, out):
    pad = jnp.zeros((out.shape[1] - first.shape[0], out.shape[2]), F32)
    for i, value in enumerate((first, second)):
        out[i] = rows_of([read(value), pad]).astype(LOW)


def pack_rest_kernel(z, rest, proj_t, near_in, near_their, far_in, far_their, near, scratch):
    c, t = lax.axis_index("ctx"), lax.axis_index("tp")
    scratch[t] = proj_t[: z.part, :].astype(F32)
    scratch[t ^ (1 + 2 * c)] = near_in[: z.part, :].astype(F32)
    scratch[t ^ (3 - 2 * c)] = near_their[: z.part, :].astype(F32)
    scratch[t ^ 2, z.half_of(c), :] = far_in[: z.chunk, :].astype(F32)
    scratch[t ^ 2, z.half_of(1 - c), :] = far_their[: z.chunk, :].astype(F32)
    near[:, : 2 * z.ff - z.early] = rest[...]
    near[:, 2 * z.ff - z.early :] = lanes([scratch[i] for i in range(4)]).astype(LOW)


def frame_of(z, keep, received, frame):
    zero = jnp.zeros((z.pad, z.width), F32)
    pieces = []
    for ref in (keep, received):
        pieces.append(jnp.where(frame == 0, ref[:, 0, :].astype(F32), ref[:, 1, :].astype(F32)))
        pieces.append(zero)
    return rows_of(pieces)


def frame_kernel(z, keep, received, stream, normal, inverse, normal_their):
    c = lax.axis_index("ctx")
    values = frame_of(z, keep, received, c)
    stream[...] = values.astype(LOW)
    n, i = normalise(values)
    normal[...] = n
    inverse[...] = jnp.broadcast_to(i, inverse.shape)
    normal_their[...] = normalise(frame_of(z, received, keep, 1 - c))[0]


def cot_kernel(z, keep, received, out):
    c = lax.axis_index("ctx")
    out[0] = frame_of(z, keep, received, c).astype(LOW)
    out[1] = frame_of(z, received, keep, 1 - c).astype(LOW)


def attend_kernel(z, *refs):
    refs = list(refs)
    if z.direct:
        own, near, near_their, far, far_their = refs[:5]
        refs = refs[5:]
    else:
        whole, vec_in, up_in, qv_in = refs[:4]
        refs = refs[4:]
    normal, small, w_out, normed_out, act, attended, soft_out = refs[:7]
    if z.direct:
        c, b = lax.axis_index("ctx"), lax.axis_index("fsdp")
        gather = refs[7]
        for ref, at in ((own, b), (near, b ^ (1 + c)), (near_their, b ^ (2 - c))):
            w_out[at] = ref[: z.part, :]
            gather[at] = ref[z.part :, :].astype(F32)
        w_out[b ^ 3, z.half_of(c), :] = far[: z.chunk, :]
        w_out[b ^ 3, z.half_of(1 - c), :] = far_their[: z.chunk, :]
        gather[b ^ 3] = far[z.chunk :, :].astype(F32)
        blocks = [gather[i] for i in range(4)]
        w = HD // 4
        vec = lanes([g[:8, : z.shard] for g in blocks])
        up = lanes([g[: z.ff // HD, UP_AT : UP_AT + w] for g in blocks])
        qv = lanes([g[: 2 * z.heads, QV_AT : QV_AT + w] for g in blocks])
    else:
        w_out[...] = whole[...]
        vec, up, qv = vec_in[...], up_in[...], qv_in[...]
    up_row = lanes([up[i : i + 1] for i in range(z.ff // HD)])
    query_b = lanes([qv[2 * h : 2 * h + 1] for h in range(z.heads)])
    value_b = lanes([qv[2 * h + 1 : 2 * h + 2] for h in range(z.heads)])
    small[...] = vec
    small[6:7, : z.ff] = up_row
    normed = (normal[...] * vec[0:1] + vec[1:2]).astype(LOW)
    normed_out[...] = normed
    projected = dot(normed, w_out[...].reshape(z.width, 3 * z.inner), NN)
    n = z.inner
    query = ((projected[:, :n] + query_b) * QUERY_SCALE).astype(LOW)
    key = projected[:, n : 2 * n].astype(LOW)
    value = (projected[:, 2 * n :] + value_b).astype(LOW)
    act[0] = query
    act[1] = key
    act[2] = value
    place = lax.broadcasted_iota(jnp.int32, (z.rows, z.rows), 1)
    valid = (place < z.half) | ((place >= z.padded) & (place < z.padded + z.half))
    done = []
    for h in range(z.heads):
        cut = slice(h * HD, (h + 1) * HD)
        scores = jnp.where(valid, dot(query[:, cut], key[:, cut], NT), -1e30)
        exponent = jnp.exp(scores - jnp.max(scores, axis=-1, keepdims=True))
        soft = exponent * (1.0 / jnp.sum(exponent, axis=-1, keepdims=True))
        soft_out[h] = soft
        done.append(dot(soft.astype(LOW), value[:, cut], NN))
    attended[...] = z.squeeze(lanes(done)).astype(LOW)


def feed_kernel(z, *refs):
    refs = list(refs)
    if z.direct:
        feed, feed_in, feed_their, near, near_in, near_their, far, far_their, last_far, last_far_their = refs[:10]
        refs = refs[10:]
    else:
        whole = refs[0]
        refs = refs[1:]
    att = refs[:3]
    stream, cot, small = refs[3:6]
    w_out, middle_out, acts, part_out, own_att, small_out = refs[6:12]
    sends, heads = refs[12:-1], refs[-1]
    t = lax.axis_index("tp")
    if z.direct:
        c, b = lax.axis_index("ctx"), lax.axis_index("fsdp")
        mine, other = z.half_of(c), z.half_of(1 - c)
        first, last = pl.ds(0, z.early), pl.ds(z.early, z.cols - z.early)
        for at, one, two in ((b, feed, near), (b ^ (1 + c), feed_in, near_in), (b ^ (2 - c), feed_their, near_their)):
            w_out[at, :, first] = one[...]
            w_out[at, :, last] = two[...]
        w_out[b ^ 3, mine, first] = far[...]
        w_out[b ^ 3, other, first] = far_their[...]
        w_out[b ^ 3, mine, last] = last_far[...]
        w_out[b ^ 3, other, last] = last_far_their[...]
    else:
        w_out[...] = whole[...]
    n = z.inner
    w_up = w_out[:, :, : z.ff].reshape(z.width, z.ff)
    w_down_t = w_out[:, :, z.ff : 2 * z.ff].reshape(z.width, z.ff)
    w_proj_t = w_out[:, :, 2 * z.ff :].reshape(z.width, z.nt * n)
    grad_out_low = cot[0]
    grad_out = grad_out_low.astype(F32)
    heads[t] = z.spread(read(att[0]))
    heads[t ^ 3] = z.spread(read(att[1]))
    heads[t ^ 1] = z.spread(att[2][0].astype(F32)[: z.dense])
    heads[t ^ 2] = z.spread(att[2][1].astype(F32)[: z.dense])
    attended = lanes([heads[i] for i in range(z.nt)]).astype(LOW)
    acts[4] = attended
    branch = dot(attended, w_proj_t, NT)
    middle = stream[...].astype(F32) + branch + small[2:3]
    middle_out[...] = middle
    normal, inverse = normalise(middle)
    gain = small[3:4]
    normed = (normal * gain + small[4:5]).astype(LOW)
    acts[0] = normed
    hidden, slope = gelu_and_slope(dot(normed, w_up, NN) + small[6:7, : z.ff])
    acts[1] = hidden.astype(LOW)
    grad_pre = (dot(grad_out_low, w_down_t, NN) * slope).astype(LOW)
    acts[2] = grad_pre
    grad_normed = dot(grad_pre, w_up, NT)
    part = grad_out * (1.0 / z.nt) + norm_backward(grad_normed, normal, inverse, gain)
    part_out[...] = part
    low = part.astype(LOW)
    acts[3] = low
    grad_att = dot(low, w_proj_t, NN)
    for i in range(z.nt):
        heads[i] = grad_att[:, i * n : (i + 1) * n]
    own_att[...] = heads[t]
    for k in range(1, z.nt):
        sends[k - 1][...] = z.squeeze(heads[t ^ k]).astype(LOW)
    small_out[...] = jnp.zeros(small_out.shape, F32)
    small_out[2:3] = total_rows(part)
    small_out[3:4] = total_rows(grad_normed * normal)
    small_out[4:5] = total_rows(grad_normed)
    small_out[5:6] = total_rows(grad_out) * (1.0 / z.nt)
    small_out[6:7, : z.ff] = total_rows(grad_pre.astype(F32))


def down_kernel(z, acts, w, kept, sent, scratch):
    h = row_half(lax.axis_index("tp"))
    w_down_t = w[:, :, z.ff : 2 * z.ff].reshape(z.width, z.ff)
    scratch[...] = dot(acts[1], w_down_t, NT)
    kept[...] = scratch[z.live_rows(h), :]
    sent[...] = scratch[z.live_rows(1 - h), :].astype(LOW)


def add_low_kernel(kept, received, out):
    rows = kept.shape[0]
    out[:rows, :] = (kept[...] + read(received)).astype(LOW)
    if out.shape[0] > rows:
        out[rows:, :] = jnp.zeros((out.shape[0] - rows, out.shape[1]), LOW)


def store_own(z, value, at, keep):
    cols = pl.ds(at, value.shape[1])
    c, b = (lax.axis_index("ctx"), lax.axis_index("fsdp")) if z.direct else (0, 0)
    for j in range(4):
        whole = value[j * z.part : (j + 1) * z.part]
        if z.direct:
            keep[j ^ b, :, cols] = jnp.where(c == 0, whole[: z.chunk], whole[z.chunk :])
        else:
            keep[j, :, cols] = whole


def both_frames(left, right, left_their, right_their):
    return dot(left, right, TN) + dot(left_their, right_their, TN)


def feed_grad_kernel(z, acts, theirs, cot, keep):
    store_own(z, both_frames(acts[0], acts[2], theirs[0], theirs[2]), 0, keep)
    store_own(z, both_frames(cot[0], acts[1], cot[1], theirs[1]), z.ff, keep)


def proj_grad_kernel(z, acts, theirs, own, *refs):
    value = both_frames(acts[3], acts[4], theirs[3], theirs[4])
    if not z.direct:
        store_own(z, value, 0, own)
        return
    sends, keep = refs[:3], refs[3]
    store_own(z, value, 0, keep)
    own[...] = keep[0]
    for k in range(1, 4):
        sends[k - 1][...] = keep[k].astype(LOW)


def qkv_grad_kernel(z, normed, grads, normal_their, grads_their, small, keep):
    normed_their = (normal_their[...] * small[0:1] + small[1:2]).astype(LOW)
    store_own(z, both_frames(normed[...], grads[...], normed_their, grads_their[...]), 0, keep)


def split_kernel(keep, out, kept):
    c = lax.axis_index("ctx")
    n = keep.shape[2]
    for target, at, kind in ((out, (1 + c, 3), LOW), (kept, (0, 2 - c), F32)):
        for i in range(2):
            target[i, :, :n] = keep[at[i]].astype(kind)
            if target.shape[2] > n:
                target[i, :, n:] = jnp.zeros((target.shape[1], target.shape[2] - n), kind)


def by_half(mine, other):
    c = lax.axis_index("ctx")
    return rows_of([jnp.where(c == 0, mine, other), jnp.where(c == 0, other, mine)])


def feed_final_kernel(z, own, theirs, up, down):
    total = by_half(own[...], read(theirs))
    up[...] = total[:, : z.ff]
    down[...] = total[:, z.ff :]


def unfold(z, v):
    return rows_of([v[:, i * z.inner : (i + 1) * z.inner] for i in range(4)])


def fold(v):
    n = v.shape[0] // 4
    return lanes([v[i * n : (i + 1) * n] for i in range(4)])


def back_kernel(z, *refs):
    own_att, got = refs[0], refs[1 : z.nt]
    act, soft, w, normal, inverse, part, small, small_in = refs[z.nt : z.nt + 8]
    grads_out, qv_out, kept, sent, scratch = refs[z.nt + 8 :]
    t = lax.axis_index("tp")
    grad_att = (own_att[...] + z.spread(sum(read(g) for g in got))).astype(LOW)
    parts = [[], [], []]
    query, key, value = act[0], act[1], act[2]
    for h in range(z.heads):
        cut = slice(h * HD, (h + 1) * HD)
        ga = grad_att[:, cut]
        p = soft[h]
        grad_soft = dot(ga, value[:, cut], NT)
        delta = jnp.sum(p * grad_soft, axis=-1, keepdims=True)
        grad_scores = (p * (grad_soft - delta)).astype(LOW)
        parts[0].append((dot(grad_scores, key[:, cut], NN).astype(LOW).astype(F32) * QUERY_SCALE).astype(LOW))
        parts[1].append(dot(grad_scores, query[:, cut], TN).astype(LOW))
        parts[2].append(dot(p.astype(LOW), ga, TN).astype(LOW))
    grads = lanes(parts[0] + parts[1] + parts[2])
    grads_out[...] = grads
    n = z.inner
    qv_out[...] = total_rows(grads.astype(F32))
    grad_normed = dot(grads, w[...].reshape(z.width, 3 * n), NT)
    scratch[...] = part[...] + norm_backward(grad_normed, normal[...], inverse[:, :1], small[0:1])
    row = lax.broadcasted_iota(jnp.int32, (8, z.width), 0)
    vec = small_in[...]
    vec = jnp.where(row == 0, total_rows(grad_normed * normal[...]), vec)
    vec = jnp.where(row == 1, total_rows(grad_normed), vec)
    h = row_half(t)
    for at in (z.half, z.padded + z.half):
        scratch[at : at + 6, :] = vec[:6]
    kept[...] = scratch[z.half_rows(h), :]
    sent[...] = scratch[z.half_rows(1 - h), :].astype(LOW)


def out_total_kernel(z, own, received, middle, small, out):
    rows = z.live_rows(row_half(lax.axis_index("tp")))
    out[...] = (middle[rows, :] + read(own) + read(received) + small[5:6]).astype(LOW)


def in_pair_kernel(z, kept, received, own, *refs):
    parts, (out, proj_kept, scratch) = refs[:3], refs[3:]
    t = lax.axis_index("tp")
    proj = own[...] + sum(read(p) for p in parts)
    for i in range(z.nt):
        scratch[i] = fold(proj[:, i * z.inner : (i + 1) * z.inner])
    proj_kept[0] = scratch[t]
    proj_kept[1] = scratch[t ^ 1]
    out[...] = rows_of([kept[...] + read(received), scratch[t ^ 2], scratch[t ^ 3]]).astype(LOW)


def sum_rows_kernel(z, own, received, small, qv, *refs):
    if z.direct:
        proj_kept, out, vec, proj_own = refs
    else:
        out, vec = refs
    arrived = read(received)
    total = read(own)[: z.padded] + arrived[: z.padded]
    if z.direct:
        tail = arrived[z.padded :]
        proj_own[...] = proj_kept[0] + tail[: z.tail]
        out[...] = rows_of([total, proj_kept[1] + tail[z.tail :]]).astype(LOW)
    else:
        out[...] = total.astype(LOW)
    vec[...] = jnp.zeros(vec.shape, F32)
    vec[:6, :] = total[z.half : z.half + 6]
    vec[8:9, : z.ff] = small[6:7, : z.ff]
    vec[9:10, : 3 * z.inner] = qv[...]


def cross_kernel(kept, received, own, out):
    n = kept.shape[2]
    own[...] = kept[0] + received[0, :, :n].astype(F32)
    out[...] = (kept[1] + received[1, :, :n].astype(F32)).astype(LOW)


def cross_qkv_kernel(z, kept, received, small, own, out):
    own[...] = kept[0] + received[0].astype(F32)
    out[: z.chunk, :] = (kept[1] + received[1].astype(F32)).astype(LOW)
    out[z.chunk :, :] = small[...].astype(LOW)


def small_kernel(z, vec, near, cross, far, own, scratch):
    c, b = lax.axis_index("ctx"), lax.axis_index("fsdp")
    vectors = vec[...]
    up = rows_of([vectors[8:9, i * HD : (i + 1) * HD] for i in range(z.ff // HD)])
    pieces = []
    for h in range(z.heads):
        pieces.append(vectors[9:10, h * HD : (h + 1) * HD])
        pieces.append(vectors[9:10, 2 * z.inner + h * HD : 2 * z.inner + (h + 1) * HD])
    qv_rows = rows_of(pieces)
    scratch[...] = jnp.zeros(scratch.shape, F32)
    w = HD // 4
    for i in range(4):
        scratch[i, :8, : z.shard] = vectors[:8, i * z.shard : (i + 1) * z.shard]
        scratch[i, : z.ff // HD, UP_AT : UP_AT + w] = up[:, i * w : (i + 1) * w]
        scratch[i, : 2 * z.heads, QV_AT : QV_AT + w] = qv_rows[:, i * w : (i + 1) * w]
    near[...] = scratch[b ^ (1 + c)].astype(LOW)
    cross[...] = scratch[b ^ (2 - c)]
    far[...] = scratch[b ^ 3].astype(LOW)
    own[...] = scratch[b]


def halves_of(z, own, received):
    h = row_half(lax.axis_index("tp"))
    return jnp.where(h == 0, own, received), jnp.where(h == 0, received, own)


def swap_kernel(z, out_own, out_in, in_own, in_in, *refs):
    n = z.padded
    pad = jnp.zeros((z.pad, z.width), F32)
    out_mine, out_theirs = halves_of(z, read(out_own), read(out_in))
    arrived = read(in_in)
    in_mine, in_theirs = halves_of(z, read(in_own)[:n], arrived[:n])
    theirs = [out_theirs, pad, in_theirs]
    if z.direct:
        proj_own, mine, sent, proj = refs
        total = proj_own[...] + arrived[n:]
        proj[...] = total
        theirs.append(total)
    else:
        mine, sent = refs
    mine[0] = rows_of([out_mine, pad])
    mine[1] = in_mine
    sent[...] = rows_of(theirs).astype(LOW)


def last_kernel(z, feed, feed_in, qkv, qkv_in, small, near, far, feed_total, feed_sent, qkv_total, qkv_sent):
    value = feed[...] + read(feed_in)
    feed_total[...] = value
    feed_sent[...] = value.astype(LOW)
    value = qkv[...] + qkv_in[: z.chunk, :].astype(F32)
    tail = small[...] + read(near) + read(far) + qkv_in[z.chunk :, :].astype(F32)
    for out, kind in ((qkv_total, F32), (qkv_sent, LOW)):
        out[: z.chunk, :] = value.astype(kind)
        out[z.chunk :, :] = tail.astype(kind)


def qkv_final_kernel(z, own, theirs, qkv, up, qv, *vectors):
    both = by_half(own[: z.chunk, :], theirs[: z.chunk, :].astype(F32))
    for i in range(3):
        qkv[i] = both[:, i * z.inner : (i + 1) * z.inner]
    tail = own[z.chunk :, :] + theirs[z.chunk :, :].astype(F32)
    w = HD // 4
    up[...] = tail[: z.ff // HD, UP_AT : UP_AT + w]
    for h in range(z.heads):
        qv[h] = tail[2 * h : 2 * h + 2, QV_AT : QV_AT + w]
    for i, v in enumerate(vectors):
        v[...] = tail[i : i + 1, : z.shard].reshape(z.shard)


def place_kernel(z, mine, theirs, out, *scratch):
    c = lax.axis_index("ctx")
    target = scratch[0] if scratch else out
    mine, theirs = mine[: z.half], theirs[: z.half]
    target[:, 0, :] = jnp.where(c == 0, mine, theirs)
    target[:, 1, :] = jnp.where(c == 0, theirs, mine)
    if scratch:
        out[...] = target[...].astype(out.dtype)


def final_kernel(z, mine, theirs, *refs):
    arrived = read(theirs)
    if z.direct:
        proj_own, feed_own, feed_in, qkv_own, qkv_in, output, input_grad, proj, up, down, *rest = refs
        other = arrived[2 * z.padded :]
        proj[...] = by_half(unfold(z, proj_own[...]), unfold(z, other)).T
        feed_final_kernel(z, feed_own, feed_in, up, down)
        qkv_final_kernel(z, qkv_own, qkv_in, *rest[:-1])
        scratch = rest[-1]
    else:
        output, input_grad, scratch = refs
    place_kernel(z, mine[1], arrived[z.padded : 2 * z.padded], input_grad)
    place_kernel(z, mine[0], arrived[: z.padded], output, scratch)


def build(nf, nc, nt):
    def local(
        inputs,
        norm1_gain,
        norm1_bias,
        qkv_weight,
        qv_bias,
        proj_weight,
        proj_bias,
        norm2_gain,
        norm2_bias,
        fc1_weight,
        fc1_bias,
        fc2_weight,
        fc2_bias,
        cotangent,
    ):
        z = Sizes(nf, nt, inputs, qv_bias, fc1_weight)
        part = functools.partial
        rows, width, inner, ff, chunk = z.rows, z.width, z.inner, z.ff, z.chunk
        f = lax.axis_index("fsdp")
        tie = lax.optimization_barrier

        def other_core(value):
            return lax.ppermute(value, "ctx", [(0, 1), (1, 0)])

        def to_tp(value, k):
            return lax.ppermute(value, "tp", [(i, i ^ k) for i in range(nt)])

        def to_far(value):
            return lax.ppermute(value, "fsdp", [(i, i ^ 3) for i in range(nf)])

        def neighbours(value, order):
            pairs = [(2 * i + c, 2 * (i ^ order[c]) + c) for i in range(nf) for c in range(2)]
            return lax.ppermute(value, ("fsdp", "ctx"), pairs)

        def to_near(value):
            return neighbours(value, (1, 2))

        def to_cross(value):
            return neighbours(value, (2, 1))

        def proj_near(value):
            pairs = [(c * nt + i, c * nt + (i ^ (1 + 2 * c))) for i in range(nt) for c in range(2)]
            return lax.ppermute(value, ("ctx", "tp"), pairs)

        def pair_of(first, second):
            return call(pair_kernel, [shape((2,) + first.shape, LOW)], [first, second], name="pair")[0]

        qkv3 = qkv_weight.transpose(1, 0, 2)
        down_t = fc2_weight.T
        qv3 = qv_bias.transpose(1, 0, 2)
        x_raw, cot_raw = inputs.transpose(1, 0, 2), cotangent.transpose(1, 0, 2)
        vectors = [norm1_gain, norm1_bias, proj_bias, norm2_gain, norm2_bias, fc2_bias]

        x_recv = other_core(x_raw)
        cot_recv = other_core(cot_raw)
        def frames(x_recv, cot_recv):
            stream, normal_one, inverse_one, normal_their = call(
                part(frame_kernel, z),
                [shape((rows, width), LOW), shape((rows, width), F32), shape((rows, 128), F32), shape((rows, width), F32)],
                [x_raw, x_recv],
                name="frame",
            )
            (cot,) = call(part(cot_kernel, z), [shape((2, rows, width), LOW)], [cot_raw, cot_recv], name="cotangent")
            return stream, normal_one, inverse_one, normal_their, cot

        if z.direct:
            sources = [qkv3, proj_weight, fc1_bias, qv3] + vectors
            near, far, proj_t, proj_half = call(
                part(pack_kernel, z),
                [
                    shape((z.part + EXTRA, 3 * inner), LOW),
                    shape((chunk + EXTRA, 3 * inner), LOW),
                    shape((z.part + 104, inner), LOW),
                    shape((chunk, inner), LOW),
                ],
                sources,
                [pltpu.VMEM(s.shape, s.dtype) for s in sources] + [pltpu.SemaphoreType.DMA((len(sources),))],
                name="pack",
                mib=56,
                in_specs=[ANY] * len(sources),
            )
            near, far, proj_t, proj_half, x_recv, cot_recv = tie((near, far, proj_t, proj_half, x_recv, cot_recv))
            got = [to_near(near), to_far(far)]
            proj_got = [proj_near(proj_t), to_tp(proj_half, 2)]
            feed_own, feed_rest = call(
                part(stage_kernel, z),
                [shape((z.part, z.early), LOW), shape((z.part, 2 * ff - z.early), LOW)],
                [fc1_weight, down_t],
                [pltpu.VMEM((z.part, ff), LOW)] * 2 + [pltpu.SemaphoreType.DMA((2,))],
                name="stage",
                mib=20,
                in_specs=[ANY] * 2,
            )
            stream, normal_one, inverse_one, normal_their, cot = frames(x_recv, cot_recv)
            feed_in = to_near(feed_own)
            got, proj_got, feed_rest, stream, normal_one, inverse_one, normal_their, cot = tie(
                (got, proj_got, feed_rest, stream, normal_one, inverse_one, normal_their, cot)
            )
            shared = [other_core(g) for g in got]
            qkv_in = [near, got[0], shared[0], got[1], shared[1]]
            (rest_near,) = call(
                part(pack_rest_kernel, z),
                [shape((z.part, z.cols - z.early), LOW)],
                [feed_rest, proj_t, proj_got[0], other_core(proj_got[0]), proj_got[1], other_core(proj_got[1])],
                [pltpu.VMEM((nt, z.part, inner), F32)],
                name="pack_rest",
            )
            near_in = to_near(rest_near)
            far_in = []
            for value in (feed_in, near_in):
                (half,) = call(part(cut_kernel, z), [shape((chunk, value.shape[1]), LOW)], [value], name="cut")
                far_in.append(to_cross(half))
        else:
            stream, normal_one, inverse_one, normal_their, cot = frames(x_recv, cot_recv)
            whole = lax.all_gather(qkv3, "fsdp", axis=1, tiled=True)
            whole = whole.transpose(1, 0, 2).reshape(4, z.part, 3 * inner)
            vec = jnp.stack(vectors + [vectors[0]] * 2).astype(F32)
            qv_rows = qv3.reshape(2 * z.heads, -1).astype(F32)
            gathered = [lax.all_gather(v, "fsdp", axis=1, tiled=True) for v in (vec, fc1_bias.astype(F32), qv_rows)]
            qkv_in = [whole] + gathered
            proj_t = proj_weight.T
            rest = jnp.concatenate([fc1_weight, down_t, lax.all_gather(proj_t, "tp", axis=1, tiled=True)], 1)
            rest_in = [lax.all_gather(rest, "fsdp", axis=0, tiled=True).reshape(4, z.part, z.cols)]

        small, w_qkv, normed_one, act, attended, soft = call(
            part(attend_kernel, z),
            [
                shape((8, width), F32),
                shape((4, z.part, 3 * inner), LOW),
                shape((rows, width), LOW),
                shape((3, rows, inner), LOW),
                shape((z.dense, 128), LOW),
                shape((z.heads, rows, rows), F32),
            ],
            qkv_in + [normal_one],
            [pltpu.VMEM((4, EXTRA, 3 * inner), F32)] if z.direct else [],
            name="attend",
        )
        att_one = to_tp(attended, 3)
        (att_two,) = call(pair_kernel, [shape((2, z.dense + 16, 128), LOW)], [attended, att_one], name="pair")
        att_two = to_tp(att_two, 1)
        if z.direct:
            att_two, far_in = tie((att_two, far_in))
            rest_in = [feed_own, feed_in, other_core(feed_in), rest_near, near_in, other_core(near_in)]
            rest_in += [far_in[0], other_core(far_in[0]), far_in[1], other_core(far_in[1])]

        (w_rest, middle, acts, part_middle, own_att, small_two, *att_sends) = (
            call(
                part(feed_kernel, z),
                [
                    shape((4, z.part, z.cols), LOW),
                    shape((rows, width), F32),
                    shape((5, rows, width), LOW),
                    shape((rows, width), F32),
                    shape((rows, inner), F32),
                    shape((8, width), F32),
                ]
                + [shape((z.dense, 128), LOW)] * (nt - 1),
                rest_in + [attended, att_one, att_two, stream, cot, small],
                [pltpu.VMEM((nt, rows, inner), F32)],
                name="feed",
            )
        )
        att_got = [to_tp(att_sends[k - 1], k) for k in (3, 2, 1)]
        acts_their = other_core(acts)
        kept_rows = chunk if z.direct else z.part
        (keep,) = call(
            part(feed_grad_kernel, z),
            [shape((4, kept_rows, 2 * ff), F32)],
            [acts, acts_their, cot],
            name="feed_grad",
        )
        proj_own, *sends = call(
            part(proj_grad_kernel, z),
            [shape((chunk, nt * inner), F32)] + [shape((chunk, nt * inner), LOW)] * 3
            if z.direct
            else [shape((4, z.part, nt * inner), F32)],
            [acts, acts_their],
            [pltpu.VMEM((4, chunk, nt * inner), F32)] if z.direct else [],
            name="proj_grad",
        )
        proj_full = proj_own
        out_kept, out_sent = call(
            part(down_kernel, z),
            [shape((z.half, width), F32), shape((z.half, width), LOW)],
            [acts, w_rest],
            [pltpu.VMEM((rows, width), F32)],
            name="down",
        )
        out_one = to_tp(out_sent, 1)
        if z.direct:
            grad_sent, grad_kept = call(
                split_kernel,
                [shape((2, chunk, z.wide), LOW), shape((2, chunk, 2 * ff), F32)],
                [keep],
                name="split",
            )
            grad_in = to_near(grad_sent)
            att_got, out_one, grad_kept, proj_own, sends = tie((att_got, out_one, grad_kept, proj_own, sends))
            proj_in = [lax.ppermute(sends[k - 1], "fsdp", [(i, i ^ k) for i in range(nf)]) for k in (3, 1)]
        (out_low,) = call(add_low_kernel, [shape((z.half, width), LOW)], [out_kept, out_one], name="out_pair")
        out_two = to_tp(out_low, 2)

        grads, qv_sum, in_kept, in_sent = call(
            part(back_kernel, z),
            [
                shape((rows, 3 * inner), LOW),
                shape((1, 3 * inner), F32),
                shape((z.padded, width), F32),
                shape((z.padded, width), LOW),
            ],
            [own_att] + att_got + [act, soft, w_qkv, normal_one, inverse_one, part_middle, small, small_two],
            [pltpu.VMEM((rows, width), F32)],
            name="back",
        )
        in_one = to_tp(in_sent, 1)
        grads_their = other_core(grads)
        if z.direct:
            grads_their, last_send = tie((grads_their, sends[1]))
            proj_in.append(lax.ppermute(last_send, "fsdp", [(i, i ^ 2) for i in range(nf)]))
        (keep_qkv,) = call(
            part(qkv_grad_kernel, z),
            [shape((4, kept_rows, 3 * inner), F32)],
            [normed_one, grads, normal_their, grads_their, small],
            name="qkv_grad",
        )
        extra = z.tail if z.direct else 0
        if z.direct:
            in_one, out_two, proj_in, keep_qkv = tie((in_one, out_two, proj_in, keep_qkv))
            in_low, proj_kept = call(
                part(in_pair_kernel, z),
                [shape((z.padded + 2 * extra, width), LOW), shape((2, extra, width), F32)],
                [in_kept, in_one, proj_own] + proj_in,
                [pltpu.VMEM((nt, extra, width), F32)],
                name="in_pair",
            )
            qkv_sent, qkv_kept = call(
                split_kernel,
                [shape((2, chunk, 3 * inner), LOW), shape((2, chunk, 3 * inner), F32)],
                [keep_qkv],
                name="split_qkv",
            )
            qkv_in = to_near(qkv_sent)
        else:
            (in_low,) = call(add_low_kernel, [shape((z.padded, width), LOW)], [in_kept, in_one], name="in_pair")
        in_two = to_tp(in_low, 2)
        (out_low,) = call(
            part(out_total_kernel, z), [shape((z.half, width), LOW)], [out_low, out_two, middle, small], name="out_total"
        )
        out_in = to_tp(out_low, 1)
        if z.direct:
            grad_own, cross = call(
                cross_kernel,
                [shape((chunk, 2 * ff), F32), shape((chunk, 2 * ff), LOW)],
                [grad_kept, grad_in],
                name="cross",
            )
            cross = to_cross(cross)
            in_two, out_in, qkv_in = tie((in_two, out_in, qkv_in))
        in_low, vec, *proj_own = call(
            part(sum_rows_kernel, z),
            [shape((z.padded + extra, width), LOW), shape((VEC_ROWS, width), F32)]
            + ([shape((extra, width), F32)] if extra else []),
            [in_low, in_two, small_two, qv_sum] + ([proj_kept] if extra else []),
            name="sum_rows",
        )
        in_in = to_tp(in_low, 1)
        proj_all = []
        if z.direct:
            near, side, far, small_own = call(
                part(small_kernel, z),
                [shape((EXTRA, 3 * inner), LOW), shape((EXTRA, 3 * inner), F32)] * 2,
                [vec],
                [pltpu.VMEM((4, EXTRA, 3 * inner), F32)],
                name="small",
            )
            qkv_own, qkv_sent = call(
                part(cross_qkv_kernel, z),
                [shape((chunk, 3 * inner), F32), shape((chunk + EXTRA, 3 * inner), LOW)],
                [qkv_kept, qkv_in, side],
                name="cross_qkv",
            )
            qkv_in = to_cross(qkv_sent)
            far = to_far(far)
            near = to_near(near)
            in_in, cross, qkv_in, near, far = tie((in_in, cross, qkv_in, near, far))
            proj_all = proj_own
            feed_own, feed_sent, qkv_own, qkv_sent = call(
                part(last_kernel, z),
                [
                    shape((chunk, 2 * ff), F32),
                    shape((chunk, 2 * ff), LOW),
                    shape((chunk + EXTRA, 3 * inner), F32),
                    shape((chunk + EXTRA, 3 * inner), LOW),
                ],
                [grad_own, cross, qkv_own, qkv_in, small_own, near, far],
                name="last",
            )
            feed_in, qkv_in = other_core(feed_sent), other_core(qkv_sent)
        mine, theirs, *proj_own = call(
            part(swap_kernel, z),
            [shape((2, z.padded, width), F32), shape((rows + (z.tail if proj_all else 0), width), LOW)]
            + ([shape((z.tail, width), F32)] if proj_all else []),
            [out_low, out_in, in_low, in_in] + proj_all,
            name="swap",
        )
        theirs = other_core(theirs)
        results = [shape((z.half, 2, width), LOW), shape((z.half, 2, width), F32)]
        scratch = [pltpu.VMEM((z.half, 2, width), F32)]
        if z.direct:
            output, input_grad, proj_grad, fc1_grad, fc2_grad, qkv_grad, up_grad, qv_grad, *vec_grads = call(
                part(final_kernel, z),
                results
                + [
                    shape((inner, z.shard), F32),
                    shape((z.shard, ff), F32),
                    shape((z.shard, ff), F32),
                    shape((3, z.shard, inner), F32),
                    shape(fc1_bias.shape, F32),
                    shape(qv3.shape, F32),
                ]
                + [shape((z.shard,), F32)] * 6,
                [mine, theirs, proj_own[0], feed_own, feed_in, qkv_own, qkv_in],
                scratch,
                name="final",
            )
        else:
            output, input_grad = call(part(final_kernel, z), results, [mine, theirs], scratch, name="final")

            def scatter(value):
                value = value.reshape(width, -1).astype(LOW)
                return lax.psum_scatter(value, "fsdp", scatter_dimension=0, tiled=True).astype(F32)

            total = scatter(keep)
            fc1_grad, fc2_grad = total[:, :ff], total[:, ff:]
            qkv_grad = scatter(keep_qkv).reshape(z.shard, 3, inner).transpose(1, 0, 2)
            proj_grad = scatter(proj_full).astype(LOW)
            proj_grad = lax.psum_scatter(proj_grad, "tp", scatter_dimension=1, tiled=True).astype(F32).T

            def own_columns(value):
                value = lax.psum(value, ("fsdp", "ctx"))
                return lax.dynamic_slice_in_dim(value, f * (value.shape[1] // nf), value.shape[1] // nf, 1)

            vec_grads = own_columns(vec[:6])
            up_grad = own_columns(vec[8, :ff].reshape(-1, HD))
            qv_grad = vec[9, : 3 * inner].reshape(3, z.heads, HD)[0::2].transpose(1, 0, 2)
            qv_grad = own_columns(qv_grad.reshape(2 * z.heads, HD)).reshape(qv3.shape)
        return (
            output.transpose(1, 0, 2),
            input_grad.transpose(1, 0, 2),
            vec_grads[0],
            vec_grads[1],
            qkv_grad.transpose(1, 0, 2),
            qv_grad.transpose(1, 0, 2),
            proj_grad,
            vec_grads[2],
            vec_grads[3],
            vec_grads[4],
            fc1_grad,
            up_grad,
            fc2_grad.T,
            vec_grads[5],
        )

    return local


def solution(mesh):
    sizes = mesh.shape
    return jax.shard_map(
        build(sizes["fsdp"], sizes["ctx"], sizes["tp"]),
        mesh=mesh,
        in_specs=(
            P("fsdp", "ctx", None),
            P("fsdp"),
            P("fsdp"),
            P("fsdp", None, "tp"),
            P(None, "tp", "fsdp"),
            P("tp", "fsdp"),
            P("fsdp"),
            P("fsdp"),
            P("fsdp"),
            P("fsdp", "tp"),
            P("tp", "fsdp"),
            P("tp", "fsdp"),
            P("fsdp"),
            P("fsdp", "ctx", None),
        ),
        out_specs=(
            P("fsdp", "ctx", None),
            P("fsdp", "ctx", None),
            P("fsdp"),
            P("fsdp"),
            P("fsdp", None, "tp"),
            P(None, "tp", "fsdp"),
            P("tp", "fsdp"),
            P("fsdp"),
            P("fsdp"),
            P("fsdp"),
            P("fsdp", "tp"),
            P("tp", "fsdp"),
            P("tp", "fsdp"),
            P("fsdp"),
        ),
        check_vma=False,
    )
```

```python
import functools

import jax
import jax.numpy as jnp
from jax import lax
from jax.experimental import pallas as pl
from jax.experimental.pallas import tpu as pltpu
from jax.sharding import PartitionSpec as P

HD = 64
EPSILON = 1e-06
QUERY_SCALE = 0.125
F32 = jnp.float32
LOW = jnp.bfloat16
NN = ((1,), (0,))
NT = ((1,), (1,))
TN = ((0,), (0,))
VMEM = pl.BlockSpec(memory_space=pltpu.VMEM)
ANY = pl.BlockSpec(memory_space=pl.ANY)
EXTRA = 16
VEC_ROWS = 16
UP_AT, QV_AT = 256, 384


def dot(left, right, dims):
    return lax.dot_general(left, right, (dims, ((), ())), preferred_element_type=F32)


def shape(dims, kind):
    return jax.ShapeDtypeStruct(tuple(dims), kind)


def call(kernel, outs, args, scratch=(), name=None, mib=20, in_specs=None, alias=None):
    return pl.pallas_call(
        kernel,
        out_shape=tuple(outs),
        in_specs=in_specs or [VMEM] * len(args),
        out_specs=tuple([VMEM] * len(outs)),
        scratch_shapes=list(scratch),
        input_output_aliases=alias or {},
        name=name,
        compiler_params=pltpu.CompilerParams(vmem_limit_bytes=mib << 20),
    )(*args)


def gelu_and_slope(v):
    cdf = 0.5 * (1.0 + lax.erf(v * 0.7071067811865476))
    density = jnp.exp(-0.5 * v * v) * 0.3989422804014327
    return v * cdf, cdf + v * density


def mean(v):
    return jnp.mean(v, axis=-1, keepdims=True)


def total_rows(v):
    return jnp.sum(v, axis=0, keepdims=True)


def normalise(v):
    centred = v - mean(v)
    inverse = lax.rsqrt(mean(centred * centred) + EPSILON)
    return centred * inverse, inverse


def norm_backward(grad_normed, normal, inverse, gain):
    scaled = grad_normed * gain
    return inverse * (scaled - mean(scaled) - normal * mean(scaled * normal))


def row_half(t):
    return t & 1


def lanes(parts):
    return jnp.concatenate(parts, axis=1)


def rows_of(parts):
    return jnp.concatenate(parts, axis=0)


def read(ref):
    return ref[...].astype(F32)


class Sizes:
    def __init__(self, nf, nt, inputs, qv_bias, fc1_weight):
        self.nf, self.nt = nf, nt
        _, self.half, self.width = inputs.shape
        self.shard = self.width // nf
        self.heads = qv_bias.shape[1]
        self.inner = self.heads * HD
        self.ff = fc1_weight.shape[1]
        self.pad = -self.half % 8
        self.padded = self.half + self.pad
        self.rows = 2 * self.padded
        self.part = self.width // 4
        self.chunk = self.part // 2
        self.tail = self.chunk // 4
        self.direct = nf == 4
        self.cols = 2 * self.ff + nt * self.inner
        self.early = 1280 if self.ff == 768 else self.ff
        self.wide = 2 * self.ff
        self.dense = self.rows * self.inner // 128

    def live_rows(self, h):
        return pl.ds(pl.multiple_of(h * self.padded, 8), self.half)

    def half_rows(self, h):
        return pl.ds(pl.multiple_of(h * self.padded, 8), self.padded)

    def half_of(self, c):
        return pl.ds(pl.multiple_of(c * self.chunk, 16), self.chunk)

    def squeeze(self, v):
        return rows_of([v[:, :128], lanes([v[: self.padded, 128:], v[self.padded :, 128:]])])

    def spread(self, v):
        tail = v[self.rows :]
        return lanes([v[: self.rows], rows_of([tail[:, :HD], tail[:, HD:]])])


def fetch(sources, copies, sem):
    moves = [pltpu.make_async_copy(s, d, sem.at[i]) for i, (s, d) in enumerate(zip(sources, copies))]
    for m in moves:
        m.start()
    for m in moves:
        m.wait()


def stage_kernel(z, up, down_t, out, rest, one, two, sem):
    fetch((up, down_t), (one, two), sem)
    first = z.early - z.ff
    out[:, : z.ff] = one[...]
    out[:, z.ff :] = two[:, :first]
    rest[...] = two[:, first:]


def pack_kernel(z, *refs):
    sources, (near, far, proj_t, proj_half) = refs[:10], refs[10:14]
    copies, sem = refs[14:24], refs[24]
    fetch(sources, copies, sem)
    qkv, proj, up_b, qv_b = copies[:4]
    vectors = copies[4:]
    c = lax.axis_index("ctx")
    whole = lanes([read(qkv.at[i]) for i in range(3)])
    near[: z.part, :] = whole.astype(LOW)
    far[: z.chunk, :] = jnp.where(c == 0, whole[: z.chunk], whole[z.chunk :]).astype(LOW)
    row = lax.broadcasted_iota(jnp.int32, (EXTRA, z.shard), 0)
    vec = jnp.zeros((EXTRA, z.shard), F32)
    for i, v in enumerate(vectors):
        vec = jnp.where(row == i, read(v).reshape(1, z.shard), vec)
    biases = read(qv_b)
    biases = rows_of([biases[h, i : i + 1] for h in range(z.heads) for i in range(2)])
    for out, at in ((near, z.part), (far, z.chunk)):
        out[at:, :] = jnp.zeros((EXTRA, 3 * z.inner), LOW)
        out[at:, : z.shard] = vec.astype(LOW)
        out[at : at + up_b.shape[0], UP_AT : UP_AT + up_b.shape[1]] = up_b[...]
        out[at : at + 2 * z.heads, QV_AT : QV_AT + biases.shape[1]] = biases.astype(LOW)
    turned = read(proj).T
    proj_t[...] = rows_of([turned, jnp.zeros((proj_t.shape[0] - z.part, z.inner), F32)]).astype(LOW)
    proj_half[...] = jnp.where(c == 0, turned[: z.chunk], turned[z.chunk :]).astype(LOW)


def cut_kernel(z, value, out):
    out[...] = value[z.half_of(lax.axis_index("ctx")), :]


def pair_kernel(first, second, out):
    pad = jnp.zeros((out.shape[1] - first.shape[0], out.shape[2]), F32)
    for i, value in enumerate((first, second)):
        out[i] = rows_of([read(value), pad]).astype(LOW)


def pack_rest_kernel(z, rest, proj_t, near_in, near_their, far_in, far_their, near, scratch):
    c, t = lax.axis_index("ctx"), lax.axis_index("tp")
    scratch[t] = proj_t[: z.part, :].astype(F32)
    scratch[t ^ (1 + 2 * c)] = near_in[: z.part, :].astype(F32)
    scratch[t ^ (3 - 2 * c)] = near_their[: z.part, :].astype(F32)
    scratch[t ^ 2, z.half_of(c), :] = far_in[: z.chunk, :].astype(F32)
    scratch[t ^ 2, z.half_of(1 - c), :] = far_their[: z.chunk, :].astype(F32)
    near[:, : 2 * z.ff - z.early] = rest[...]
    near[:, 2 * z.ff - z.early :] = lanes([scratch[i] for i in range(4)]).astype(LOW)


def frame_of(z, keep, received, frame):
    zero = jnp.zeros((z.pad, z.width), F32)
    pieces = []
    for ref in (keep, received):
        pieces.append(jnp.where(frame == 0, ref[:, 0, :].astype(F32), ref[:, 1, :].astype(F32)))
        pieces.append(zero)
    return rows_of(pieces)


def frame_kernel(z, keep, received, stream, normal, inverse, normal_their):
    c = lax.axis_index("ctx")
    values = frame_of(z, keep, received, c)
    stream[...] = values.astype(LOW)
    n, i = normalise(values)
    normal[...] = n
    inverse[...] = jnp.broadcast_to(i, inverse.shape)
    normal_their[...] = normalise(frame_of(z, received, keep, 1 - c))[0]


def cot_kernel(z, keep, received, out):
    c = lax.axis_index("ctx")
    out[0] = frame_of(z, keep, received, c).astype(LOW)
    out[1] = frame_of(z, received, keep, 1 - c).astype(LOW)


def attend_kernel(z, *refs):
    refs = list(refs)
    if z.direct:
        own, near, near_their, far, far_their = refs[:5]
        refs = refs[5:]
    else:
        whole, vec_in, up_in, qv_in = refs[:4]
        refs = refs[4:]
    normal, small, w_out, normed_out, act, attended, soft_out = refs[:7]
    if z.direct:
        c, b = lax.axis_index("ctx"), lax.axis_index("fsdp")
        gather = refs[7]
        for ref, at in ((own, b), (near, b ^ (1 + c)), (near_their, b ^ (2 - c))):
            w_out[at] = ref[: z.part, :]
            gather[at] = ref[z.part :, :].astype(F32)
        w_out[b ^ 3, z.half_of(c), :] = far[: z.chunk, :]
        w_out[b ^ 3, z.half_of(1 - c), :] = far_their[: z.chunk, :]
        gather[b ^ 3] = far[z.chunk :, :].astype(F32)
        blocks = [gather[i] for i in range(4)]
        w = HD // 4
        vec = lanes([g[:8, : z.shard] for g in blocks])
        up = lanes([g[: z.ff // HD, UP_AT : UP_AT + w] for g in blocks])
        qv = lanes([g[: 2 * z.heads, QV_AT : QV_AT + w] for g in blocks])
    else:
        w_out[...] = whole[...]
        vec, up, qv = vec_in[...], up_in[...], qv_in[...]
    up_row = lanes([up[i : i + 1] for i in range(z.ff // HD)])
    query_b = lanes([qv[2 * h : 2 * h + 1] for h in range(z.heads)])
    value_b = lanes([qv[2 * h + 1 : 2 * h + 2] for h in range(z.heads)])
    small[...] = vec
    small[6:7, : z.ff] = up_row
    normed = (normal[...] * vec[0:1] + vec[1:2]).astype(LOW)
    normed_out[...] = normed
    projected = dot(normed, w_out[...].reshape(z.width, 3 * z.inner), NN)
    n = z.inner
    query = ((projected[:, :n] + query_b) * QUERY_SCALE).astype(LOW)
    key = projected[:, n : 2 * n].astype(LOW)
    value = (projected[:, 2 * n :] + value_b).astype(LOW)
    act[0] = query
    act[1] = key
    act[2] = value
    place = lax.broadcasted_iota(jnp.int32, (z.rows, z.rows), 1)
    valid = (place < z.half) | ((place >= z.padded) & (place < z.padded + z.half))
    done = []
    for h in range(z.heads):
        cut = slice(h * HD, (h + 1) * HD)
        scores = jnp.where(valid, dot(query[:, cut], key[:, cut], NT), -1e30)
        exponent = jnp.exp(scores - jnp.max(scores, axis=-1, keepdims=True))
        soft = exponent * (1.0 / jnp.sum(exponent, axis=-1, keepdims=True))
        soft_out[h] = soft
        done.append(dot(soft.astype(LOW), value[:, cut], NN))
    attended[...] = z.squeeze(lanes(done)).astype(LOW)


def feed_kernel(z, *refs):
    refs = list(refs)
    if z.direct:
        feed, feed_in, feed_their, near, near_in, near_their, far, far_their, last_far, last_far_their = refs[:10]
        refs = refs[10:]
    else:
        whole = refs[0]
        refs = refs[1:]
    att = refs[:3]
    stream, cot, small = refs[3:6]
    w_out, middle_out, acts, part_out, own_att, small_out = refs[6:12]
    sends, heads = refs[12:-1], refs[-1]
    t = lax.axis_index("tp")
    if z.direct:
        c, b = lax.axis_index("ctx"), lax.axis_index("fsdp")
        mine, other = z.half_of(c), z.half_of(1 - c)
        first, last = pl.ds(0, z.early), pl.ds(z.early, z.cols - z.early)
        for at, one, two in ((b, feed, near), (b ^ (1 + c), feed_in, near_in), (b ^ (2 - c), feed_their, near_their)):
            w_out[at, :, first] = one[...]
            w_out[at, :, last] = two[...]
        w_out[b ^ 3, mine, first] = far[...]
        w_out[b ^ 3, other, first] = far_their[...]
        w_out[b ^ 3, mine, last] = last_far[...]
        w_out[b ^ 3, other, last] = last_far_their[...]
    else:
        w_out[...] = whole[...]
    n = z.inner
    w_up = w_out[:, :, : z.ff].reshape(z.width, z.ff)
    w_down_t = w_out[:, :, z.ff : 2 * z.ff].reshape(z.width, z.ff)
    w_proj_t = w_out[:, :, 2 * z.ff :].reshape(z.width, z.nt * n)
    grad_out_low = cot[0]
    grad_out = grad_out_low.astype(F32)
    heads[t] = z.spread(read(att[0]))
    heads[t ^ 3] = z.spread(read(att[1]))
    heads[t ^ 1] = z.spread(att[2][0].astype(F32)[: z.dense])
    heads[t ^ 2] = z.spread(att[2][1].astype(F32)[: z.dense])
    attended = lanes([heads[i] for i in range(z.nt)]).astype(LOW)
    acts[4] = attended
    branch = dot(attended, w_proj_t, NT)
    middle = stream[...].astype(F32) + branch + small[2:3]
    middle_out[...] = middle
    normal, inverse = normalise(middle)
    gain = small[3:4]
    normed = (normal * gain + small[4:5]).astype(LOW)
    acts[0] = normed
    hidden, slope = gelu_and_slope(dot(normed, w_up, NN) + small[6:7, : z.ff])
    acts[1] = hidden.astype(LOW)
    grad_pre = (dot(grad_out_low, w_down_t, NN) * slope).astype(LOW)
    acts[2] = grad_pre
    grad_normed = dot(grad_pre, w_up, NT)
    part = grad_out * (1.0 / z.nt) + norm_backward(grad_normed, normal, inverse, gain)
    part_out[...] = part
    low = part.astype(LOW)
    acts[3] = low
    grad_att = dot(low, w_proj_t, NN)
    for i in range(z.nt):
        heads[i] = grad_att[:, i * n : (i + 1) * n]
    own_att[...] = heads[t]
    for k in range(1, z.nt):
        sends[k - 1][...] = z.squeeze(heads[t ^ k]).astype(LOW)
    small_out[...] = jnp.zeros(small_out.shape, F32)
    small_out[2:3] = total_rows(part)
    small_out[3:4] = total_rows(grad_normed * normal)
    small_out[4:5] = total_rows(grad_normed)
    small_out[5:6] = total_rows(grad_out) * (1.0 / z.nt)
    small_out[6:7, : z.ff] = total_rows(grad_pre.astype(F32))


def down_kernel(z, acts, w, kept, sent, scratch):
    h = row_half(lax.axis_index("tp"))
    w_down_t = w[:, :, z.ff : 2 * z.ff].reshape(z.width, z.ff)
    scratch[...] = dot(acts[1], w_down_t, NT)
    kept[...] = scratch[z.live_rows(h), :]
    sent[...] = scratch[z.live_rows(1 - h), :].astype(LOW)


def add_low_kernel(kept, received, out):
    rows = kept.shape[0]
    out[:rows, :] = (kept[...] + read(received)).astype(LOW)
    if out.shape[0] > rows:
        out[rows:, :] = jnp.zeros((out.shape[0] - rows, out.shape[1]), LOW)


def store_own(z, value, at, keep):
    cols = pl.ds(at, value.shape[1])
    c, b = (lax.axis_index("ctx"), lax.axis_index("fsdp")) if z.direct else (0, 0)
    for j in range(4):
        whole = value[j * z.part : (j + 1) * z.part]
        if z.direct:
            keep[j ^ b, :, cols] = jnp.where(c == 0, whole[: z.chunk], whole[z.chunk :])
        else:
            keep[j, :, cols] = whole


def both_frames(left, right, left_their, right_their):
    return dot(left, right, TN) + dot(left_their, right_their, TN)


def feed_grad_kernel(z, acts, theirs, cot, keep):
    store_own(z, both_frames(acts[0], acts[2], theirs[0], theirs[2]), 0, keep)
    store_own(z, both_frames(cot[0], acts[1], cot[1], theirs[1]), z.ff, keep)


def proj_grad_kernel(z, acts, theirs, own, *refs):
    value = both_frames(acts[3], acts[4], theirs[3], theirs[4])
    if not z.direct:
        store_own(z, value, 0, own)
        return
    sends, keep = refs[:3], refs[3]
    store_own(z, value, 0, keep)
    own[...] = keep[0]
    for k in range(1, 4):
        sends[k - 1][...] = keep[k].astype(LOW)


def qkv_grad_kernel(z, normed, grads, normal_their, grads_their, small, keep):
    normed_their = (normal_their[...] * small[0:1] + small[1:2]).astype(LOW)
    store_own(z, both_frames(normed[...], grads[...], normed_their, grads_their[...]), 0, keep)


def split_kernel(keep, out, kept):
    c = lax.axis_index("ctx")
    n = keep.shape[2]
    for target, at, kind in ((out, (1 + c, 3), LOW), (kept, (0, 2 - c), F32)):
        for i in range(2):
            target[i, :, :n] = keep[at[i]].astype(kind)
            if target.shape[2] > n:
                target[i, :, n:] = jnp.zeros((target.shape[1], target.shape[2] - n), kind)


def by_half(mine, other):
    c = lax.axis_index("ctx")
    return rows_of([jnp.where(c == 0, mine, other), jnp.where(c == 0, other, mine)])


def feed_final_kernel(z, own, theirs, up, down):
    total = by_half(own[...], read(theirs))
    up[...] = total[:, : z.ff]
    down[...] = total[:, z.ff :]


def unfold(z, v):
    return rows_of([v[:, i * z.inner : (i + 1) * z.inner] for i in range(4)])


def fold(v):
    n = v.shape[0] // 4
    return lanes([v[i * n : (i + 1) * n] for i in range(4)])


def back_kernel(z, *refs):
    own_att, got = refs[0], refs[1 : z.nt]
    act, soft, w, normal, inverse, part, small, small_in = refs[z.nt : z.nt + 8]
    grads_out, qv_out, kept, sent, scratch = refs[z.nt + 8 :]
    t = lax.axis_index("tp")
    grad_att = (own_att[...] + z.spread(sum(read(g) for g in got))).astype(LOW)
    parts = [[], [], []]
    query, key, value = act[0], act[1], act[2]
    for h in range(z.heads):
        cut = slice(h * HD, (h + 1) * HD)
        ga = grad_att[:, cut]
        p = soft[h]
        grad_soft = dot(ga, value[:, cut], NT)
        delta = jnp.sum(p * grad_soft, axis=-1, keepdims=True)
        grad_scores = (p * (grad_soft - delta)).astype(LOW)
        parts[0].append((dot(grad_scores, key[:, cut], NN).astype(LOW).astype(F32) * QUERY_SCALE).astype(LOW))
        parts[1].append(dot(grad_scores, query[:, cut], TN).astype(LOW))
        parts[2].append(dot(p.astype(LOW), ga, TN).astype(LOW))
    grads = lanes(parts[0] + parts[1] + parts[2])
    grads_out[...] = grads
    n = z.inner
    qv_out[...] = total_rows(grads.astype(F32))
    grad_normed = dot(grads, w[...].reshape(z.width, 3 * n), NT)
    scratch[...] = part[...] + norm_backward(grad_normed, normal[...], inverse[:, :1], small[0:1])
    row = lax.broadcasted_iota(jnp.int32, (8, z.width), 0)
    vec = small_in[...]
    vec = jnp.where(row == 0, total_rows(grad_normed * normal[...]), vec)
    vec = jnp.where(row == 1, total_rows(grad_normed), vec)
    h = row_half(t)
    for at in (z.half, z.padded + z.half):
        scratch[at : at + 6, :] = vec[:6]
    kept[...] = scratch[z.half_rows(h), :]
    sent[...] = scratch[z.half_rows(1 - h), :].astype(LOW)


def out_total_kernel(z, own, received, middle, small, out):
    rows = z.live_rows(row_half(lax.axis_index("tp")))
    out[...] = (middle[rows, :] + read(own) + read(received) + small[5:6]).astype(LOW)


def in_pair_kernel(z, kept, received, own, *refs):
    parts, (out, proj_kept, scratch) = refs[:3], refs[3:]
    t = lax.axis_index("tp")
    proj = own[...] + sum(read(p) for p in parts)
    for i in range(z.nt):
        scratch[i] = fold(proj[:, i * z.inner : (i + 1) * z.inner])
    proj_kept[0] = scratch[t]
    proj_kept[1] = scratch[t ^ 1]
    out[...] = rows_of([kept[...] + read(received), scratch[t ^ 2], scratch[t ^ 3]]).astype(LOW)


def sum_rows_kernel(z, own, received, small, qv, *refs):
    if z.direct:
        proj_kept, out, vec, proj_own = refs
    else:
        out, vec = refs
    arrived = read(received)
    total = read(own)[: z.padded] + arrived[: z.padded]
    if z.direct:
        tail = arrived[z.padded :]
        proj_own[...] = proj_kept[0] + tail[: z.tail]
        out[...] = rows_of([total, proj_kept[1] + tail[z.tail :]]).astype(LOW)
    else:
        out[...] = total.astype(LOW)
    vec[...] = jnp.zeros(vec.shape, F32)
    vec[:6, :] = total[z.half : z.half + 6]
    vec[8:9, : z.ff] = small[6:7, : z.ff]
    vec[9:10, : 3 * z.inner] = qv[...]


def cross_kernel(kept, received, own, out):
    n = kept.shape[2]
    own[...] = kept[0] + received[0, :, :n].astype(F32)
    out[...] = (kept[1] + received[1, :, :n].astype(F32)).astype(LOW)


def cross_qkv_kernel(z, kept, received, small, own, out):
    own[...] = kept[0] + received[0].astype(F32)
    out[: z.chunk, :] = (kept[1] + received[1].astype(F32)).astype(LOW)
    out[z.chunk :, :] = small[...].astype(LOW)


def small_kernel(z, vec, near, cross, far, own, scratch):
    c, b = lax.axis_index("ctx"), lax.axis_index("fsdp")
    vectors = vec[...]
    up = rows_of([vectors[8:9, i * HD : (i + 1) * HD] for i in range(z.ff // HD)])
    pieces = []
    for h in range(z.heads):
        pieces.append(vectors[9:10, h * HD : (h + 1) * HD])
        pieces.append(vectors[9:10, 2 * z.inner + h * HD : 2 * z.inner + (h + 1) * HD])
    qv_rows = rows_of(pieces)
    scratch[...] = jnp.zeros(scratch.shape, F32)
    w = HD // 4
    for i in range(4):
        scratch[i, :8, : z.shard] = vectors[:8, i * z.shard : (i + 1) * z.shard]
        scratch[i, : z.ff // HD, UP_AT : UP_AT + w] = up[:, i * w : (i + 1) * w]
        scratch[i, : 2 * z.heads, QV_AT : QV_AT + w] = qv_rows[:, i * w : (i + 1) * w]
    near[...] = scratch[b ^ (1 + c)].astype(LOW)
    cross[...] = scratch[b ^ (2 - c)]
    far[...] = scratch[b ^ 3].astype(LOW)
    own[...] = scratch[b]


def halves_of(z, own, received):
    h = row_half(lax.axis_index("tp"))
    return jnp.where(h == 0, own, received), jnp.where(h == 0, received, own)


def swap_kernel(z, out_own, out_in, in_own, in_in, *refs):
    n = z.padded
    pad = jnp.zeros((z.pad, z.width), F32)
    out_mine, out_theirs = halves_of(z, read(out_own), read(out_in))
    arrived = read(in_in)
    in_mine, in_theirs = halves_of(z, read(in_own)[:n], arrived[:n])
    theirs = [out_theirs, pad, in_theirs]
    if z.direct:
        proj_own, mine, sent, proj = refs
        total = proj_own[...] + arrived[n:]
        proj[...] = total
        theirs.append(total)
    else:
        mine, sent = refs
    mine[0] = rows_of([out_mine, pad])
    mine[1] = in_mine
    sent[...] = rows_of(theirs).astype(LOW)


def last_kernel(z, feed, feed_in, qkv, qkv_in, small, near, far, feed_total, feed_sent, qkv_total, qkv_sent):
    value = feed[...] + read(feed_in)
    feed_total[...] = value
    feed_sent[...] = value.astype(LOW)
    value = qkv[...] + qkv_in[: z.chunk, :].astype(F32)
    tail = small[...] + read(near) + read(far) + qkv_in[z.chunk :, :].astype(F32)
    for out, kind in ((qkv_total, F32), (qkv_sent, LOW)):
        out[: z.chunk, :] = value.astype(kind)
        out[z.chunk :, :] = tail.astype(kind)


def qkv_final_kernel(z, own, theirs, qkv, up, qv, *vectors):
    both = by_half(own[: z.chunk, :], theirs[: z.chunk, :].astype(F32))
    for i in range(3):
        qkv[i] = both[:, i * z.inner : (i + 1) * z.inner]
    tail = own[z.chunk :, :] + theirs[z.chunk :, :].astype(F32)
    w = HD // 4
    up[...] = tail[: z.ff // HD, UP_AT : UP_AT + w]
    for h in range(z.heads):
        qv[h] = tail[2 * h : 2 * h + 2, QV_AT : QV_AT + w]
    for i, v in enumerate(vectors):
        v[...] = tail[i : i + 1, : z.shard].reshape(z.shard)


def place_kernel(z, mine, theirs, out, *scratch):
    c = lax.axis_index("ctx")
    target = scratch[0] if scratch else out
    mine, theirs = mine[: z.half], theirs[: z.half]
    target[:, 0, :] = jnp.where(c == 0, mine, theirs)
    target[:, 1, :] = jnp.where(c == 0, theirs, mine)
    if scratch:
        out[...] = target[...].astype(out.dtype)


def final_kernel(z, mine, theirs, *refs):
    arrived = read(theirs)
    if z.direct:
        proj_own, feed_own, feed_in, qkv_own, qkv_in, output, input_grad, proj, up, down, *rest = refs
        other = arrived[2 * z.padded :]
        proj[...] = by_half(unfold(z, proj_own[...]), unfold(z, other)).T
        feed_final_kernel(z, feed_own, feed_in, up, down)
        qkv_final_kernel(z, qkv_own, qkv_in, *rest[:-1])
        scratch = rest[-1]
    else:
        output, input_grad, scratch = refs
    place_kernel(z, mine[1], arrived[z.padded : 2 * z.padded], input_grad)
    place_kernel(z, mine[0], arrived[: z.padded], output, scratch)


def build(nf, nc, nt):
    def local(
        inputs,
        norm1_gain,
        norm1_bias,
        qkv_weight,
        qv_bias,
        proj_weight,
        proj_bias,
        norm2_gain,
        norm2_bias,
        fc1_weight,
        fc1_bias,
        fc2_weight,
        fc2_bias,
        cotangent,
    ):
        z = Sizes(nf, nt, inputs, qv_bias, fc1_weight)
        part = functools.partial
        rows, width, inner, ff, chunk = z.rows, z.width, z.inner, z.ff, z.chunk
        f = lax.axis_index("fsdp")
        tie = lax.optimization_barrier

        def other_core(value):
            return lax.ppermute(value, "ctx", [(0, 1), (1, 0)])

        def to_tp(value, k):
            return lax.ppermute(value, "tp", [(i, i ^ k) for i in range(nt)])

        def to_far(value):
            return lax.ppermute(value, "fsdp", [(i, i ^ 3) for i in range(nf)])

        def neighbours(value, order):
            pairs = [(2 * i + c, 2 * (i ^ order[c]) + c) for i in range(nf) for c in range(2)]
            return lax.ppermute(value, ("fsdp", "ctx"), pairs)

        def to_near(value):
            return neighbours(value, (1, 2))

        def to_cross(value):
            return neighbours(value, (2, 1))

        def proj_near(value):
            pairs = [(c * nt + i, c * nt + (i ^ (1 + 2 * c))) for i in range(nt) for c in range(2)]
            return lax.ppermute(value, ("ctx", "tp"), pairs)

        def pair_of(first, second):
            return call(pair_kernel, [shape((2,) + first.shape, LOW)], [first, second], name="pair")[0]

        qkv3 = qkv_weight.transpose(1, 0, 2)
        down_t = fc2_weight.T
        qv3 = qv_bias.transpose(1, 0, 2)
        x_raw, cot_raw = inputs.transpose(1, 0, 2), cotangent.transpose(1, 0, 2)
        vectors = [norm1_gain, norm1_bias, proj_bias, norm2_gain, norm2_bias, fc2_bias]

        x_recv = other_core(x_raw)
        cot_recv = None if z.direct else other_core(cot_raw)
        def frames(x_recv, cot_mine, cot_recv):
            stream, normal_one, inverse_one, normal_their = call(
                part(frame_kernel, z),
                [shape((rows, width), LOW), shape((rows, width), F32), shape((rows, 128), F32), shape((rows, width), F32)],
                [x_raw, x_recv],
                name="frame",
            )
            (cot,) = call(part(cot_kernel, z), [shape((2, rows, width), LOW)], [cot_mine, cot_recv], name="cotangent")
            return stream, normal_one, inverse_one, normal_their, cot

        if z.direct:
            sources = [qkv3, proj_weight, fc1_bias, qv3] + vectors
            near, far, proj_t, proj_half = call(
                part(pack_kernel, z),
                [
                    shape((z.part + EXTRA, 3 * inner), LOW),
                    shape((chunk + EXTRA, 3 * inner), LOW),
                    shape((z.part + 104, inner), LOW),
                    shape((chunk, inner), LOW),
                ],
                sources,
                [pltpu.VMEM(s.shape, s.dtype) for s in sources] + [pltpu.SemaphoreType.DMA((len(sources),))],
                name="pack",
                mib=56,
                in_specs=[ANY] * len(sources),
            )
            near, far, proj_t, proj_half, x_recv, cot_raw = tie((near, far, proj_t, proj_half, x_recv, cot_raw))
            cot_recv = other_core(cot_raw)
            got = [to_near(near), to_far(far)]
            proj_got = [proj_near(proj_t), to_tp(proj_half, 2)]
            feed_own, feed_rest = call(
                part(stage_kernel, z),
                [shape((z.part, z.early), LOW), shape((z.part, 2 * ff - z.early), LOW)],
                [fc1_weight, down_t],
                [pltpu.VMEM((z.part, ff), LOW)] * 2 + [pltpu.SemaphoreType.DMA((2,))],
                name="stage",
                mib=20,
                in_specs=[ANY] * 2,
            )
            stream, normal_one, inverse_one, normal_their, cot = frames(x_recv, cot_raw, cot_recv)
            feed_in = to_near(feed_own)
            got, proj_got, feed_rest, stream, normal_one, inverse_one, normal_their, cot = tie(
                (got, proj_got, feed_rest, stream, normal_one, inverse_one, normal_their, cot)
            )
            shared = [other_core(g) for g in got]
            qkv_in = [near, got[0], shared[0], got[1], shared[1]]
            (rest_near,) = call(
                part(pack_rest_kernel, z),
                [shape((z.part, z.cols - z.early), LOW)],
                [feed_rest, proj_t, proj_got[0], other_core(proj_got[0]), proj_got[1], other_core(proj_got[1])],
                [pltpu.VMEM((nt, z.part, inner), F32)],
                name="pack_rest",
            )
            near_in = to_near(rest_near)
            far_in = []
            for value in (feed_in, near_in):
                (half,) = call(part(cut_kernel, z), [shape((chunk, value.shape[1]), LOW)], [value], name="cut")
                far_in.append(to_cross(half))
        else:
            stream, normal_one, inverse_one, normal_their, cot = frames(x_recv, cot_raw, cot_recv)
            whole = lax.all_gather(qkv3, "fsdp", axis=1, tiled=True)
            whole = whole.transpose(1, 0, 2).reshape(4, z.part, 3 * inner)
            vec = jnp.stack(vectors + [vectors[0]] * 2).astype(F32)
            qv_rows = qv3.reshape(2 * z.heads, -1).astype(F32)
            gathered = [lax.all_gather(v, "fsdp", axis=1, tiled=True) for v in (vec, fc1_bias.astype(F32), qv_rows)]
            qkv_in = [whole] + gathered
            proj_t = proj_weight.T
            rest = jnp.concatenate([fc1_weight, down_t, lax.all_gather(proj_t, "tp", axis=1, tiled=True)], 1)
            rest_in = [lax.all_gather(rest, "fsdp", axis=0, tiled=True).reshape(4, z.part, z.cols)]

        small, w_qkv, normed_one, act, attended, soft = call(
            part(attend_kernel, z),
            [
                shape((8, width), F32),
                shape((4, z.part, 3 * inner), LOW),
                shape((rows, width), LOW),
                shape((3, rows, inner), LOW),
                shape((z.dense, 128), LOW),
                shape((z.heads, rows, rows), F32),
            ],
            qkv_in + [normal_one],
            [pltpu.VMEM((4, EXTRA, 3 * inner), F32)] if z.direct else [],
            name="attend",
        )
        att_one = to_tp(attended, 3)
        (att_two,) = call(pair_kernel, [shape((2, z.dense + 16, 128), LOW)], [attended, att_one], name="pair")
        att_two = to_tp(att_two, 1)
        if z.direct:
            att_two, far_in = tie((att_two, far_in))
            rest_in = [feed_own, feed_in, other_core(feed_in), rest_near, near_in, other_core(near_in)]
            rest_in += [far_in[0], other_core(far_in[0]), far_in[1], other_core(far_in[1])]

        (w_rest, middle, acts, part_middle, own_att, small_two, *att_sends) = (
            call(
                part(feed_kernel, z),
                [
                    shape((4, z.part, z.cols), LOW),
                    shape((rows, width), F32),
                    shape((5, rows, width), LOW),
                    shape((rows, width), F32),
                    shape((rows, inner), F32),
                    shape((8, width), F32),
                ]
                + [shape((z.dense, 128), LOW)] * (nt - 1),
                rest_in + [attended, att_one, att_two, stream, cot, small],
                [pltpu.VMEM((nt, rows, inner), F32)],
                name="feed",
            )
        )
        att_got = [to_tp(att_sends[k - 1], k) for k in (3, 2, 1)]
        acts_their = other_core(acts)
        kept_rows = chunk if z.direct else z.part
        (keep,) = call(
            part(feed_grad_kernel, z),
            [shape((4, kept_rows, 2 * ff), F32)],
            [acts, acts_their, cot],
            name="feed_grad",
        )
        proj_own, *sends = call(
            part(proj_grad_kernel, z),
            [shape((chunk, nt * inner), F32)] + [shape((chunk, nt * inner), LOW)] * 3
            if z.direct
            else [shape((4, z.part, nt * inner), F32)],
            [acts, acts_their],
            [pltpu.VMEM((4, chunk, nt * inner), F32)] if z.direct else [],
            name="proj_grad",
        )
        proj_full = proj_own
        out_kept, out_sent = call(
            part(down_kernel, z),
            [shape((z.half, width), F32), shape((z.half, width), LOW)],
            [acts, w_rest],
            [pltpu.VMEM((rows, width), F32)],
            name="down",
        )
        out_one = to_tp(out_sent, 1)
        if z.direct:
            grad_sent, grad_kept = call(
                split_kernel,
                [shape((2, chunk, z.wide), LOW), shape((2, chunk, 2 * ff), F32)],
                [keep],
                name="split",
            )
            grad_in = to_near(grad_sent)
            att_got, out_one, grad_kept, proj_own, sends = tie((att_got, out_one, grad_kept, proj_own, sends))
            proj_in = [lax.ppermute(sends[k - 1], "fsdp", [(i, i ^ k) for i in range(nf)]) for k in (3, 1)]
        (out_low,) = call(add_low_kernel, [shape((z.half, width), LOW)], [out_kept, out_one], name="out_pair")
        out_two = to_tp(out_low, 2)

        grads, qv_sum, in_kept, in_sent = call(
            part(back_kernel, z),
            [
                shape((rows, 3 * inner), LOW),
                shape((1, 3 * inner), F32),
                shape((z.padded, width), F32),
                shape((z.padded, width), LOW),
            ],
            [own_att] + att_got + [act, soft, w_qkv, normal_one, inverse_one, part_middle, small, small_two],
            [pltpu.VMEM((rows, width), F32)],
            name="back",
        )
        in_one = to_tp(in_sent, 1)
        grads_their = other_core(grads)
        if z.direct:
            grads_their, last_send = tie((grads_their, sends[1]))
            proj_in.append(lax.ppermute(last_send, "fsdp", [(i, i ^ 2) for i in range(nf)]))
        (keep_qkv,) = call(
            part(qkv_grad_kernel, z),
            [shape((4, kept_rows, 3 * inner), F32)],
            [normed_one, grads, normal_their, grads_their, small],
            name="qkv_grad",
        )
        extra = z.tail if z.direct else 0
        if z.direct:
            in_one, out_two, proj_in, keep_qkv = tie((in_one, out_two, proj_in, keep_qkv))
            in_low, proj_kept = call(
                part(in_pair_kernel, z),
                [shape((z.padded + 2 * extra, width), LOW), shape((2, extra, width), F32)],
                [in_kept, in_one, proj_own] + proj_in,
                [pltpu.VMEM((nt, extra, width), F32)],
                name="in_pair",
            )
            qkv_sent, qkv_kept = call(
                split_kernel,
                [shape((2, chunk, 3 * inner), LOW), shape((2, chunk, 3 * inner), F32)],
                [keep_qkv],
                name="split_qkv",
            )
            qkv_in = to_near(qkv_sent)
        else:
            (in_low,) = call(add_low_kernel, [shape((z.padded, width), LOW)], [in_kept, in_one], name="in_pair")
        in_two = to_tp(in_low, 2)
        (out_low,) = call(
            part(out_total_kernel, z), [shape((z.half, width), LOW)], [out_low, out_two, middle, small], name="out_total"
        )
        out_in = to_tp(out_low, 1)
        if z.direct:
            grad_own, cross = call(
                cross_kernel,
                [shape((chunk, 2 * ff), F32), shape((chunk, 2 * ff), LOW)],
                [grad_kept, grad_in],
                name="cross",
            )
            cross = to_cross(cross)
            in_two, out_in, qkv_in = tie((in_two, out_in, qkv_in))
        in_low, vec, *proj_own = call(
            part(sum_rows_kernel, z),
            [shape((z.padded + extra, width), LOW), shape((VEC_ROWS, width), F32)]
            + ([shape((extra, width), F32)] if extra else []),
            [in_low, in_two, small_two, qv_sum] + ([proj_kept] if extra else []),
            name="sum_rows",
        )
        in_in = to_tp(in_low, 1)
        proj_all = []
        if z.direct:
            near, side, far, small_own = call(
                part(small_kernel, z),
                [shape((EXTRA, 3 * inner), LOW), shape((EXTRA, 3 * inner), F32)] * 2,
                [vec],
                [pltpu.VMEM((4, EXTRA, 3 * inner), F32)],
                name="small",
            )
            qkv_own, qkv_sent = call(
                part(cross_qkv_kernel, z),
                [shape((chunk, 3 * inner), F32), shape((chunk + EXTRA, 3 * inner), LOW)],
                [qkv_kept, qkv_in, side],
                name="cross_qkv",
            )
            qkv_in = to_cross(qkv_sent)
            far = to_far(far)
            near = to_near(near)
            in_in, cross, qkv_in, near, far = tie((in_in, cross, qkv_in, near, far))
            proj_all = proj_own
            feed_own, feed_sent, qkv_own, qkv_sent = call(
                part(last_kernel, z),
                [
                    shape((chunk, 2 * ff), F32),
                    shape((chunk, 2 * ff), LOW),
                    shape((chunk + EXTRA, 3 * inner), F32),
                    shape((chunk + EXTRA, 3 * inner), LOW),
                ],
                [grad_own, cross, qkv_own, qkv_in, small_own, near, far],
                name="last",
            )
            feed_in, qkv_in = other_core(feed_sent), other_core(qkv_sent)
        mine, theirs, *proj_own = call(
            part(swap_kernel, z),
            [shape((2, z.padded, width), F32), shape((rows + (z.tail if proj_all else 0), width), LOW)]
            + ([shape((z.tail, width), F32)] if proj_all else []),
            [out_low, out_in, in_low, in_in] + proj_all,
            name="swap",
        )
        theirs = other_core(theirs)
        results = [shape((z.half, 2, width), LOW), shape((z.half, 2, width), F32)]
        scratch = [pltpu.VMEM((z.half, 2, width), F32)]
        if z.direct:
            output, input_grad, proj_grad, fc1_grad, fc2_grad, qkv_grad, up_grad, qv_grad, *vec_grads = call(
                part(final_kernel, z),
                results
                + [
                    shape((inner, z.shard), F32),
                    shape((z.shard, ff), F32),
                    shape((z.shard, ff), F32),
                    shape((3, z.shard, inner), F32),
                    shape(fc1_bias.shape, F32),
                    shape(qv3.shape, F32),
                ]
                + [shape((z.shard,), F32)] * 6,
                [mine, theirs, proj_own[0], feed_own, feed_in, qkv_own, qkv_in],
                scratch,
                name="final",
            )
        else:
            output, input_grad = call(part(final_kernel, z), results, [mine, theirs], scratch, name="final")

            def scatter(value):
                value = value.reshape(width, -1).astype(LOW)
                return lax.psum_scatter(value, "fsdp", scatter_dimension=0, tiled=True).astype(F32)

            total = scatter(keep)
            fc1_grad, fc2_grad = total[:, :ff], total[:, ff:]
            qkv_grad = scatter(keep_qkv).reshape(z.shard, 3, inner).transpose(1, 0, 2)
            proj_grad = scatter(proj_full).astype(LOW)
            proj_grad = lax.psum_scatter(proj_grad, "tp", scatter_dimension=1, tiled=True).astype(F32).T

            def own_columns(value):
                value = lax.psum(value, ("fsdp", "ctx"))
                return lax.dynamic_slice_in_dim(value, f * (value.shape[1] // nf), value.shape[1] // nf, 1)

            vec_grads = own_columns(vec[:6])
            up_grad = own_columns(vec[8, :ff].reshape(-1, HD))
            qv_grad = vec[9, : 3 * inner].reshape(3, z.heads, HD)[0::2].transpose(1, 0, 2)
            qv_grad = own_columns(qv_grad.reshape(2 * z.heads, HD)).reshape(qv3.shape)
        return (
            output.transpose(1, 0, 2),
            input_grad.transpose(1, 0, 2),
            vec_grads[0],
            vec_grads[1],
            qkv_grad.transpose(1, 0, 2),
            qv_grad.transpose(1, 0, 2),
            proj_grad,
            vec_grads[2],
            vec_grads[3],
            vec_grads[4],
            fc1_grad,
            up_grad,
            fc2_grad.T,
            vec_grads[5],
        )

    return local


def solution(mesh):
    sizes = mesh.shape
    return jax.shard_map(
        build(sizes["fsdp"], sizes["ctx"], sizes["tp"]),
        mesh=mesh,
        in_specs=(
            P("fsdp", "ctx", None),
            P("fsdp"),
            P("fsdp"),
            P("fsdp", None, "tp"),
            P(None, "tp", "fsdp"),
            P("tp", "fsdp"),
            P("fsdp"),
            P("fsdp"),
            P("fsdp"),
            P("fsdp", "tp"),
            P("tp", "fsdp"),
            P("tp", "fsdp"),
            P("fsdp"),
            P("fsdp", "ctx", None),
        ),
        out_specs=(
            P("fsdp", "ctx", None),
            P("fsdp", "ctx", None),
            P("fsdp"),
            P("fsdp"),
            P("fsdp", None, "tp"),
            P(None, "tp", "fsdp"),
            P("tp", "fsdp"),
            P("fsdp"),
            P("fsdp"),
            P("fsdp"),
            P("fsdp", "tp"),
            P("tp", "fsdp"),
            P("tp", "fsdp"),
            P("fsdp"),
        ),
        check_vma=False,
    )
```
